32 devices in a mesh: dp: 8 (over z, y), seq: 4 (over x, core).
Axes of the slice: x: 2, y: 2, z: 4, core: 2. Of those that a mesh axis runs over, the one named last changes fastest.
Arguments:
- tokens: bfloat16 [8, 1024, 1472], P('dp', 'seq'), may hold values from -6 to 6
- cotangent: bfloat16 [8, 1024, 1472], P('dp', 'seq'), may hold values from -6 to 6
- lengths: int32 [8], P('dp'), may hold values from 769 to 1024, as said below
- w_query: float32 [1472, 384], P('dp', 'seq'), may hold values from -0.0390625 to 0.0390625
- w_key_value: float32 [2, 1472, 384], P(None, 'dp', 'seq'), may hold values from -0.15625 to 0.15625
- w_output: float32 [1472, 384], P('dp', 'seq'), may hold values from -1.25 to 1.25
- w_gate_up: float32 [2, 1472, 3584], P(None, 'dp', 'seq'), may hold values from -0.15625 to 0.15625
- w_down: float32 [1472, 3584], P('dp', 'seq'), may hold values from -0.09375 to 0.09375
- norm_gains: float32 [2, 1472], P(None, 'dp'), may hold values from 0.1 to 1.9
- position_bias: float32 [32, 6], P('dp'), may hold values from -4 to 4
Outputs:
- layer_output: bfloat16 [8, 1024, 1472], P('dp', 'seq')
- input_grad: bfloat16 [8, 1024, 1472], P('dp', 'seq')
- query_grad: float32 [1472, 384], P('dp', 'seq')
- key_value_grad: float32 [2, 1472, 384], P(None, 'dp', 'seq')
- output_grad: float32 [1472, 384], P('dp', 'seq')
- gate_up_grad: float32 [2, 1472, 3584], P(None, 'dp', 'seq')
- down_grad: float32 [1472, 3584], P('dp', 'seq')
- gains_grad: float32 [2, 1472], P(None, 'dp')
- bias_grad: float32 [32, 6], P('dp')
The draws below stay inside these ranges and needn't reach their ends.
Inputs may be any that keep to these rules, and one draw needn't show every extreme that they name: Row r's first lengths[r] bytes are real and the rest are padding; some row is full and some row is exactly 769 long.
All inputs are finite; a program needn't handle non-finite values.
Results may differ from the reference program's by a relative error of at most 0.023.
The reference program's roundings to bfloat16 on the way count: a program that leaves them out, or rounds other values in their place, can miss the bound.
Values may be sent and summed in bfloat16 or wider, within the bound.
A program may use at most 320 MiB of HBM per device.

```python
import jax
import jax.numpy as jnp
from jax import lax

D = 1472
HEADS = 6
FF = 3584
BUCKETS = 32
TOK_DEV = 256
INNER = 384
LEN = 1024
ROWS = 8


def draw_lengths(key, part):
    key = jax.random.fold_in(key, 7)
    first_key, second_key, third_key = jax.random.split(key, 3)
    cuts = jax.random.randint(first_key, (ROWS,), 0, TOK_DEV)
    full_row = jax.random.randint(second_key, (), 0, ROWS)
    short_row = (full_row + 1 + jax.random.randint(third_key, (), 0, ROWS - 1)) % ROWS
    positions = jnp.arange(ROWS)
    cuts = jnp.where(positions == full_row, 0, cuts)
    cuts = jnp.where(positions == short_row, TOK_DEV - 1, cuts)
    return (LEN - cuts).astype(jnp.int32)


def shard_levels(rng, dims, pieces, smallest, largest):
    def one(axis_at, parts):
        draws = jax.random.uniform(jax.random.fold_in(jax.random.fold_in(rng, 6), axis_at), (parts,), jnp.float32, smallest / len(pieces), largest / len(pieces))
        return jnp.repeat(jnp.exp(draws), dims[axis_at] // parts).reshape((-1,) + (1,) * (len(dims) - axis_at - 1))

    level = one(*pieces[0])
    for cut in pieces[1:]:
        level = level * one(*cut)
    return level


def centred(own_key, extent, deviation, bound, pieces=(), kind=jnp.bfloat16):
    gain = shard_levels(own_key, extent, pieces, -0.22, 0.18) if pieces else 1.0
    entries = jax.random.normal(own_key, extent, jnp.float32) * deviation * gain
    return jnp.minimum(jnp.maximum(entries, -bound), bound).astype(kind)


def setup_inputs(seed: int = 0) -> dict:
    keys = jax.random.split(jax.random.key(seed), 11)
    return {
        "tokens": centred(keys[0], (ROWS, LEN, D), 1.0, 6.0, ((0, 8), (1, 4))),
        "cotangent": centred(keys[1], (ROWS, LEN, D), 1.0, 6.0, ((0, 8), (1, 4))),
        "lengths": draw_lengths(jax.random.fold_in(keys[10], 71), 0),
        "w_query": centred(keys[3], (D, INNER), (D * 16) ** -0.5, 0.0390625, ((0, 8), (1, 4)), jnp.float32),
        "w_key_value": centred(keys[4], (2, D, INNER), D ** -0.5, 0.15625, ((1, 8), (2, 4)), jnp.float32),
        "w_output": centred(keys[5], (D, INNER), (INNER // 16) ** -0.5, 1.25, ((0, 8), (1, 4)), jnp.float32),
        "w_gate_up": centred(keys[6], (2, D, FF), D ** -0.5, 0.15625, ((1, 8), (2, 4)), jnp.float32),
        "w_down": centred(keys[7], (D, FF), FF ** -0.5, 0.09375, ((0, 8), (1, 4)), jnp.float32),
        "norm_gains": jnp.clip(1.0 + 0.18 * jax.random.normal(keys[8], (2, D), jnp.float32), 0.1, 1.9),
        "position_bias": centred(keys[9], (BUCKETS, HEADS), 1.0, 4.0, ((0, 8),), jnp.float32),
    }


@jax.custom_vjp
def low(v):
    return lax.optimization_barrier(v.astype(jnp.bfloat16)).astype(jnp.float32)

@jax.custom_vjp
def low_back(v):
    return v

def low_keep(v):
    return (low(v), None)

def low_pass(kept, grad):
    return (grad,)

def back_keep(v):
    return (v, None)

def back_low(kept, grad):
    return (low(grad),)
low.defvjp(low_keep, low_pass)
low_back.defvjp(back_keep, back_low)
NEGATIVE = -1e+30
EPSILON = 1e-06
LIMITS = (12, 16, 23, 32, 46, 64, 91)
PRECISE = lax.Precision.HIGHEST

def bucket_ids(offsets):
    distance = jnp.abs(offsets)
    larger = 8 + sum(((distance >= threshold).astype(jnp.int32) for threshold in LIMITS))
    nearby = jnp.where(distance < 8, distance, larger)
    return (jnp.where(offsets > 0, 16, 0) + nearby).astype(jnp.int32)

def norm_scale(values, gain_vector):
    return values * lax.rsqrt(lax.optimization_barrier(jnp.mean(values * values, axis=-1, keepdims=True)) + EPSILON) * gain_vector

def layer(inputs, length, w_query, w_key_value, w_output, w_gate_up, w_down, norm_gains, position_bias):
    query_w = low(w_query)
    keyval_w = low(w_key_value)
    output_w = low(w_output)
    gateup_w = low(w_gate_up)
    down_w = low(w_down)
    gain_w = low(norm_gains)
    table_w = low(position_bias)
    normed = low(norm_scale(inputs, gain_w[0]))
    queries = low_back(low(jnp.dot(normed, query_w, precision=PRECISE)))
    keys_all = low_back(low(jnp.dot(normed, keyval_w[0], precision=PRECISE)))
    values_all = low_back(low(jnp.dot(normed, keyval_w[1], precision=PRECISE)))
    row_total = inputs.shape[0]
    head_count = position_bias.shape[1]
    head_dim = queries.shape[1] // head_count
    key_pos = jnp.arange(row_total, dtype=jnp.int32)
    key_valid = key_pos < length
    key_heads = keys_all.reshape(row_total, head_count, head_dim)
    value_heads = values_all.reshape(row_total, head_count, head_dim)
    table_heads = table_w.T
    block_rows = 512 if row_total % 512 == 0 else row_total

    def attend(pair_items):
        query_block, block_start = pair_items
        query_pos = block_start + jnp.arange(block_rows, dtype=jnp.int32)
        buckets = bucket_ids(key_pos[None, :] - query_pos[:, None])
        score_bias = jnp.take(table_heads, buckets, axis=1)
        scores = jnp.einsum('thc,khc->htk', query_block.reshape(block_rows, head_count, head_dim), key_heads, precision=PRECISE) + score_bias
        scores = jnp.where(key_valid[None, None, :], low_back(scores), NEGATIVE)
        probs_low = low(jax.nn.softmax(scores, axis=-1))
        mixed_heads = jnp.einsum('htk,khc->thc', probs_low, value_heads, precision=PRECISE)
        return low_back(low(mixed_heads.reshape(block_rows, head_count * head_dim)))
    block_starts = (jnp.arange(row_total // block_rows) * block_rows).astype(jnp.int32)
    query_blocks = queries.reshape(row_total // block_rows, block_rows, head_count * head_dim)
    mixed_all = lax.map(jax.checkpoint(attend), (query_blocks, block_starts)).reshape(row_total, head_count * head_dim)
    attended = low_back(jnp.einsum('tc,dc->td', mixed_all, output_w, precision=PRECISE))
    hidden_one = inputs + attended
    normed_two = low(norm_scale(hidden_one, gain_w[1]))
    gate_value = low_back(jnp.dot(normed_two, gateup_w[0], precision=PRECISE))
    upward = low_back(jnp.dot(normed_two, gateup_w[1], precision=PRECISE))
    activated = low(jax.nn.gelu(gate_value, approximate=True) * upward)
    return hidden_one + low_back(jnp.einsum('tf,df->td', activated, down_w, precision=PRECISE))

def reference(tokens, cotangent, lengths, w_query, w_key_value, w_output, w_gate_up, w_down, norm_gains, position_bias):
    weights = (w_query, w_key_value, w_output, w_gate_up, w_down, norm_gains, position_bias)

    def row_step(totals, row_items):
        inputs, incoming, length = row_items

        def forward(values, *params):
            return layer(values, length, *params)
        result, pull = jax.vjp(forward, inputs.astype(jnp.float32), *weights)
        gradients = pull(incoming.astype(jnp.float32))
        totals = tuple((acc + grad for acc, grad in zip(totals, gradients[1:])))
        return (totals, (result.astype(jnp.bfloat16), gradients[0].astype(jnp.bfloat16)))
    initial = tuple((jnp.zeros_like(weight) for weight in weights))
    totals, (outputs, input_grads) = lax.scan(row_step, initial, (tokens, cotangent, lengths))
    return (outputs, input_grads, totals[0], totals[1], totals[2], totals[3], totals[4], totals[5], totals[6])
```

```python
import functools
import jax
import jax.numpy as jnp
from jax import lax
from jax.experimental import pallas as pl
from jax.experimental.pallas import tpu as pltpu

from jax.sharding import PartitionSpec as P

MESH = pl.DeviceIdType.MESH
BF = jnp.bfloat16
F32 = jnp.float32


class Geo:
    def __init__(self, dp, seq, rows, ff, inner4):
        self.dp, self.seq = dp, seq
        self.B, self.A, self.X = 2, dp // 2, seq // 2
        self.R, self.F, self.I4 = rows, ff, inner4
        self.NH = 2 if rows % 32 == 0 else 1
        self.RH = rows // self.NH
        self.NP = 3 * self.NH
        self.NZ = 2 * (self.A - 1)
        self.NY = 2 * self.A - 1


class Place:
    def __init__(self, geo):
        d, s = lax.axis_index("dp"), lax.axis_index("seq")
        self.d, self.s = d, s
        self.z, self.y = d // 2, d % 2
        self.x, self.c = s // 2, s % 2

    def dev(self, z=None, y=None, x=None, c=None):
        z = self.z if z is None else z
        y = self.y if y is None else y
        x = self.x if x is None else x
        c = self.c if c is None else c
        return (z * 2 + y, x * 2 + c)


def remote(src, dst, ss, rs, dev):
    return pltpu.make_async_remote_copy(
        src_ref=src, dst_ref=dst, send_sem=ss, recv_sem=rs, device_id=dev, device_id_type=MESH
    )


def loop(n, body):
    def step(i, carry):
        body(i)
        return carry

    lax.fori_loop(0, n, step, 0)


def enter(geo, me):
    bar = pltpu.get_barrier_semaphore()

    def greet(dev):
        pl.semaphore_signal(bar, 1, device_id=dev, device_id_type=MESH)

    greet(me.dev(y=1 - me.y))
    greet(me.dev(c=1 - me.c))
    for k in range(1, geo.X):
        greet(me.dev(x=lax.rem(me.x + k, geo.X)))

    @pl.when(me.z > 0)
    def _():
        greet(me.dev(z=me.z - 1))

    @pl.when(me.z < geo.A - 1)
    def _():
        greet(me.dev(z=me.z + 1))

    count = 2 + (geo.X - 1) + (me.z > 0).astype(jnp.int32) + (me.z < geo.A - 1).astype(jnp.int32)
    pl.semaphore_wait(bar, count)


class LineGather:
    def __init__(self, geo, me, own, held, zs, zr, ys, yr):
        self.geo, self.me, self.own, self.held = geo, me, own, held
        self.zs, self.zr, self.ys, self.yr = zs, zr, ys, yr

    def zcopy(self, way, r, p):
        me, geo = self.me, self.geo
        q = me.z - (r - 1) if way == 0 else me.z + (r - 1)
        to = me.z + 1 if way == 0 else me.z - 1
        valid = (me.z < geo.A - 1) & (q >= 0) if way == 0 else (me.z > 0) & (q <= geo.A - 1)
        g = q * 2 + me.y
        src = self.own(p) if r == 1 else self.held(p, g)
        slot = way * (geo.A - 1) + r - 1
        copy = remote(src, self.held(p, g), self.zs.at[slot, p], self.zr.at[slot, p], me.dev(z=to))
        return copy, valid

    def zarrive(self, way, r, p):
        me, geo = self.me, self.geo
        q = me.z - r if way == 0 else me.z + r
        valid = (q >= 0) if way == 0 else (q <= geo.A - 1)
        slot = way * (geo.A - 1) + r - 1
        here = self.held(p, q * 2 + me.y)
        copy = remote(here, here, self.zs.at[slot, p], self.zr.at[slot, p], me.dev(y=1 - me.y))
        return copy, valid, q

    def ycopy(self, way, r, p):
        me, geo = self.me, self.geo
        if r == 0:
            q, slot, src = me.z, 0, self.own(p)
        else:
            q = me.z - r if way == 0 else me.z + r
            slot = 1 + way * (geo.A - 1) + r - 1
            src = self.held(p, q * 2 + me.y)
        copy = remote(
            src, self.held(p, q * 2 + me.y), self.ys.at[slot, p], self.yr.at[slot, p], me.dev(y=1 - me.y)
        )
        return copy

    def yarrive(self, way, r, p):
        me, geo = self.me, self.geo
        if r == 0:
            q, slot = me.z, 0
        else:
            q = me.z - r if way == 0 else me.z + r
            slot = 1 + way * (geo.A - 1) + r - 1
        here = self.held(p, q * 2 + 1 - me.y)
        copy = remote(here, here, self.ys.at[slot, p], self.yr.at[slot, p], me.dev(y=1 - me.y))
        return copy, q

    def valid(self, way, r):
        q = self.me.z - r if way == 0 else self.me.z + r
        return (q >= 0) if way == 0 else (q <= self.geo.A - 1)

    def begin(self, p):
        self.ycopy(0, 0, p).start()
        for way in (0, 1):
            copy, valid = self.zcopy(way, 1, p)

            @pl.when(valid)
            def _():
                copy.start()

    def step(self, r, p, on_held=None):
        for way in (0, 1):
            copy, valid, q = self.zarrive(way, r, p)

            @pl.when(valid)
            def _():
                copy.wait_recv()
                if r < self.geo.A - 1:
                    onward, may = self.zcopy(way, r + 1, p)

                    @pl.when(may)
                    def _():
                        onward.start()

                self.ycopy(way, r, p).start()
                if on_held is not None:
                    on_held(q * 2 + self.me.y)

    def ystep(self, r, p, on_held=None):
        for way in (0, 1) if r else (0,):
            copy, q = self.yarrive(way, r, p)
            valid = self.valid(way, r) if r else True

            def go():
                copy.wait_recv()
                if on_held is not None:
                    on_held(q * 2 + 1 - self.me.y)

            if r:
                pl.when(valid)(go)
            else:
                go()

    def drain(self, p):
        self.ycopy(0, 0, p).wait_send()
        for r in range(1, self.geo.A):
            for way in (0, 1):
                copy, valid = self.zcopy(way, r, p)

                @pl.when(valid)
                def _():
                    copy.wait_send()

                @pl.when(self.valid(way, r))
                def _():
                    self.ycopy(way, r, p).wait_send()


class LineScatter:
    def __init__(self, geo, me, part, ybuf, zbuf, stage, zs, zr, ys, yr, finish):
        self.__dict__.update(locals())

    def turns(self):
        geo, me = self.geo, self.me
        for k in range(geo.A - 1):
            yield 0, k, geo.A - 1 - k, k < geo.A - 1 - me.z
            yield 1, k, k, k < me.z

    def slot(self, way, k):
        return way * (self.geo.A - 1) + k

    def ycopy(self, slot, t, p):
        me = self.me
        return remote(
            self.part(p, t * 2 + 1 - me.y),
            self.ybuf(p, t),
            self.ys.at[slot, p],
            self.yr.at[slot, p],
            me.dev(y=1 - me.y),
        )

    def zcopy(self, way, k, p):
        me = self.me
        to = me.z + 1 if way == 0 else me.z - 1
        slot = self.slot(way, k)
        return remote(
            self.stage(way, p, k), self.zbuf(way, p, k), self.zs.at[slot, p], self.zr.at[slot, p], me.dev(z=to)
        )

    def ysend(self, p, k):
        for way, kk, t, valid in self.turns():
            if kk == k:

                @pl.when(valid)
                def _():
                    self.ycopy(self.slot(way, kk), t, p).start()

    def ysend_own(self, p):
        self.ycopy(self.geo.NZ, self.me.z, p).start()

    def step(self, k, p):
        geo, me = self.geo, self.me
        for way, kk, t, valid in self.turns():
            if kk == k:

                @pl.when(valid)
                def _():
                    self.ycopy(self.slot(way, k), t, p).wait_recv()
                    total = self.part(p, t * 2 + me.y)[...].astype(F32) + self.ybuf(p, t)[...].astype(F32)
                    out = self.stage(way, p, k)
                    comes = me.z > 0 if way == 0 else me.z < geo.A - 1

                    @pl.when(comes)
                    def _():
                        self.zcopy(way, k, p).wait_recv()
                        out[...] = (total + self.zbuf(way, p, k)[...].astype(F32)).astype(BF)

                    @pl.when(jnp.logical_not(comes))
                    def _():
                        out[...] = total.astype(BF)

                    self.zcopy(way, k, p).start()

    def own(self, p):
        geo, me = self.geo, self.me
        self.ycopy(geo.NZ, me.z, p).wait_recv()
        total = self.part(p, me.z * 2 + me.y)[...].astype(F32) + self.ybuf(p, me.z)[...].astype(F32)
        kup = jnp.minimum(geo.A - 1 - me.z, geo.A - 2)
        kdown = jnp.minimum(me.z, geo.A - 2)

        def arrive(way, k):
            slot = way * (geo.A - 1) + k
            here = self.zbuf(way, p, k)
            remote(here, here, self.zs.at[slot, p], self.zr.at[slot, p], me.dev(y=1 - me.y)).wait_recv()
            return here[...].astype(F32)

        @pl.when(me.z == 0)
        def _():
            self.finish(p, total + arrive(1, kdown))

        @pl.when(me.z == geo.A - 1)
        def _():
            self.finish(p, total + arrive(0, kup))

        @pl.when((me.z > 0) & (me.z < geo.A - 1))
        def _():
            self.finish(p, total + arrive(0, kup) + arrive(1, kdown))

    def drain(self, p):
        for way, k, t, valid in self.turns():

            @pl.when(valid)
            def _():
                self.ycopy(self.slot(way, k), t, p).wait_send()
                self.zcopy(way, k, p).wait_send()

        self.ycopy(self.geo.NZ, self.me.z, p).wait_send()


def gather_kernel(geo, wf, wa, WF, WA, local, zs, zr, ys, yr, azs, azr, ays, ayr, xs, xr, cs, cr):
    me = Place(geo)
    R, RH, NH, dp, X = geo.R, geo.RH, geo.NH, geo.dp, geo.X
    mine = [
        pltpu.make_async_copy(wf, WF.at[:, pl.ds(pl.multiple_of(me.d * R, 16), R), :], local.at[0]),
        pltpu.make_async_copy(wa, WA.at[me.s, pl.ds(pl.multiple_of(me.d * R, 16), R), :], local.at[1]),
    ]
    for copy in mine:
        copy.start()
    enter(geo, me)

    def own_f(p):
        return wf.at[p // NH, pl.ds(pl.multiple_of((p % NH) * RH, 16), RH), :]

    def held_f(p, g):
        return WF.at[p // NH, pl.ds(pl.multiple_of(g * R + (p % NH) * RH, 16), RH), :]

    def held_a(s, g):
        return WA.at[s, pl.ds(pl.multiple_of(g * R, 16), R), :]

    ffn = LineGather(geo, me, own_f, held_f, zs, zr, ys, yr)
    att = LineGather(geo, me, lambda p: wa, lambda p, g: held_a(me.s, g), azs, azr, ays, ayr)

    def xcopy(k, g, src):
        to = lax.rem(me.x + k, X)
        return remote(src, held_a(me.s, g), xs.at[k - 1, g], xr.at[k - 1, g], me.dev(x=to))

    def xarrive(k, g):
        src_x = lax.rem(me.x - k + X, X)
        here = held_a(src_x * 2 + me.c, g)
        return remote(here, here, xs.at[k - 1, g], xr.at[k - 1, g], me.dev(c=1 - me.c)), here

    def ccopy(k, g, src, s):
        return remote(src, held_a(s, g), cs.at[k, g], cr.at[k, g], me.dev(c=1 - me.c))

    def spread(g, src=None):
        src = held_a(me.s, g) if src is None else src
        for k in range(1, X):
            xcopy(k, g, src).start()
        ccopy(0, g, src, me.s).start()

    att.begin(0)
    spread(me.d, wa)
    loop(geo.NP, ffn.begin)
    att.ystep(0, 0, spread)
    for r in range(1, geo.A):
        att.step(r, 0, spread)
        att.ystep(r, 0, spread)

    def from_x(g):
        for k in range(1, X):
            copy, here = xarrive(k, g)
            copy.wait_recv()
            ccopy(k, g, here, lax.rem(me.x - k + X, X) * 2 + me.c).start()

    loop(dp, from_x)
    for r in range(1, geo.A):
        loop(geo.NP, lambda p: ffn.step(r, p))
    for r in range(geo.A):
        loop(geo.NP, lambda p: ffn.ystep(r, p))

    def finish(g):
        for k in range(X):
            s = lax.rem(me.x - k + X, X) * 2 + 1 - me.c
            here = held_a(s, g)
            remote(here, here, cs.at[k, g], cr.at[k, g], me.dev(c=1 - me.c)).wait_recv()
            ccopy(k, g, here, s).wait_send()
            if k:
                xcopy(k, g, here).wait_send()

    loop(dp, finish)
    att.drain(0)
    loop(geo.NP, ffn.drain)
    for copy in mine:
        copy.wait()


def scatter_kernel(
    geo, gf, ga, of, oa, yb, zb, st, cb, xb, xst, pa, ayb, azb, ast,
    zs, zr, ys, yr, azs, azr, ays, ayr, xs, xr, cs, cr,
):
    me = Place(geo)
    R, RH, NH, dp, X, A = geo.R, geo.RH, geo.NH, geo.dp, geo.X, geo.A
    enter(geo, me)

    def rows(g, p):
        return pl.ds(pl.multiple_of(g * R + (p % NH) * RH, 16), RH)

    def piece(buf, i, p):
        return buf.at[i, p // NH, pl.ds(pl.multiple_of((p % NH) * RH, 16), RH), :]

    def finish_f(p, value):
        of[p // NH, pl.ds(pl.multiple_of((p % NH) * RH, 16), RH), :] = value

    ffn = LineScatter(
        geo, me,
        lambda p, g: gf.at[p // NH, rows(g, p), :],
        lambda p, t: piece(yb, t, p),
        lambda way, p, k: piece(zb, way * (A - 1) + k, p),
        lambda way, p, k: piece(st, way * (A - 1) + k, p),
        zs, zr, ys, yr, finish_f,
    )

    def block(g):
        return pl.ds(pl.multiple_of(g * R, 16), R)

    def finish_a(p, value):
        oa[...] = value

    att = LineScatter(
        geo, me,
        lambda p, g: pa.at[block(g), :],
        lambda p, t: ayb.at[t],
        lambda way, p, k: azb.at[way * (A - 1) + k],
        lambda way, p, k: ast.at[way * (A - 1) + k],
        azs, azr, ays, ayr, finish_a,
    )

    def ccopy(k, g):
        to_x = lax.rem(me.x + k, X)
        return remote(
            ga.at[to_x * 2 + 1 - me.c, block(g), :], cb.at[k, block(g), :], cs.at[k, g], cr.at[k, g], me.dev(c=1 - me.c)
        )

    def xcopy(k, g):
        return remote(
            xst.at[k - 1, block(g), :], xb.at[k - 1, block(g), :], xs.at[k - 1, g], xr.at[k - 1, g],
            me.dev(x=lax.rem(me.x + k, X)),
        )

    def to_core(g):
        for k in (*range(1, X), 0):
            ccopy(k, g).start()

    def to_x(g):
        for k in range(1, X):
            ccopy(k, g).wait_recv()
            s = lax.rem(me.x + k, X) * 2 + me.c
            xst[k - 1, block(g), :] = (
                ga[s, block(g), :].astype(F32) + cb[k, block(g), :].astype(F32)
            ).astype(BF)
            xcopy(k, g).start()

    def meet(g):
        ccopy(0, g).wait_recv()
        total = ga[me.s, block(g), :].astype(F32) + cb[0, block(g), :].astype(F32)
        for k in range(1, X):
            xcopy(k, g).wait_recv()
            total += xb[k - 1, block(g), :].astype(F32)
        pa[block(g), :] = total.astype(BF)

    def free(g):
        for k in range(X):
            ccopy(k, g).wait_send()
            if k:
                xcopy(k, g).wait_send()

    for k in range(A - 1):
        loop(geo.NP, lambda p: ffn.ysend(p, k))
    loop(geo.NP, ffn.ysend_own)
    loop(dp, to_core)
    loop(dp, to_x)
    for k in range(A - 1):
        loop(geo.NP, lambda p: ffn.step(k, p))
    loop(geo.NP, ffn.own)
    loop(dp, meet)
    for k in range(A - 1):
        att.ysend(0, k)
    att.ysend_own(0)
    for k in range(A - 1):
        att.step(k, 0)
    att.own(0)
    loop(dp, free)
    att.drain(0)
    loop(geo.NP, ffn.drain)


def gather_weights(geo, wf, wa):
    dma = pltpu.SemaphoreType.DMA
    sems = [
        dma((2,)),
        dma((geo.NZ, geo.NP)), dma((geo.NZ, geo.NP)), dma((geo.NY, geo.NP)), dma((geo.NY, geo.NP)),
        dma((geo.NZ, 1)), dma((geo.NZ, 1)), dma((geo.NY, 1)), dma((geo.NY, 1)),
        dma((geo.X - 1, geo.dp)), dma((geo.X - 1, geo.dp)), dma((geo.X, geo.dp)), dma((geo.X, geo.dp)),
    ]
    return pl.pallas_call(
        functools.partial(gather_kernel, geo),
        out_shape=(
            jax.ShapeDtypeStruct((3, geo.dp * geo.R, geo.F), BF),
            jax.ShapeDtypeStruct((geo.seq, geo.dp * geo.R, geo.I4), BF),
        ),
        in_specs=[pl.BlockSpec(memory_space=pl.ANY)] * 2,
        out_specs=[pl.BlockSpec(memory_space=pl.ANY)] * 2,
        scratch_shapes=sems,
        compiler_params=pltpu.CompilerParams(collective_id=0, has_side_effects=True, vmem_limit_bytes=48 << 20),
        name="gather_weights",
    )(wf, wa)


def scatter_grads(geo, gf, ga):
    dma = pltpu.SemaphoreType.DMA
    n, X, A, R = geo.dp * geo.R, geo.X, geo.A, geo.R
    scratch = [
        pltpu.VMEM((A, 3, R, geo.F), BF), pltpu.VMEM((geo.NZ, 3, R, geo.F), BF), pltpu.VMEM((geo.NZ, 3, R, geo.F), BF),
        pltpu.VMEM((X, n, geo.I4), BF), pltpu.VMEM((X - 1, n, geo.I4), BF), pltpu.VMEM((X - 1, n, geo.I4), BF),
        pltpu.VMEM((n, geo.I4), BF),
        pltpu.VMEM((A, R, geo.I4), BF), pltpu.VMEM((geo.NZ, R, geo.I4), BF), pltpu.VMEM((geo.NZ, R, geo.I4), BF),
        dma((geo.NZ, geo.NP)), dma((geo.NZ, geo.NP)), dma((geo.NZ + 1, geo.NP)), dma((geo.NZ + 1, geo.NP)),
        dma((geo.NZ, 1)), dma((geo.NZ, 1)), dma((geo.NZ + 1, 1)), dma((geo.NZ + 1, 1)),
        dma((X - 1, geo.dp)), dma((X - 1, geo.dp)), dma((X, geo.dp)), dma((X, geo.dp)),
    ]
    return pl.pallas_call(
        functools.partial(scatter_kernel, geo),
        out_shape=(
            jax.ShapeDtypeStruct((3, R, geo.F), F32),
            jax.ShapeDtypeStruct((R, geo.I4), F32),
        ),
        in_specs=[pl.BlockSpec(memory_space=pltpu.VMEM)] * 2,
        out_specs=[pl.BlockSpec(memory_space=pltpu.VMEM)] * 2,
        scratch_shapes=scratch,
        compiler_params=pltpu.CompilerParams(collective_id=1, has_side_effects=True, vmem_limit_bytes=60 << 20),
        name="scatter_grads",
    )(gf, ga)


NEGATIVE = -1e30
EPSILON = 1e-06
LIMITS = (12, 16, 23, 32, 46, 64, 91)


def bucket_ids(offsets):
    distance = jnp.abs(offsets)
    larger = 8 + sum(((distance >= threshold).astype(jnp.int32) for threshold in LIMITS))
    nearby = jnp.where(distance < 8, distance, larger)
    return jnp.where(offsets > 0, 16, 0) + nearby


def norm_scale(values, gain_vector):
    return (
        values
        * lax.rsqrt(jnp.mean(values * values, axis=-1, keepdims=True) + EPSILON)
        * gain_vector
    )


def gated(gate_value, upward):
    return jax.nn.gelu(gate_value, approximate=True) * upward


def spread_features(values, geo, width):
    lead = values.shape[:-1]
    blocks = values.reshape(*lead, geo.dp, width)
    return jnp.pad(blocks, [(0, 0)] * (len(lead) + 1) + [(0, geo.R - width)]).reshape(*lead, geo.dp * geo.R)


def pack_features(values, geo, width):
    lead = values.shape[:-1]
    return values.reshape(*lead, geo.dp, geo.R)[..., :width].reshape(*lead, geo.dp * width)


def per_device(
    axes, tokens, cotangent, lengths, w_query, w_key_value, w_output, w_gate_up, w_down, norm_gains, position_bias
):
    dp, seq = axes
    width, own_inner = w_query.shape
    rows = -(-width // 16) * 16
    rows = rows if (rows - width) >= 2 else rows + 16
    geo = Geo(dp, seq, rows, w_down.shape[1], 4 * own_inner)
    model_width = dp * width
    head_count = position_bias.shape[1]
    table_rows = position_bias.shape[0]
    bucket_count = table_rows * dp
    inner_width = seq * own_inner
    head_dim = inner_width // head_count

    extra = jnp.zeros((rows - width, geo.I4), BF)
    extra = extra.at[0, :width].set(norm_gains[0].astype(BF))
    tail = jnp.concatenate([norm_gains[1].astype(BF), position_bias.astype(BF).reshape(-1)])
    extra = extra.at[1, : tail.shape[0]].set(tail)
    wa = jnp.concatenate(
        [
            jnp.concatenate([w_query, w_key_value[0], w_key_value[1], w_output], axis=1).astype(BF),
            extra,
        ],
        axis=0,
    )
    wf = jnp.pad(jnp.concatenate([w_gate_up, w_down[None]], axis=0).astype(BF), ((0, 0), (0, rows - width), (0, 0)))
    WF, WA = gather_weights(geo, wf, wa)

    blocks = WA[0].reshape(dp, rows, geo.I4)
    first_gain = blocks[:, width, :width].reshape(model_width).astype(F32)
    second_gain = blocks[:, width + 1, :width].reshape(model_width).astype(F32)
    table_full = blocks[:, width + 1, width : width + table_rows * head_count].reshape(bucket_count, head_count)
    real = WA.reshape(seq, dp, rows, 4, own_inner)[:, :, :width]
    parts = real.transpose(3, 1, 2, 0, 4).reshape(4, model_width, inner_width)
    query_full, keyval_full, output_full = parts[0], parts[1:3], parts[3]

    inputs = tokens[0].astype(jnp.float32)
    row_count = inputs.shape[0]
    normed = norm_scale(inputs, first_gain).astype(jnp.bfloat16)
    queries = jnp.dot(normed, query_full, preferred_element_type=jnp.float32).astype(jnp.bfloat16)
    projected = jnp.einsum(
        "td,sdi->sti", normed, keyval_full, preferred_element_type=jnp.float32
    ).astype(jnp.bfloat16)
    keys_all, values_all = (
        lax.all_gather(projected[0], "seq", axis=0, tiled=True),
        lax.all_gather(projected[1], "seq", axis=0, tiled=True),
    )
    incoming_low = cotangent[0]
    incoming = incoming_low.astype(jnp.float32)
    cot_all = lax.all_gather(spread_features(incoming_low, geo, width), "seq", axis=0, tiled=True)
    length_all = keys_all.shape[0]
    block_start = lax.axis_index("seq") * row_count
    query_pos = block_start + jnp.arange(row_count, dtype=jnp.int32)
    key_pos = jnp.arange(length_all, dtype=jnp.int32)
    buckets = bucket_ids(key_pos[None, :] - query_pos[:, None])
    bucket_range = jnp.arange(bucket_count, dtype=jnp.int32)
    onehot = (buckets[:, :, None] == bucket_range).astype(jnp.bfloat16)
    score_bias = jnp.einsum("tkb,bh->htk", onehot, table_full, preferred_element_type=jnp.float32)
    key_valid = key_pos < lengths[0]
    query_heads = queries.reshape(row_count, head_count, head_dim)
    key_heads = keys_all.reshape(length_all, head_count, head_dim)
    value_heads = values_all.reshape(length_all, head_count, head_dim)
    raw_scores = (
        jnp.einsum("thc,khc->htk", query_heads, key_heads, preferred_element_type=jnp.float32) + score_bias
    )
    scores = jnp.where(key_valid[None, None, :], raw_scores, NEGATIVE)
    probs = jax.nn.softmax(scores, axis=-1)
    probs_low = probs.astype(BF)
    mixed_heads = (
        jnp.einsum("htk,khc->thc", probs_low, value_heads, preferred_element_type=jnp.float32)
        .reshape(row_count, inner_width)
        .astype(jnp.bfloat16)
    )
    attended = jnp.einsum("tc,dc->td", mixed_heads, output_full, preferred_element_type=jnp.float32)
    hidden_one = inputs + attended
    normed_two = norm_scale(hidden_one, second_gain).astype(jnp.bfloat16)
    normed_two_all = lax.all_gather(spread_features(normed_two, geo, width), "seq", axis=0, tiled=True)

    gate = jnp.dot(normed_two_all, WF[0], preferred_element_type=F32)
    upward = jnp.dot(normed_two_all, WF[1], preferred_element_type=F32)
    activated = gated(gate, upward).astype(BF)
    down_term = jnp.einsum("tf,df->td", activated, WF[2], preferred_element_type=F32)
    down_weight_grad = jnp.einsum("td,tf->df", cot_all, activated, preferred_element_type=F32)
    activated_grad = jnp.dot(cot_all, WF[2], preferred_element_type=F32)
    unused_value, gate_pull = jax.vjp(gated, gate, upward)
    gate_grad, upward_grad = gate_pull(activated_grad)
    gate_grad, upward_grad = gate_grad.astype(BF), upward_grad.astype(BF)
    gate_weight_grad = jnp.einsum("td,tf->df", normed_two_all, gate_grad, preferred_element_type=F32)
    up_weight_grad = jnp.einsum("td,tf->df", normed_two_all, upward_grad, preferred_element_type=F32)
    normed_two_term = jnp.einsum("tf,df->td", gate_grad, WF[0], preferred_element_type=F32) + jnp.einsum(
        "tf,df->td", upward_grad, WF[1], preferred_element_type=F32
    )
    down_sum = lax.psum_scatter(down_term.astype(BF), "seq", scatter_dimension=0, tiled=True)
    normed_two_sum = lax.psum_scatter(normed_two_term.astype(BF), "seq", scatter_dimension=0, tiled=True)
    outputs = (hidden_one + pack_features(down_sum, geo, width).astype(F32)).astype(BF)[None]
    normed_two_grad = pack_features(normed_two_sum, geo, width).astype(F32)
    gf = jnp.stack([gate_weight_grad.astype(BF), up_weight_grad.astype(BF), down_weight_grad.astype(BF)])

    unused_two, second_pull = jax.vjp(norm_scale, hidden_one, second_gain)
    hidden_norm_grad, second_gain_grad = second_pull(normed_two_grad)
    hidden_grad = incoming + hidden_norm_grad
    hidden_low = hidden_grad.astype(jnp.bfloat16)
    output_weight_grad = jnp.einsum("td,tc->dc", hidden_low, mixed_heads, preferred_element_type=jnp.float32)
    mixed_grad = jnp.einsum("td,dc->tc", hidden_low, output_full, preferred_element_type=jnp.float32).astype(
        jnp.bfloat16
    )
    grad_heads = mixed_grad.reshape(row_count, head_count, head_dim)
    prob_grad = jnp.einsum("thc,khc->htk", grad_heads, value_heads, preferred_element_type=jnp.float32)
    inner_sum = jnp.sum(probs * prob_grad, axis=-1, keepdims=True)
    score_grad = (probs * (prob_grad - inner_sum)).astype(jnp.bfloat16)
    query_act_grad = (
        jnp.einsum("htk,khc->thc", score_grad, key_heads, preferred_element_type=jnp.float32)
        .reshape(row_count, inner_width)
        .astype(jnp.bfloat16)
    )
    key_piece = jnp.einsum(
        "htk,thc->khc", score_grad, query_heads, preferred_element_type=jnp.float32
    ).reshape(length_all, inner_width)
    value_piece = jnp.einsum(
        "htk,thc->khc", probs_low, grad_heads, preferred_element_type=jnp.float32
    ).reshape(length_all, inner_width)
    own_terms = lax.psum_scatter(
        jnp.concatenate([key_piece, value_piece], axis=1).astype(jnp.bfloat16),
        "seq",
        scatter_dimension=0,
        tiled=True,
    )
    keyval_act_grad = jnp.stack([own_terms[:, :inner_width], own_terms[:, inner_width:]])
    query_weight_grad = jnp.einsum("td,tc->dc", normed, query_act_grad, preferred_element_type=jnp.float32)
    keyval_weight_grad = jnp.einsum("td,stc->sdc", normed, keyval_act_grad, preferred_element_type=jnp.float32)
    normed_grad = jnp.einsum(
        "tc,dc->td", query_act_grad, query_full, preferred_element_type=jnp.float32
    ) + jnp.einsum("stc,sdc->td", keyval_act_grad, keyval_full, preferred_element_type=jnp.float32)
    unused_three, first_pull = jax.vjp(norm_scale, inputs, first_gain)
    input_norm_grad, first_gain_grad = first_pull(normed_grad)
    input_grad = (hidden_grad + input_norm_grad).astype(jnp.bfloat16)[None]
    table_grad = jnp.einsum("htk,tkb->bh", score_grad, onehot, preferred_element_type=jnp.float32)

    grads = jnp.stack(
        [query_weight_grad, keyval_weight_grad[0], keyval_weight_grad[1], output_weight_grad]
    ).reshape(4, dp, width, seq, own_inner)
    grads = grads.transpose(3, 1, 2, 0, 4).reshape(seq, dp, width, geo.I4).astype(BF)
    row_one = jnp.pad(first_gain_grad.reshape(dp, width), ((0, 0), (0, geo.I4 - width)))
    row_two = jnp.concatenate([second_gain_grad.reshape(dp, width), table_grad.reshape(dp, -1)], axis=1)
    row_two = jnp.pad(row_two, ((0, 0), (0, geo.I4 - row_two.shape[1])))
    more = jnp.stack([row_one, row_two], axis=1).astype(BF)
    more = jnp.pad(more, ((0, 0), (0, rows - width - 2), (0, 0)))
    ga = jnp.concatenate([grads, jnp.broadcast_to(more, (seq, *more.shape))], axis=2).reshape(seq, dp * rows, geo.I4)
    of, oa = scatter_grads(geo, gf, ga)

    main = oa[:width]
    query_part = main[:, :own_inner]
    keyval_part = jnp.stack([main[:, own_inner : 2 * own_inner], main[:, 2 * own_inner : 3 * own_inner]])
    output_part = main[:, 3 * own_inner :]
    gain_part = jnp.stack([oa[width, :width], oa[width + 1, :width]])
    table_part = oa[width + 1, width : width + table_rows * head_count].reshape(table_rows, head_count)
    return (
        outputs,
        input_grad,
        query_part,
        keyval_part,
        output_part,
        of[:2, :width],
        of[2, :width],
        gain_part,
        table_part,
    )

def solution(mesh):
    in_specs = (
        P("dp", "seq", None),
        P("dp", "seq", None),
        P("dp"),
        P("dp", "seq"),
        P(None, "dp", "seq"),
        P("dp", "seq"),
        P(None, "dp", "seq"),
        P("dp", "seq"),
        P(None, "dp"),
        P("dp", None),
    )
    out_specs = (
        P("dp", "seq", None),
        P("dp", "seq", None),
        P("dp", "seq"),
        P(None, "dp", "seq"),
        P("dp", "seq"),
        P(None, "dp", "seq"),
        P("dp", "seq"),
        P(None, "dp"),
        P("dp", None),
    )
    return jax.shard_map(
        functools.partial(per_device, (mesh.shape["dp"], mesh.shape["seq"])), mesh=mesh, in_specs=in_specs, out_specs=out_specs, check_vma=False
    )
```

```python
import functools
import jax
import jax.numpy as jnp
import numpy as np
from jax import lax
from jax.experimental import pallas as pl
from jax.experimental.pallas import tpu as pltpu

from jax.sharding import PartitionSpec as P

MESH = pl.DeviceIdType.MESH
BF = jnp.bfloat16
F32 = jnp.float32


class Geo:
    def __init__(self, dp, seq, width, ff, inner4, tokens, heads, table_rows):
        self.dp, self.seq = dp, seq
        self.W, self.TR, self.E = width, table_rows, 2 + table_rows
        rows = -(-(width + self.E) // 16) * 16
        self.D, self.N, self.T, self.L = dp * width, dp * rows, tokens, seq * tokens
        self.I, self.H = inner4 // 4 * seq, heads
        self.B, self.A, self.X = 2, dp // 2, seq // 2
        self.R, self.F, self.I4 = rows, ff, inner4
        self.NH = 2 if rows % 32 == 0 else 1
        self.RH = rows // self.NH
        self.NP = 3 * self.NH
        self.NZ = 2 * (self.A - 1)
        self.NY = 2 * self.A - 1


class Place:
    def __init__(self, geo):
        d, s = lax.axis_index("dp"), lax.axis_index("seq")
        self.d, self.s = d, s
        self.z, self.y = d // 2, d % 2
        self.x, self.c = s // 2, s % 2

    def dev(self, z=None, y=None, x=None, c=None):
        z = self.z if z is None else z
        y = self.y if y is None else y
        x = self.x if x is None else x
        c = self.c if c is None else c
        return (z * 2 + y, x * 2 + c)


def remote(src, dst, ss, rs, dev):
    return pltpu.make_async_remote_copy(
        src_ref=src, dst_ref=dst, send_sem=ss, recv_sem=rs, device_id=dev, device_id_type=MESH
    )


def loop(n, body):
    def step(i, carry):
        body(i)
        return carry

    lax.fori_loop(0, n, step, 0)


def enter(geo, me):
    bar = pltpu.get_barrier_semaphore()

    def greet(dev):
        pl.semaphore_signal(bar, 1, device_id=dev, device_id_type=MESH)

    greet(me.dev(y=1 - me.y))
    greet(me.dev(c=1 - me.c))
    for k in range(1, geo.X):
        greet(me.dev(x=lax.rem(me.x + k, geo.X)))

    @pl.when(me.z > 0)
    def _():
        greet(me.dev(z=me.z - 1))

    @pl.when(me.z < geo.A - 1)
    def _():
        greet(me.dev(z=me.z + 1))

    count = 2 + (geo.X - 1) + (me.z > 0).astype(jnp.int32) + (me.z < geo.A - 1).astype(jnp.int32)
    pl.semaphore_wait(bar, count)


class LineGather:
    def __init__(self, geo, me, own, held, zs, zr, ys, yr):
        self.geo, self.me, self.own, self.held = geo, me, own, held
        self.zs, self.zr, self.ys, self.yr = zs, zr, ys, yr

    def zcopy(self, way, r, p):
        me, geo = self.me, self.geo
        q = me.z - (r - 1) if way == 0 else me.z + (r - 1)
        to = me.z + 1 if way == 0 else me.z - 1
        valid = (me.z < geo.A - 1) & (q >= 0) if way == 0 else (me.z > 0) & (q <= geo.A - 1)
        g = q * 2 + me.y
        src = self.own(p) if r == 1 else self.held(p, g)
        slot = way * (geo.A - 1) + r - 1
        copy = remote(src, self.held(p, g), self.zs.at[slot, p], self.zr.at[slot, p], me.dev(z=to))
        return copy, valid

    def zarrive(self, way, r, p):
        me, geo = self.me, self.geo
        q = me.z - r if way == 0 else me.z + r
        valid = (q >= 0) if way == 0 else (q <= geo.A - 1)
        slot = way * (geo.A - 1) + r - 1
        here = self.held(p, q * 2 + me.y)
        copy = remote(here, here, self.zs.at[slot, p], self.zr.at[slot, p], me.dev(y=1 - me.y))
        return copy, valid, q

    def ycopy(self, way, r, p):
        me, geo = self.me, self.geo
        if r == 0:
            q, slot, src = me.z, 0, self.own(p)
        else:
            q = me.z - r if way == 0 else me.z + r
            slot = 1 + way * (geo.A - 1) + r - 1
            src = self.held(p, q * 2 + me.y)
        copy = remote(
            src, self.held(p, q * 2 + me.y), self.ys.at[slot, p], self.yr.at[slot, p], me.dev(y=1 - me.y)
        )
        return copy

    def yarrive(self, way, r, p):
        me, geo = self.me, self.geo
        if r == 0:
            q, slot = me.z, 0
        else:
            q = me.z - r if way == 0 else me.z + r
            slot = 1 + way * (geo.A - 1) + r - 1
        here = self.held(p, q * 2 + 1 - me.y)
        copy = remote(here, here, self.ys.at[slot, p], self.yr.at[slot, p], me.dev(y=1 - me.y))
        return copy, q

    def valid(self, way, r):
        q = self.me.z - r if way == 0 else self.me.z + r
        return (q >= 0) if way == 0 else (q <= self.geo.A - 1)

    def begin(self, p):
        self.ycopy(0, 0, p).start()
        for way in (0, 1):
            copy, valid = self.zcopy(way, 1, p)

            @pl.when(valid)
            def _():
                copy.start()

    def step(self, r, p, on_held=None):
        for way in (0, 1):
            copy, valid, q = self.zarrive(way, r, p)

            @pl.when(valid)
            def _():
                copy.wait_recv()
                if r < self.geo.A - 1:
                    onward, may = self.zcopy(way, r + 1, p)

                    @pl.when(may)
                    def _():
                        onward.start()

                self.ycopy(way, r, p).start()
                if on_held is not None:
                    on_held(q * 2 + self.me.y)

    def ystep(self, r, p, on_held=None):
        for way in (0, 1) if r else (0,):
            copy, q = self.yarrive(way, r, p)
            valid = self.valid(way, r) if r else True

            def go():
                copy.wait_recv()
                if on_held is not None:
                    on_held(q * 2 + 1 - self.me.y)

            if r:
                pl.when(valid)(go)
            else:
                go()

    def drain(self, p):
        self.ycopy(0, 0, p).wait_send()
        for r in range(1, self.geo.A):
            for way in (0, 1):
                copy, valid = self.zcopy(way, r, p)

                @pl.when(valid)
                def _():
                    copy.wait_send()

                @pl.when(self.valid(way, r))
                def _():
                    self.ycopy(way, r, p).wait_send()


class LineScatter:
    def __init__(self, geo, me, part, ybuf, zbuf, stage, zs, zr, ys, yr, finish):
        self.__dict__.update(locals())

    def turns(self):
        geo, me = self.geo, self.me
        for k in range(geo.A - 1):
            yield 0, k, geo.A - 1 - k, k < geo.A - 1 - me.z
            yield 1, k, k, k < me.z

    def slot(self, way, k):
        return way * (self.geo.A - 1) + k

    def ycopy(self, slot, t, p):
        me = self.me
        return remote(
            self.part(p, t * 2 + 1 - me.y),
            self.ybuf(p, t),
            self.ys.at[slot, p],
            self.yr.at[slot, p],
            me.dev(y=1 - me.y),
        )

    def zcopy(self, way, k, p):
        me = self.me
        to = me.z + 1 if way == 0 else me.z - 1
        slot = self.slot(way, k)
        return remote(
            self.stage(way, p, k), self.zbuf(way, p, k), self.zs.at[slot, p], self.zr.at[slot, p], me.dev(z=to)
        )

    def ysend(self, p, k):
        for way, kk, t, valid in self.turns():
            if kk == k:

                @pl.when(valid)
                def _():
                    self.ycopy(self.slot(way, kk), t, p).start()

    def ysend_own(self, p):
        self.ycopy(self.geo.NZ, self.me.z, p).start()

    def step(self, k, p):
        geo, me = self.geo, self.me
        for way, kk, t, valid in self.turns():
            if kk == k:

                @pl.when(valid)
                def _():
                    self.ycopy(self.slot(way, k), t, p).wait_recv()
                    total = self.part(p, t * 2 + me.y)[...].astype(F32) + self.ybuf(p, t)[...].astype(F32)
                    out = self.stage(way, p, k)
                    comes = me.z > 0 if way == 0 else me.z < geo.A - 1

                    @pl.when(comes)
                    def _():
                        self.zcopy(way, k, p).wait_recv()
                        out[...] = (total + self.zbuf(way, p, k)[...].astype(F32)).astype(BF)

                    @pl.when(jnp.logical_not(comes))
                    def _():
                        out[...] = total.astype(BF)

                    self.zcopy(way, k, p).start()

    def own(self, p):
        geo, me = self.geo, self.me
        self.ycopy(geo.NZ, me.z, p).wait_recv()
        total = self.part(p, me.z * 2 + me.y)[...].astype(F32) + self.ybuf(p, me.z)[...].astype(F32)
        kup = jnp.minimum(geo.A - 1 - me.z, geo.A - 2)
        kdown = jnp.minimum(me.z, geo.A - 2)

        def arrive(way, k):
            slot = way * (geo.A - 1) + k
            here = self.zbuf(way, p, k)
            remote(here, here, self.zs.at[slot, p], self.zr.at[slot, p], me.dev(y=1 - me.y)).wait_recv()
            return here[...].astype(F32)

        @pl.when(me.z == 0)
        def _():
            self.finish(p, total + arrive(1, kdown))

        @pl.when(me.z == geo.A - 1)
        def _():
            self.finish(p, total + arrive(0, kup))

        @pl.when((me.z > 0) & (me.z < geo.A - 1))
        def _():
            self.finish(p, total + arrive(0, kup) + arrive(1, kdown))

    def drain(self, p):
        for way, k, t, valid in self.turns():

            @pl.when(valid)
            def _():
                self.ycopy(self.slot(way, k), t, p).wait_send()
                self.zcopy(way, k, p).wait_send()

        self.ycopy(self.geo.NZ, self.me.z, p).wait_send()


NEGATIVE = -1e30
EPSILON = 1e-06
LIMITS = (12, 16, 23, 32, 46, 64, 91)


def bucket_ids(offsets):
    distance = jnp.abs(offsets)
    larger = 8 + sum(((distance >= threshold).astype(jnp.int32) for threshold in LIMITS))
    nearby = jnp.where(distance < 8, distance, larger)
    return jnp.where(offsets > 0, 16, 0) + nearby


def norm_scale(values, gain_vector):
    return (
        values
        * lax.rsqrt(jnp.mean(values * values, axis=-1, keepdims=True) + EPSILON)
        * gain_vector
    )


def gated(gate_value, upward):
    return jax.nn.gelu(gate_value, approximate=True) * upward


def gather_kernel(geo, wf, wa, WF, WA, local, zs, zr, ys, yr, azs, azr, ays, ayr, xs, xr, cs, cr):
    me = Place(geo)
    R, RH, NH, dp, X = geo.R, geo.RH, geo.NH, geo.dp, geo.X
    mine = [
        pltpu.make_async_copy(wf, WF.at[:, pl.ds(pl.multiple_of(me.d * R, 16), R), :], local.at[0]),
        pltpu.make_async_copy(wa, WA.at[me.s, pl.ds(pl.multiple_of(me.d * R, 16), R), :], local.at[1]),
    ]
    for copy in mine:
        copy.start()
    enter(geo, me)

    def own_f(p):
        return wf.at[p // NH, pl.ds(pl.multiple_of((p % NH) * RH, 16), RH), :]

    def held_f(p, g):
        return WF.at[p // NH, pl.ds(pl.multiple_of(g * R + (p % NH) * RH, 16), RH), :]

    def held_a(s, g):
        return WA.at[s, pl.ds(pl.multiple_of(g * R, 16), R), :]

    ffn = LineGather(geo, me, own_f, held_f, zs, zr, ys, yr)
    att = LineGather(geo, me, lambda p: wa, lambda p, g: held_a(me.s, g), azs, azr, ays, ayr)

    def xcopy(k, g, src):
        to = lax.rem(me.x + k, X)
        return remote(src, held_a(me.s, g), xs.at[k - 1, g], xr.at[k - 1, g], me.dev(x=to))

    def xarrive(k, g):
        src_x = lax.rem(me.x - k + X, X)
        here = held_a(src_x * 2 + me.c, g)
        return remote(here, here, xs.at[k - 1, g], xr.at[k - 1, g], me.dev(c=1 - me.c)), here

    def ccopy(k, g, src, s):
        return remote(src, held_a(s, g), cs.at[k, g], cr.at[k, g], me.dev(c=1 - me.c))

    def spread(g, src=None):
        src = held_a(me.s, g) if src is None else src
        for k in range(1, X):
            xcopy(k, g, src).start()
        ccopy(0, g, src, me.s).start()

    att.begin(0)
    spread(me.d, wa)
    loop(geo.NP, ffn.begin)
    att.ystep(0, 0, spread)
    for r in range(1, geo.A):
        att.step(r, 0, spread)
        att.ystep(r, 0, spread)

    def from_x(g):
        for k in range(1, X):
            copy, here = xarrive(k, g)
            copy.wait_recv()
            ccopy(k, g, here, lax.rem(me.x - k + X, X) * 2 + me.c).start()

    loop(dp, from_x)
    for r in range(1, geo.A):
        loop(geo.NP, lambda p: ffn.step(r, p))
    for r in range(geo.A):
        loop(geo.NP, lambda p: ffn.ystep(r, p))

    def finish(g):
        for k in range(X):
            s = lax.rem(me.x - k + X, X) * 2 + 1 - me.c
            here = held_a(s, g)
            remote(here, here, cs.at[k, g], cr.at[k, g], me.dev(c=1 - me.c)).wait_recv()
            ccopy(k, g, here, s).wait_send()
            if k:
                xcopy(k, g, here).wait_send()

    loop(dp, finish)
    att.drain(0)
    loop(geo.NP, ffn.drain)
    for copy in mine:
        copy.wait()


def scatter_kernel(
    geo, gf, ga, of, oa, yb, zb, st, cb, xb, xst, pa, ayb, azb, ast,
    zs, zr, ys, yr, azs, azr, ays, ayr, xs, xr, cs, cr,
):
    me = Place(geo)
    R, RH, NH, dp, X, A = geo.R, geo.RH, geo.NH, geo.dp, geo.X, geo.A
    enter(geo, me)

    def rows(g, p):
        return pl.ds(pl.multiple_of(g * R + (p % NH) * RH, 16), RH)

    def piece(buf, i, p):
        return buf.at[i, p // NH, pl.ds(pl.multiple_of((p % NH) * RH, 16), RH), :]

    def finish_f(p, value):
        of[p // NH, pl.ds(pl.multiple_of((p % NH) * RH, 16), RH), :] = value

    ffn = LineScatter(
        geo, me,
        lambda p, g: gf.at[p // NH, rows(g, p), :],
        lambda p, t: piece(yb, t, p),
        lambda way, p, k: piece(zb, way * (A - 1) + k, p),
        lambda way, p, k: piece(st, way * (A - 1) + k, p),
        zs, zr, ys, yr, finish_f,
    )

    def block(g):
        return pl.ds(pl.multiple_of(g * R, 16), R)

    def finish_a(p, value):
        oa[...] = value

    att = LineScatter(
        geo, me,
        lambda p, g: pa.at[block(g), :],
        lambda p, t: ayb.at[t],
        lambda way, p, k: azb.at[way * (A - 1) + k],
        lambda way, p, k: ast.at[way * (A - 1) + k],
        azs, azr, ays, ayr, finish_a,
    )

    def ccopy(k, g):
        to_x = lax.rem(me.x + k, X)
        return remote(
            ga.at[to_x * 2 + 1 - me.c, block(g), :], cb.at[k, block(g), :], cs.at[k, g], cr.at[k, g], me.dev(c=1 - me.c)
        )

    def xcopy(k, g):
        return remote(
            xst.at[k - 1, block(g), :], xb.at[k - 1, block(g), :], xs.at[k - 1, g], xr.at[k - 1, g],
            me.dev(x=lax.rem(me.x + k, X)),
        )

    def to_core(g):
        for k in (*range(1, X), 0):
            ccopy(k, g).start()

    def to_x(g):
        for k in range(1, X):
            ccopy(k, g).wait_recv()
            s = lax.rem(me.x + k, X) * 2 + me.c
            xst[k - 1, block(g), :] = (
                ga[s, block(g), :].astype(F32) + cb[k, block(g), :].astype(F32)
            ).astype(BF)
            xcopy(k, g).start()

    def meet(g):
        ccopy(0, g).wait_recv()
        total = ga[me.s, block(g), :].astype(F32) + cb[0, block(g), :].astype(F32)
        for k in range(1, X):
            xcopy(k, g).wait_recv()
            total += xb[k - 1, block(g), :].astype(F32)
        pa[block(g), :] = total.astype(BF)

    def free(g):
        for k in range(X):
            ccopy(k, g).wait_send()
            if k:
                xcopy(k, g).wait_send()

    for k in range(A - 1):
        loop(geo.NP, lambda p: ffn.ysend(p, k))
    loop(geo.NP, ffn.ysend_own)
    loop(dp, to_core)
    loop(dp, to_x)
    for k in range(A - 1):
        loop(geo.NP, lambda p: ffn.step(k, p))
    loop(geo.NP, ffn.own)
    loop(dp, meet)
    for k in range(A - 1):
        att.ysend(0, k)
    att.ysend_own(0)
    for k in range(A - 1):
        att.step(k, 0)
    att.own(0)
    loop(dp, free)
    att.drain(0)
    loop(geo.NP, ffn.drain)


def gather_weights(geo, wf, wa):
    dma = pltpu.SemaphoreType.DMA
    sems = [
        dma((2,)),
        dma((geo.NZ, geo.NP)), dma((geo.NZ, geo.NP)), dma((geo.NY, geo.NP)), dma((geo.NY, geo.NP)),
        dma((geo.NZ, 1)), dma((geo.NZ, 1)), dma((geo.NY, 1)), dma((geo.NY, 1)),
        dma((geo.X - 1, geo.dp)), dma((geo.X - 1, geo.dp)), dma((geo.X, geo.dp)), dma((geo.X, geo.dp)),
    ]
    return pl.pallas_call(
        functools.partial(gather_kernel, geo),
        out_shape=(
            jax.ShapeDtypeStruct((3, geo.dp * geo.R, geo.F), BF),
            jax.ShapeDtypeStruct((geo.seq, geo.dp * geo.R, geo.I4), BF),
        ),
        in_specs=[pl.BlockSpec(memory_space=pl.ANY)] * 2,
        out_specs=[pl.BlockSpec(memory_space=pl.ANY)] * 2,
        scratch_shapes=sems,
        compiler_params=pltpu.CompilerParams(collective_id=0, has_side_effects=True, vmem_limit_bytes=48 << 20),
        name="gather_weights",
    )(wf, wa)


def scatter_grads(geo, gf, ga):
    dma = pltpu.SemaphoreType.DMA
    n, X, A, R = geo.dp * geo.R, geo.X, geo.A, geo.R
    scratch = [
        pltpu.VMEM((A, 3, R, geo.F), BF), pltpu.VMEM((geo.NZ, 3, R, geo.F), BF), pltpu.VMEM((geo.NZ, 3, R, geo.F), BF),
        pltpu.VMEM((X, n, geo.I4), BF), pltpu.VMEM((X - 1, n, geo.I4), BF), pltpu.VMEM((X - 1, n, geo.I4), BF),
        pltpu.VMEM((n, geo.I4), BF),
        pltpu.VMEM((A, R, geo.I4), BF), pltpu.VMEM((geo.NZ, R, geo.I4), BF), pltpu.VMEM((geo.NZ, R, geo.I4), BF),
        dma((geo.NZ, geo.NP)), dma((geo.NZ, geo.NP)), dma((geo.NZ + 1, geo.NP)), dma((geo.NZ + 1, geo.NP)),
        dma((geo.NZ, 1)), dma((geo.NZ, 1)), dma((geo.NZ + 1, 1)), dma((geo.NZ + 1, 1)),
        dma((X - 1, geo.dp)), dma((X - 1, geo.dp)), dma((X, geo.dp)), dma((X, geo.dp)),
    ]
    return pl.pallas_call(
        functools.partial(scatter_kernel, geo),
        out_shape=(
            jax.ShapeDtypeStruct((3, R, geo.F), F32),
            jax.ShapeDtypeStruct((R, geo.I4), F32),
        ),
        in_specs=[pl.BlockSpec(memory_space=pltpu.VMEM)] * 2,
        out_specs=[pl.BlockSpec(memory_space=pltpu.VMEM)] * 2,
        scratch_shapes=scratch,
        compiler_params=pltpu.CompilerParams(collective_id=1, has_side_effects=True, vmem_limit_bytes=60 << 20),
        name="scatter_grads",
    )(gf, ga)


class SeqGather:
    def __init__(self, geo, me, held, xs, xr, cs, cr):
        self.geo, self.me, self.held = geo, me, held
        self.xs, self.xr, self.cs, self.cr = xs, xr, cs, cr

    def ccopy(self, k):
        me, X = self.me, self.geo.X
        here = self.held(lax.rem(me.x - k + X, X) * 2 + me.c)
        return remote(here, here, self.cs.at[k], self.cr.at[k], me.dev(c=1 - me.c))

    def xcopy(self, k):
        me = self.me
        here = self.held(me.s)
        return remote(here, here, self.xs.at[k - 1], self.xr.at[k - 1], me.dev(x=lax.rem(me.x + k, self.geo.X)))

    def begin(self):
        for k in range(1, self.geo.X):
            self.xcopy(k).start()
        self.ccopy(0).start()

    def relay(self):
        for k in range(1, self.geo.X):
            self.xcopy(k).wait_recv()
            self.ccopy(k).start()

    def finish(self):
        for k in range(self.geo.X):
            self.ccopy(k).wait_recv()
            self.ccopy(k).wait_send()
            if k:
                self.xcopy(k).wait_send()


def dot(a, b, dims=((1,), (0,))):
    return lax.dot_general(a, b, (dims, ((), ())), preferred_element_type=F32)


NT = ((1,), (1,))
TN = ((0,), (0,))


def constants(geo):
    own, I4, S, I, N = geo.I4 // 4, geo.I4, geo.seq, geo.I, geo.N
    perm_in = np.zeros((S * I4, 3 * I), np.float32)
    perm_out = np.zeros((I, S * I4), np.float32)
    i = np.arange(own)
    for s in range(S):
        for kind in range(3):
            perm_in[s * I4 + kind * own + i, kind * I + s * own + i] = 1
        perm_out[s * own + i, s * I4 + 3 * own + i] = 1
    place = np.arange(N)
    tile = np.zeros((I4, N), np.float32)
    inside = place % geo.R < geo.W
    tile[(place % geo.R)[inside], place[inside]] = 1
    group = np.tile((place // geo.R * 16).astype(np.float32), (8, 1))
    offset = np.arange(512) - 256
    distance = np.abs(offset)
    larger = 8 + sum((distance >= limit).astype(np.int32) for limit in LIMITS)
    bucket = np.where(offset > 0, 16, 0) + np.where(distance < 8, distance, larger)
    onehot = np.zeros((geo.dp * 16, 512), np.float32)
    for b in range(geo.dp * geo.TR):
        onehot[b // geo.TR * 16 + 16 - geo.E + 2 + b % geo.TR] = bucket == b
    return [jnp.asarray(v, BF) for v in (perm_in, perm_out, tile)] + [jnp.asarray(group), jnp.asarray(onehot, BF)]


def shear(value, sign):
    rows, lanes = value.shape
    row = lax.broadcasted_iota(jnp.int32, (rows, 1), 0)
    bit = 1
    while bit < rows:
        moved = pltpu.roll(value, bit if sign > 0 else lanes - bit, 1)
        value = jnp.where((row & bit) != 0, moved, value)
        bit *= 2
    return value


def gelu_parts(g):
    k0 = np.float32(np.sqrt(2 / np.pi))
    t = jnp.tanh(k0 * (g + np.float32(0.044715) * (g * g * g)))
    half = 0.5 * (1.0 + t)
    slope = half + 0.5 * g * (1.0 - t * t) * (k0 * (1.0 + np.float32(3 * 0.044715) * (g * g)))
    return g * half, slope


def forward_kernel(
    geo, length, x_in, c_in, wf, wa, cpi, cpo, ctile, cgroup, conehot,
    oWA, onormed, oqkv, oKV, oP, omixed, ohid, oX2, oC, oact, opart, ogain,
    WF, WA, xv, C, X2, KV, normed, A, qkv, strip, mixed, hid, pst, act, part, got, gain, pin, pout, tile, group, onehot,
    local, outs, psem, zs, zr, ys, yr, azs, azr, ays, ayr, xs, xr, cs, cr, gxs, gxr, gcs, gcr, ps, pr,
):
    me = Place(geo)
    R, RH, NH, dp, X, T, N, I = geo.R, geo.RH, geo.NH, geo.dp, geo.X, geo.T, geo.N, geo.I
    I4, S, L = geo.I4, geo.seq, geo.L
    block = lambda i, n: pl.ds(pl.multiple_of(i * n, 16), n)
    loads = [
        (wa, WA.at[me.s, block(me.d, R), :]),
        (wf, WF.at[:, block(me.d, R), :]),
        (c_in, C.at[block(me.s, T), :]),
        (x_in, xv),
        (cpi, pin), (cpo, pout), (ctile, tile), (cgroup, group), (conehot, onehot),
    ]
    loads = [pltpu.make_async_copy(src, dst, local.at[i]) for i, (src, dst) in enumerate(loads)]
    for copy in loads:
        copy.start()
    enter(geo, me)

    def own_f(p):
        return wf.at[p // NH, pl.ds(pl.multiple_of((p % NH) * RH, 16), RH), :]

    def held_f(p, g):
        return WF.at[p // NH, pl.ds(pl.multiple_of(g * R + (p % NH) * RH, 16), RH), :]

    def held_a(s, g):
        return WA.at[s, block(g, R), :]

    ffn = LineGather(geo, me, own_f, held_f, zs, zr, ys, yr)
    att = LineGather(geo, me, lambda p: wa, lambda p, g: held_a(me.s, g), azs, azr, ays, ayr)

    def xcopy(k, g, src):
        to = lax.rem(me.x + k, X)
        return remote(src, held_a(me.s, g), xs.at[k - 1, g], xr.at[k - 1, g], me.dev(x=to))

    def xarrive(k, g):
        src_x = lax.rem(me.x - k + X, X)
        here = held_a(src_x * 2 + me.c, g)
        return remote(here, here, xs.at[k - 1, g], xr.at[k - 1, g], me.dev(c=1 - me.c)), here

    def ccopy(k, g, src, s):
        return remote(src, held_a(s, g), cs.at[k, g], cr.at[k, g], me.dev(c=1 - me.c))

    def spread(g, src=None):
        src = held_a(me.s, g) if src is None else src
        for k in range(1, X):
            xcopy(k, g, src).start()
        ccopy(0, g, src, me.s).start()

    seq = [
        SeqGather(geo, me, (lambda ref: lambda s: ref.at[block(s, T), :])(ref), gxs.at[i], gxr.at[i], gcs.at[i], gcr.at[i])
        for i, ref in enumerate((C, KV, X2))
    ]
    gather_c, gather_kv, gather_x2 = seq

    att.begin(0)
    spread(me.d, wa)
    loop(geo.NP, ffn.begin)
    att.ystep(0, 0, spread)
    for r in range(1, geo.A):
        att.step(r, 0, spread)
        att.ystep(r, 0, spread)
    loads[2].wait()
    gather_c.begin()

    def from_x(g):
        for k in range(1, X):
            copy, here = xarrive(k, g)
            copy.wait_recv()
            ccopy(k, g, here, lax.rem(me.x - k + X, X) * 2 + me.c).start()

    loop(dp, from_x)
    for i in (3, 4, 5, 6, 7, 8):
        loads[i].wait()

    def settle(g):
        for k in range(X):
            s = lax.rem(me.x - k + X, X) * 2 + 1 - me.c
            here = held_a(s, g)
            remote(here, here, cs.at[k, g], cr.at[k, g], me.dev(c=1 - me.c)).wait_recv()

    loop(dp, settle)
    loads[0].wait()
    loop(geo.NP, lambda p: ffn.step(1, p))

    extra = jnp.concatenate([WA[0, g * R + R - 16 : g * R + R, :] for g in range(dp)], axis=0)
    spread_rows = dot(extra, tile[...])
    row = lax.broadcasted_iota(jnp.int32, (dp * 16, N), 0).astype(F32)
    gains = []
    for e in range(2):
        hit = row == group[0:1, :] + np.float32(16 - geo.E + e)
        gains.append(jnp.sum(jnp.where(hit, spread_rows, 0.0), axis=0, keepdims=True))
    gain[...] = jnp.concatenate(gains + [jnp.zeros((6, N), F32)], axis=0)
    bias = dot(extra[:, :128] if I4 >= 128 else extra, onehot[...], TN)

    inputs = xv[...].astype(F32)
    scale = lax.rsqrt(jnp.sum(inputs * inputs, axis=-1, keepdims=True) / np.float32(geo.D) + EPSILON)
    normed[...] = (inputs * scale * gain[0:1, :]).astype(BF)
    for s in range(S):
        A[:, s * I4 : (s + 1) * I4] = dot(normed[...], WA[s]).astype(BF)
    qkv[...] = dot(A[...], pin[...]).astype(BF)
    KV[block(me.s, T), :] = qkv[:, I:]
    gather_kv.begin()
    writes = []

    def write(src, dst):
        copy = pltpu.make_async_copy(src, dst, outs.at[len(writes)])
        copy.start()
        writes.append(copy)

    write(WA, oWA)
    write(normed, onormed)
    write(qkv, oqkv)
    write(gain, ogain)
    NB = L // 128
    for h in range(geo.H):
        band = shear(jnp.broadcast_to(bias[h : h + 1, :], (128, 512)), 1)[:, 128:512].astype(BF)
        strip[h, :, (NB - 2) * 128 : (NB + 1) * 128] = band
        far = (NB - 2) * 128
        strip[h, :, :far] = jnp.broadcast_to(bias[h : h + 1, 0:1], (128, far)).astype(BF)
        strip[h, :, (NB + 1) * 128 :] = jnp.broadcast_to(bias[h : h + 1, 511:512], (128, far)).astype(BF)
    gather_c.relay()
    gather_kv.relay()
    gather_kv.finish()
    write(KV, oKV)

    hd = I // geo.H
    per = 128 // hd
    valid = lax.broadcasted_iota(jnp.int32, (1, L), 1) < length[0]

    def pair(t):
        lanes = pl.ds(pl.multiple_of(t * 128, 128), 128)
        head = lax.broadcasted_iota(jnp.int32, (1, 128), 1) // hd
        keys = KV[:, lanes]
        values = KV[:, pl.ds(pl.multiple_of(I + t * 128, 128), 128)]
        queries = qkv[:, lanes]
        outs_ = jnp.zeros((T, 128), F32)
        for e in range(per):
            h = t * per + e
            scores = dot(jnp.where(head == e, queries, jnp.zeros_like(queries)), keys, NT)
            shift = [
                strip[h, :, pl.ds(pl.multiple_of((NB - 1 - me.s * (T // 128) - b) * 128, 128), L)].astype(F32)
                for b in range(T // 128)
            ]
            scores = jnp.where(valid, scores + jnp.concatenate(shift, axis=0), np.float32(NEGATIVE))
            top = jnp.max(scores, axis=-1, keepdims=True)
            probs = jnp.exp(scores - top)
            probs = probs * (1.0 / jnp.sum(probs, axis=-1, keepdims=True))
            copy = pltpu.make_async_copy(pst.at[e], oP.at[h], psem.at[e])

            @pl.when(t > 0)
            def _():
                copy.wait()

            pst[e] = probs
            copy.start()
            mine = dot(probs.astype(BF), values)
            outs_ = jnp.where(head == e, mine, outs_)
        mixed[:, lanes] = outs_.astype(BF)

    def with_step(t):
        pair(t)
        for r in range(2, geo.A):
            share = -(-geo.NP // (I // 128))

            def go(i):
                p = t * share + i

                @pl.when(p < geo.NP)
                def _():
                    if r == 2:
                        ffn.step(r, p)

            loop(share, go)

    loop(I // 128, with_step)
    for e in range(per):
        pltpu.make_async_copy(pst.at[e], oP.at[e], psem.at[e]).wait()
    write(mixed, omixed)

    spread_mixed = dot(mixed[...], pout[...]).astype(BF)
    total = xv[...].astype(F32)
    for s in range(S):
        total += dot(spread_mixed[:, s * I4 : (s + 1) * I4], WA[s], NT)
    hid[...] = total
    scale = lax.rsqrt(jnp.sum(total * total, axis=-1, keepdims=True) / np.float32(geo.D) + EPSILON)
    X2[block(me.s, T), :] = (total * scale * gain[1:2, :]).astype(BF)
    gather_x2.begin()
    write(hid, ohid)
    gather_c.finish()
    write(C, oC)
    for r in range(3, geo.A):
        loop(geo.NP, lambda p: ffn.step(r, p))
    gather_x2.relay()
    for r in range(geo.A):
        loop(geo.NP, lambda p: ffn.ystep(r, p))
    gather_x2.finish()
    write(X2, oX2)
    loads[1].wait()

    def pcopy(n, k):
        return remote(part.at[0, n, k], got.at[n, k], ps.at[n, k], pr.at[n, k], me.dev(c=1 - me.c))

    def tokens_block(i):
        k = X - 1 - i // 2
        e = i % 2
        s = lax.rem(me.x + k, X) * 2 + lax.rem(1 + e + me.c, 2)
        rows = block(s, T)
        xb = X2[rows, :]
        gate = dot(xb, WF[0])
        upward = dot(xb, WF[1])
        back = dot(C[rows, :], WF[2])
        value, slope = gelu_parts(gate)
        activated = (value * upward).astype(BF)
        first = (back * upward * slope).astype(BF)
        second = (back * value).astype(BF)
        act[0, rows, :] = first
        act[1, rows, :] = second
        act[2, rows, :] = activated
        part[e, 0, k] = (dot(first, WF[0], NT) + dot(second, WF[1], NT)).astype(BF)
        part[e, 1, k] = dot(activated, WF[2], NT).astype(BF)

        @pl.when(e == 0)
        def _():
            pcopy(0, k).start()
            pcopy(1, k).start()

    loop(2 * X, tokens_block)
    write(act, oact)
    for k in range(X - 1, -1, -1):
        for n in range(2):
            pcopy(n, k).wait_recv()
            part[1, n, k] = (part[1, n, k].astype(F32) + got[n, k].astype(F32)).astype(BF)
    write(part.at[1], opart)
    for k in range(X):
        for n in range(2):
            pcopy(n, k).wait_send()

    def finish(g):
        for k in range(X):
            s = lax.rem(me.x - k + X, X) * 2 + 1 - me.c
            here = held_a(s, g)
            ccopy(k, g, here, s).wait_send()
            if k:
                xcopy(k, g, here).wait_send()

    loop(dp, finish)
    att.drain(0)
    loop(geo.NP, ffn.drain)
    for copy in writes:
        copy.wait()


def forward(geo, length, x, c, wf, wa):
    dma = pltpu.SemaphoreType.DMA
    S, N, F, T, L, I, H, X, I4 = geo.seq, geo.N, geo.F, geo.T, geo.L, geo.I, geo.H, geo.X, geo.I4
    per = 128 // (I // H)
    consts = constants(geo)
    out_shape = [
        ((S, N, I4), BF), ((T, N), BF), ((T, 3 * I), BF), ((L, 2 * I), BF), ((H, T, L), F32), ((T, I), BF),
        ((T, N), F32), ((L, N), BF), ((L, N), BF), ((3, L, F), BF), ((2, X, T, N), BF), ((8, N), F32),
    ]
    V = pltpu.VMEM
    scratch = [
        V((3, N, F), BF), V((S, N, I4), BF), V((T, N), BF), V((L, N), BF), V((L, N), BF), V((L, 2 * I), BF),
        V((T, N), BF), V((T, S * I4), BF), V((T, 3 * I), BF), V((H, 128, 2 * L - 128), BF), V((T, I), BF), V((T, N), F32),
        V((per, T, L), F32), V((3, L, F), BF), V((2, 2, X, T, N), BF), V((2, X, T, N), BF), V((8, N), F32),
        *[V(v.shape, v.dtype) for v in consts],
        dma((9,)), dma((12,)), dma((per,)),
        dma((geo.NZ, geo.NP)), dma((geo.NZ, geo.NP)), dma((geo.NY, geo.NP)), dma((geo.NY, geo.NP)),
        dma((geo.NZ, 1)), dma((geo.NZ, 1)), dma((geo.NY, 1)), dma((geo.NY, 1)),
        dma((X - 1, geo.dp)), dma((X - 1, geo.dp)), dma((X, geo.dp)), dma((X, geo.dp)),
        dma((3, X - 1)), dma((3, X - 1)), dma((3, X)), dma((3, X)),
        dma((2, X)), dma((2, X)),
    ]
    return pl.pallas_call(
        functools.partial(forward_kernel, geo),
        out_shape=[jax.ShapeDtypeStruct(*v) for v in out_shape],
        in_specs=[pl.BlockSpec(memory_space=pltpu.SMEM)] + [pl.BlockSpec(memory_space=pl.ANY)] * 9,
        out_specs=[pl.BlockSpec(memory_space=pl.ANY)] * len(out_shape),
        scratch_shapes=scratch,
        compiler_params=pltpu.CompilerParams(collective_id=0, has_side_effects=True, vmem_limit_bytes=63 << 20),
        name="forward",
    )(length, x, c, wf, wa, *consts)


def spread_features(values, geo, width):
    lead = values.shape[:-1]
    blocks = values.reshape(*lead, geo.dp, width)
    return jnp.pad(blocks, [(0, 0)] * (len(lead) + 1) + [(0, geo.R - width)]).reshape(*lead, geo.dp * geo.R)


def pack_features(values, geo, width):
    lead = values.shape[:-1]
    return values.reshape(*lead, geo.dp, geo.R)[..., :width].reshape(*lead, geo.dp * width)


def general_path(
    axes, tokens, cotangent, lengths, w_query, w_key_value, w_output, w_gate_up, w_down, norm_gains, position_bias
):
    dp, seq = axes
    width, own_inner = w_query.shape
    table_rows, head_count = position_bias.shape
    geo = Geo(dp, seq, width, w_down.shape[1], 4 * own_inner, tokens.shape[1], head_count, table_rows)
    rows = geo.R
    model_width = geo.D
    bucket_count = table_rows * dp
    inner_width = geo.I
    head_dim = inner_width // head_count

    lanes = lambda v: jnp.pad(v, ((0, 0), (0, geo.I4 - v.shape[1])))
    wa = jnp.concatenate(
        [
            jnp.concatenate([w_query, w_key_value[0], w_key_value[1], w_output], axis=1).astype(BF),
            jnp.zeros((rows - width - geo.E, geo.I4), BF),
            lanes(norm_gains.astype(BF)),
            lanes(position_bias.astype(BF)),
        ],
        axis=0,
    )
    wf = jnp.pad(jnp.concatenate([w_gate_up, w_down[None]], axis=0).astype(BF), ((0, 0), (0, rows - width), (0, 0)))
    WF, WA = gather_weights(geo, wf, wa)

    blocks = WA[0].reshape(dp, rows, geo.I4)
    first_gain = blocks[:, rows - geo.E, :width].reshape(model_width).astype(F32)
    second_gain = blocks[:, rows - geo.E + 1, :width].reshape(model_width).astype(F32)
    table_full = blocks[:, rows - table_rows :, :head_count].reshape(bucket_count, head_count)
    real = WA.reshape(seq, dp, rows, 4, own_inner)[:, :, :width]
    parts = real.transpose(3, 1, 2, 0, 4).reshape(4, model_width, inner_width)
    query_full, keyval_full, output_full = parts[0], parts[1:3], parts[3]

    inputs = tokens[0].astype(jnp.float32)
    row_count = inputs.shape[0]
    normed = norm_scale(inputs, first_gain).astype(jnp.bfloat16)
    queries = jnp.dot(normed, query_full, preferred_element_type=jnp.float32).astype(jnp.bfloat16)
    projected = jnp.einsum(
        "td,sdi->sti", normed, keyval_full, preferred_element_type=jnp.float32
    ).astype(jnp.bfloat16)
    keys_all, values_all = (
        lax.all_gather(projected[0], "seq", axis=0, tiled=True),
        lax.all_gather(projected[1], "seq", axis=0, tiled=True),
    )
    incoming_low = cotangent[0]
    incoming = incoming_low.astype(jnp.float32)
    cot_all = lax.all_gather(spread_features(incoming_low, geo, width), "seq", axis=0, tiled=True)
    length_all = keys_all.shape[0]
    block_start = lax.axis_index("seq") * row_count
    query_pos = block_start + jnp.arange(row_count, dtype=jnp.int32)
    key_pos = jnp.arange(length_all, dtype=jnp.int32)
    buckets = bucket_ids(key_pos[None, :] - query_pos[:, None])
    bucket_range = jnp.arange(bucket_count, dtype=jnp.int32)
    onehot = (buckets[:, :, None] == bucket_range).astype(jnp.bfloat16)
    score_bias = jnp.einsum("tkb,bh->htk", onehot, table_full, preferred_element_type=jnp.float32)
    key_valid = key_pos < lengths[0]
    query_heads = queries.reshape(row_count, head_count, head_dim)
    key_heads = keys_all.reshape(length_all, head_count, head_dim)
    value_heads = values_all.reshape(length_all, head_count, head_dim)
    raw_scores = (
        jnp.einsum("thc,khc->htk", query_heads, key_heads, preferred_element_type=jnp.float32) + score_bias
    )
    scores = jnp.where(key_valid[None, None, :], raw_scores, NEGATIVE)
    probs = jax.nn.softmax(scores, axis=-1)
    probs_low = probs.astype(BF)
    mixed_heads = (
        jnp.einsum("htk,khc->thc", probs_low, value_heads, preferred_element_type=jnp.float32)
        .reshape(row_count, inner_width)
        .astype(jnp.bfloat16)
    )
    attended = jnp.einsum("tc,dc->td", mixed_heads, output_full, preferred_element_type=jnp.float32)
    hidden_one = inputs + attended
    normed_two = norm_scale(hidden_one, second_gain).astype(jnp.bfloat16)
    normed_two_all = lax.all_gather(spread_features(normed_two, geo, width), "seq", axis=0, tiled=True)

    gate = jnp.dot(normed_two_all, WF[0], preferred_element_type=F32)
    upward = jnp.dot(normed_two_all, WF[1], preferred_element_type=F32)
    activated = gated(gate, upward).astype(BF)
    down_term = jnp.einsum("tf,df->td", activated, WF[2], preferred_element_type=F32)
    down_weight_grad = jnp.einsum("td,tf->df", cot_all, activated, preferred_element_type=F32)
    activated_grad = jnp.dot(cot_all, WF[2], preferred_element_type=F32)
    unused_value, gate_pull = jax.vjp(gated, gate, upward)
    gate_grad, upward_grad = gate_pull(activated_grad)
    gate_grad, upward_grad = gate_grad.astype(BF), upward_grad.astype(BF)
    gate_weight_grad = jnp.einsum("td,tf->df", normed_two_all, gate_grad, preferred_element_type=F32)
    up_weight_grad = jnp.einsum("td,tf->df", normed_two_all, upward_grad, preferred_element_type=F32)
    normed_two_term = jnp.einsum("tf,df->td", gate_grad, WF[0], preferred_element_type=F32) + jnp.einsum(
        "tf,df->td", upward_grad, WF[1], preferred_element_type=F32
    )
    down_sum = lax.psum_scatter(down_term.astype(BF), "seq", scatter_dimension=0, tiled=True)
    normed_two_sum = lax.psum_scatter(normed_two_term.astype(BF), "seq", scatter_dimension=0, tiled=True)
    outputs = (hidden_one + pack_features(down_sum, geo, width).astype(F32)).astype(BF)[None]
    normed_two_grad = pack_features(normed_two_sum, geo, width).astype(F32)
    gf = jnp.stack([gate_weight_grad.astype(BF), up_weight_grad.astype(BF), down_weight_grad.astype(BF)])

    unused_two, second_pull = jax.vjp(norm_scale, hidden_one, second_gain)
    hidden_norm_grad, second_gain_grad = second_pull(normed_two_grad)
    hidden_grad = incoming + hidden_norm_grad
    hidden_low = hidden_grad.astype(jnp.bfloat16)
    output_weight_grad = jnp.einsum("td,tc->dc", hidden_low, mixed_heads, preferred_element_type=jnp.float32)
    mixed_grad = jnp.einsum("td,dc->tc", hidden_low, output_full, preferred_element_type=jnp.float32).astype(
        jnp.bfloat16
    )
    grad_heads = mixed_grad.reshape(row_count, head_count, head_dim)
    prob_grad = jnp.einsum("thc,khc->htk", grad_heads, value_heads, preferred_element_type=jnp.float32)
    inner_sum = jnp.sum(probs * prob_grad, axis=-1, keepdims=True)
    score_grad = (probs * (prob_grad - inner_sum)).astype(jnp.bfloat16)
    query_act_grad = (
        jnp.einsum("htk,khc->thc", score_grad, key_heads, preferred_element_type=jnp.float32)
        .reshape(row_count, inner_width)
        .astype(jnp.bfloat16)
    )
    key_piece = jnp.einsum(
        "htk,thc->khc", score_grad, query_heads, preferred_element_type=jnp.float32
    ).reshape(length_all, inner_width)
    value_piece = jnp.einsum(
        "htk,thc->khc", probs_low, grad_heads, preferred_element_type=jnp.float32
    ).reshape(length_all, inner_width)
    own_terms = lax.psum_scatter(
        jnp.concatenate([key_piece, value_piece], axis=1).astype(jnp.bfloat16),
        "seq",
        scatter_dimension=0,
        tiled=True,
    )
    keyval_act_grad = jnp.stack([own_terms[:, :inner_width], own_terms[:, inner_width:]])
    query_weight_grad = jnp.einsum("td,tc->dc", normed, query_act_grad, preferred_element_type=jnp.float32)
    keyval_weight_grad = jnp.einsum("td,stc->sdc", normed, keyval_act_grad, preferred_element_type=jnp.float32)
    normed_grad = jnp.einsum(
        "tc,dc->td", query_act_grad, query_full, preferred_element_type=jnp.float32
    ) + jnp.einsum("stc,sdc->td", keyval_act_grad, keyval_full, preferred_element_type=jnp.float32)
    unused_three, first_pull = jax.vjp(norm_scale, inputs, first_gain)
    input_norm_grad, first_gain_grad = first_pull(normed_grad)
    input_grad = (hidden_grad + input_norm_grad).astype(jnp.bfloat16)[None]
    table_grad = jnp.einsum("htk,tkb->bh", score_grad, onehot, preferred_element_type=jnp.float32)

    grads = jnp.stack(
        [query_weight_grad, keyval_weight_grad[0], keyval_weight_grad[1], output_weight_grad]
    ).reshape(4, dp, width, seq, own_inner)
    grads = grads.transpose(3, 1, 2, 0, 4).reshape(seq, dp, width, geo.I4).astype(BF)
    wide = lambda v: jnp.pad(v, ((0, 0), (0, 0), (0, geo.I4 - v.shape[2])))
    more = jnp.concatenate(
        [
            jnp.zeros((dp, rows - width - geo.E, geo.I4), F32),
            wide(first_gain_grad.reshape(dp, 1, width)),
            wide(second_gain_grad.reshape(dp, 1, width)),
            wide(table_grad.reshape(dp, table_rows, head_count)),
        ],
        axis=1,
    ).astype(BF)
    ga = jnp.concatenate([grads, jnp.broadcast_to(more, (seq, *more.shape))], axis=2).reshape(seq, dp * rows, geo.I4)
    of, oa = scatter_grads(geo, gf, ga)

    main = oa[:width]
    query_part = main[:, :own_inner]
    keyval_part = jnp.stack([main[:, own_inner : 2 * own_inner], main[:, 2 * own_inner : 3 * own_inner]])
    output_part = main[:, 3 * own_inner :]
    gain_part = oa[rows - geo.E : rows - table_rows, :width]
    table_part = oa[rows - table_rows :, :head_count]
    return (
        outputs,
        input_grad,
        query_part,
        keyval_part,
        output_part,
        of[:2, :width],
        of[2, :width],
        gain_part,
        table_part,
    )

def fused_path(
    axes, tokens, cotangent, lengths, w_query, w_key_value, w_output, w_gate_up, w_down, norm_gains, position_bias
):
    dp, seq = axes
    width, own_inner = w_query.shape
    table_rows, head_count = position_bias.shape
    geo = Geo(dp, seq, width, w_down.shape[1], 4 * own_inner, tokens.shape[1], head_count, table_rows)
    rows = geo.R
    model_width = geo.D
    bucket_count = table_rows * dp
    inner_width = geo.I
    head_dim = inner_width // head_count

    lanes = lambda v: jnp.pad(v, ((0, 0), (0, geo.I4 - v.shape[1])))
    wa = jnp.concatenate(
        [
            jnp.concatenate([w_query, w_key_value[0], w_key_value[1], w_output], axis=1).astype(BF),
            jnp.zeros((rows - width - geo.E, geo.I4), BF),
            lanes(norm_gains.astype(BF)),
            lanes(position_bias.astype(BF)),
        ],
        axis=0,
    )
    wf = jnp.pad(jnp.concatenate([w_gate_up, w_down[None]], axis=0).astype(BF), ((0, 0), (0, rows - width), (0, 0)))
    xp = spread_features(tokens[0], geo, width)
    cp = spread_features(cotangent[0], geo, width)
    WA, normed_p, qkv, KV, probs, mixed_heads, hid_p, X2, C, act, part, gain = forward(geo, lengths, xp, cp, wf, wa)

    real = WA.reshape(seq, dp, rows, 4, own_inner)[:, :, :width]
    parts = real.transpose(3, 1, 2, 0, 4).reshape(4, model_width, inner_width)
    query_full, keyval_full, output_full = parts[0], parts[1:3], parts[3]
    first_gain = pack_features(gain[0], geo, width)
    second_gain = pack_features(gain[1], geo, width)
    inputs = tokens[0].astype(jnp.float32)
    row_count = inputs.shape[0]
    normed = pack_features(normed_p, geo, width)
    incoming = cotangent[0].astype(F32)
    length_all = geo.L
    block_start = lax.axis_index("seq") * row_count
    query_pos = block_start + jnp.arange(row_count, dtype=jnp.int32)
    key_pos = jnp.arange(length_all, dtype=jnp.int32)
    buckets = bucket_ids(key_pos[None, :] - query_pos[:, None])
    bucket_range = jnp.arange(bucket_count, dtype=jnp.int32)
    onehot = (buckets[:, :, None] == bucket_range).astype(jnp.bfloat16)
    query_heads = qkv[:, :inner_width].reshape(row_count, head_count, head_dim)
    key_heads = KV[:, :inner_width].reshape(length_all, head_count, head_dim)
    value_heads = KV[:, inner_width:].reshape(length_all, head_count, head_dim)
    probs_low = probs.astype(BF)
    hidden_one = pack_features(hid_p, geo, width)

    total = part[:, 0].astype(F32)
    for k in range(1, geo.X):
        shift = [(x * 2 + c, (x + k) % geo.X * 2 + c) for x in range(geo.X) for c in range(2)]
        total += lax.ppermute(part[:, k], "seq", shift).astype(F32)
    normed_two_grad = pack_features(total[0], geo, width)
    outputs = (hidden_one + pack_features(total[1], geo, width)).astype(BF)[None]
    gf = jnp.stack(
        [
            jnp.einsum("td,tf->df", X2, act[0], preferred_element_type=F32).astype(BF),
            jnp.einsum("td,tf->df", X2, act[1], preferred_element_type=F32).astype(BF),
            jnp.einsum("td,tf->df", C, act[2], preferred_element_type=F32).astype(BF),
        ]
    )
    unused_two, second_pull = jax.vjp(norm_scale, hidden_one, second_gain)
    hidden_norm_grad, second_gain_grad = second_pull(normed_two_grad)
    hidden_grad = incoming + hidden_norm_grad
    hidden_low = hidden_grad.astype(jnp.bfloat16)
    output_weight_grad = jnp.einsum("td,tc->dc", hidden_low, mixed_heads, preferred_element_type=jnp.float32)
    mixed_grad = jnp.einsum("td,dc->tc", hidden_low, output_full, preferred_element_type=jnp.float32).astype(
        jnp.bfloat16
    )
    grad_heads = mixed_grad.reshape(row_count, head_count, head_dim)
    prob_grad = jnp.einsum("thc,khc->htk", grad_heads, value_heads, preferred_element_type=jnp.float32)
    inner_sum = jnp.sum(probs * prob_grad, axis=-1, keepdims=True)
    score_grad = (probs * (prob_grad - inner_sum)).astype(jnp.bfloat16)
    query_act_grad = (
        jnp.einsum("htk,khc->thc", score_grad, key_heads, preferred_element_type=jnp.float32)
        .reshape(row_count, inner_width)
        .astype(jnp.bfloat16)
    )
    key_piece = jnp.einsum(
        "htk,thc->khc", score_grad, query_heads, preferred_element_type=jnp.float32
    ).reshape(length_all, inner_width)
    value_piece = jnp.einsum(
        "htk,thc->khc", probs_low, grad_heads, preferred_element_type=jnp.float32
    ).reshape(length_all, inner_width)
    own_terms = lax.psum_scatter(
        jnp.concatenate([key_piece, value_piece], axis=1).astype(jnp.bfloat16),
        "seq",
        scatter_dimension=0,
        tiled=True,
    )
    keyval_act_grad = jnp.stack([own_terms[:, :inner_width], own_terms[:, inner_width:]])
    query_weight_grad = jnp.einsum("td,tc->dc", normed, query_act_grad, preferred_element_type=jnp.float32)
    keyval_weight_grad = jnp.einsum("td,stc->sdc", normed, keyval_act_grad, preferred_element_type=jnp.float32)
    normed_grad = jnp.einsum(
        "tc,dc->td", query_act_grad, query_full, preferred_element_type=jnp.float32
    ) + jnp.einsum("stc,sdc->td", keyval_act_grad, keyval_full, preferred_element_type=jnp.float32)
    unused_three, first_pull = jax.vjp(norm_scale, inputs, first_gain)
    input_norm_grad, first_gain_grad = first_pull(normed_grad)
    input_grad = (hidden_grad + input_norm_grad).astype(jnp.bfloat16)[None]
    table_grad = jnp.einsum("htk,tkb->bh", score_grad, onehot, preferred_element_type=jnp.float32)

    grads = jnp.stack(
        [query_weight_grad, keyval_weight_grad[0], keyval_weight_grad[1], output_weight_grad]
    ).reshape(4, dp, width, seq, own_inner)
    grads = grads.transpose(3, 1, 2, 0, 4).reshape(seq, dp, width, geo.I4).astype(BF)
    wide = lambda v: jnp.pad(v, ((0, 0), (0, 0), (0, geo.I4 - v.shape[2])))
    more = jnp.concatenate(
        [
            jnp.zeros((dp, rows - width - geo.E, geo.I4), F32),
            wide(first_gain_grad.reshape(dp, 1, width)),
            wide(second_gain_grad.reshape(dp, 1, width)),
            wide(table_grad.reshape(dp, table_rows, head_count)),
        ],
        axis=1,
    ).astype(BF)
    ga = jnp.concatenate([grads, jnp.broadcast_to(more, (seq, *more.shape))], axis=2).reshape(seq, dp * rows, geo.I4)
    of, oa = scatter_grads(geo, gf, ga)

    main = oa[:width]
    query_part = main[:, :own_inner]
    keyval_part = jnp.stack([main[:, own_inner : 2 * own_inner], main[:, 2 * own_inner : 3 * own_inner]])
    output_part = main[:, 3 * own_inner :]
    gain_part = oa[rows - geo.E : rows - table_rows, :width]
    table_part = oa[rows - table_rows :, :head_count]
    return (
        outputs,
        input_grad,
        query_part,
        keyval_part,
        output_part,
        of[:2, :width],
        of[2, :width],
        gain_part,
        table_part,
    )

def per_device(axes, *arrays):
    tokens, w_query, w_down, position_bias = arrays[0], arrays[3], arrays[7], arrays[9]
    geo = Geo(*axes, w_query.shape[0], w_down.shape[1], 4 * w_query.shape[1], tokens.shape[1], position_bias.shape[1],
              position_bias.shape[0])
    aligned = geo.F % 128 == 0 and geo.I4 % 128 == 0 and 2 * geo.R % 128 == 0 and geo.T % 128 == 0 and geo.I % 128 == 0
    small = (3 * geo.F + geo.seq * geo.I4 + 2 * geo.L) * geo.N * 2 <= 24 << 20
    return (fused_path if aligned and small else general_path)(axes, *arrays)


def solution(mesh):
    in_specs = (
        P("dp", "seq", None),
        P("dp", "seq", None),
        P("dp"),
        P("dp", "seq"),
        P(None, "dp", "seq"),
        P("dp", "seq"),
        P(None, "dp", "seq"),
        P("dp", "seq"),
        P(None, "dp"),
        P("dp", None),
    )
    out_specs = (
        P("dp", "seq", None),
        P("dp", "seq", None),
        P("dp", "seq"),
        P(None, "dp", "seq"),
        P("dp", "seq"),
        P(None, "dp", "seq"),
        P("dp", "seq"),
        P(None, "dp"),
        P("dp", None),
    )
    return jax.shard_map(
        functools.partial(per_device, (mesh.shape["dp"], mesh.shape["seq"])), mesh=mesh, in_specs=in_specs, out_specs=out_specs, check_vma=False
    )
```

```python
import functools
import jax
import jax.numpy as jnp
import numpy as np
from jax import lax
from jax.experimental import pallas as pl
from jax.experimental.pallas import tpu as pltpu

from jax.sharding import PartitionSpec as P

MESH = pl.DeviceIdType.MESH
BF = jnp.bfloat16
F32 = jnp.float32


class Geo:
    def __init__(self, dp, seq, width, ff, inner4, tokens, heads, table_rows):
        self.dp, self.seq = dp, seq
        self.W, self.TR, self.E = width, table_rows, 2 + table_rows
        rows = -(-(width + self.E) // 16) * 16
        self.D, self.N, self.T, self.L = dp * width, dp * rows, tokens, seq * tokens
        self.I, self.H = inner4 // 4 * seq, heads
        self.B, self.A, self.X = 2, dp // 2, seq // 2
        self.R, self.F, self.I4 = rows, ff, inner4
        self.NH = 2 if rows % 32 == 0 else 1
        self.RH = rows // self.NH
        self.NP = 3 * self.NH
        self.NZ = 2 * (self.A - 1)
        self.NY = 2 * self.A - 1


class Place:
    def __init__(self, geo):
        d, s = lax.axis_index("dp"), lax.axis_index("seq")
        self.d, self.s = d, s
        self.z, self.y = d // 2, d % 2
        self.x, self.c = s // 2, s % 2

    def dev(self, z=None, y=None, x=None, c=None):
        z = self.z if z is None else z
        y = self.y if y is None else y
        x = self.x if x is None else x
        c = self.c if c is None else c
        return (z * 2 + y, x * 2 + c)


def remote(src, dst, ss, rs, dev):
    return pltpu.make_async_remote_copy(
        src_ref=src, dst_ref=dst, send_sem=ss, recv_sem=rs, device_id=dev, device_id_type=MESH
    )


def loop(n, body):
    def step(i, carry):
        body(i)
        return carry

    lax.fori_loop(0, n, step, 0)


def enter(geo, me):
    bar = pltpu.get_barrier_semaphore()

    def greet(dev):
        pl.semaphore_signal(bar, 1, device_id=dev, device_id_type=MESH)

    greet(me.dev(y=1 - me.y))
    greet(me.dev(c=1 - me.c))
    for k in range(1, geo.X):
        greet(me.dev(x=lax.rem(me.x + k, geo.X)))

    @pl.when(me.z > 0)
    def _():
        greet(me.dev(z=me.z - 1))

    @pl.when(me.z < geo.A - 1)
    def _():
        greet(me.dev(z=me.z + 1))

    count = 2 + (geo.X - 1) + (me.z > 0).astype(jnp.int32) + (me.z < geo.A - 1).astype(jnp.int32)
    pl.semaphore_wait(bar, count)


class LineGather:
    def __init__(self, geo, me, own, held, zs, zr, ys, yr):
        self.geo, self.me, self.own, self.held = geo, me, own, held
        self.zs, self.zr, self.ys, self.yr = zs, zr, ys, yr

    def zcopy(self, way, r, p):
        me, geo = self.me, self.geo
        q = me.z - (r - 1) if way == 0 else me.z + (r - 1)
        to = me.z + 1 if way == 0 else me.z - 1
        valid = (me.z < geo.A - 1) & (q >= 0) if way == 0 else (me.z > 0) & (q <= geo.A - 1)
        g = q * 2 + me.y
        src = self.own(p) if r == 1 else self.held(p, g)
        slot = way * (geo.A - 1) + r - 1
        copy = remote(src, self.held(p, g), self.zs.at[slot, p], self.zr.at[slot, p], me.dev(z=to))
        return copy, valid

    def zarrive(self, way, r, p):
        me, geo = self.me, self.geo
        q = me.z - r if way == 0 else me.z + r
        valid = (q >= 0) if way == 0 else (q <= geo.A - 1)
        slot = way * (geo.A - 1) + r - 1
        here = self.held(p, q * 2 + me.y)
        copy = remote(here, here, self.zs.at[slot, p], self.zr.at[slot, p], me.dev(y=1 - me.y))
        return copy, valid, q

    def ycopy(self, way, r, p):
        me, geo = self.me, self.geo
        if r == 0:
            q, slot, src = me.z, 0, self.own(p)
        else:
            q = me.z - r if way == 0 else me.z + r
            slot = 1 + way * (geo.A - 1) + r - 1
            src = self.held(p, q * 2 + me.y)
        copy = remote(
            src, self.held(p, q * 2 + me.y), self.ys.at[slot, p], self.yr.at[slot, p], me.dev(y=1 - me.y)
        )
        return copy

    def yarrive(self, way, r, p):
        me, geo = self.me, self.geo
        if r == 0:
            q, slot = me.z, 0
        else:
            q = me.z - r if way == 0 else me.z + r
            slot = 1 + way * (geo.A - 1) + r - 1
        here = self.held(p, q * 2 + 1 - me.y)
        copy = remote(here, here, self.ys.at[slot, p], self.yr.at[slot, p], me.dev(y=1 - me.y))
        return copy, q

    def valid(self, way, r):
        q = self.me.z - r if way == 0 else self.me.z + r
        return (q >= 0) if way == 0 else (q <= self.geo.A - 1)

    def begin(self, p):
        self.ycopy(0, 0, p).start()
        for way in (0, 1):
            copy, valid = self.zcopy(way, 1, p)

            @pl.when(valid)
            def _():
                copy.start()

    def step(self, r, p, on_held=None):
        for way in (0, 1):
            copy, valid, q = self.zarrive(way, r, p)

            @pl.when(valid)
            def _():
                copy.wait_recv()
                if r < self.geo.A - 1:
                    onward, may = self.zcopy(way, r + 1, p)

                    @pl.when(may)
                    def _():
                        onward.start()

                self.ycopy(way, r, p).start()
                if on_held is not None:
                    on_held(q * 2 + self.me.y)

    def ystep(self, r, p, on_held=None):
        for way in (0, 1) if r else (0,):
            copy, q = self.yarrive(way, r, p)
            valid = self.valid(way, r) if r else True

            def go():
                copy.wait_recv()
                if on_held is not None:
                    on_held(q * 2 + 1 - self.me.y)

            if r:
                pl.when(valid)(go)
            else:
                go()

    def drain(self, p):
        self.ycopy(0, 0, p).wait_send()
        for r in range(1, self.geo.A):
            for way in (0, 1):
                copy, valid = self.zcopy(way, r, p)

                @pl.when(valid)
                def _():
                    copy.wait_send()

                @pl.when(self.valid(way, r))
                def _():
                    self.ycopy(way, r, p).wait_send()


class LineScatter:
    def __init__(self, geo, me, part, ybuf, zbuf, stage, zs, zr, ys, yr, finish):
        self.__dict__.update(locals())

    def turns(self):
        geo, me = self.geo, self.me
        for k in range(geo.A - 1):
            yield 0, k, geo.A - 1 - k, k < geo.A - 1 - me.z
            yield 1, k, k, k < me.z

    def slot(self, way, k):
        return way * (self.geo.A - 1) + k

    def ycopy(self, slot, t, p):
        me = self.me
        return remote(
            self.part(p, t * 2 + 1 - me.y),
            self.ybuf(p, t),
            self.ys.at[slot, p],
            self.yr.at[slot, p],
            me.dev(y=1 - me.y),
        )

    def zcopy(self, way, k, p):
        me = self.me
        to = me.z + 1 if way == 0 else me.z - 1
        slot = self.slot(way, k)
        return remote(
            self.stage(way, p, k), self.zbuf(way, p, k), self.zs.at[slot, p], self.zr.at[slot, p], me.dev(z=to)
        )

    def ysend(self, p, k):
        for way, kk, t, valid in self.turns():
            if kk == k:

                @pl.when(valid)
                def _():
                    self.ycopy(self.slot(way, kk), t, p).start()

    def ysend_own(self, p):
        self.ycopy(self.geo.NZ, self.me.z, p).start()

    def step(self, k, p):
        geo, me = self.geo, self.me
        for way, kk, t, valid in self.turns():
            if kk == k:

                @pl.when(valid)
                def _():
                    self.ycopy(self.slot(way, k), t, p).wait_recv()
                    total = self.part(p, t * 2 + me.y)[...].astype(F32) + self.ybuf(p, t)[...].astype(F32)
                    out = self.stage(way, p, k)
                    comes = me.z > 0 if way == 0 else me.z < geo.A - 1

                    @pl.when(comes)
                    def _():
                        self.zcopy(way, k, p).wait_recv()
                        out[...] = (total + self.zbuf(way, p, k)[...].astype(F32)).astype(BF)

                    @pl.when(jnp.logical_not(comes))
                    def _():
                        out[...] = total.astype(BF)

                    self.zcopy(way, k, p).start()

    def own(self, p):
        geo, me = self.geo, self.me
        self.ycopy(geo.NZ, me.z, p).wait_recv()
        total = self.part(p, me.z * 2 + me.y)[...].astype(F32) + self.ybuf(p, me.z)[...].astype(F32)
        kup = jnp.minimum(geo.A - 1 - me.z, geo.A - 2)
        kdown = jnp.minimum(me.z, geo.A - 2)

        def arrive(way, k):
            slot = way * (geo.A - 1) + k
            here = self.zbuf(way, p, k)
            remote(here, here, self.zs.at[slot, p], self.zr.at[slot, p], me.dev(y=1 - me.y)).wait_recv()
            return here[...].astype(F32)

        @pl.when(me.z == 0)
        def _():
            self.finish(p, total + arrive(1, kdown))

        @pl.when(me.z == geo.A - 1)
        def _():
            self.finish(p, total + arrive(0, kup))

        @pl.when((me.z > 0) & (me.z < geo.A - 1))
        def _():
            self.finish(p, total + arrive(0, kup) + arrive(1, kdown))

    def drain(self, p):
        for way, k, t, valid in self.turns():

            @pl.when(valid)
            def _():
                self.ycopy(self.slot(way, k), t, p).wait_send()
                self.zcopy(way, k, p).wait_send()

        self.ycopy(self.geo.NZ, self.me.z, p).wait_send()


NEGATIVE = -1e30
EPSILON = 1e-06
LIMITS = (12, 16, 23, 32, 46, 64, 91)


def bucket_ids(offsets):
    distance = jnp.abs(offsets)
    larger = 8 + sum(((distance >= threshold).astype(jnp.int32) for threshold in LIMITS))
    nearby = jnp.where(distance < 8, distance, larger)
    return jnp.where(offsets > 0, 16, 0) + nearby


def norm_scale(values, gain_vector):
    return (
        values
        * lax.rsqrt(jnp.mean(values * values, axis=-1, keepdims=True) + EPSILON)
        * gain_vector
    )


def gated(gate_value, upward):
    return jax.nn.gelu(gate_value, approximate=True) * upward


def gather_kernel(geo, wf, wa, WF, WA, local, zs, zr, ys, yr, azs, azr, ays, ayr, xs, xr, cs, cr):
    me = Place(geo)
    R, RH, NH, dp, X = geo.R, geo.RH, geo.NH, geo.dp, geo.X
    mine = [
        pltpu.make_async_copy(wf, WF.at[:, pl.ds(pl.multiple_of(me.d * R, 16), R), :], local.at[0]),
        pltpu.make_async_copy(wa, WA.at[me.s, pl.ds(pl.multiple_of(me.d * R, 16), R), :], local.at[1]),
    ]
    for copy in mine:
        copy.start()
    enter(geo, me)

    def own_f(p):
        return wf.at[p // NH, pl.ds(pl.multiple_of((p % NH) * RH, 16), RH), :]

    def held_f(p, g):
        return WF.at[p // NH, pl.ds(pl.multiple_of(g * R + (p % NH) * RH, 16), RH), :]

    def held_a(s, g):
        return WA.at[s, pl.ds(pl.multiple_of(g * R, 16), R), :]

    ffn = LineGather(geo, me, own_f, held_f, zs, zr, ys, yr)
    att = LineGather(geo, me, lambda p: wa, lambda p, g: held_a(me.s, g), azs, azr, ays, ayr)

    def xcopy(k, g, src):
        to = lax.rem(me.x + k, X)
        return remote(src, held_a(me.s, g), xs.at[k - 1, g], xr.at[k - 1, g], me.dev(x=to))

    def xarrive(k, g):
        src_x = lax.rem(me.x - k + X, X)
        here = held_a(src_x * 2 + me.c, g)
        return remote(here, here, xs.at[k - 1, g], xr.at[k - 1, g], me.dev(c=1 - me.c)), here

    def ccopy(k, g, src, s):
        return remote(src, held_a(s, g), cs.at[k, g], cr.at[k, g], me.dev(c=1 - me.c))

    def spread(g, src=None):
        src = held_a(me.s, g) if src is None else src
        for k in range(1, X):
            xcopy(k, g, src).start()
        ccopy(0, g, src, me.s).start()

    att.begin(0)
    spread(me.d, wa)
    loop(geo.NP, ffn.begin)
    att.ystep(0, 0, spread)
    for r in range(1, geo.A):
        att.step(r, 0, spread)
        att.ystep(r, 0, spread)

    def from_x(g):
        for k in range(1, X):
            copy, here = xarrive(k, g)
            copy.wait_recv()
            ccopy(k, g, here, lax.rem(me.x - k + X, X) * 2 + me.c).start()

    loop(dp, from_x)
    for r in range(1, geo.A):
        loop(geo.NP, lambda p: ffn.step(r, p))
    for r in range(geo.A):
        loop(geo.NP, lambda p: ffn.ystep(r, p))

    def finish(g):
        for k in range(X):
            s = lax.rem(me.x - k + X, X) * 2 + 1 - me.c
            here = held_a(s, g)
            remote(here, here, cs.at[k, g], cr.at[k, g], me.dev(c=1 - me.c)).wait_recv()
            ccopy(k, g, here, s).wait_send()
            if k:
                xcopy(k, g, here).wait_send()

    loop(dp, finish)
    att.drain(0)
    loop(geo.NP, ffn.drain)
    for copy in mine:
        copy.wait()


def scatter_kernel(
    geo, gf, ga, of, oa, yb, zb, st, cb, xb, xst, pa, ayb, azb, ast,
    zs, zr, ys, yr, azs, azr, ays, ayr, xs, xr, cs, cr,
):
    me = Place(geo)
    R, RH, NH, dp, X, A = geo.R, geo.RH, geo.NH, geo.dp, geo.X, geo.A
    enter(geo, me)

    def rows(g, p):
        return pl.ds(pl.multiple_of(g * R + (p % NH) * RH, 16), RH)

    def piece(buf, i, p):
        return buf.at[i, p // NH, pl.ds(pl.multiple_of((p % NH) * RH, 16), RH), :]

    def finish_f(p, value):
        of[p // NH, pl.ds(pl.multiple_of((p % NH) * RH, 16), RH), :] = value

    ffn = LineScatter(
        geo, me,
        lambda p, g: gf.at[p // NH, rows(g, p), :],
        lambda p, t: piece(yb, t, p),
        lambda way, p, k: piece(zb, way * (A - 1) + k, p),
        lambda way, p, k: piece(st, way * (A - 1) + k, p),
        zs, zr, ys, yr, finish_f,
    )

    def block(g):
        return pl.ds(pl.multiple_of(g * R, 16), R)

    def finish_a(p, value):
        oa[...] = value

    att = LineScatter(
        geo, me,
        lambda p, g: pa.at[block(g), :],
        lambda p, t: ayb.at[t],
        lambda way, p, k: azb.at[way * (A - 1) + k],
        lambda way, p, k: ast.at[way * (A - 1) + k],
        azs, azr, ays, ayr, finish_a,
    )

    def ccopy(k, g):
        to_x = lax.rem(me.x + k, X)
        return remote(
            ga.at[to_x * 2 + 1 - me.c, block(g), :], cb.at[k, block(g), :], cs.at[k, g], cr.at[k, g], me.dev(c=1 - me.c)
        )

    def xcopy(k, g):
        return remote(
            xst.at[k - 1, block(g), :], xb.at[k - 1, block(g), :], xs.at[k - 1, g], xr.at[k - 1, g],
            me.dev(x=lax.rem(me.x + k, X)),
        )

    def to_core(g):
        for k in (*range(1, X), 0):
            ccopy(k, g).start()

    def to_x(g):
        for k in range(1, X):
            ccopy(k, g).wait_recv()
            s = lax.rem(me.x + k, X) * 2 + me.c
            xst[k - 1, block(g), :] = (
                ga[s, block(g), :].astype(F32) + cb[k, block(g), :].astype(F32)
            ).astype(BF)
            xcopy(k, g).start()

    def meet(g):
        ccopy(0, g).wait_recv()
        total = ga[me.s, block(g), :].astype(F32) + cb[0, block(g), :].astype(F32)
        for k in range(1, X):
            xcopy(k, g).wait_recv()
            total += xb[k - 1, block(g), :].astype(F32)
        pa[block(g), :] = total.astype(BF)

    def free(g):
        for k in range(X):
            ccopy(k, g).wait_send()
            if k:
                xcopy(k, g).wait_send()

    for k in range(A - 1):
        loop(geo.NP, lambda p: ffn.ysend(p, k))
    loop(geo.NP, ffn.ysend_own)
    loop(dp, to_core)
    loop(dp, to_x)
    for k in range(A - 1):
        loop(geo.NP, lambda p: ffn.step(k, p))
    loop(geo.NP, ffn.own)
    loop(dp, meet)
    for k in range(A - 1):
        att.ysend(0, k)
    att.ysend_own(0)
    for k in range(A - 1):
        att.step(k, 0)
    att.own(0)
    loop(dp, free)
    att.drain(0)
    loop(geo.NP, ffn.drain)


def gather_weights(geo, wf, wa):
    dma = pltpu.SemaphoreType.DMA
    sems = [
        dma((2,)),
        dma((geo.NZ, geo.NP)), dma((geo.NZ, geo.NP)), dma((geo.NY, geo.NP)), dma((geo.NY, geo.NP)),
        dma((geo.NZ, 1)), dma((geo.NZ, 1)), dma((geo.NY, 1)), dma((geo.NY, 1)),
        dma((geo.X - 1, geo.dp)), dma((geo.X - 1, geo.dp)), dma((geo.X, geo.dp)), dma((geo.X, geo.dp)),
    ]
    return pl.pallas_call(
        functools.partial(gather_kernel, geo),
        out_shape=(
            jax.ShapeDtypeStruct((3, geo.dp * geo.R, geo.F), BF),
            jax.ShapeDtypeStruct((geo.seq, geo.dp * geo.R, geo.I4), BF),
        ),
        in_specs=[pl.BlockSpec(memory_space=pl.ANY)] * 2,
        out_specs=[pl.BlockSpec(memory_space=pl.ANY)] * 2,
        scratch_shapes=sems,
        compiler_params=pltpu.CompilerParams(collective_id=0, has_side_effects=True, vmem_limit_bytes=48 << 20),
        name="gather_weights",
    )(wf, wa)


def scatter_grads(geo, gf, ga):
    dma = pltpu.SemaphoreType.DMA
    n, X, A, R = geo.dp * geo.R, geo.X, geo.A, geo.R
    scratch = [
        pltpu.VMEM((A, 3, R, geo.F), BF), pltpu.VMEM((geo.NZ, 3, R, geo.F), BF), pltpu.VMEM((geo.NZ, 3, R, geo.F), BF),
        pltpu.VMEM((X, n, geo.I4), BF), pltpu.VMEM((X - 1, n, geo.I4), BF), pltpu.VMEM((X - 1, n, geo.I4), BF),
        pltpu.VMEM((n, geo.I4), BF),
        pltpu.VMEM((A, R, geo.I4), BF), pltpu.VMEM((geo.NZ, R, geo.I4), BF), pltpu.VMEM((geo.NZ, R, geo.I4), BF),
        dma((geo.NZ, geo.NP)), dma((geo.NZ, geo.NP)), dma((geo.NZ + 1, geo.NP)), dma((geo.NZ + 1, geo.NP)),
        dma((geo.NZ, 1)), dma((geo.NZ, 1)), dma((geo.NZ + 1, 1)), dma((geo.NZ + 1, 1)),
        dma((X - 1, geo.dp)), dma((X - 1, geo.dp)), dma((X, geo.dp)), dma((X, geo.dp)),
    ]
    return pl.pallas_call(
        functools.partial(scatter_kernel, geo),
        out_shape=(
            jax.ShapeDtypeStruct((3, R, geo.F), F32),
            jax.ShapeDtypeStruct((R, geo.I4), F32),
        ),
        in_specs=[pl.BlockSpec(memory_space=pltpu.VMEM)] * 2,
        out_specs=[pl.BlockSpec(memory_space=pltpu.VMEM)] * 2,
        scratch_shapes=scratch,
        compiler_params=pltpu.CompilerParams(collective_id=1, has_side_effects=True, vmem_limit_bytes=60 << 20),
        name="scatter_grads",
    )(gf, ga)


class SeqGather:
    def __init__(self, geo, me, held, xs, xr, cs, cr):
        self.geo, self.me, self.held = geo, me, held
        self.xs, self.xr, self.cs, self.cr = xs, xr, cs, cr

    def ccopy(self, k):
        me, X = self.me, self.geo.X
        here = self.held(lax.rem(me.x - k + X, X) * 2 + me.c)
        return remote(here, here, self.cs.at[k], self.cr.at[k], me.dev(c=1 - me.c))

    def xcopy(self, k):
        me = self.me
        here = self.held(me.s)
        return remote(here, here, self.xs.at[k - 1], self.xr.at[k - 1], me.dev(x=lax.rem(me.x + k, self.geo.X)))

    def begin(self):
        for k in range(1, self.geo.X):
            self.xcopy(k).start()
        self.ccopy(0).start()

    def relay(self):
        for k in range(1, self.geo.X):
            self.xcopy(k).wait_recv()
            self.ccopy(k).start()

    def finish(self):
        for k in range(self.geo.X):
            self.ccopy(k).wait_recv()
            self.ccopy(k).wait_send()
            if k:
                self.xcopy(k).wait_send()


def dot(a, b, dims=((1,), (0,))):
    return lax.dot_general(a, b, (dims, ((), ())), preferred_element_type=F32)


NT = ((1,), (1,))
TN = ((0,), (0,))


def constants(geo):
    own, I4, S, I, N = geo.I4 // 4, geo.I4, geo.seq, geo.I, geo.N
    perm_out = np.zeros((I, S * I4), np.float32)
    i = np.arange(own)
    for s in range(S):
        perm_out[s * own + i, s * I4 + 3 * own + i] = 1
    place = np.arange(N)
    tile = np.zeros((I4, N), np.float32)
    inside = place % geo.R < geo.W
    tile[(place % geo.R)[inside], place[inside]] = 1
    group = np.tile((place // geo.R * 16).astype(np.float32), (8, 1))
    offset = np.arange(512) - 256
    distance = np.abs(offset)
    larger = 8 + sum((distance >= limit).astype(np.int32) for limit in LIMITS)
    bucket = np.where(offset > 0, 16, 0) + np.where(distance < 8, distance, larger)
    onehot = np.zeros((geo.dp * 16, 512), np.float32)
    for b in range(geo.dp * geo.TR):
        onehot[b // geo.TR * 16 + 16 - geo.E + 2 + b % geo.TR] = bucket == b
    return [jnp.asarray(v, BF) for v in (perm_out, tile)] + [jnp.asarray(group), jnp.asarray(onehot, BF)]


def shear(value, sign):
    rows, lanes = value.shape
    row = lax.broadcasted_iota(jnp.int32, (rows, 1), 0)
    bit = 1
    while bit < rows:
        moved = pltpu.roll(value, bit if sign > 0 else lanes - bit, 1)
        value = jnp.where((row & bit) != 0, moved, value)
        bit *= 2
    return value


def gelu_parts(g):
    k0 = np.float32(np.sqrt(2 / np.pi))
    t = jnp.tanh(k0 * (g + np.float32(0.044715) * (g * g * g)))
    half = 0.5 * (1.0 + t)
    slope = half + 0.5 * g * (1.0 - t * t) * (k0 * (1.0 + np.float32(3 * 0.044715) * (g * g)))
    return g * half, slope


def forward_kernel(
    geo, length, x_in, c_in, wf, wa, cpo, ctile, cgroup, conehot,
    oWA, oqkv, oKV, oP, omixed, ohid, oX2, oC, oact, opart, ogain,
    WF, WA, xv, C, X2, KV, qkv, strip, mixed, hid, pst, act, part, got, gain, pout, tile, group, onehot,
    local, outs, psem, zs, zr, ys, yr, azs, azr, ays, ayr, xs, xr, cs, cr, gxs, gxr, gcs, gcr, ps, pr,
):
    me = Place(geo)
    R, RH, NH, dp, X, T, N, I = geo.R, geo.RH, geo.NH, geo.dp, geo.X, geo.T, geo.N, geo.I
    I4, S, L = geo.I4, geo.seq, geo.L
    block = lambda i, n: pl.ds(pl.multiple_of(i * n, 16), n)
    loads = [
        (wa, WA.at[me.s, block(me.d, R), :]),
        (wf, WF.at[:, block(me.d, R), :]),
        (c_in, C.at[block(me.s, T), :]),
        (x_in, xv),
        (cpo, pout), (ctile, tile), (cgroup, group), (conehot, onehot),
    ]
    loads = [pltpu.make_async_copy(src, dst, local.at[i]) for i, (src, dst) in enumerate(loads)]
    for copy in loads:
        copy.start()
    enter(geo, me)

    def own_f(p):
        return wf.at[p // NH, pl.ds(pl.multiple_of((p % NH) * RH, 16), RH), :]

    def held_f(p, g):
        return WF.at[p // NH, pl.ds(pl.multiple_of(g * R + (p % NH) * RH, 16), RH), :]

    def held_a(s, g):
        return WA.at[s, block(g, R), :]

    ffn = LineGather(geo, me, own_f, held_f, zs, zr, ys, yr)
    att = LineGather(geo, me, lambda p: wa, lambda p, g: held_a(me.s, g), azs, azr, ays, ayr)

    def xcopy(k, g, src):
        to = lax.rem(me.x + k, X)
        return remote(src, held_a(me.s, g), xs.at[k - 1, g], xr.at[k - 1, g], me.dev(x=to))

    def xarrive(k, g):
        src_x = lax.rem(me.x - k + X, X)
        here = held_a(src_x * 2 + me.c, g)
        return remote(here, here, xs.at[k - 1, g], xr.at[k - 1, g], me.dev(c=1 - me.c)), here

    def ccopy(k, g, src, s):
        return remote(src, held_a(s, g), cs.at[k, g], cr.at[k, g], me.dev(c=1 - me.c))

    def spread(g, src=None):
        src = held_a(me.s, g) if src is None else src
        for k in range(1, X):
            xcopy(k, g, src).start()
        ccopy(0, g, src, me.s).start()

    seq = [
        SeqGather(geo, me, (lambda ref: lambda s: ref.at[block(s, T), :])(ref), gxs.at[i], gxr.at[i], gcs.at[i], gcr.at[i])
        for i, ref in enumerate((C, KV, X2))
    ]
    gather_c, gather_kv, gather_x2 = seq

    att.begin(0)
    spread(me.d, wa)
    loop(geo.NP, ffn.begin)
    att.ystep(0, 0, spread)
    for r in range(1, geo.A):
        att.step(r, 0, spread)
        att.ystep(r, 0, spread)
    loads[2].wait()
    gather_c.begin()

    def from_x(g):
        for k in range(1, X):
            copy, here = xarrive(k, g)
            copy.wait_recv()
            ccopy(k, g, here, lax.rem(me.x - k + X, X) * 2 + me.c).start()

    loop(dp, from_x)
    for i in (3, 4, 5, 6, 7):
        loads[i].wait()

    def settle(g):
        for k in range(X):
            s = lax.rem(me.x - k + X, X) * 2 + 1 - me.c
            here = held_a(s, g)
            remote(here, here, cs.at[k, g], cr.at[k, g], me.dev(c=1 - me.c)).wait_recv()

    loop(dp, settle)
    loads[0].wait()
    loop(geo.NP, lambda p: ffn.step(1, p))

    extra = jnp.concatenate([WA[0, g * R + R - 16 : g * R + R, :] for g in range(dp)], axis=0)
    spread_rows = dot(extra, tile[...])
    row = lax.broadcasted_iota(jnp.int32, (dp * 16, N), 0).astype(F32)
    gains = []
    for e in range(2):
        hit = row == group[0:1, :] + np.float32(16 - geo.E + e)
        gains.append(jnp.sum(jnp.where(hit, spread_rows, 0.0), axis=0, keepdims=True))
    gain[...] = jnp.concatenate(gains + [jnp.zeros((6, N), F32)], axis=0)
    bias = dot(extra[:, :128] if I4 >= 128 else extra, onehot[...], TN)

    inputs = xv[...].astype(F32)
    scale = lax.rsqrt(jnp.sum(inputs * inputs, axis=-1, keepdims=True) / np.float32(geo.D) + EPSILON)
    normed = (inputs * scale * gain[0:1, :]).astype(BF)
    columns = jnp.concatenate([dot(normed, WA[s]) for s in range(S)], axis=1)
    for kind in range(3):
        moved = pltpu.roll(columns, (3 - kind) * (I4 // 4), 1).astype(BF)
        qkv[:, kind * I : (kind + 1) * I] = dot(moved, pout[...], NT).astype(BF)
    KV[block(me.s, T), :] = qkv[:, I:]
    gather_kv.begin()
    writes = []

    def write(src, dst):
        copy = pltpu.make_async_copy(src, dst, outs.at[len(writes)])
        copy.start()
        writes.append(copy)

    write(WA, oWA)
    write(qkv, oqkv)
    write(gain, ogain)
    NB = L // 128
    for h in range(geo.H):
        band = shear(jnp.broadcast_to(bias[h : h + 1, :], (128, 512)), 1)[:, 128:512].astype(BF)
        strip[h, :, (NB - 2) * 128 : (NB + 1) * 128] = band
        far = (NB - 2) * 128
        strip[h, :, :far] = jnp.broadcast_to(bias[h : h + 1, 0:1], (128, far)).astype(BF)
        strip[h, :, (NB + 1) * 128 :] = jnp.broadcast_to(bias[h : h + 1, 511:512], (128, far)).astype(BF)
    gather_c.relay()
    gather_kv.relay()
    gather_kv.finish()
    write(KV, oKV)

    hd = I // geo.H
    per = 128 // hd
    valid = lax.broadcasted_iota(jnp.int32, (1, L), 1) < length[0]

    def pair(t):
        lanes = pl.ds(pl.multiple_of(t * 128, 128), 128)
        head = lax.broadcasted_iota(jnp.int32, (1, 128), 1) // hd
        keys = KV[:, lanes]
        values = KV[:, pl.ds(pl.multiple_of(I + t * 128, 128), 128)]
        queries = qkv[:, lanes]
        outs_ = jnp.zeros((T, 128), F32)
        for e in range(per):
            h = t * per + e
            scores = dot(jnp.where(head == e, queries, jnp.zeros_like(queries)), keys, NT)
            shift = [
                strip[h, :, pl.ds(pl.multiple_of((NB - 1 - me.s * (T // 128) - b) * 128, 128), L)].astype(F32)
                for b in range(T // 128)
            ]
            scores = jnp.where(valid, scores + jnp.concatenate(shift, axis=0), np.float32(NEGATIVE))
            top = jnp.max(scores, axis=-1, keepdims=True)
            probs = jnp.exp(scores - top)
            probs = probs * (1.0 / jnp.sum(probs, axis=-1, keepdims=True))
            copy = pltpu.make_async_copy(pst.at[e], oP.at[h], psem.at[e])

            @pl.when(t > 0)
            def _():
                copy.wait()

            pst[e] = probs
            copy.start()
            mine = dot(probs.astype(BF), values)
            outs_ = jnp.where(head == e, mine, outs_)
        mixed[:, lanes] = outs_.astype(BF)

    def with_step(t):
        pair(t)
        for r in range(2, geo.A):
            share = -(-geo.NP // (I // 128))

            def go(i):
                p = t * share + i

                @pl.when(p < geo.NP)
                def _():
                    if r == 2:
                        ffn.step(r, p)

            loop(share, go)

    loop(I // 128, with_step)
    for e in range(per):
        pltpu.make_async_copy(pst.at[e], oP.at[e], psem.at[e]).wait()
    write(mixed, omixed)

    spread_mixed = dot(mixed[...], pout[...]).astype(BF)
    total = xv[...].astype(F32)
    for s in range(S):
        total += dot(spread_mixed[:, s * I4 : (s + 1) * I4], WA[s], NT)
    hid[...] = total
    scale = lax.rsqrt(jnp.sum(total * total, axis=-1, keepdims=True) / np.float32(geo.D) + EPSILON)
    X2[block(me.s, T), :] = (total * scale * gain[1:2, :]).astype(BF)
    gather_x2.begin()
    write(hid, ohid)
    gather_c.finish()
    write(C, oC)
    for r in range(3, geo.A):
        loop(geo.NP, lambda p: ffn.step(r, p))
    gather_x2.relay()
    for r in range(geo.A):
        loop(geo.NP, lambda p: ffn.ystep(r, p))
    gather_x2.finish()
    write(X2, oX2)
    loads[1].wait()

    def pcopy(n, k):
        return remote(part.at[0, n, k], got.at[n, k], ps.at[n, k], pr.at[n, k], me.dev(c=1 - me.c))

    def tokens_block(i):
        k = X - 1 - i // 2
        e = i % 2
        s = lax.rem(me.x + k, X) * 2 + lax.rem(1 + e + me.c, 2)
        rows = block(s, T)
        xb = X2[rows, :]
        gate = dot(xb, WF[0])
        upward = dot(xb, WF[1])
        back = dot(C[rows, :], WF[2])
        value, slope = gelu_parts(gate)
        activated = (value * upward).astype(BF)
        first = (back * upward * slope).astype(BF)
        second = (back * value).astype(BF)
        act[0, rows, :] = first
        act[1, rows, :] = second
        act[2, rows, :] = activated
        part[e, 0, k] = (dot(first, WF[0], NT) + dot(second, WF[1], NT)).astype(BF)
        part[e, 1, k] = dot(activated, WF[2], NT).astype(BF)

        @pl.when(e == 0)
        def _():
            pcopy(0, k).start()
            pcopy(1, k).start()

    loop(2 * X, tokens_block)
    write(act, oact)
    for k in range(X - 1, -1, -1):
        for n in range(2):
            pcopy(n, k).wait_recv()
            part[1, n, k] = (part[1, n, k].astype(F32) + got[n, k].astype(F32)).astype(BF)
    write(part.at[1], opart)
    for k in range(X):
        for n in range(2):
            pcopy(n, k).wait_send()

    def finish(g):
        for k in range(X):
            s = lax.rem(me.x - k + X, X) * 2 + 1 - me.c
            here = held_a(s, g)
            ccopy(k, g, here, s).wait_send()
            if k:
                xcopy(k, g, here).wait_send()

    loop(dp, finish)
    att.drain(0)
    loop(geo.NP, ffn.drain)
    for copy in writes:
        copy.wait()


def forward(geo, length, x, c, wf, wa):
    dma = pltpu.SemaphoreType.DMA
    S, N, F, T, L, I, H, X, I4 = geo.seq, geo.N, geo.F, geo.T, geo.L, geo.I, geo.H, geo.X, geo.I4
    per = 128 // (I // H)
    consts = constants(geo)
    out_shape = [
        ((S, N, I4), BF), ((T, 3 * I), BF), ((L, 2 * I), BF), ((H, T, L), F32), ((T, I), BF),
        ((T, N), F32), ((L, N), BF), ((L, N), BF), ((3, L, F), BF), ((2, X, T, N), BF), ((8, N), F32),
    ]
    V = pltpu.VMEM
    scratch = [
        V((3, N, F), BF), V((S, N, I4), BF), V((T, N), BF), V((L, N), BF), V((L, N), BF), V((L, 2 * I), BF),
        V((T, 3 * I), BF), V((H, 128, 2 * L - 128), BF), V((T, I), BF), V((T, N), F32),
        V((per, T, L), F32), V((3, L, F), BF), V((2, 2, X, T, N), BF), V((2, X, T, N), BF), V((8, N), F32),
        *[V(v.shape, v.dtype) for v in consts],
        dma((8,)), dma((11,)), dma((per,)),
        dma((geo.NZ, geo.NP)), dma((geo.NZ, geo.NP)), dma((geo.NY, geo.NP)), dma((geo.NY, geo.NP)),
        dma((geo.NZ, 1)), dma((geo.NZ, 1)), dma((geo.NY, 1)), dma((geo.NY, 1)),
        dma((X - 1, geo.dp)), dma((X - 1, geo.dp)), dma((X, geo.dp)), dma((X, geo.dp)),
        dma((3, X - 1)), dma((3, X - 1)), dma((3, X)), dma((3, X)),
        dma((2, X)), dma((2, X)),
    ]
    return pl.pallas_call(
        functools.partial(forward_kernel, geo),
        out_shape=[jax.ShapeDtypeStruct(*v) for v in out_shape],
        in_specs=[pl.BlockSpec(memory_space=pltpu.SMEM)] + [pl.BlockSpec(memory_space=pl.ANY)] * 8,
        out_specs=[pl.BlockSpec(memory_space=pl.ANY)] * len(out_shape),
        scratch_shapes=scratch,
        compiler_params=pltpu.CompilerParams(collective_id=0, has_side_effects=True, vmem_limit_bytes=63 << 20),
        name="forward",
    )(length, x, c, wf, wa, *consts)


class SeqScatter:
    def __init__(self, geo, me, part, cb, xb, cs, cr, xs, xr):
        self.__dict__.update(locals())

    def ccopy(self, k):
        me = self.me
        to = lax.rem(me.x + k, self.geo.X)
        return remote(self.part(to * 2 + 1 - me.c), self.cb(k), self.cs.at[k], self.cr.at[k], me.dev(c=1 - me.c))

    def xcopy(self, k):
        me = self.me
        to = lax.rem(me.x + k, self.geo.X)
        return remote(self.part(to * 2 + me.c), self.xb(k), self.xs.at[k - 1], self.xr.at[k - 1], me.dev(x=to))

    def to_core(self):
        for k in (*range(1, self.geo.X), 0):
            self.ccopy(k).start()

    def to_x(self):
        for k in range(1, self.geo.X):
            self.ccopy(k).wait_recv()
            out = self.part(lax.rem(self.me.x + k, self.geo.X) * 2 + self.me.c)
            out[...] = (out[...].astype(F32) + self.cb(k)[...].astype(F32)).astype(BF)
            self.xcopy(k).start()

    def meet(self):
        self.ccopy(0).wait_recv()
        total = self.part(self.me.s)[...].astype(F32) + self.cb(0)[...].astype(F32)
        for k in range(1, self.geo.X):
            self.xcopy(k).wait_recv()
            total += self.xb(k)[...].astype(F32)
        return total

    def drain(self):
        for k in range(self.geo.X):
            self.ccopy(k).wait_send()
            if k:
                self.xcopy(k).wait_send()


class DpScatter:
    def __init__(self, geo, me, part, ybuf, zbuf, ys, yr, zs, zr, finish):
        self.__dict__.update(locals())

    def owner(self, i):
        A, z = self.geo.A, self.me.z
        up, down = A - 1 - z, z
        both = jnp.minimum(up, down)
        half = i // 2
        early = jnp.where(i % 2 == 0, A - 1 - half, half)
        late = jnp.where(up > down, A - 1 - (i - both), i - both)
        return jnp.where(i == A - 1, z, jnp.where(i < 2 * both, early, late))

    def ycopy(self, t, p):
        me = self.me
        return remote(
            self.part(p, t * 2 + 1 - me.y), self.ybuf(p, t), self.ys.at[t, p], self.yr.at[t, p], me.dev(y=1 - me.y)
        )

    def zslot(self, up, t):
        return jnp.where(up, self.geo.A - 1 - t, self.geo.A - t)

    def zcopy(self, t, p):
        me = self.me
        up = t > me.z
        slot = self.zslot(up, t)
        to = jnp.where(up, me.z + 1, me.z - 1)
        return remote(
            self.part(p, t * 2 + me.y), self.zbuf(p, slot), self.zs.at[t, p], self.zr.at[slot, p], me.dev(z=to)
        )

    def zarrive(self, up, t, p):
        slot = self.zslot(up, t)
        here = self.zbuf(p, slot)
        remote(here, here, self.zs.at[t, p], self.zr.at[slot, p], self.me.dev(y=1 - self.me.y)).wait_recv()
        return here[...].astype(F32)

    def ysend(self, i, p):
        self.ycopy(self.owner(i), p).start()

    def event(self, i, p):
        geo, me = self.geo, self.me
        t = self.owner(i)
        self.ycopy(t, p).wait_recv()
        mine = self.part(p, t * 2 + me.y)

        def both():
            return mine[...].astype(F32) + self.ybuf(p, t)[...].astype(F32)

        if i == geo.A - 1:

            @pl.when(me.z == 0)
            def _():
                self.finish(p, both() + self.zarrive(False, t, p))

            @pl.when(me.z == geo.A - 1)
            def _():
                self.finish(p, both() + self.zarrive(True, t, p))

            @pl.when((me.z > 0) & (me.z < geo.A - 1))
            def _():
                self.finish(p, both() + self.zarrive(True, t, p) + self.zarrive(False, t, p))

            return
        up = t > me.z
        comes = (up & (me.z > 0)) | (jnp.logical_not(up) & (me.z < geo.A - 1))

        @pl.when(comes)
        def _():
            mine[...] = (both() + self.zarrive(up, t, p)).astype(BF)

        @pl.when(jnp.logical_not(comes))
        def _():
            mine[...] = both().astype(BF)

        self.zcopy(t, p).start()

    def drain(self, p):
        for i in range(self.geo.A):
            t = self.owner(i)
            self.ycopy(t, p).wait_send()
            if i < self.geo.A - 1:
                self.zcopy(t, p).wait_send()


def backward_kernel(
    geo, x_in, iWA, iqkv, iKV, iP, imixed, ihid, iX2, iC, iact, ipart, igain, cpo, ctile, cgroup, conehot,
    of, oa, olayer, oinput,
    G, XC, act, yb, zb, WA, ayb, azb, cb, xb, xv, hid, qkv, KV, mixed, pk, px, pst, ds, kcb, kxb,
    hgrad, gbias, extra, gain, pout, tile, group, onehot,
    local, psem, outs, pxs, pxr, kcs, kcr, kxs, kxr, acs, acr, axs, axr, ys, yr, zs, zr, ays, ayr, azs, azr,
):
    me = Place(geo)
    R, RH, NH, dp, X, T, N, I = geo.R, geo.RH, geo.NH, geo.dp, geo.X, geo.T, geo.N, geo.I
    I4, S, L, A, NP = geo.I4, geo.seq, geo.L, geo.A, geo.NP
    block = lambda i, n: pl.ds(pl.multiple_of(i * n, 16), n)
    dKV = act.at[0, :, : 2 * I]
    dM, dq = act.at[1, :T, :I], act.at[1, T : 2 * T, :I]
    half = S * I4 // 2
    rights = [act.at[2, : 2 * T, :half], act.at[2, 2 * T : 4 * T, :half]]
    lefts = XC.at[N : N + 2 * T, :]
    hlow = lefts.at[T:, :]
    loads = [
        (iact, act), (iX2, XC.at[:L, :]), (iC, XC.at[L:, :]), (ipart.at[:, 0], pk), (ihid, hid), (igain, gain),
        (iWA, WA), (cpo, pout), (iKV, KV), (iqkv, qkv), (imixed, mixed), (x_in, xv), (ctile, tile), (cgroup, group),
        (conehot, onehot),
    ]
    loads = [pltpu.make_async_copy(src, dst, local.at[i]) for i, (src, dst) in enumerate(loads)]
    for copy in loads:
        copy.start()
    hd = I // geo.H
    per = 128 // hd

    def pload(t, e):
        return pltpu.make_async_copy(iP.at[t * per + e], pst.at[e], psem.at[e])

    for e in range(per):
        pload(0, e).start()
    enter(geo, me)

    def pcopy(n, k):
        to = me.dev(x=lax.rem(me.x + k, X))
        return remote(ipart.at[n, k], px.at[n, k - 1], pxs.at[n, k - 1], pxr.at[n, k - 1], to)

    for n in range(2):
        for k in range(1, X):
            pcopy(n, k).start()

    def rows_of(g, p):
        return pl.ds(pl.multiple_of(g * R + (p % NH) * RH, 16), RH)

    def piece(buf, i, p):
        return buf.at[i, p // NH, pl.ds(pl.multiple_of((p % NH) * RH, 16), RH), :]

    def finish_f(p, value):
        of[p // NH, pl.ds(pl.multiple_of((p % NH) * RH, 16), RH), :] = value

    ffn = DpScatter(
        geo, me, lambda p, g: G.at[p // NH, rows_of(g, p), :], lambda p, t: piece(yb, t, p),
        lambda p, i: piece(zb, i, p), ys, yr, zs, zr, finish_f,
    )
    for i in range(3):
        loads[i].wait()

    def weight_rows(i):
        t = ffn.owner(i)
        lanes = pl.ds(pl.multiple_of(t * 2 * R, 128), 2 * R)
        rows = pl.ds(pl.multiple_of(t * 2 * R, 16), 2 * R)
        for m in range(3):
            left = XC[:L, lanes] if m < 2 else XC[L:, lanes]
            G[m, rows, :] = dot(left, act[m], TN).astype(BF)

            def go(h):
                ffn.ysend(i, m * NH + h)

            loop(NH, go)

    loop(A, weight_rows)

    for i in range(3, len(loads)):
        loads[i].wait()
    for k in range(1, X):
        pcopy(0, k).wait_recv()
    grad = pk[0].astype(F32)
    for k in range(1, X):
        grad += px[0, k - 1].astype(F32)
    hidden = hid[...]
    scale = lax.rsqrt(jnp.sum(hidden * hidden, axis=-1, keepdims=True) / np.float32(geo.D) + EPSILON)
    unit = hidden * scale
    gain_two = jnp.sum(grad * unit, axis=0, keepdims=True)
    pull = grad * gain[1:2, :]
    inner = jnp.sum(pull * unit, axis=-1, keepdims=True) / np.float32(geo.D)
    cot = XC[pl.ds(pl.multiple_of(L + me.s * T, 16), T), :].astype(F32)
    total = cot + scale * (pull - unit * inner)
    hgrad[...] = total
    hlow[...] = total.astype(BF)
    columns = jnp.concatenate([dot(hlow[...], WA[s]) for s in range(S)], axis=1).astype(BF)
    dM[...] = dot(columns, pout[...], NT).astype(BF)
    ds[...] = jnp.zeros_like(ds)
    gbias[...] = jnp.zeros_like(gbias)

    def pair(t):
        lanes = pl.ds(pl.multiple_of(t * 128, 128), 128)
        vlanes = pl.ds(pl.multiple_of(I + t * 128, 128), 128)
        head = lax.broadcasted_iota(jnp.int32, (1, 128), 1) // hd
        keys, values, queries, back = KV[:, lanes], KV[:, vlanes], qkv[:, lanes], dM[:, lanes]
        zero = jnp.zeros_like(queries)
        q_grad = jnp.zeros((T, 128), F32)
        k_grad = jnp.zeros((L, 128), F32)
        v_grad = jnp.zeros((L, 128), F32)
        for e in range(per):
            h = t * per + e
            own_back = jnp.where(head == e, back, zero)
            pload(t, e).wait()
            probs = pst[e]
            prob_grad = dot(own_back, values, NT)
            both = jnp.sum(probs * prob_grad, axis=-1, keepdims=True)
            score = (probs * (prob_grad - both)).astype(BF)
            v_grad += dot(probs.astype(BF), own_back, TN)

            @pl.when(t + 1 < I // 128)
            def _():
                pload(t + 1, e).start()

            q_grad = jnp.where(head == e, dot(score, keys), q_grad)
            k_grad += dot(score, jnp.where(head == e, queries, zero), TN)
            ds[:, 128 : 128 + L] = score
            near = jnp.zeros((128, 384), F32)
            place = lax.broadcasted_iota(jnp.int32, (1, L), 1)
            low = jnp.zeros((1, 1), F32)
            high = jnp.zeros((1, 1), F32)
            for b in range(T // 128):
                row_block = me.s * (T // 128) + b
                near += ds[b * 128 : (b + 1) * 128, pl.ds(pl.multiple_of(row_block * 128, 128), 384)].astype(F32)
                sums = jnp.sum(score[b * 128 : (b + 1) * 128, :].astype(F32), axis=0, keepdims=True)
                low += jnp.sum(jnp.where(place < (row_block - 1) * 128, sums, 0.0), axis=-1, keepdims=True)
                high += jnp.sum(jnp.where(place >= (row_block + 2) * 128, sums, 0.0), axis=-1, keepdims=True)
            near = jnp.concatenate([jnp.zeros((128, 128), F32), near], axis=1)
            line = jnp.sum(shear(near, -1), axis=0, keepdims=True)
            spot = lax.broadcasted_iota(jnp.int32, (1, 512), 1)
            line += jnp.where(spot == 0, low, 0.0) + jnp.where(spot == 511, high, 0.0)
            gbias[pl.ds(h, 1), :] = line
        dq[:, lanes] = q_grad.astype(BF)
        dKV[:, lanes] = k_grad.astype(BF)
        dKV[:, vlanes] = v_grad.astype(BF)

    events = [(i, p) for i in range(A) for p in range(NP)]

    def run(count):
        for _ in range(min(count, len(events))):
            i, p = events.pop(0)
            ffn.event(i, p)

    run(2)
    for t in range(I // 128):
        pair(t)
        run(2)
    key_scatter = SeqScatter(
        geo, me, lambda s: dKV.at[block(s, T), :], lambda k: kcb.at[k], lambda k: kxb.at[k - 1], kcs, kcr, kxs, kxr
    )
    key_scatter.to_core()

    for k in range(1, X):
        pcopy(1, k).wait_recv()
    total = hid[...] + pk[1].astype(F32)
    for k in range(1, X):
        total += px[1, k - 1].astype(F32)
    pk[1] = total.astype(BF)
    layer_out = pltpu.make_async_copy(pk.at[1], olayer, outs.at[0])
    layer_out.start()
    key_scatter.to_x()
    run(2)
    tokens = xv[...].astype(F32)
    scale = lax.rsqrt(jnp.sum(tokens * tokens, axis=-1, keepdims=True) / np.float32(geo.D) + EPSILON)
    lefts[:T, :] = (tokens * scale * gain[0:1, :]).astype(BF)
    columns = dot(mixed[...], pout[...]).astype(BF)
    for i, right in enumerate(rights):
        right[T:, :] = columns[:, i * half : (i + 1) * half]
    key_value = key_scatter.meet().astype(BF)
    columns = jnp.zeros((T, S * I4), F32)
    for kind, value in enumerate((dq[...], key_value[:, :I], key_value[:, I:])):
        columns += pltpu.roll(dot(value, pout[...]), S * I4 - (3 - kind) * (I4 // 4), 1)
    columns = columns.astype(BF)
    for i, right in enumerate(rights):
        right[:T, :] = columns[:, i * half : (i + 1) * half]
    grad = jnp.zeros((T, N), F32)
    for s in range(S):
        grad += dot(columns[:, s * I4 : (s + 1) * I4], WA[s], NT)
    unit = tokens * scale
    gain_one = jnp.sum(grad * unit, axis=0, keepdims=True)
    pull = grad * gain[0:1, :]
    inner = jnp.sum(pull * unit, axis=-1, keepdims=True) / np.float32(geo.D)
    xv[...] = (hgrad[...] + scale * (pull - unit * inner)).astype(BF)
    input_out = pltpu.make_async_copy(xv, oinput, outs.at[1])
    input_out.start()

    row = lax.broadcasted_iota(jnp.int32, (dp * 16, N), 0).astype(F32)
    spread_gain = jnp.where(row == group[0:1, :] + np.float32(16 - geo.E), gain_one, 0.0)
    spread_gain = jnp.where(row == group[0:1, :] + np.float32(17 - geo.E), gain_two, spread_gain)
    rest = dot(spread_gain.astype(BF), tile[...], NT)
    table = dot(onehot[...], gbias[...].astype(BF), NT)
    if I4 > 128:
        table = jnp.concatenate([table, jnp.zeros((dp * 16, I4 - 128), F32)], axis=1)
    extra[...] = rest + table

    def part_g(s, g):
        return XC.at[block(g, R), pl.ds(pl.multiple_of(s * I4, 128), I4)]

    att = DpScatter(
        geo, me, lambda p, g: part_g(me.s, g), lambda p, t: ayb.at[t], lambda p, i: azb.at[i],
        ays, ayr, azs, azr, lambda p, value: oa.__setitem__(..., value),
    )
    def turn(j):
        t = att.owner(j // 2)
        return t * 2 + jnp.where(j % 2 == 0, 1 - me.y, me.y)

    def scatter(g):
        return SeqScatter(
            geo, me, lambda s: part_g(s, g), lambda k: cb.at[k, block(g, R), :], lambda k: xb.at[k - 1, block(g, R), :],
            acs.at[g], acr.at[g], axs.at[g], axr.at[g],
        )

    def attention_rows(i):
        t = att.owner(i)
        lanes = pl.ds(pl.multiple_of(t * 2 * R, 128), 2 * R)
        rows = pl.ds(pl.multiple_of(t * 2 * R, 16), 2 * R)
        for n, right in enumerate(rights):
            XC[rows, n * half : (n + 1) * half] = dot(lefts[:, lanes], right[...], TN).astype(BF)
        for y in range(2):
            g = t * 2 + y
            rows = pl.ds(pl.multiple_of(g * R + R - 16, 16), 16)
            more = extra[pl.ds(pl.multiple_of(g * 16, 16), 16), :]
            for s in range(S):
                lane = slice(s * I4, (s + 1) * I4)
                XC[rows, lane] = (XC[rows, lane].astype(F32) + more).astype(BF)
        scatter(t * 2 + 1 - me.y).to_core()
        scatter(t * 2 + me.y).to_core()

    for i in range(A):
        attention_rows(i)
        run(1)
    for j in range(dp):
        scatter(turn(j)).to_x()
    run(1)
    for j in range(dp):
        g = turn(j)
        part_g(me.s, g)[...] = scatter(g).meet().astype(BF)
        if j % 2 == 0:
            att.ysend(j // 2, 0)
        run(1)
    for i in range(A):
        att.event(i, 0)
        run(1)
    run(len(events))

    for n in range(2):
        for k in range(1, X):
            pcopy(n, k).wait_send()
    key_scatter.drain()
    loop(dp, lambda g: scatter(g).drain())
    att.drain(0)
    loop(NP, ffn.drain)
    layer_out.wait()
    input_out.wait()


def backward(geo, x, saved):
    dma = pltpu.SemaphoreType.DMA
    S, N, F, T, L, I, X, I4, A, R = geo.seq, geo.N, geo.F, geo.T, geo.L, geo.I, geo.X, geo.I4, geo.A, geo.R
    per = 128 // (I // geo.H)
    consts = constants(geo)
    V = pltpu.VMEM
    scratch = [
        V((3, N, F), BF), V((2 * L, N), BF), V((3, L, F), BF), V((A, 3, R, F), BF), V((A + 1, 3, R, F), BF),
        V((S, N, I4), BF), V((A, R, I4), BF), V((A + 1, R, I4), BF),
        V((X, N, I4), BF), V((X - 1, N, I4), BF),
        V((T, N), BF), V((T, N), F32), V((T, 3 * I), BF), V((L, 2 * I), BF), V((T, I), BF),
        V((2, T, N), BF), V((2, X - 1, T, N), BF), V((per, T, L), F32), V((T, L + 256), BF),
        V((X, T, 2 * I), BF), V((X - 1, T, 2 * I), BF),
        V((T, N), F32), V((128, 512), F32), V((geo.dp * 16, I4), F32), V((8, N), F32),
        *[V(v.shape, v.dtype) for v in consts],
        dma((15,)), dma((per,)), dma((2,)),
        dma((2, X - 1)), dma((2, X - 1)), dma((X,)), dma((X,)), dma((X - 1,)), dma((X - 1,)),
        dma((geo.dp, X)), dma((geo.dp, X)), dma((geo.dp, X - 1)), dma((geo.dp, X - 1)),
        dma((A, geo.NP)), dma((A, geo.NP)), dma((A, geo.NP)), dma((A + 1, geo.NP)),
        dma((A, 1)), dma((A, 1)), dma((A, 1)), dma((A + 1, 1)),
    ]
    return pl.pallas_call(
        functools.partial(backward_kernel, geo),
        out_shape=[
            jax.ShapeDtypeStruct((3, R, F), F32), jax.ShapeDtypeStruct((R, I4), F32),
            jax.ShapeDtypeStruct((T, N), BF), jax.ShapeDtypeStruct((T, N), BF),
        ],
        in_specs=[pl.BlockSpec(memory_space=pl.ANY)] * (1 + len(saved) + len(consts)),
        out_specs=[pl.BlockSpec(memory_space=pltpu.VMEM)] * 2 + [pl.BlockSpec(memory_space=pl.ANY)] * 2,
        scratch_shapes=scratch,
        compiler_params=pltpu.CompilerParams(collective_id=2, has_side_effects=True, vmem_limit_bytes=63 << 20),
        name="backward",
    )(x, *saved, *consts)


def spread_features(values, geo, width):
    lead = values.shape[:-1]
    blocks = values.reshape(*lead, geo.dp, width)
    return jnp.pad(blocks, [(0, 0)] * (len(lead) + 1) + [(0, geo.R - width)]).reshape(*lead, geo.dp * geo.R)


def pack_features(values, geo, width):
    lead = values.shape[:-1]
    return values.reshape(*lead, geo.dp, geo.R)[..., :width].reshape(*lead, geo.dp * width)


def general_path(
    axes, tokens, cotangent, lengths, w_query, w_key_value, w_output, w_gate_up, w_down, norm_gains, position_bias
):
    dp, seq = axes
    width, own_inner = w_query.shape
    table_rows, head_count = position_bias.shape
    geo = Geo(dp, seq, width, w_down.shape[1], 4 * own_inner, tokens.shape[1], head_count, table_rows)
    rows = geo.R
    model_width = geo.D
    bucket_count = table_rows * dp
    inner_width = geo.I
    head_dim = inner_width // head_count

    lanes = lambda v: jnp.pad(v, ((0, 0), (0, geo.I4 - v.shape[1])))
    wa = jnp.concatenate(
        [
            jnp.concatenate([w_query, w_key_value[0], w_key_value[1], w_output], axis=1).astype(BF),
            jnp.zeros((rows - width - geo.E, geo.I4), BF),
            lanes(norm_gains.astype(BF)),
            lanes(position_bias.astype(BF)),
        ],
        axis=0,
    )
    wf = jnp.pad(jnp.concatenate([w_gate_up, w_down[None]], axis=0).astype(BF), ((0, 0), (0, rows - width), (0, 0)))
    WF, WA = gather_weights(geo, wf, wa)

    blocks = WA[0].reshape(dp, rows, geo.I4)
    first_gain = blocks[:, rows - geo.E, :width].reshape(model_width).astype(F32)
    second_gain = blocks[:, rows - geo.E + 1, :width].reshape(model_width).astype(F32)
    table_full = blocks[:, rows - table_rows :, :head_count].reshape(bucket_count, head_count)
    real = WA.reshape(seq, dp, rows, 4, own_inner)[:, :, :width]
    parts = real.transpose(3, 1, 2, 0, 4).reshape(4, model_width, inner_width)
    query_full, keyval_full, output_full = parts[0], parts[1:3], parts[3]

    inputs = tokens[0].astype(jnp.float32)
    row_count = inputs.shape[0]
    normed = norm_scale(inputs, first_gain).astype(jnp.bfloat16)
    queries = jnp.dot(normed, query_full, preferred_element_type=jnp.float32).astype(jnp.bfloat16)
    projected = jnp.einsum(
        "td,sdi->sti", normed, keyval_full, preferred_element_type=jnp.float32
    ).astype(jnp.bfloat16)
    keys_all, values_all = (
        lax.all_gather(projected[0], "seq", axis=0, tiled=True),
        lax.all_gather(projected[1], "seq", axis=0, tiled=True),
    )
    incoming_low = cotangent[0]
    incoming = incoming_low.astype(jnp.float32)
    cot_all = lax.all_gather(spread_features(incoming_low, geo, width), "seq", axis=0, tiled=True)
    length_all = keys_all.shape[0]
    block_start = lax.axis_index("seq") * row_count
    query_pos = block_start + jnp.arange(row_count, dtype=jnp.int32)
    key_pos = jnp.arange(length_all, dtype=jnp.int32)
    buckets = bucket_ids(key_pos[None, :] - query_pos[:, None])
    bucket_range = jnp.arange(bucket_count, dtype=jnp.int32)
    onehot = (buckets[:, :, None] == bucket_range).astype(jnp.bfloat16)
    score_bias = jnp.einsum("tkb,bh->htk", onehot, table_full, preferred_element_type=jnp.float32)
    key_valid = key_pos < lengths[0]
    query_heads = queries.reshape(row_count, head_count, head_dim)
    key_heads = keys_all.reshape(length_all, head_count, head_dim)
    value_heads = values_all.reshape(length_all, head_count, head_dim)
    raw_scores = (
        jnp.einsum("thc,khc->htk", query_heads, key_heads, preferred_element_type=jnp.float32) + score_bias
    )
    scores = jnp.where(key_valid[None, None, :], raw_scores, NEGATIVE)
    probs = jax.nn.softmax(scores, axis=-1)
    probs_low = probs.astype(BF)
    mixed_heads = (
        jnp.einsum("htk,khc->thc", probs_low, value_heads, preferred_element_type=jnp.float32)
        .reshape(row_count, inner_width)
        .astype(jnp.bfloat16)
    )
    attended = jnp.einsum("tc,dc->td", mixed_heads, output_full, preferred_element_type=jnp.float32)
    hidden_one = inputs + attended
    normed_two = norm_scale(hidden_one, second_gain).astype(jnp.bfloat16)
    normed_two_all = lax.all_gather(spread_features(normed_two, geo, width), "seq", axis=0, tiled=True)

    gate = jnp.dot(normed_two_all, WF[0], preferred_element_type=F32)
    upward = jnp.dot(normed_two_all, WF[1], preferred_element_type=F32)
    activated = gated(gate, upward).astype(BF)
    down_term = jnp.einsum("tf,df->td", activated, WF[2], preferred_element_type=F32)
    down_weight_grad = jnp.einsum("td,tf->df", cot_all, activated, preferred_element_type=F32)
    activated_grad = jnp.dot(cot_all, WF[2], preferred_element_type=F32)
    unused_value, gate_pull = jax.vjp(gated, gate, upward)
    gate_grad, upward_grad = gate_pull(activated_grad)
    gate_grad, upward_grad = gate_grad.astype(BF), upward_grad.astype(BF)
    gate_weight_grad = jnp.einsum("td,tf->df", normed_two_all, gate_grad, preferred_element_type=F32)
    up_weight_grad = jnp.einsum("td,tf->df", normed_two_all, upward_grad, preferred_element_type=F32)
    normed_two_term = jnp.einsum("tf,df->td", gate_grad, WF[0], preferred_element_type=F32) + jnp.einsum(
        "tf,df->td", upward_grad, WF[1], preferred_element_type=F32
    )
    down_sum = lax.psum_scatter(down_term.astype(BF), "seq", scatter_dimension=0, tiled=True)
    normed_two_sum = lax.psum_scatter(normed_two_term.astype(BF), "seq", scatter_dimension=0, tiled=True)
    outputs = (hidden_one + pack_features(down_sum, geo, width).astype(F32)).astype(BF)[None]
    normed_two_grad = pack_features(normed_two_sum, geo, width).astype(F32)
    gf = jnp.stack([gate_weight_grad.astype(BF), up_weight_grad.astype(BF), down_weight_grad.astype(BF)])

    unused_two, second_pull = jax.vjp(norm_scale, hidden_one, second_gain)
    hidden_norm_grad, second_gain_grad = second_pull(normed_two_grad)
    hidden_grad = incoming + hidden_norm_grad
    hidden_low = hidden_grad.astype(jnp.bfloat16)
    output_weight_grad = jnp.einsum("td,tc->dc", hidden_low, mixed_heads, preferred_element_type=jnp.float32)
    mixed_grad = jnp.einsum("td,dc->tc", hidden_low, output_full, preferred_element_type=jnp.float32).astype(
        jnp.bfloat16
    )
    grad_heads = mixed_grad.reshape(row_count, head_count, head_dim)
    prob_grad = jnp.einsum("thc,khc->htk", grad_heads, value_heads, preferred_element_type=jnp.float32)
    inner_sum = jnp.sum(probs * prob_grad, axis=-1, keepdims=True)
    score_grad = (probs * (prob_grad - inner_sum)).astype(jnp.bfloat16)
    query_act_grad = (
        jnp.einsum("htk,khc->thc", score_grad, key_heads, preferred_element_type=jnp.float32)
        .reshape(row_count, inner_width)
        .astype(jnp.bfloat16)
    )
    key_piece = jnp.einsum(
        "htk,thc->khc", score_grad, query_heads, preferred_element_type=jnp.float32
    ).reshape(length_all, inner_width)
    value_piece = jnp.einsum(
        "htk,thc->khc", probs_low, grad_heads, preferred_element_type=jnp.float32
    ).reshape(length_all, inner_width)
    own_terms = lax.psum_scatter(
        jnp.concatenate([key_piece, value_piece], axis=1).astype(jnp.bfloat16),
        "seq",
        scatter_dimension=0,
        tiled=True,
    )
    keyval_act_grad = jnp.stack([own_terms[:, :inner_width], own_terms[:, inner_width:]])
    query_weight_grad = jnp.einsum("td,tc->dc", normed, query_act_grad, preferred_element_type=jnp.float32)
    keyval_weight_grad = jnp.einsum("td,stc->sdc", normed, keyval_act_grad, preferred_element_type=jnp.float32)
    normed_grad = jnp.einsum(
        "tc,dc->td", query_act_grad, query_full, preferred_element_type=jnp.float32
    ) + jnp.einsum("stc,sdc->td", keyval_act_grad, keyval_full, preferred_element_type=jnp.float32)
    unused_three, first_pull = jax.vjp(norm_scale, inputs, first_gain)
    input_norm_grad, first_gain_grad = first_pull(normed_grad)
    input_grad = (hidden_grad + input_norm_grad).astype(jnp.bfloat16)[None]
    table_grad = jnp.einsum("htk,tkb->bh", score_grad, onehot, preferred_element_type=jnp.float32)

    grads = jnp.stack(
        [query_weight_grad, keyval_weight_grad[0], keyval_weight_grad[1], output_weight_grad]
    ).reshape(4, dp, width, seq, own_inner)
    grads = grads.transpose(3, 1, 2, 0, 4).reshape(seq, dp, width, geo.I4).astype(BF)
    wide = lambda v: jnp.pad(v, ((0, 0), (0, 0), (0, geo.I4 - v.shape[2])))
    more = jnp.concatenate(
        [
            jnp.zeros((dp, rows - width - geo.E, geo.I4), F32),
            wide(first_gain_grad.reshape(dp, 1, width)),
            wide(second_gain_grad.reshape(dp, 1, width)),
            wide(table_grad.reshape(dp, table_rows, head_count)),
        ],
        axis=1,
    ).astype(BF)
    ga = jnp.concatenate([grads, jnp.broadcast_to(more, (seq, *more.shape))], axis=2).reshape(seq, dp * rows, geo.I4)
    of, oa = scatter_grads(geo, gf, ga)

    main = oa[:width]
    query_part = main[:, :own_inner]
    keyval_part = jnp.stack([main[:, own_inner : 2 * own_inner], main[:, 2 * own_inner : 3 * own_inner]])
    output_part = main[:, 3 * own_inner :]
    gain_part = oa[rows - geo.E : rows - table_rows, :width]
    table_part = oa[rows - table_rows :, :head_count]
    return (
        outputs,
        input_grad,
        query_part,
        keyval_part,
        output_part,
        of[:2, :width],
        of[2, :width],
        gain_part,
        table_part,
    )

def fused_path(
    axes, tokens, cotangent, lengths, w_query, w_key_value, w_output, w_gate_up, w_down, norm_gains, position_bias
):
    dp, seq = axes
    width, own_inner = w_query.shape
    table_rows, head_count = position_bias.shape
    geo = Geo(dp, seq, width, w_down.shape[1], 4 * own_inner, tokens.shape[1], head_count, table_rows)
    rows = geo.R

    lanes = lambda v: jnp.pad(v, ((0, 0), (0, geo.I4 - v.shape[1])))
    wa = jnp.concatenate(
        [
            jnp.concatenate([w_query, w_key_value[0], w_key_value[1], w_output], axis=1).astype(BF),
            jnp.zeros((rows - width - geo.E, geo.I4), BF),
            lanes(norm_gains.astype(BF)),
            lanes(position_bias.astype(BF)),
        ],
        axis=0,
    )
    wf = jnp.pad(jnp.concatenate([w_gate_up, w_down[None]], axis=0).astype(BF), ((0, 0), (0, rows - width), (0, 0)))
    xp = spread_features(tokens[0], geo, width)
    cp = spread_features(cotangent[0], geo, width)
    saved = forward(geo, lengths, xp, cp, wf, wa)
    of, oa, layer, grad = backward(geo, xp, saved)
    outputs = pack_features(layer, geo, width)[None]
    input_grad = pack_features(grad, geo, width)[None]

    main = oa[:width]
    query_part = main[:, :own_inner]
    keyval_part = jnp.stack([main[:, own_inner : 2 * own_inner], main[:, 2 * own_inner : 3 * own_inner]])
    output_part = main[:, 3 * own_inner :]
    gain_part = oa[rows - geo.E : rows - table_rows, :width]
    table_part = oa[rows - table_rows :, :head_count]
    return (
        outputs,
        input_grad,
        query_part,
        keyval_part,
        output_part,
        of[:2, :width],
        of[2, :width],
        gain_part,
        table_part,
    )

def per_device(axes, *arrays):
    tokens, w_query, w_down, position_bias = arrays[0], arrays[3], arrays[7], arrays[9]
    geo = Geo(*axes, w_query.shape[0], w_down.shape[1], 4 * w_query.shape[1], tokens.shape[1], position_bias.shape[1],
              position_bias.shape[0])
    aligned = geo.F % 128 == 0 and geo.I4 % 128 == 0 and 2 * geo.R % 128 == 0 and geo.T % 128 == 0 and geo.I % 128 == 0
    aligned = aligned and max(2 * geo.I, geo.seq * geo.I4 // 2) <= geo.F and 4 * geo.T <= geo.L and geo.N + 2 * geo.T <= 2 * geo.L
    small = (3 * geo.F + geo.seq * geo.I4 + 2 * geo.L) * geo.N * 2 <= 24 << 20
    return (fused_path if aligned and small else general_path)(axes, *arrays)


def solution(mesh):
    in_specs = (
        P("dp", "seq", None),
        P("dp", "seq", None),
        P("dp"),
        P("dp", "seq"),
        P(None, "dp", "seq"),
        P("dp", "seq"),
        P(None, "dp", "seq"),
        P("dp", "seq"),
        P(None, "dp"),
        P("dp", None),
    )
    out_specs = (
        P("dp", "seq", None),
        P("dp", "seq", None),
        P("dp", "seq"),
        P(None, "dp", "seq"),
        P("dp", "seq"),
        P(None, "dp", "seq"),
        P("dp", "seq"),
        P(None, "dp"),
        P("dp", None),
    )
    return jax.shard_map(
        functools.partial(per_device, (mesh.shape["dp"], mesh.shape["seq"])), mesh=mesh, in_specs=in_specs, out_specs=out_specs, check_vma=False
    )
```

```python
import functools
import jax
import jax.numpy as jnp
import numpy as np
from jax import lax
from jax.experimental import pallas as pl
from jax.experimental.pallas import tpu as pltpu

from jax.sharding import PartitionSpec as P

MESH = pl.DeviceIdType.MESH
BF = jnp.bfloat16
F32 = jnp.float32


class Geo:
    def __init__(self, dp, seq, width, ff, inner4, tokens, heads, table_rows):
        self.dp, self.seq = dp, seq
        self.W, self.TR, self.E = width, table_rows, 2 + table_rows
        rows = -(-(width + self.E) // 16) * 16
        self.D, self.N, self.T, self.L = dp * width, dp * rows, tokens, seq * tokens
        self.I, self.H = inner4 // 4 * seq, heads
        self.B, self.A, self.X = 2, dp // 2, seq // 2
        self.R, self.F, self.I4 = rows, ff, inner4
        self.NH = 2 if rows % 32 == 0 else 1
        self.RH = rows // self.NH
        self.NP = 3 * self.NH
        self.NZ = 2 * (self.A - 1)
        self.NY = 2 * self.A - 1


class Place:
    def __init__(self, geo):
        d, s = lax.axis_index("dp"), lax.axis_index("seq")
        self.d, self.s = d, s
        self.z, self.y = d // 2, d % 2
        self.x, self.c = s // 2, s % 2

    def dev(self, z=None, y=None, x=None, c=None):
        z = self.z if z is None else z
        y = self.y if y is None else y
        x = self.x if x is None else x
        c = self.c if c is None else c
        return (z * 2 + y, x * 2 + c)


def remote(src, dst, ss, rs, dev):
    return pltpu.make_async_remote_copy(
        src_ref=src, dst_ref=dst, send_sem=ss, recv_sem=rs, device_id=dev, device_id_type=MESH
    )


def loop(n, body):
    def step(i, carry):
        body(i)
        return carry

    lax.fori_loop(0, n, step, 0)


def enter(geo, me):
    bar = pltpu.get_barrier_semaphore()

    def greet(dev):
        pl.semaphore_signal(bar, 1, device_id=dev, device_id_type=MESH)

    greet(me.dev(y=1 - me.y))
    greet(me.dev(c=1 - me.c))
    for k in range(1, geo.X):
        greet(me.dev(x=lax.rem(me.x + k, geo.X)))

    @pl.when(me.z > 0)
    def _():
        greet(me.dev(z=me.z - 1))

    @pl.when(me.z < geo.A - 1)
    def _():
        greet(me.dev(z=me.z + 1))

    count = 2 + (geo.X - 1) + (me.z > 0).astype(jnp.int32) + (me.z < geo.A - 1).astype(jnp.int32)
    pl.semaphore_wait(bar, count)


class LineGather:
    def __init__(self, geo, me, own, held, zs, zr, ys, yr, first_y=1 << 20, bzs=None, bzr=None):
        self.geo, self.me, self.own, self.held = geo, me, own, held
        self.zs, self.zr, self.ys, self.yr = zs, zr, ys, yr
        self.first_y, self.bzs, self.bzr = first_y, bzs, bzr

    def from_z(self, way, r):
        q = self.me.z - r if way == 0 else self.me.z + r
        return q, (q >= 0) if way == 0 else (q <= self.geo.A - 1)

    def sems(self, way, r, p, other):
        slot = way * (self.geo.A - 1) + r - 1
        if other:
            return self.bzs.at[slot, p - self.first_y], self.bzr.at[slot, p - self.first_y]
        return self.zs.at[slot, p], self.zr.at[slot, p]

    def zcopy(self, way, r, p, other=False):
        me, geo = self.me, self.geo
        q, there = self.from_z(way, r - 1)
        to = me.z + 1 if way == 0 else me.z - 1
        valid = ((me.z < geo.A - 1) if way == 0 else (me.z > 0)) & there
        here = self.held(p, q * 2 + (1 - me.y if other else me.y))
        src = self.own(p) if r == 1 and not other else here
        return remote(src, here, *self.sems(way, r, p, other), me.dev(z=to)), valid

    def zarrive(self, way, r, p, other=False):
        q, valid = self.from_z(way, r)
        here = self.held(p, q * 2 + (1 - self.me.y if other else self.me.y))
        return remote(here, here, *self.sems(way, r, p, other), self.me.dev(y=1 - self.me.y)), valid, q

    def yslot(self, way, r):
        return 1 + way * (self.geo.A - 1) + r - 1 if r else 0

    def ycopy(self, way, r, p):
        me, slot = self.me, self.yslot(way, r)
        q, _ = self.from_z(way, r)
        src = self.held(p, q * 2 + me.y) if r else self.own(p)
        return remote(src, self.held(p, q * 2 + me.y), self.ys.at[slot, p], self.yr.at[slot, p], me.dev(y=1 - me.y))

    def yarrive(self, way, r, p):
        me, slot = self.me, self.yslot(way, r)
        q, _ = self.from_z(way, r)
        here = self.held(p, q * 2 + 1 - me.y)
        return remote(here, here, self.ys.at[slot, p], self.yr.at[slot, p], me.dev(y=1 - me.y)), q

    def begin_y(self, p):
        self.ycopy(0, 0, p).start()

    def begin_z(self, p, other=False):
        for way in (0, 1):
            copy, valid = self.zcopy(way, 1, p, other)

            @pl.when(valid)
            def _():
                copy.start()

    def begin(self, p):
        self.begin_y(p)
        self.begin_z(p)

    def turn(self, p):
        self.yarrive(0, 0, p)[0].wait_recv()
        self.begin_z(p, True)

    def step(self, r, p, on_held=None, kinds=(False,), pass_y=True):
        for other in kinds:
            for way in (0, 1):
                copy, valid, q = self.zarrive(way, r, p, other)

                @pl.when(valid)
                def _():
                    copy.wait_recv()
                    if r < self.geo.A - 1:
                        onward, may = self.zcopy(way, r + 1, p, other)

                        @pl.when(may)
                        def _():
                            onward.start()

                    if pass_y:
                        self.ycopy(way, r, p).start()
                    if on_held is not None:
                        on_held(q * 2 + self.me.y)

    def step_both(self, r, p):
        self.step(r, p, None, (False, True), False)

    def ystep(self, r, p, on_held=None):
        for way in (0, 1) if r else (0,):
            copy, q = self.yarrive(way, r, p)

            def go():
                copy.wait_recv()
                if on_held is not None:
                    on_held(q * 2 + 1 - self.me.y)

            if r:
                pl.when(self.from_z(way, r)[1])(go)
            else:
                go()

    def drain(self, p, kinds=(False,), pass_y=True):
        self.ycopy(0, 0, p).wait_send()
        for r in range(1, self.geo.A):
            for way in (0, 1):
                for other in kinds:
                    copy, valid = self.zcopy(way, r, p, other)

                    @pl.when(valid)
                    def _():
                        copy.wait_send()

                if pass_y:

                    @pl.when(self.from_z(way, r)[1])
                    def _():
                        self.ycopy(way, r, p).wait_send()


class LineScatter:
    def __init__(self, geo, me, part, ybuf, zbuf, stage, zs, zr, ys, yr, finish):
        self.__dict__.update(locals())

    def turns(self):
        geo, me = self.geo, self.me
        for k in range(geo.A - 1):
            yield 0, k, geo.A - 1 - k, k < geo.A - 1 - me.z
            yield 1, k, k, k < me.z

    def slot(self, way, k):
        return way * (self.geo.A - 1) + k

    def ycopy(self, slot, t, p):
        me = self.me
        return remote(
            self.part(p, t * 2 + 1 - me.y),
            self.ybuf(p, t),
            self.ys.at[slot, p],
            self.yr.at[slot, p],
            me.dev(y=1 - me.y),
        )

    def zcopy(self, way, k, p):
        me = self.me
        to = me.z + 1 if way == 0 else me.z - 1
        slot = self.slot(way, k)
        return remote(
            self.stage(way, p, k), self.zbuf(way, p, k), self.zs.at[slot, p], self.zr.at[slot, p], me.dev(z=to)
        )

    def ysend(self, p, k):
        for way, kk, t, valid in self.turns():
            if kk == k:

                @pl.when(valid)
                def _():
                    self.ycopy(self.slot(way, kk), t, p).start()

    def ysend_own(self, p):
        self.ycopy(self.geo.NZ, self.me.z, p).start()

    def step(self, k, p):
        geo, me = self.geo, self.me
        for way, kk, t, valid in self.turns():
            if kk == k:

                @pl.when(valid)
                def _():
                    self.ycopy(self.slot(way, k), t, p).wait_recv()
                    total = self.part(p, t * 2 + me.y)[...].astype(F32) + self.ybuf(p, t)[...].astype(F32)
                    out = self.stage(way, p, k)
                    comes = me.z > 0 if way == 0 else me.z < geo.A - 1

                    @pl.when(comes)
                    def _():
                        self.zcopy(way, k, p).wait_recv()
                        out[...] = (total + self.zbuf(way, p, k)[...].astype(F32)).astype(BF)

                    @pl.when(jnp.logical_not(comes))
                    def _():
                        out[...] = total.astype(BF)

                    self.zcopy(way, k, p).start()

    def own(self, p):
        geo, me = self.geo, self.me
        self.ycopy(geo.NZ, me.z, p).wait_recv()
        total = self.part(p, me.z * 2 + me.y)[...].astype(F32) + self.ybuf(p, me.z)[...].astype(F32)
        kup = jnp.minimum(geo.A - 1 - me.z, geo.A - 2)
        kdown = jnp.minimum(me.z, geo.A - 2)

        def arrive(way, k):
            slot = way * (geo.A - 1) + k
            here = self.zbuf(way, p, k)
            remote(here, here, self.zs.at[slot, p], self.zr.at[slot, p], me.dev(y=1 - me.y)).wait_recv()
            return here[...].astype(F32)

        @pl.when(me.z == 0)
        def _():
            self.finish(p, total + arrive(1, kdown))

        @pl.when(me.z == geo.A - 1)
        def _():
            self.finish(p, total + arrive(0, kup))

        @pl.when((me.z > 0) & (me.z < geo.A - 1))
        def _():
            self.finish(p, total + arrive(0, kup) + arrive(1, kdown))

    def drain(self, p):
        for way, k, t, valid in self.turns():

            @pl.when(valid)
            def _():
                self.ycopy(self.slot(way, k), t, p).wait_send()
                self.zcopy(way, k, p).wait_send()

        self.ycopy(self.geo.NZ, self.me.z, p).wait_send()


NEGATIVE = -1e30
EPSILON = 1e-06
LIMITS = (12, 16, 23, 32, 46, 64, 91)


def bucket_ids(offsets):
    distance = jnp.abs(offsets)
    larger = 8 + sum(((distance >= threshold).astype(jnp.int32) for threshold in LIMITS))
    nearby = jnp.where(distance < 8, distance, larger)
    return jnp.where(offsets > 0, 16, 0) + nearby


def norm_scale(values, gain_vector):
    return (
        values
        * lax.rsqrt(jnp.mean(values * values, axis=-1, keepdims=True) + EPSILON)
        * gain_vector
    )


def gated(gate_value, upward):
    return jax.nn.gelu(gate_value, approximate=True) * upward


def gather_kernel(geo, wf, wa, WF, WA, local, zs, zr, ys, yr, azs, azr, ays, ayr, xs, xr, cs, cr):
    me = Place(geo)
    R, RH, NH, dp, X = geo.R, geo.RH, geo.NH, geo.dp, geo.X
    mine = [
        pltpu.make_async_copy(wf, WF.at[:, pl.ds(pl.multiple_of(me.d * R, 16), R), :], local.at[0]),
        pltpu.make_async_copy(wa, WA.at[me.s, pl.ds(pl.multiple_of(me.d * R, 16), R), :], local.at[1]),
    ]
    for copy in mine:
        copy.start()
    enter(geo, me)

    def own_f(p):
        return wf.at[p // NH, pl.ds(pl.multiple_of((p % NH) * RH, 16), RH), :]

    def held_f(p, g):
        return WF.at[p // NH, pl.ds(pl.multiple_of(g * R + (p % NH) * RH, 16), RH), :]

    def held_a(s, g):
        return WA.at[s, pl.ds(pl.multiple_of(g * R, 16), R), :]

    ffn = LineGather(geo, me, own_f, held_f, zs, zr, ys, yr)
    att = LineGather(geo, me, lambda p: wa, lambda p, g: held_a(me.s, g), azs, azr, ays, ayr)

    def xcopy(k, g, src):
        to = lax.rem(me.x + k, X)
        return remote(src, held_a(me.s, g), xs.at[k - 1, g], xr.at[k - 1, g], me.dev(x=to))

    def xarrive(k, g):
        src_x = lax.rem(me.x - k + X, X)
        here = held_a(src_x * 2 + me.c, g)
        return remote(here, here, xs.at[k - 1, g], xr.at[k - 1, g], me.dev(c=1 - me.c)), here

    def ccopy(k, g, src, s):
        return remote(src, held_a(s, g), cs.at[k, g], cr.at[k, g], me.dev(c=1 - me.c))

    def spread(g, src=None):
        src = held_a(me.s, g) if src is None else src
        for k in range(1, X):
            xcopy(k, g, src).start()
        ccopy(0, g, src, me.s).start()

    att.begin(0)
    spread(me.d, wa)
    loop(geo.NP, ffn.begin)
    att.ystep(0, 0, spread)
    for r in range(1, geo.A):
        att.step(r, 0, spread)
        att.ystep(r, 0, spread)

    def from_x(g):
        for k in range(1, X):
            copy, here = xarrive(k, g)
            copy.wait_recv()
            ccopy(k, g, here, lax.rem(me.x - k + X, X) * 2 + me.c).start()

    loop(dp, from_x)
    for r in range(1, geo.A):
        loop(geo.NP, lambda p: ffn.step(r, p))
    for r in range(geo.A):
        loop(geo.NP, lambda p: ffn.ystep(r, p))

    def finish(g):
        for k in range(X):
            s = lax.rem(me.x - k + X, X) * 2 + 1 - me.c
            here = held_a(s, g)
            remote(here, here, cs.at[k, g], cr.at[k, g], me.dev(c=1 - me.c)).wait_recv()
            ccopy(k, g, here, s).wait_send()
            if k:
                xcopy(k, g, here).wait_send()

    loop(dp, finish)
    att.drain(0)
    loop(geo.NP, ffn.drain)
    for copy in mine:
        copy.wait()


def scatter_kernel(
    geo, gf, ga, of, oa, yb, zb, st, cb, xb, xst, pa, ayb, azb, ast,
    zs, zr, ys, yr, azs, azr, ays, ayr, xs, xr, cs, cr,
):
    me = Place(geo)
    R, RH, NH, dp, X, A = geo.R, geo.RH, geo.NH, geo.dp, geo.X, geo.A
    enter(geo, me)

    def rows(g, p):
        return pl.ds(pl.multiple_of(g * R + (p % NH) * RH, 16), RH)

    def piece(buf, i, p):
        return buf.at[i, p // NH, pl.ds(pl.multiple_of((p % NH) * RH, 16), RH), :]

    def finish_f(p, value):
        of[p // NH, pl.ds(pl.multiple_of((p % NH) * RH, 16), RH), :] = value

    ffn = LineScatter(
        geo, me,
        lambda p, g: gf.at[p // NH, rows(g, p), :],
        lambda p, t: piece(yb, t, p),
        lambda way, p, k: piece(zb, way * (A - 1) + k, p),
        lambda way, p, k: piece(st, way * (A - 1) + k, p),
        zs, zr, ys, yr, finish_f,
    )

    def block(g):
        return pl.ds(pl.multiple_of(g * R, 16), R)

    def finish_a(p, value):
        oa[...] = value

    att = LineScatter(
        geo, me,
        lambda p, g: pa.at[block(g), :],
        lambda p, t: ayb.at[t],
        lambda way, p, k: azb.at[way * (A - 1) + k],
        lambda way, p, k: ast.at[way * (A - 1) + k],
        azs, azr, ays, ayr, finish_a,
    )

    def ccopy(k, g):
        to_x = lax.rem(me.x + k, X)
        return remote(
            ga.at[to_x * 2 + 1 - me.c, block(g), :], cb.at[k, block(g), :], cs.at[k, g], cr.at[k, g], me.dev(c=1 - me.c)
        )

    def xcopy(k, g):
        return remote(
            xst.at[k - 1, block(g), :], xb.at[k - 1, block(g), :], xs.at[k - 1, g], xr.at[k - 1, g],
            me.dev(x=lax.rem(me.x + k, X)),
        )

    def to_core(g):
        for k in (*range(1, X), 0):
            ccopy(k, g).start()

    def to_x(g):
        for k in range(1, X):
            ccopy(k, g).wait_recv()
            s = lax.rem(me.x + k, X) * 2 + me.c
            xst[k - 1, block(g), :] = (
                ga[s, block(g), :].astype(F32) + cb[k, block(g), :].astype(F32)
            ).astype(BF)
            xcopy(k, g).start()

    def meet(g):
        ccopy(0, g).wait_recv()
        total = ga[me.s, block(g), :].astype(F32) + cb[0, block(g), :].astype(F32)
        for k in range(1, X):
            xcopy(k, g).wait_recv()
            total += xb[k - 1, block(g), :].astype(F32)
        pa[block(g), :] = total.astype(BF)

    def free(g):
        for k in range(X):
            ccopy(k, g).wait_send()
            if k:
                xcopy(k, g).wait_send()

    for k in range(A - 1):
        loop(geo.NP, lambda p: ffn.ysend(p, k))
    loop(geo.NP, ffn.ysend_own)
    loop(dp, to_core)
    loop(dp, to_x)
    for k in range(A - 1):
        loop(geo.NP, lambda p: ffn.step(k, p))
    loop(geo.NP, ffn.own)
    loop(dp, meet)
    for k in range(A - 1):
        att.ysend(0, k)
    att.ysend_own(0)
    for k in range(A - 1):
        att.step(k, 0)
    att.own(0)
    loop(dp, free)
    att.drain(0)
    loop(geo.NP, ffn.drain)


def gather_weights(geo, wf, wa):
    dma = pltpu.SemaphoreType.DMA
    sems = [
        dma((2,)),
        dma((geo.NZ, geo.NP)), dma((geo.NZ, geo.NP)), dma((geo.NY, geo.NP)), dma((geo.NY, geo.NP)),
        dma((geo.NZ, 1)), dma((geo.NZ, 1)), dma((geo.NY, 1)), dma((geo.NY, 1)),
        dma((geo.X - 1, geo.dp)), dma((geo.X - 1, geo.dp)), dma((geo.X, geo.dp)), dma((geo.X, geo.dp)),
    ]
    return pl.pallas_call(
        functools.partial(gather_kernel, geo),
        out_shape=(
            jax.ShapeDtypeStruct((3, geo.dp * geo.R, geo.F), BF),
            jax.ShapeDtypeStruct((geo.seq, geo.dp * geo.R, geo.I4), BF),
        ),
        in_specs=[pl.BlockSpec(memory_space=pl.ANY)] * 2,
        out_specs=[pl.BlockSpec(memory_space=pl.ANY)] * 2,
        scratch_shapes=sems,
        compiler_params=pltpu.CompilerParams(collective_id=0, has_side_effects=True, vmem_limit_bytes=48 << 20),
        name="gather_weights",
    )(wf, wa)


def scatter_grads(geo, gf, ga):
    dma = pltpu.SemaphoreType.DMA
    n, X, A, R = geo.dp * geo.R, geo.X, geo.A, geo.R
    scratch = [
        pltpu.VMEM((A, 3, R, geo.F), BF), pltpu.VMEM((geo.NZ, 3, R, geo.F), BF), pltpu.VMEM((geo.NZ, 3, R, geo.F), BF),
        pltpu.VMEM((X, n, geo.I4), BF), pltpu.VMEM((X - 1, n, geo.I4), BF), pltpu.VMEM((X - 1, n, geo.I4), BF),
        pltpu.VMEM((n, geo.I4), BF),
        pltpu.VMEM((A, R, geo.I4), BF), pltpu.VMEM((geo.NZ, R, geo.I4), BF), pltpu.VMEM((geo.NZ, R, geo.I4), BF),
        dma((geo.NZ, geo.NP)), dma((geo.NZ, geo.NP)), dma((geo.NZ + 1, geo.NP)), dma((geo.NZ + 1, geo.NP)),
        dma((geo.NZ, 1)), dma((geo.NZ, 1)), dma((geo.NZ + 1, 1)), dma((geo.NZ + 1, 1)),
        dma((X - 1, geo.dp)), dma((X - 1, geo.dp)), dma((X, geo.dp)), dma((X, geo.dp)),
    ]
    return pl.pallas_call(
        functools.partial(scatter_kernel, geo),
        out_shape=(
            jax.ShapeDtypeStruct((3, R, geo.F), F32),
            jax.ShapeDtypeStruct((R, geo.I4), F32),
        ),
        in_specs=[pl.BlockSpec(memory_space=pltpu.VMEM)] * 2,
        out_specs=[pl.BlockSpec(memory_space=pltpu.VMEM)] * 2,
        scratch_shapes=scratch,
        compiler_params=pltpu.CompilerParams(collective_id=1, has_side_effects=True, vmem_limit_bytes=60 << 20),
        name="scatter_grads",
    )(gf, ga)


class SeqGather:
    def __init__(self, geo, me, held, xs, xr, cs, cr):
        self.geo, self.me, self.held = geo, me, held
        self.xs, self.xr, self.cs, self.cr = xs, xr, cs, cr

    def ccopy(self, k):
        me, X = self.me, self.geo.X
        here = self.held(lax.rem(me.x - k + X, X) * 2 + me.c)
        return remote(here, here, self.cs.at[k], self.cr.at[k], me.dev(c=1 - me.c))

    def xcopy(self, k):
        me = self.me
        here = self.held(me.s)
        return remote(here, here, self.xs.at[k - 1], self.xr.at[k - 1], me.dev(x=lax.rem(me.x + k, self.geo.X)))

    def begin(self):
        for k in range(1, self.geo.X):
            self.xcopy(k).start()
        self.ccopy(0).start()

    def relay(self):
        for k in range(1, self.geo.X):
            self.xcopy(k).wait_recv()
            self.ccopy(k).start()

    def finish(self):
        for k in range(self.geo.X):
            self.ccopy(k).wait_recv()
            self.ccopy(k).wait_send()
            if k:
                self.xcopy(k).wait_send()


def dot(a, b, dims=((1,), (0,))):
    return lax.dot_general(a, b, (dims, ((), ())), preferred_element_type=F32)


NT = ((1,), (1,))
TN = ((0,), (0,))


def constants(geo):
    own, I4, S, I, N = geo.I4 // 4, geo.I4, geo.seq, geo.I, geo.N
    perm_out = np.zeros((I, S * I4), np.float32)
    i = np.arange(own)
    for s in range(S):
        perm_out[s * own + i, s * I4 + 3 * own + i] = 1
    place = np.arange(N)
    tile = np.zeros((I4, N), np.float32)
    inside = place % geo.R < geo.W
    tile[(place % geo.R)[inside], place[inside]] = 1
    group = np.tile((place // geo.R * 16).astype(np.float32), (8, 1))
    offset = np.arange(512) - 256
    distance = np.abs(offset)
    larger = 8 + sum((distance >= limit).astype(np.int32) for limit in LIMITS)
    bucket = np.where(offset > 0, 16, 0) + np.where(distance < 8, distance, larger)
    onehot = np.zeros((geo.dp * 16, 512), np.float32)
    for b in range(geo.dp * geo.TR):
        onehot[b // geo.TR * 16 + 16 - geo.E + 2 + b % geo.TR] = bucket == b
    return [jnp.asarray(v, BF) for v in (perm_out, tile)] + [jnp.asarray(group), jnp.asarray(onehot, BF)]


def shear(value, sign):
    rows, lanes = value.shape
    row = lax.broadcasted_iota(jnp.int32, (rows, 1), 0)
    bit = 1
    while bit < rows:
        moved = pltpu.roll(value, bit if sign > 0 else lanes - bit, 1)
        value = jnp.where((row & bit) != 0, moved, value)
        bit *= 2
    return value


def gelu_parts(g):
    k0 = np.float32(np.sqrt(2 / np.pi))
    t = jnp.tanh(k0 * (g + np.float32(0.044715) * (g * g * g)))
    half = 0.5 * (1.0 + t)
    slope = half + 0.5 * g * (1.0 - t * t) * (k0 * (1.0 + np.float32(3 * 0.044715) * (g * g)))
    return g * half, slope


def forward_kernel(
    geo, length, x_in, c_in, wf, wa, cpo, ctile, cgroup, conehot,
    oWA, oqkv, oKV, oP, omixed, ohid, oX2, oC, oact, opart, ogain,
    WF, WA, xv, C, X2, KV, qkv, strip, mixed, hid, pst, act, part, got, gain, pout, tile, group, onehot,
    local, outs, psem, zs, zr, ys, yr, bzs, bzr, azs, azr, ays, ayr, xs, xr, cs, cr, gxs, gxr, gcs, gcr, ps, pr,
):
    me = Place(geo)
    R, RH, NH, dp, X, T, N, I = geo.R, geo.RH, geo.NH, geo.dp, geo.X, geo.T, geo.N, geo.I
    I4, S, L = geo.I4, geo.seq, geo.L
    block = lambda i, n: pl.ds(pl.multiple_of(i * n, 16), n)
    loads = [
        (wa, WA.at[me.s, block(me.d, R), :]),
        (wf, WF.at[:, block(me.d, R), :]),
        (c_in, C.at[block(me.s, T), :]),
        (x_in, xv),
        (cpo, pout), (ctile, tile), (cgroup, group), (conehot, onehot),
    ]
    loads = [pltpu.make_async_copy(src, dst, local.at[i]) for i, (src, dst) in enumerate(loads)]
    for copy in loads:
        copy.start()
    enter(geo, me)

    def own_f(p):
        return wf.at[p // NH, pl.ds(pl.multiple_of((p % NH) * RH, 16), RH), :]

    def held_f(p, g):
        return WF.at[p // NH, pl.ds(pl.multiple_of(g * R + (p % NH) * RH, 16), RH), :]

    def held_a(s, g):
        return WA.at[s, block(g, R), :]

    last = geo.NP - 1
    ffn = LineGather(geo, me, own_f, held_f, zs, zr, ys, yr, last, bzs, bzr)
    att = LineGather(geo, me, lambda p: wa, lambda p, g: held_a(me.s, g), azs, azr, ays, ayr)

    def xcopy(k, g, src):
        to = lax.rem(me.x + k, X)
        return remote(src, held_a(me.s, g), xs.at[k - 1, g], xr.at[k - 1, g], me.dev(x=to))

    def xarrive(k, g):
        src_x = lax.rem(me.x - k + X, X)
        here = held_a(src_x * 2 + me.c, g)
        return remote(here, here, xs.at[k - 1, g], xr.at[k - 1, g], me.dev(c=1 - me.c)), here

    def ccopy(k, g, src, s):
        return remote(src, held_a(s, g), cs.at[k, g], cr.at[k, g], me.dev(c=1 - me.c))

    def spread(g, src=None):
        src = held_a(me.s, g) if src is None else src
        for k in range(1, X):
            xcopy(k, g, src).start()
        ccopy(0, g, src, me.s).start()

    half = T // 2

    def seq_gather(i, ref, first, count):
        held = lambda s: ref.at[pl.ds(pl.multiple_of(s * T + first, 16), count), :]
        return SeqGather(geo, me, held, gxs.at[i], gxr.at[i], gcs.at[i], gcr.at[i])

    gather_c, gather_kv = seq_gather(0, C, 0, T), seq_gather(1, KV, 0, T)
    gather_x2 = [seq_gather(2, X2, 0, half), seq_gather(3, X2, half, half)]

    att.begin(0)
    spread(me.d, wa)
    ffn.begin_y(last)
    loop(last, ffn.begin)
    ffn.begin_z(last)
    events = [(r, p) for r in range(1, geo.A) for p in (*range(last), last)]

    def run(count):
        for _ in range(min(count, len(events))):
            r, p = events.pop(0)
            if p == last:
                ffn.step_both(r, p)
            else:
                ffn.step(r, p)

    att.ystep(0, 0, spread)
    for r in range(1, geo.A):
        att.step(r, 0, spread)
        att.ystep(r, 0, spread)
    ffn.turn(last)

    def from_x(g):
        for k in range(1, X):
            copy, here = xarrive(k, g)
            copy.wait_recv()
            ccopy(k, g, here, lax.rem(me.x - k + X, X) * 2 + me.c).start()

    for g in range(dp):
        from_x(g)
        if g >= 3:
            run(1)
    for i in (3, 4, 5, 6, 7):
        loads[i].wait()

    def settle(g):
        for k in range(X):
            s = lax.rem(me.x - k + X, X) * 2 + 1 - me.c
            here = held_a(s, g)
            remote(here, here, cs.at[k, g], cr.at[k, g], me.dev(c=1 - me.c)).wait_recv()

    loop(dp, settle)
    loads[0].wait()

    extra = jnp.concatenate([WA[0, g * R + R - 16 : g * R + R, :] for g in range(dp)], axis=0)
    spread_rows = dot(extra, tile[...])
    row = lax.broadcasted_iota(jnp.int32, (dp * 16, N), 0).astype(F32)
    gains = []
    for e in range(2):
        hit = row == group[0:1, :] + np.float32(16 - geo.E + e)
        gains.append(jnp.sum(jnp.where(hit, spread_rows, 0.0), axis=0, keepdims=True))
    gain[...] = jnp.concatenate(gains + [jnp.zeros((6, N), F32)], axis=0)
    bias = dot(extra[:, :128] if I4 >= 128 else extra, onehot[...], TN)

    inputs = xv[...].astype(F32)
    scale = lax.rsqrt(jnp.sum(inputs * inputs, axis=-1, keepdims=True) / np.float32(geo.D) + EPSILON)
    normed = (inputs * scale * gain[0:1, :]).astype(BF)
    columns = jnp.concatenate([dot(normed, WA[s]) for s in range(S)], axis=1)
    for kind in range(3):
        moved = pltpu.roll(columns, (3 - kind) * (I4 // 4), 1).astype(BF)
        qkv[:, kind * I : (kind + 1) * I] = dot(moved, pout[...], NT).astype(BF)
    KV[block(me.s, T), :] = qkv[:, I:]
    gather_kv.begin()
    loads[2].wait()
    gather_c.begin()
    run(1)
    writes = []

    def write(src, dst):
        copy = pltpu.make_async_copy(src, dst, outs.at[len(writes)])
        copy.start()
        writes.append(copy)

    write(WA, oWA)
    write(qkv, oqkv)
    write(gain, ogain)
    NB = L // 128
    for h in range(geo.H):
        band = shear(jnp.broadcast_to(bias[h : h + 1, :], (128, 512)), 1)[:, 128:512].astype(BF)
        strip[h, :, (NB - 2) * 128 : (NB + 1) * 128] = band
        far = (NB - 2) * 128
        strip[h, :, :far] = jnp.broadcast_to(bias[h : h + 1, 0:1], (128, far)).astype(BF)
        strip[h, :, (NB + 1) * 128 :] = jnp.broadcast_to(bias[h : h + 1, 511:512], (128, far)).astype(BF)
    run(1)
    gather_kv.relay()
    gather_kv.finish()
    run(1)
    write(KV, oKV)

    hd = I // geo.H
    per = 128 // hd
    valid = lax.broadcasted_iota(jnp.int32, (1, L), 1) < length[0]

    def pair(t, first):
        rows = slice(first, first + half)
        lanes = pl.ds(pl.multiple_of(t * 128, 128), 128)
        head = lax.broadcasted_iota(jnp.int32, (1, 128), 1) // hd
        keys = KV[:, lanes]
        values = KV[:, pl.ds(pl.multiple_of(I + t * 128, 128), 128)]
        queries = qkv[rows, lanes]
        outs_ = jnp.zeros((half, 128), F32)
        for e in range(per):
            h = t * per + e
            scores = dot(jnp.where(head == e, queries, jnp.zeros_like(queries)), keys, NT)
            shift = [
                strip[h, :, pl.ds(pl.multiple_of((NB - 1 - me.s * (T // 128) - b) * 128, 128), L)].astype(F32)
                for b in range(first // 128, (first + half) // 128)
            ]
            scores = jnp.where(valid, scores + jnp.concatenate(shift, axis=0), np.float32(NEGATIVE))
            top = jnp.max(scores, axis=-1, keepdims=True)
            probs = jnp.exp(scores - top)
            probs = probs * (1.0 / jnp.sum(probs, axis=-1, keepdims=True))
            copy = pltpu.make_async_copy(pst.at[e], oP.at[h, rows, :], psem.at[e])

            @pl.when((t > 0) | (first > 0))
            def _():
                copy.wait()

            pst[e] = probs
            copy.start()
            mine = dot(probs.astype(BF), values)
            outs_ = jnp.where(head == e, mine, outs_)
        mixed[rows, lanes] = outs_.astype(BF)

    for first in (0, half):
        rows = slice(first, first + half)
        for t in range(I // 128):
            pair(t, first)
            if t < 2:
                run(1)
        spread_mixed = dot(mixed[rows, :], pout[...]).astype(BF)
        total = xv[rows, :].astype(F32)
        for s in range(S):
            total += dot(spread_mixed[:, s * I4 : (s + 1) * I4], WA[s], NT)
        hid[rows, :] = total
        scale = lax.rsqrt(jnp.sum(total * total, axis=-1, keepdims=True) / np.float32(geo.D) + EPSILON)
        X2[pl.ds(pl.multiple_of(me.s * T + first, 16), half), :] = (total * scale * gain[1:2, :]).astype(BF)
        gather_x2[first // half].begin()
        run(1)
        if first == 0:
            gather_c.relay()
    for e in range(per):
        pltpu.make_async_copy(pst.at[e], oP.at[e, half:, :], psem.at[e]).wait()
    write(mixed, omixed)
    write(hid, ohid)
    gather_c.finish()
    write(C, oC)
    gather_x2[0].relay()
    run(len(events))
    gather_x2[1].relay()
    for r in range(geo.A):
        loop(last, lambda p: ffn.ystep(r, p))
    for part_x2 in gather_x2:
        part_x2.finish()
    write(X2, oX2)
    loads[1].wait()

    def pcopy(n, k):
        return remote(part.at[0, n, k], got.at[n, k], ps.at[n, k], pr.at[n, k], me.dev(c=1 - me.c))

    def tokens_block(i):
        k = X - 1 - i // 2
        e = i % 2
        s = lax.rem(me.x + k, X) * 2 + lax.rem(1 + e + me.c, 2)
        rows = block(s, T)
        xb = X2[rows, :]
        gate = dot(xb, WF[0])
        upward = dot(xb, WF[1])
        back = dot(C[rows, :], WF[2])
        value, slope = gelu_parts(gate)
        activated = (value * upward).astype(BF)
        first = (back * upward * slope).astype(BF)
        second = (back * value).astype(BF)
        act[0, rows, :] = first
        act[1, rows, :] = second
        act[2, rows, :] = activated
        part[e, 0, k] = (dot(first, WF[0], NT) + dot(second, WF[1], NT)).astype(BF)
        part[e, 1, k] = dot(activated, WF[2], NT).astype(BF)

        @pl.when(e == 0)
        def _():
            pcopy(0, k).start()
            pcopy(1, k).start()

    loop(2 * X, tokens_block)
    write(act, oact)
    for k in range(X - 1, -1, -1):
        for n in range(2):
            pcopy(n, k).wait_recv()
            part[1, n, k] = (part[1, n, k].astype(F32) + got[n, k].astype(F32)).astype(BF)
    write(part.at[1], opart)
    for k in range(X):
        for n in range(2):
            pcopy(n, k).wait_send()

    def finish(g):
        for k in range(X):
            s = lax.rem(me.x - k + X, X) * 2 + 1 - me.c
            here = held_a(s, g)
            ccopy(k, g, here, s).wait_send()
            if k:
                xcopy(k, g, here).wait_send()

    loop(dp, finish)
    att.drain(0)
    loop(last, ffn.drain)
    ffn.drain(last, (False, True), False)
    for copy in writes:
        copy.wait()


def forward(geo, length, x, c, wf, wa):
    dma = pltpu.SemaphoreType.DMA
    S, N, F, T, L, I, H, X, I4 = geo.seq, geo.N, geo.F, geo.T, geo.L, geo.I, geo.H, geo.X, geo.I4
    per = 128 // (I // H)
    consts = constants(geo)
    out_shape = [
        ((S, N, I4), BF), ((T, 3 * I), BF), ((L, 2 * I), BF), ((H, T, L), F32), ((T, I), BF),
        ((T, N), F32), ((L, N), BF), ((L, N), BF), ((3, L, F), BF), ((2, X, T, N), BF), ((8, N), F32),
    ]
    V = pltpu.VMEM
    scratch = [
        V((3, N, F), BF), V((S, N, I4), BF), V((T, N), BF), V((L, N), BF), V((L, N), BF), V((L, 2 * I), BF),
        V((T, 3 * I), BF), V((H, 128, 2 * L - 128), BF), V((T, I), BF), V((T, N), F32),
        V((per, T // 2, L), F32), V((3, L, F), BF), V((2, 2, X, T, N), BF), V((2, X, T, N), BF), V((8, N), F32),
        *[V(v.shape, v.dtype) for v in consts],
        dma((8,)), dma((11,)), dma((per,)),
        dma((geo.NZ, geo.NP)), dma((geo.NZ, geo.NP)), dma((geo.NY, geo.NP)), dma((geo.NY, geo.NP)),
        dma((geo.NZ, 1)), dma((geo.NZ, 1)),
        dma((geo.NZ, 1)), dma((geo.NZ, 1)), dma((geo.NY, 1)), dma((geo.NY, 1)),
        dma((X - 1, geo.dp)), dma((X - 1, geo.dp)), dma((X, geo.dp)), dma((X, geo.dp)),
        dma((4, X - 1)), dma((4, X - 1)), dma((4, X)), dma((4, X)),
        dma((2, X)), dma((2, X)),
    ]
    return pl.pallas_call(
        functools.partial(forward_kernel, geo),
        out_shape=[jax.ShapeDtypeStruct(*v) for v in out_shape],
        in_specs=[pl.BlockSpec(memory_space=pltpu.SMEM)] + [pl.BlockSpec(memory_space=pl.ANY)] * 8,
        out_specs=[pl.BlockSpec(memory_space=pl.ANY)] * len(out_shape),
        scratch_shapes=scratch,
        compiler_params=pltpu.CompilerParams(collective_id=0, has_side_effects=True, vmem_limit_bytes=63 << 20),
        name="forward",
    )(length, x, c, wf, wa, *consts)


class SeqScatter:
    def __init__(self, geo, me, part, cb, xb, cs, cr, xs, xr):
        self.__dict__.update(locals())

    def ccopy(self, k):
        me = self.me
        to = lax.rem(me.x + k, self.geo.X)
        return remote(self.part(to * 2 + 1 - me.c), self.cb(k), self.cs.at[k], self.cr.at[k], me.dev(c=1 - me.c))

    def xcopy(self, k):
        me = self.me
        to = lax.rem(me.x + k, self.geo.X)
        return remote(self.part(to * 2 + me.c), self.xb(k), self.xs.at[k - 1], self.xr.at[k - 1], me.dev(x=to))

    def to_core(self):
        for k in (*range(1, self.geo.X), 0):
            self.ccopy(k).start()

    def to_x(self):
        for k in range(1, self.geo.X):
            self.ccopy(k).wait_recv()
            out = self.part(lax.rem(self.me.x + k, self.geo.X) * 2 + self.me.c)
            out[...] = (out[...].astype(F32) + self.cb(k)[...].astype(F32)).astype(BF)
            self.xcopy(k).start()

    def meet(self):
        self.ccopy(0).wait_recv()
        total = self.part(self.me.s)[...].astype(F32) + self.cb(0)[...].astype(F32)
        for k in range(1, self.geo.X):
            self.xcopy(k).wait_recv()
            total += self.xb(k)[...].astype(F32)
        return total

    def drain(self):
        for k in range(self.geo.X):
            self.ccopy(k).wait_send()
            if k:
                self.xcopy(k).wait_send()


class DpScatter:
    def __init__(self, geo, me, part, ybuf, zbuf, ys, yr, zs, zr, finish, first_z=1 << 20, zbuf2=None, zs2=None, zr2=None):
        self.__dict__.update(locals())

    def owner(self, i):
        A, z = self.geo.A, self.me.z
        up, down = A - 1 - z, z
        both = jnp.minimum(up, down)
        half = i // 2
        early = jnp.where((i % 2 == 0) == (up >= down), A - 1 - half, half)
        late = jnp.where(up > down, A - 1 - (i - both), i - both)
        return jnp.where(i == A - 1, z, jnp.where(i < 2 * both, early, late))

    def ycopy(self, t, p):
        me = self.me
        return remote(
            self.part(p, t * 2 + 1 - me.y), self.ybuf(p, t), self.ys.at[t, p], self.yr.at[t, p], me.dev(y=1 - me.y)
        )

    def zparts(self, t, slot, p, other):
        if other:
            return self.zbuf2(p, slot), self.zs2.at[t, p - self.first_z], self.zr2.at[slot, p - self.first_z]
        return self.zbuf(p, slot), self.zs.at[t, p], self.zr.at[slot, p]

    def mine(self, t, p, other=False):
        return self.part(p, t * 2 + (1 - self.me.y if other else self.me.y))

    def zslot(self, up, t):
        return jnp.where(up, self.geo.A - 1 - t, self.geo.A - t)

    def zcopy(self, t, p, other=False):
        me = self.me
        up = t > me.z
        dst, ss, rs = self.zparts(t, self.zslot(up, t), p, other)
        return remote(self.mine(t, p, other), dst, ss, rs, me.dev(z=jnp.where(up, me.z + 1, me.z - 1)))

    def zarrive(self, up, t, p, other=False):
        here, ss, rs = self.zparts(t, self.zslot(up, t), p, other)
        remote(here, here, ss, rs, self.me.dev(y=1 - self.me.y)).wait_recv()
        return here[...].astype(F32)

    def ysend(self, i, p):
        self.ycopy(self.owner(i), p).start()

    def arrived(self, t, p, base, put, other=False):
        geo, me = self.geo, self.me

        @pl.when(me.z == 0)
        def _():
            put(base() + self.zarrive(False, t, p, other))

        @pl.when(me.z == geo.A - 1)
        def _():
            put(base() + self.zarrive(True, t, p, other))

        @pl.when((me.z > 0) & (me.z < geo.A - 1))
        def _():
            put(base() + self.zarrive(True, t, p, other) + self.zarrive(False, t, p, other))

    def onward(self, t, p, base, other=False, plain=False):
        geo, me = self.geo, self.me
        mine = self.mine(t, p, other)
        up = t > me.z
        comes = (up & (me.z > 0)) | (jnp.logical_not(up) & (me.z < geo.A - 1))

        @pl.when(comes)
        def _():
            mine[...] = (base() + self.zarrive(up, t, p, other)).astype(BF)

        if not plain:

            @pl.when(jnp.logical_not(comes))
            def _():
                mine[...] = base().astype(BF)

        self.zcopy(t, p, other).start()

    def event(self, i, p):
        t = self.owner(i)
        mine = self.mine(t, p)
        own = lambda: mine[...].astype(F32)
        if p >= self.first_z:
            theirs = self.mine(t, p, True)
            their = lambda: theirs[...].astype(F32)
            if i < self.geo.A - 1:
                self.onward(t, p, their, True, True)
                self.onward(t, p, own, False, True)
            else:
                self.arrived(t, p, their, lambda v: theirs.__setitem__(..., v.astype(BF)), True)
                self.ycopy(t, p).start()
            return
        self.ycopy(t, p).wait_recv()
        both = lambda: own() + self.ybuf(p, t)[...].astype(F32)
        if i == self.geo.A - 1:
            self.arrived(t, p, both, lambda v: self.finish(p, v))
        else:
            self.onward(t, p, both)

    def last(self, p):
        t = self.me.z
        mine = self.mine(t, p)
        self.ycopy(t, p).wait_recv()
        both = lambda: mine[...].astype(F32) + self.ybuf(p, t)[...].astype(F32)
        self.arrived(t, p, both, lambda v: self.finish(p, v))

    def drain(self, p, second=False):
        for i in range(self.geo.A):
            t = self.owner(i)
            if not second or i == self.geo.A - 1:
                self.ycopy(t, p).wait_send()
            if i < self.geo.A - 1:
                for other in (False, True) if second else (False,):
                    self.zcopy(t, p, other).wait_send()


def backward_kernel(
    geo, x_in, iWA, iqkv, iKV, iP, imixed, ihid, iX2, iC, iact, ipart, igain, cpo, ctile, cgroup, conehot,
    of, oa, olayer, oinput,
    G, XC, act, yb, zb, WA, ayb, azb, cb, xb, xv, hid, qkv, KV, mixed, pk, px, pst, kcb, kxb, zb2,
    hgrad, gbias, extra, gain, pout, tile, group, onehot,
    local, psem, outs, pxs, pxr, kcs, kcr, kxs, kxr, acs, acr, axs, axr, ys, yr, zs, zr, zs2, zr2, ays, ayr, azs, azr,
):
    me = Place(geo)
    R, RH, NH, dp, X, T, N, I = geo.R, geo.RH, geo.NH, geo.dp, geo.X, geo.T, geo.N, geo.I
    I4, S, L, A, NP = geo.I4, geo.seq, geo.L, geo.A, geo.NP
    block = lambda i, n: pl.ds(pl.multiple_of(i * n, 16), n)
    dKV = act.at[0, :, : 2 * I]
    dM, dq = act.at[1, :T, :I], act.at[1, T : 2 * T, :I]
    half = S * I4 // 2
    rights = [act.at[2, : 2 * T, :half], act.at[2, 2 * T : 4 * T, :half]]
    lefts = XC.at[N : N + 2 * T, :]
    hlow = lefts.at[T:, :]
    ds = pk.at[0, :, : L + 256]
    loads = [
        (iact, act), (iX2, XC.at[:L, :]), (iC, XC.at[L:, :]), (ipart.at[:, 0], pk), (ihid, hid), (igain, gain),
        (iWA, WA), (cpo, pout), (iKV, KV), (iqkv, qkv), (imixed, mixed), (x_in, xv), (ctile, tile), (cgroup, group),
        (conehot, onehot),
    ]
    loads = [pltpu.make_async_copy(src, dst, local.at[i]) for i, (src, dst) in enumerate(loads)]
    for copy in loads:
        copy.start()
    hd = I // geo.H
    per = 128 // hd

    def pload(t, e):
        return pltpu.make_async_copy(iP.at[t * per + e], pst.at[e], psem.at[e])

    for e in range(per):
        pload(0, e).start()
    enter(geo, me)

    def pcopy(n, k):
        to = me.dev(x=lax.rem(me.x + k, X))
        return remote(ipart.at[n, k], px.at[n, k - 1], pxs.at[n, k - 1], pxr.at[n, k - 1], to)

    for n in range(2):
        for k in range(1, X):
            pcopy(n, k).start()

    def rows_of(g, p):
        return pl.ds(pl.multiple_of(g * R + (p % NH) * RH, 16), RH)

    def piece(buf, i, p):
        return buf.at[i, p // NH, pl.ds(pl.multiple_of((p % NH) * RH, 16), RH), :]

    def finish_f(p, value):
        of[p // NH, pl.ds(pl.multiple_of((p % NH) * RH, 16), RH), :] = value

    last = NP - 1
    ffn = DpScatter(
        geo, me, lambda p, g: G.at[p // NH, rows_of(g, p), :], lambda p, t: piece(yb, t, p),
        lambda p, i: piece(zb, i, p), ys, yr, zs, zr, finish_f,
        last, lambda p, i: zb2.at[i], zs2, zr2,
    )
    for i in range(3):
        loads[i].wait()

    def weight_rows(i):
        t = ffn.owner(i)
        lanes = pl.ds(pl.multiple_of(t * 2 * R, 128), 2 * R)
        rows = pl.ds(pl.multiple_of(t * 2 * R, 16), 2 * R)
        for m in range(3):
            left = XC[:L, lanes] if m < 2 else XC[L:, lanes]
            G[m, rows, :] = dot(left, act[m], TN).astype(BF)

            def go(h):
                p = m * NH + h

                @pl.when((p < last) & ((i < A - 1) | (p < NP // 2)))
                def _():
                    ffn.ysend(i, p)

            loop(NH, go)

    loop(A, weight_rows)

    edge = (me.z == 0) | (me.z == A - 1)
    queues = [(kind, [(i, p) for i in range(A) for p in (last, *range(last))]) for kind in (edge, jnp.logical_not(edge))]

    def run(*counts):
        for (kind, events), count in zip(queues, counts):
            now = [events.pop(0) for _ in range(min(count, len(events)))]
            if now:

                @pl.when(kind)
                def _():
                    for i, p in now:
                        ffn.event(i, p)

    run(3, 0)

    for i in range(3, len(loads)):
        loads[i].wait()
    for k in range(1, X):
        pcopy(0, k).wait_recv()
    grad = pk[0].astype(F32)
    for k in range(1, X):
        grad += px[0, k - 1].astype(F32)
    hidden = hid[...]
    scale = lax.rsqrt(jnp.sum(hidden * hidden, axis=-1, keepdims=True) / np.float32(geo.D) + EPSILON)
    unit = hidden * scale
    gain_two = jnp.sum(grad * unit, axis=0, keepdims=True)
    pull = grad * gain[1:2, :]
    inner = jnp.sum(pull * unit, axis=-1, keepdims=True) / np.float32(geo.D)
    cot = XC[pl.ds(pl.multiple_of(L + me.s * T, 16), T), :].astype(F32)
    total = cot + scale * (pull - unit * inner)
    hgrad[...] = total
    hlow[...] = total.astype(BF)
    columns = jnp.concatenate([dot(hlow[...], WA[s]) for s in range(S)], axis=1).astype(BF)
    dM[...] = dot(columns, pout[...], NT).astype(BF)
    ds[...] = jnp.zeros_like(ds)
    gbias[...] = jnp.zeros_like(gbias)
    run(3, 1)

    def pair(t):
        lanes = pl.ds(pl.multiple_of(t * 128, 128), 128)
        vlanes = pl.ds(pl.multiple_of(I + t * 128, 128), 128)
        head = lax.broadcasted_iota(jnp.int32, (1, 128), 1) // hd
        keys, values, queries, back = KV[:, lanes], KV[:, vlanes], qkv[:, lanes], dM[:, lanes]
        zero = jnp.zeros_like(queries)
        q_grad = jnp.zeros((T, 128), F32)
        k_grad = jnp.zeros((L, 128), F32)
        v_grad = jnp.zeros((L, 128), F32)
        for e in range(per):
            h = t * per + e
            own_back = jnp.where(head == e, back, zero)
            pload(t, e).wait()
            probs = pst[e]
            prob_grad = dot(own_back, values, NT)
            both = jnp.sum(probs * prob_grad, axis=-1, keepdims=True)
            score = (probs * (prob_grad - both)).astype(BF)
            v_grad += dot(probs.astype(BF), own_back, TN)

            @pl.when(t + 1 < I // 128)
            def _():
                pload(t + 1, e).start()

            q_grad = jnp.where(head == e, dot(score, keys), q_grad)
            k_grad += dot(score, jnp.where(head == e, queries, zero), TN)
            ds[:, 128 : 128 + L] = score
            near = jnp.zeros((128, 384), F32)
            place = lax.broadcasted_iota(jnp.int32, (1, L), 1)
            low = jnp.zeros((1, 1), F32)
            high = jnp.zeros((1, 1), F32)
            for b in range(T // 128):
                row_block = me.s * (T // 128) + b
                near += ds[b * 128 : (b + 1) * 128, pl.ds(pl.multiple_of(row_block * 128, 128), 384)].astype(F32)
                sums = jnp.sum(score[b * 128 : (b + 1) * 128, :].astype(F32), axis=0, keepdims=True)
                low += jnp.sum(jnp.where(place < (row_block - 1) * 128, sums, 0.0), axis=-1, keepdims=True)
                high += jnp.sum(jnp.where(place >= (row_block + 2) * 128, sums, 0.0), axis=-1, keepdims=True)
            near = jnp.concatenate([jnp.zeros((128, 128), F32), near], axis=1)
            line = jnp.sum(shear(near, -1), axis=0, keepdims=True)
            spot = lax.broadcasted_iota(jnp.int32, (1, 512), 1)
            line += jnp.where(spot == 0, low, 0.0) + jnp.where(spot == 511, high, 0.0)
            gbias[pl.ds(h, 1), :] = line
        dq[:, lanes] = q_grad.astype(BF)
        dKV[:, lanes] = k_grad.astype(BF)
        dKV[:, vlanes] = v_grad.astype(BF)

    for t in range(I // 128):
        pair(t)
        run(*((1, 1), (1, 1), (2, 1))[min(t, 2)])
    key_scatter = SeqScatter(
        geo, me, lambda s: dKV.at[block(s, T), :], lambda k: kcb.at[k], lambda k: kxb.at[k - 1], kcs, kcr, kxs, kxr
    )
    key_scatter.to_core()

    for k in range(1, X):
        pcopy(1, k).wait_recv()
    total = hid[...] + pk[1].astype(F32)
    for k in range(1, X):
        total += px[1, k - 1].astype(F32)
    pk[1] = total.astype(BF)
    layer_out = pltpu.make_async_copy(pk.at[1], olayer, outs.at[0])
    layer_out.start()
    key_scatter.to_x()
    run(1, 1)
    tokens = xv[...].astype(F32)
    scale = lax.rsqrt(jnp.sum(tokens * tokens, axis=-1, keepdims=True) / np.float32(geo.D) + EPSILON)
    lefts[:T, :] = (tokens * scale * gain[0:1, :]).astype(BF)
    columns = dot(mixed[...], pout[...]).astype(BF)
    for i, right in enumerate(rights):
        right[T:, :] = columns[:, i * half : (i + 1) * half]
    run(2, 2)
    key_value = key_scatter.meet().astype(BF)
    run(0, 3)
    columns = jnp.zeros((T, S * I4), F32)
    for kind, value in enumerate((dq[...], key_value[:, :I], key_value[:, I:])):
        columns += pltpu.roll(dot(value, pout[...]), S * I4 - (3 - kind) * (I4 // 4), 1)
    columns = columns.astype(BF)
    for i, right in enumerate(rights):
        right[:T, :] = columns[:, i * half : (i + 1) * half]
    grad = jnp.zeros((T, N), F32)
    for s in range(S):
        grad += dot(columns[:, s * I4 : (s + 1) * I4], WA[s], NT)
    unit = tokens * scale
    gain_one = jnp.sum(grad * unit, axis=0, keepdims=True)
    pull = grad * gain[0:1, :]
    inner = jnp.sum(pull * unit, axis=-1, keepdims=True) / np.float32(geo.D)
    xv[...] = (hgrad[...] + scale * (pull - unit * inner)).astype(BF)
    input_out = pltpu.make_async_copy(xv, oinput, outs.at[1])
    input_out.start()

    row = lax.broadcasted_iota(jnp.int32, (dp * 16, N), 0).astype(F32)
    spread_gain = jnp.where(row == group[0:1, :] + np.float32(16 - geo.E), gain_one, 0.0)
    spread_gain = jnp.where(row == group[0:1, :] + np.float32(17 - geo.E), gain_two, spread_gain)
    rest = dot(spread_gain.astype(BF), tile[...], NT)
    table = dot(onehot[...], gbias[...].astype(BF), NT)
    if I4 > 128:
        table = jnp.concatenate([table, jnp.zeros((dp * 16, I4 - 128), F32)], axis=1)
    extra[...] = rest + table

    def part_g(s, g):
        return XC.at[block(g, R), pl.ds(pl.multiple_of(s * I4, 128), I4)]

    att = DpScatter(
        geo, me, lambda p, g: part_g(me.s, g), lambda p, t: ayb.at[t], lambda p, i: azb.at[i],
        ays, ayr, azs, azr, lambda p, value: oa.__setitem__(..., value),
    )
    def turn(j):
        t = att.owner(j // 2)
        return t * 2 + jnp.where(j % 2 == 0, 1 - me.y, me.y)

    def scatter(g):
        return SeqScatter(
            geo, me, lambda s: part_g(s, g), lambda k: cb.at[k, block(g, R), :], lambda k: xb.at[k - 1, block(g, R), :],
            acs.at[g], acr.at[g], axs.at[g], axr.at[g],
        )

    def attention_rows(i):
        t = att.owner(i)
        lanes = pl.ds(pl.multiple_of(t * 2 * R, 128), 2 * R)
        rows = pl.ds(pl.multiple_of(t * 2 * R, 16), 2 * R)
        for n, right in enumerate(rights):
            XC[rows, n * half : (n + 1) * half] = dot(lefts[:, lanes], right[...], TN).astype(BF)
        for y in range(2):
            g = t * 2 + y
            rows = pl.ds(pl.multiple_of(g * R + R - 16, 16), 16)
            more = extra[pl.ds(pl.multiple_of(g * 16, 16), 16), :]
            for s in range(S):
                lane = slice(s * I4, (s + 1) * I4)
                XC[rows, lane] = (XC[rows, lane].astype(F32) + more).astype(BF)
        scatter(t * 2 + 1 - me.y).to_core()
        scatter(t * 2 + me.y).to_core()

    for i in range(A):
        attention_rows(i)
        run((2, 0, 2, 1)[min(i, 3)], (3, 1, 1, 1)[min(i, 3)])
    held = [p for p in range(last) if p >= NP // 2]
    for j in range(dp):
        scatter(turn(j)).to_x()
    run(0, 1)
    for j in range(dp):
        g = turn(j)
        part_g(me.s, g)[...] = scatter(g).meet().astype(BF)
        if j % 2 == 0:
            att.ysend(j // 2, 0)
        elif held:
            ffn.ysend(A - 1, held.pop(0))
        if j >= 2:
            run(1, 1)
        if j % 2 and j >= 3:
            att.event((j - 3) // 2, 0)
    while held:
        ffn.ysend(A - 1, held.pop(0))
    att.event(A - 1, 0)
    run(*(len(events) for _, events in queues))
    ffn.last(last)

    for n in range(2):
        for k in range(1, X):
            pcopy(n, k).wait_send()
    key_scatter.drain()
    loop(dp, lambda g: scatter(g).drain())
    att.drain(0)
    loop(last, ffn.drain)
    ffn.drain(last, True)
    layer_out.wait()
    input_out.wait()


def backward(geo, x, saved):
    dma = pltpu.SemaphoreType.DMA
    S, N, F, T, L, I, X, I4, A, R = geo.seq, geo.N, geo.F, geo.T, geo.L, geo.I, geo.X, geo.I4, geo.A, geo.R
    per = 128 // (I // geo.H)
    consts = constants(geo)
    V = pltpu.VMEM
    scratch = [
        V((3, N, F), BF), V((2 * L, N), BF), V((3, L, F), BF), V((A, 3, R, F), BF), V((A + 1, 3, R, F), BF),
        V((S, N, I4), BF), V((A, R, I4), BF), V((A + 1, R, I4), BF),
        V((X, N, I4), BF), V((X - 1, N, I4), BF),
        V((T, N), BF), V((T, N), F32), V((T, 3 * I), BF), V((L, 2 * I), BF), V((T, I), BF),
        V((2, T, N), BF), V((2, X - 1, T, N), BF), V((per, T, L), F32),
        V((X, T, 2 * I), BF), V((X - 1, T, 2 * I), BF), V((A + 1, geo.RH, F), BF),
        V((T, N), F32), V((128, 512), F32), V((geo.dp * 16, I4), F32), V((8, N), F32),
        *[V(v.shape, v.dtype) for v in consts],
        dma((15,)), dma((per,)), dma((2,)),
        dma((2, X - 1)), dma((2, X - 1)), dma((X,)), dma((X,)), dma((X - 1,)), dma((X - 1,)),
        dma((geo.dp, X)), dma((geo.dp, X)), dma((geo.dp, X - 1)), dma((geo.dp, X - 1)),
        dma((A, geo.NP)), dma((A, geo.NP)), dma((A, geo.NP)), dma((A + 1, geo.NP)),
        dma((A, 1)), dma((A + 1, 1)),
        dma((A, 1)), dma((A, 1)), dma((A, 1)), dma((A + 1, 1)),
    ]
    return pl.pallas_call(
        functools.partial(backward_kernel, geo),
        out_shape=[
            jax.ShapeDtypeStruct((3, R, F), F32), jax.ShapeDtypeStruct((R, I4), F32),
            jax.ShapeDtypeStruct((T, N), BF), jax.ShapeDtypeStruct((T, N), BF),
        ],
        in_specs=[pl.BlockSpec(memory_space=pl.ANY)] * (1 + len(saved) + len(consts)),
        out_specs=[pl.BlockSpec(memory_space=pltpu.VMEM)] * 2 + [pl.BlockSpec(memory_space=pl.ANY)] * 2,
        scratch_shapes=scratch,
        compiler_params=pltpu.CompilerParams(collective_id=2, has_side_effects=True, vmem_limit_bytes=63 << 20),
        name="backward",
    )(x, *saved, *consts)


def spread_features(values, geo, width):
    lead = values.shape[:-1]
    blocks = values.reshape(*lead, geo.dp, width)
    return jnp.pad(blocks, [(0, 0)] * (len(lead) + 1) + [(0, geo.R - width)]).reshape(*lead, geo.dp * geo.R)


def pack_features(values, geo, width):
    lead = values.shape[:-1]
    return values.reshape(*lead, geo.dp, geo.R)[..., :width].reshape(*lead, geo.dp * width)


def general_path(
    axes, tokens, cotangent, lengths, w_query, w_key_value, w_output, w_gate_up, w_down, norm_gains, position_bias
):
    dp, seq = axes
    width, own_inner = w_query.shape
    table_rows, head_count = position_bias.shape
    geo = Geo(dp, seq, width, w_down.shape[1], 4 * own_inner, tokens.shape[1], head_count, table_rows)
    rows = geo.R
    model_width = geo.D
    bucket_count = table_rows * dp
    inner_width = geo.I
    head_dim = inner_width // head_count

    lanes = lambda v: jnp.pad(v, ((0, 0), (0, geo.I4 - v.shape[1])))
    wa = jnp.concatenate(
        [
            jnp.concatenate([w_query, w_key_value[0], w_key_value[1], w_output], axis=1).astype(BF),
            jnp.zeros((rows - width - geo.E, geo.I4), BF),
            lanes(norm_gains.astype(BF)),
            lanes(position_bias.astype(BF)),
        ],
        axis=0,
    )
    wf = jnp.pad(jnp.concatenate([w_gate_up, w_down[None]], axis=0).astype(BF), ((0, 0), (0, rows - width), (0, 0)))
    WF, WA = gather_weights(geo, wf, wa)

    blocks = WA[0].reshape(dp, rows, geo.I4)
    first_gain = blocks[:, rows - geo.E, :width].reshape(model_width).astype(F32)
    second_gain = blocks[:, rows - geo.E + 1, :width].reshape(model_width).astype(F32)
    table_full = blocks[:, rows - table_rows :, :head_count].reshape(bucket_count, head_count)
    real = WA.reshape(seq, dp, rows, 4, own_inner)[:, :, :width]
    parts = real.transpose(3, 1, 2, 0, 4).reshape(4, model_width, inner_width)
    query_full, keyval_full, output_full = parts[0], parts[1:3], parts[3]

    inputs = tokens[0].astype(jnp.float32)
    row_count = inputs.shape[0]
    normed = norm_scale(inputs, first_gain).astype(jnp.bfloat16)
    queries = jnp.dot(normed, query_full, preferred_element_type=jnp.float32).astype(jnp.bfloat16)
    projected = jnp.einsum(
        "td,sdi->sti", normed, keyval_full, preferred_element_type=jnp.float32
    ).astype(jnp.bfloat16)
    keys_all, values_all = (
        lax.all_gather(projected[0], "seq", axis=0, tiled=True),
        lax.all_gather(projected[1], "seq", axis=0, tiled=True),
    )
    incoming_low = cotangent[0]
    incoming = incoming_low.astype(jnp.float32)
    cot_all = lax.all_gather(spread_features(incoming_low, geo, width), "seq", axis=0, tiled=True)
    length_all = keys_all.shape[0]
    block_start = lax.axis_index("seq") * row_count
    query_pos = block_start + jnp.arange(row_count, dtype=jnp.int32)
    key_pos = jnp.arange(length_all, dtype=jnp.int32)
    buckets = bucket_ids(key_pos[None, :] - query_pos[:, None])
    bucket_range = jnp.arange(bucket_count, dtype=jnp.int32)
    onehot = (buckets[:, :, None] == bucket_range).astype(jnp.bfloat16)
    score_bias = jnp.einsum("tkb,bh->htk", onehot, table_full, preferred_element_type=jnp.float32)
    key_valid = key_pos < lengths[0]
    query_heads = queries.reshape(row_count, head_count, head_dim)
    key_heads = keys_all.reshape(length_all, head_count, head_dim)
    value_heads = values_all.reshape(length_all, head_count, head_dim)
    raw_scores = (
        jnp.einsum("thc,khc->htk", query_heads, key_heads, preferred_element_type=jnp.float32) + score_bias
    )
    scores = jnp.where(key_valid[None, None, :], raw_scores, NEGATIVE)
    probs = jax.nn.softmax(scores, axis=-1)
    probs_low = probs.astype(BF)
    mixed_heads = (
        jnp.einsum("htk,khc->thc", probs_low, value_heads, preferred_element_type=jnp.float32)
        .reshape(row_count, inner_width)
        .astype(jnp.bfloat16)
    )
    attended = jnp.einsum("tc,dc->td", mixed_heads, output_full, preferred_element_type=jnp.float32)
    hidden_one = inputs + attended
    normed_two = norm_scale(hidden_one, second_gain).astype(jnp.bfloat16)
    normed_two_all = lax.all_gather(spread_features(normed_two, geo, width), "seq", axis=0, tiled=True)

    gate = jnp.dot(normed_two_all, WF[0], preferred_element_type=F32)
    upward = jnp.dot(normed_two_all, WF[1], preferred_element_type=F32)
    activated = gated(gate, upward).astype(BF)
    down_term = jnp.einsum("tf,df->td", activated, WF[2], preferred_element_type=F32)
    down_weight_grad = jnp.einsum("td,tf->df", cot_all, activated, preferred_element_type=F32)
    activated_grad = jnp.dot(cot_all, WF[2], preferred_element_type=F32)
    unused_value, gate_pull = jax.vjp(gated, gate, upward)
    gate_grad, upward_grad = gate_pull(activated_grad)
    gate_grad, upward_grad = gate_grad.astype(BF), upward_grad.astype(BF)
    gate_weight_grad = jnp.einsum("td,tf->df", normed_two_all, gate_grad, preferred_element_type=F32)
    up_weight_grad = jnp.einsum("td,tf->df", normed_two_all, upward_grad, preferred_element_type=F32)
    normed_two_term = jnp.einsum("tf,df->td", gate_grad, WF[0], preferred_element_type=F32) + jnp.einsum(
        "tf,df->td", upward_grad, WF[1], preferred_element_type=F32
    )
    down_sum = lax.psum_scatter(down_term.astype(BF), "seq", scatter_dimension=0, tiled=True)
    normed_two_sum = lax.psum_scatter(normed_two_term.astype(BF), "seq", scatter_dimension=0, tiled=True)
    outputs = (hidden_one + pack_features(down_sum, geo, width).astype(F32)).astype(BF)[None]
    normed_two_grad = pack_features(normed_two_sum, geo, width).astype(F32)
    gf = jnp.stack([gate_weight_grad.astype(BF), up_weight_grad.astype(BF), down_weight_grad.astype(BF)])

    unused_two, second_pull = jax.vjp(norm_scale, hidden_one, second_gain)
    hidden_norm_grad, second_gain_grad = second_pull(normed_two_grad)
    hidden_grad = incoming + hidden_norm_grad
    hidden_low = hidden_grad.astype(jnp.bfloat16)
    output_weight_grad = jnp.einsum("td,tc->dc", hidden_low, mixed_heads, preferred_element_type=jnp.float32)
    mixed_grad = jnp.einsum("td,dc->tc", hidden_low, output_full, preferred_element_type=jnp.float32).astype(
        jnp.bfloat16
    )
    grad_heads = mixed_grad.reshape(row_count, head_count, head_dim)
    prob_grad = jnp.einsum("thc,khc->htk", grad_heads, value_heads, preferred_element_type=jnp.float32)
    inner_sum = jnp.sum(probs * prob_grad, axis=-1, keepdims=True)
    score_grad = (probs * (prob_grad - inner_sum)).astype(jnp.bfloat16)
    query_act_grad = (
        jnp.einsum("htk,khc->thc", score_grad, key_heads, preferred_element_type=jnp.float32)
        .reshape(row_count, inner_width)
        .astype(jnp.bfloat16)
    )
    key_piece = jnp.einsum(
        "htk,thc->khc", score_grad, query_heads, preferred_element_type=jnp.float32
    ).reshape(length_all, inner_width)
    value_piece = jnp.einsum(
        "htk,thc->khc", probs_low, grad_heads, preferred_element_type=jnp.float32
    ).reshape(length_all, inner_width)
    own_terms = lax.psum_scatter(
        jnp.concatenate([key_piece, value_piece], axis=1).astype(jnp.bfloat16),
        "seq",
        scatter_dimension=0,
        tiled=True,
    )
    keyval_act_grad = jnp.stack([own_terms[:, :inner_width], own_terms[:, inner_width:]])
    query_weight_grad = jnp.einsum("td,tc->dc", normed, query_act_grad, preferred_element_type=jnp.float32)
    keyval_weight_grad = jnp.einsum("td,stc->sdc", normed, keyval_act_grad, preferred_element_type=jnp.float32)
    normed_grad = jnp.einsum(
        "tc,dc->td", query_act_grad, query_full, preferred_element_type=jnp.float32
    ) + jnp.einsum("stc,sdc->td", keyval_act_grad, keyval_full, preferred_element_type=jnp.float32)
    unused_three, first_pull = jax.vjp(norm_scale, inputs, first_gain)
    input_norm_grad, first_gain_grad = first_pull(normed_grad)
    input_grad = (hidden_grad + input_norm_grad).astype(jnp.bfloat16)[None]
    table_grad = jnp.einsum("htk,tkb->bh", score_grad, onehot, preferred_element_type=jnp.float32)

    grads = jnp.stack(
        [query_weight_grad, keyval_weight_grad[0], keyval_weight_grad[1], output_weight_grad]
    ).reshape(4, dp, width, seq, own_inner)
    grads = grads.transpose(3, 1, 2, 0, 4).reshape(seq, dp, width, geo.I4).astype(BF)
    wide = lambda v: jnp.pad(v, ((0, 0), (0, 0), (0, geo.I4 - v.shape[2])))
    more = jnp.concatenate(
        [
            jnp.zeros((dp, rows - width - geo.E, geo.I4), F32),
            wide(first_gain_grad.reshape(dp, 1, width)),
            wide(second_gain_grad.reshape(dp, 1, width)),
            wide(table_grad.reshape(dp, table_rows, head_count)),
        ],
        axis=1,
    ).astype(BF)
    ga = jnp.concatenate([grads, jnp.broadcast_to(more, (seq, *more.shape))], axis=2).reshape(seq, dp * rows, geo.I4)
    of, oa = scatter_grads(geo, gf, ga)

    main = oa[:width]
    query_part = main[:, :own_inner]
    keyval_part = jnp.stack([main[:, own_inner : 2 * own_inner], main[:, 2 * own_inner : 3 * own_inner]])
    output_part = main[:, 3 * own_inner :]
    gain_part = oa[rows - geo.E : rows - table_rows, :width]
    table_part = oa[rows - table_rows :, :head_count]
    return (
        outputs,
        input_grad,
        query_part,
        keyval_part,
        output_part,
        of[:2, :width],
        of[2, :width],
        gain_part,
        table_part,
    )

def fused_path(
    axes, tokens, cotangent, lengths, w_query, w_key_value, w_output, w_gate_up, w_down, norm_gains, position_bias
):
    dp, seq = axes
    width, own_inner = w_query.shape
    table_rows, head_count = position_bias.shape
    geo = Geo(dp, seq, width, w_down.shape[1], 4 * own_inner, tokens.shape[1], head_count, table_rows)
    rows = geo.R

    lanes = lambda v: jnp.pad(v, ((0, 0), (0, geo.I4 - v.shape[1])))
    wa = jnp.concatenate(
        [
            jnp.concatenate([w_query, w_key_value[0], w_key_value[1], w_output], axis=1).astype(BF),
            jnp.zeros((rows - width - geo.E, geo.I4), BF),
            lanes(norm_gains.astype(BF)),
            lanes(position_bias.astype(BF)),
        ],
        axis=0,
    )
    wf = jnp.pad(jnp.concatenate([w_gate_up, w_down[None]], axis=0).astype(BF), ((0, 0), (0, rows - width), (0, 0)))
    xp = spread_features(tokens[0], geo, width)
    cp = spread_features(cotangent[0], geo, width)
    saved = forward(geo, lengths, xp, cp, wf, wa)
    of, oa, layer, grad = backward(geo, xp, saved)
    outputs = pack_features(layer, geo, width)[None]
    input_grad = pack_features(grad, geo, width)[None]

    main = oa[:width]
    query_part = main[:, :own_inner]
    keyval_part = jnp.stack([main[:, own_inner : 2 * own_inner], main[:, 2 * own_inner : 3 * own_inner]])
    output_part = main[:, 3 * own_inner :]
    gain_part = oa[rows - geo.E : rows - table_rows, :width]
    table_part = oa[rows - table_rows :, :head_count]
    return (
        outputs,
        input_grad,
        query_part,
        keyval_part,
        output_part,
        of[:2, :width],
        of[2, :width],
        gain_part,
        table_part,
    )

def per_device(axes, *arrays):
    tokens, w_query, w_down, position_bias = arrays[0], arrays[3], arrays[7], arrays[9]
    geo = Geo(*axes, w_query.shape[0], w_down.shape[1], 4 * w_query.shape[1], tokens.shape[1], position_bias.shape[1],
              position_bias.shape[0])
    aligned = geo.F % 128 == 0 and geo.I4 % 128 == 0 and 2 * geo.R % 128 == 0 and geo.T % 128 == 0 and geo.I % 128 == 0
    aligned = aligned and max(2 * geo.I, geo.seq * geo.I4 // 2) <= geo.F and 4 * geo.T <= geo.L and geo.N + 2 * geo.T <= 2 * geo.L and geo.L + 256 <= geo.N
    small = (3 * geo.F + geo.seq * geo.I4 + 2 * geo.L) * geo.N * 2 <= 24 << 20
    return (fused_path if aligned and small else general_path)(axes, *arrays)


def solution(mesh):
    in_specs = (
        P("dp", "seq", None),
        P("dp", "seq", None),
        P("dp"),
        P("dp", "seq"),
        P(None, "dp", "seq"),
        P("dp", "seq"),
        P(None, "dp", "seq"),
        P("dp", "seq"),
        P(None, "dp"),
        P("dp", None),
    )
    out_specs = (
        P("dp", "seq", None),
        P("dp", "seq", None),
        P("dp", "seq"),
        P(None, "dp", "seq"),
        P("dp", "seq"),
        P(None, "dp", "seq"),
        P("dp", "seq"),
        P(None, "dp"),
        P("dp", None),
    )
    return jax.shard_map(
        functools.partial(per_device, (mesh.shape["dp"], mesh.shape["seq"])), mesh=mesh, in_specs=in_specs, out_specs=out_specs, check_vma=False
    )
```

```python
import functools
import jax
import jax.numpy as jnp
import numpy as np
from jax import lax
from jax.experimental import pallas as pl
from jax.experimental.pallas import tpu as pltpu

from jax.sharding import PartitionSpec as P

MESH = pl.DeviceIdType.MESH
BF = jnp.bfloat16
F32 = jnp.float32


class Geo:
    def __init__(self, dp, seq, width, ff, inner4, tokens, heads, table_rows):
        self.dp, self.seq = dp, seq
        self.W, self.TR, self.E = width, table_rows, 2 + table_rows
        rows = -(-(width + self.E) // 16) * 16
        self.D, self.N, self.T, self.L = dp * width, dp * rows, tokens, seq * tokens
        self.I, self.H = inner4 // 4 * seq, heads
        self.B, self.A, self.X = 2, dp // 2, seq // 2
        self.R, self.F, self.I4 = rows, ff, inner4
        self.NH = 2 if rows % 32 == 0 else 1
        self.RH = rows // self.NH
        self.NP = 3 * self.NH
        self.NZ = 2 * (self.A - 1)
        self.NY = 2 * self.A - 1


class Place:
    def __init__(self, geo):
        d, s = lax.axis_index("dp"), lax.axis_index("seq")
        self.d, self.s = d, s
        self.z, self.y = d // 2, d % 2
        self.x, self.c = s // 2, s % 2

    def dev(self, z=None, y=None, x=None, c=None):
        z = self.z if z is None else z
        y = self.y if y is None else y
        x = self.x if x is None else x
        c = self.c if c is None else c
        return (z * 2 + y, x * 2 + c)


def remote(src, dst, ss, rs, dev):
    return pltpu.make_async_remote_copy(
        src_ref=src, dst_ref=dst, send_sem=ss, recv_sem=rs, device_id=dev, device_id_type=MESH
    )


def loop(n, body):
    def step(i, carry):
        body(i)
        return carry

    lax.fori_loop(0, n, step, 0)


def enter(geo, me):
    bar = pltpu.get_barrier_semaphore()

    def greet(dev):
        pl.semaphore_signal(bar, 1, device_id=dev, device_id_type=MESH)

    greet(me.dev(y=1 - me.y))
    greet(me.dev(c=1 - me.c))
    for k in range(1, geo.X):
        greet(me.dev(x=lax.rem(me.x + k, geo.X)))

    @pl.when(me.z > 0)
    def _():
        greet(me.dev(z=me.z - 1))

    @pl.when(me.z < geo.A - 1)
    def _():
        greet(me.dev(z=me.z + 1))

    count = 2 + (geo.X - 1) + (me.z > 0).astype(jnp.int32) + (me.z < geo.A - 1).astype(jnp.int32)
    pl.semaphore_wait(bar, count)


class LineGather:
    def __init__(self, geo, me, own, held, zs, zr, ys, yr, first_y=1 << 20, bzs=None, bzr=None):
        self.geo, self.me, self.own, self.held = geo, me, own, held
        self.zs, self.zr, self.ys, self.yr = zs, zr, ys, yr
        self.first_y, self.bzs, self.bzr = first_y, bzs, bzr

    def from_z(self, way, r):
        q = self.me.z - r if way == 0 else self.me.z + r
        return q, (q >= 0) if way == 0 else (q <= self.geo.A - 1)

    def sems(self, way, r, p, other):
        slot = way * (self.geo.A - 1) + r - 1
        if other:
            return self.bzs.at[slot, p - self.first_y], self.bzr.at[slot, p - self.first_y]
        return self.zs.at[slot, p], self.zr.at[slot, p]

    def zcopy(self, way, r, p, other=False):
        me, geo = self.me, self.geo
        q, there = self.from_z(way, r - 1)
        to = me.z + 1 if way == 0 else me.z - 1
        valid = ((me.z < geo.A - 1) if way == 0 else (me.z > 0)) & there
        here = self.held(p, q * 2 + (1 - me.y if other else me.y))
        src = self.own(p) if r == 1 and not other else here
        return remote(src, here, *self.sems(way, r, p, other), me.dev(z=to)), valid

    def zarrive(self, way, r, p, other=False):
        q, valid = self.from_z(way, r)
        here = self.held(p, q * 2 + (1 - self.me.y if other else self.me.y))
        return remote(here, here, *self.sems(way, r, p, other), self.me.dev(y=1 - self.me.y)), valid, q

    def yslot(self, way, r):
        return 1 + way * (self.geo.A - 1) + r - 1 if r else 0

    def ycopy(self, way, r, p):
        me, slot = self.me, self.yslot(way, r)
        q, _ = self.from_z(way, r)
        src = self.held(p, q * 2 + me.y) if r else self.own(p)
        return remote(src, self.held(p, q * 2 + me.y), self.ys.at[slot, p], self.yr.at[slot, p], me.dev(y=1 - me.y))

    def yarrive(self, way, r, p):
        me, slot = self.me, self.yslot(way, r)
        q, _ = self.from_z(way, r)
        here = self.held(p, q * 2 + 1 - me.y)
        return remote(here, here, self.ys.at[slot, p], self.yr.at[slot, p], me.dev(y=1 - me.y)), q

    def begin_y(self, p):
        self.ycopy(0, 0, p).start()

    def begin_z(self, p, other=False):
        for way in (0, 1):
            copy, valid = self.zcopy(way, 1, p, other)

            @pl.when(valid)
            def _():
                copy.start()

    def begin(self, p):
        self.begin_y(p)
        self.begin_z(p)

    def turn(self, p):
        self.yarrive(0, 0, p)[0].wait_recv()
        self.begin_z(p, True)

    def step(self, r, p, on_held=None, kinds=(False,), pass_y=True):
        for other in kinds:
            for way in (0, 1):
                copy, valid, q = self.zarrive(way, r, p, other)

                @pl.when(valid)
                def _():
                    copy.wait_recv()
                    if r < self.geo.A - 1:
                        onward, may = self.zcopy(way, r + 1, p, other)

                        @pl.when(may)
                        def _():
                            onward.start()

                    if pass_y:
                        self.ycopy(way, r, p).start()
                    if on_held is not None:
                        on_held(q * 2 + self.me.y)

    def step_both(self, r, p):
        self.step(r, p, None, (False, True), False)

    def ystep(self, r, p, on_held=None):
        for way in (0, 1) if r else (0,):
            copy, q = self.yarrive(way, r, p)

            def go():
                copy.wait_recv()
                if on_held is not None:
                    on_held(q * 2 + 1 - self.me.y)

            if r:
                pl.when(self.from_z(way, r)[1])(go)
            else:
                go()

    def drain(self, p, kinds=(False,), pass_y=True):
        self.ycopy(0, 0, p).wait_send()
        for r in range(1, self.geo.A):
            for way in (0, 1):
                for other in kinds:
                    copy, valid = self.zcopy(way, r, p, other)

                    @pl.when(valid)
                    def _():
                        copy.wait_send()

                if pass_y:

                    @pl.when(self.from_z(way, r)[1])
                    def _():
                        self.ycopy(way, r, p).wait_send()


class LineScatter:
    def __init__(self, geo, me, part, ybuf, zbuf, stage, zs, zr, ys, yr, finish):
        self.__dict__.update(locals())

    def turns(self):
        geo, me = self.geo, self.me
        for k in range(geo.A - 1):
            yield 0, k, geo.A - 1 - k, k < geo.A - 1 - me.z
            yield 1, k, k, k < me.z

    def slot(self, way, k):
        return way * (self.geo.A - 1) + k

    def ycopy(self, slot, t, p):
        me = self.me
        return remote(
            self.part(p, t * 2 + 1 - me.y),
            self.ybuf(p, t),
            self.ys.at[slot, p],
            self.yr.at[slot, p],
            me.dev(y=1 - me.y),
        )

    def zcopy(self, way, k, p):
        me = self.me
        to = me.z + 1 if way == 0 else me.z - 1
        slot = self.slot(way, k)
        return remote(
            self.stage(way, p, k), self.zbuf(way, p, k), self.zs.at[slot, p], self.zr.at[slot, p], me.dev(z=to)
        )

    def ysend(self, p, k):
        for way, kk, t, valid in self.turns():
            if kk == k:

                @pl.when(valid)
                def _():
                    self.ycopy(self.slot(way, kk), t, p).start()

    def ysend_own(self, p):
        self.ycopy(self.geo.NZ, self.me.z, p).start()

    def step(self, k, p):
        geo, me = self.geo, self.me
        for way, kk, t, valid in self.turns():
            if kk == k:

                @pl.when(valid)
                def _():
                    self.ycopy(self.slot(way, k), t, p).wait_recv()
                    total = self.part(p, t * 2 + me.y)[...].astype(F32) + self.ybuf(p, t)[...].astype(F32)
                    out = self.stage(way, p, k)
                    comes = me.z > 0 if way == 0 else me.z < geo.A - 1

                    @pl.when(comes)
                    def _():
                        self.zcopy(way, k, p).wait_recv()
                        out[...] = (total + self.zbuf(way, p, k)[...].astype(F32)).astype(BF)

                    @pl.when(jnp.logical_not(comes))
                    def _():
                        out[...] = total.astype(BF)

                    self.zcopy(way, k, p).start()

    def own(self, p):
        geo, me = self.geo, self.me
        self.ycopy(geo.NZ, me.z, p).wait_recv()
        total = self.part(p, me.z * 2 + me.y)[...].astype(F32) + self.ybuf(p, me.z)[...].astype(F32)
        kup = jnp.minimum(geo.A - 1 - me.z, geo.A - 2)
        kdown = jnp.minimum(me.z, geo.A - 2)

        def arrive(way, k):
            slot = way * (geo.A - 1) + k
            here = self.zbuf(way, p, k)
            remote(here, here, self.zs.at[slot, p], self.zr.at[slot, p], me.dev(y=1 - me.y)).wait_recv()
            return here[...].astype(F32)

        @pl.when(me.z == 0)
        def _():
            self.finish(p, total + arrive(1, kdown))

        @pl.when(me.z == geo.A - 1)
        def _():
            self.finish(p, total + arrive(0, kup))

        @pl.when((me.z > 0) & (me.z < geo.A - 1))
        def _():
            self.finish(p, total + arrive(0, kup) + arrive(1, kdown))

    def drain(self, p):
        for way, k, t, valid in self.turns():

            @pl.when(valid)
            def _():
                self.ycopy(self.slot(way, k), t, p).wait_send()
                self.zcopy(way, k, p).wait_send()

        self.ycopy(self.geo.NZ, self.me.z, p).wait_send()


NEGATIVE = -1e30
EPSILON = 1e-06
LIMITS = (12, 16, 23, 32, 46, 64, 91)


def bucket_ids(offsets):
    distance = jnp.abs(offsets)
    larger = 8 + sum(((distance >= threshold).astype(jnp.int32) for threshold in LIMITS))
    nearby = jnp.where(distance < 8, distance, larger)
    return jnp.where(offsets > 0, 16, 0) + nearby


def norm_scale(values, gain_vector):
    return (
        values
        * lax.rsqrt(jnp.mean(values * values, axis=-1, keepdims=True) + EPSILON)
        * gain_vector
    )


def gated(gate_value, upward):
    return jax.nn.gelu(gate_value, approximate=True) * upward


def gather_kernel(geo, wf, wa, WF, WA, local, zs, zr, ys, yr, azs, azr, ays, ayr, xs, xr, cs, cr):
    me = Place(geo)
    R, RH, NH, dp, X = geo.R, geo.RH, geo.NH, geo.dp, geo.X
    mine = [
        pltpu.make_async_copy(wf, WF.at[:, pl.ds(pl.multiple_of(me.d * R, 16), R), :], local.at[0]),
        pltpu.make_async_copy(wa, WA.at[me.s, pl.ds(pl.multiple_of(me.d * R, 16), R), :], local.at[1]),
    ]
    for copy in mine:
        copy.start()
    enter(geo, me)

    def own_f(p):
        return wf.at[p // NH, pl.ds(pl.multiple_of((p % NH) * RH, 16), RH), :]

    def held_f(p, g):
        return WF.at[p // NH, pl.ds(pl.multiple_of(g * R + (p % NH) * RH, 16), RH), :]

    def held_a(s, g):
        return WA.at[s, pl.ds(pl.multiple_of(g * R, 16), R), :]

    ffn = LineGather(geo, me, own_f, held_f, zs, zr, ys, yr)
    att = LineGather(geo, me, lambda p: wa, lambda p, g: held_a(me.s, g), azs, azr, ays, ayr)

    def xcopy(k, g, src):
        to = lax.rem(me.x + k, X)
        return remote(src, held_a(me.s, g), xs.at[k - 1, g], xr.at[k - 1, g], me.dev(x=to))

    def xarrive(k, g):
        src_x = lax.rem(me.x - k + X, X)
        here = held_a(src_x * 2 + me.c, g)
        return remote(here, here, xs.at[k - 1, g], xr.at[k - 1, g], me.dev(c=1 - me.c)), here

    def ccopy(k, g, src, s):
        return remote(src, held_a(s, g), cs.at[k, g], cr.at[k, g], me.dev(c=1 - me.c))

    def spread(g, src=None):
        src = held_a(me.s, g) if src is None else src
        for k in range(1, X):
            xcopy(k, g, src).start()
        ccopy(0, g, src, me.s).start()

    att.begin(0)
    spread(me.d, wa)
    loop(geo.NP, ffn.begin)
    att.ystep(0, 0, spread)
    for r in range(1, geo.A):
        att.step(r, 0, spread)
        att.ystep(r, 0, spread)

    def from_x(g):
        for k in range(1, X):
            copy, here = xarrive(k, g)
            copy.wait_recv()
            ccopy(k, g, here, lax.rem(me.x - k + X, X) * 2 + me.c).start()

    loop(dp, from_x)
    for r in range(1, geo.A):
        loop(geo.NP, lambda p: ffn.step(r, p))
    for r in range(geo.A):
        loop(geo.NP, lambda p: ffn.ystep(r, p))

    def finish(g):
        for k in range(X):
            s = lax.rem(me.x - k + X, X) * 2 + 1 - me.c
            here = held_a(s, g)
            remote(here, here, cs.at[k, g], cr.at[k, g], me.dev(c=1 - me.c)).wait_recv()
            ccopy(k, g, here, s).wait_send()
            if k:
                xcopy(k, g, here).wait_send()

    loop(dp, finish)
    att.drain(0)
    loop(geo.NP, ffn.drain)
    for copy in mine:
        copy.wait()


def scatter_kernel(
    geo, gf, ga, of, oa, yb, zb, st, cb, xb, xst, pa, ayb, azb, ast,
    zs, zr, ys, yr, azs, azr, ays, ayr, xs, xr, cs, cr,
):
    me = Place(geo)
    R, RH, NH, dp, X, A = geo.R, geo.RH, geo.NH, geo.dp, geo.X, geo.A
    enter(geo, me)

    def rows(g, p):
        return pl.ds(pl.multiple_of(g * R + (p % NH) * RH, 16), RH)

    def piece(buf, i, p):
        return buf.at[i, p // NH, pl.ds(pl.multiple_of((p % NH) * RH, 16), RH), :]

    def finish_f(p, value):
        of[p // NH, pl.ds(pl.multiple_of((p % NH) * RH, 16), RH), :] = value

    ffn = LineScatter(
        geo, me,
        lambda p, g: gf.at[p // NH, rows(g, p), :],
        lambda p, t: piece(yb, t, p),
        lambda way, p, k: piece(zb, way * (A - 1) + k, p),
        lambda way, p, k: piece(st, way * (A - 1) + k, p),
        zs, zr, ys, yr, finish_f,
    )

    def block(g):
        return pl.ds(pl.multiple_of(g * R, 16), R)

    def finish_a(p, value):
        oa[...] = value

    att = LineScatter(
        geo, me,
        lambda p, g: pa.at[block(g), :],
        lambda p, t: ayb.at[t],
        lambda way, p, k: azb.at[way * (A - 1) + k],
        lambda way, p, k: ast.at[way * (A - 1) + k],
        azs, azr, ays, ayr, finish_a,
    )

    def ccopy(k, g):
        to_x = lax.rem(me.x + k, X)
        return remote(
            ga.at[to_x * 2 + 1 - me.c, block(g), :], cb.at[k, block(g), :], cs.at[k, g], cr.at[k, g], me.dev(c=1 - me.c)
        )

    def xcopy(k, g):
        return remote(
            xst.at[k - 1, block(g), :], xb.at[k - 1, block(g), :], xs.at[k - 1, g], xr.at[k - 1, g],
            me.dev(x=lax.rem(me.x + k, X)),
        )

    def to_core(g):
        for k in (*range(1, X), 0):
            ccopy(k, g).start()

    def to_x(g):
        for k in range(1, X):
            ccopy(k, g).wait_recv()
            s = lax.rem(me.x + k, X) * 2 + me.c
            xst[k - 1, block(g), :] = (
                ga[s, block(g), :].astype(F32) + cb[k, block(g), :].astype(F32)
            ).astype(BF)
            xcopy(k, g).start()

    def meet(g):
        ccopy(0, g).wait_recv()
        total = ga[me.s, block(g), :].astype(F32) + cb[0, block(g), :].astype(F32)
        for k in range(1, X):
            xcopy(k, g).wait_recv()
            total += xb[k - 1, block(g), :].astype(F32)
        pa[block(g), :] = total.astype(BF)

    def free(g):
        for k in range(X):
            ccopy(k, g).wait_send()
            if k:
                xcopy(k, g).wait_send()

    for k in range(A - 1):
        loop(geo.NP, lambda p: ffn.ysend(p, k))
    loop(geo.NP, ffn.ysend_own)
    loop(dp, to_core)
    loop(dp, to_x)
    for k in range(A - 1):
        loop(geo.NP, lambda p: ffn.step(k, p))
    loop(geo.NP, ffn.own)
    loop(dp, meet)
    for k in range(A - 1):
        att.ysend(0, k)
    att.ysend_own(0)
    for k in range(A - 1):
        att.step(k, 0)
    att.own(0)
    loop(dp, free)
    att.drain(0)
    loop(geo.NP, ffn.drain)


def gather_weights(geo, wf, wa):
    dma = pltpu.SemaphoreType.DMA
    sems = [
        dma((2,)),
        dma((geo.NZ, geo.NP)), dma((geo.NZ, geo.NP)), dma((geo.NY, geo.NP)), dma((geo.NY, geo.NP)),
        dma((geo.NZ, 1)), dma((geo.NZ, 1)), dma((geo.NY, 1)), dma((geo.NY, 1)),
        dma((geo.X - 1, geo.dp)), dma((geo.X - 1, geo.dp)), dma((geo.X, geo.dp)), dma((geo.X, geo.dp)),
    ]
    return pl.pallas_call(
        functools.partial(gather_kernel, geo),
        out_shape=(
            jax.ShapeDtypeStruct((3, geo.dp * geo.R, geo.F), BF),
            jax.ShapeDtypeStruct((geo.seq, geo.dp * geo.R, geo.I4), BF),
        ),
        in_specs=[pl.BlockSpec(memory_space=pl.ANY)] * 2,
        out_specs=[pl.BlockSpec(memory_space=pl.ANY)] * 2,
        scratch_shapes=sems,
        compiler_params=pltpu.CompilerParams(collective_id=0, has_side_effects=True, vmem_limit_bytes=48 << 20),
        name="gather_weights",
    )(wf, wa)


def scatter_grads(geo, gf, ga):
    dma = pltpu.SemaphoreType.DMA
    n, X, A, R = geo.dp * geo.R, geo.X, geo.A, geo.R
    scratch = [
        pltpu.VMEM((A, 3, R, geo.F), BF), pltpu.VMEM((geo.NZ, 3, R, geo.F), BF), pltpu.VMEM((geo.NZ, 3, R, geo.F), BF),
        pltpu.VMEM((X, n, geo.I4), BF), pltpu.VMEM((X - 1, n, geo.I4), BF), pltpu.VMEM((X - 1, n, geo.I4), BF),
        pltpu.VMEM((n, geo.I4), BF),
        pltpu.VMEM((A, R, geo.I4), BF), pltpu.VMEM((geo.NZ, R, geo.I4), BF), pltpu.VMEM((geo.NZ, R, geo.I4), BF),
        dma((geo.NZ, geo.NP)), dma((geo.NZ, geo.NP)), dma((geo.NZ + 1, geo.NP)), dma((geo.NZ + 1, geo.NP)),
        dma((geo.NZ, 1)), dma((geo.NZ, 1)), dma((geo.NZ + 1, 1)), dma((geo.NZ + 1, 1)),
        dma((X - 1, geo.dp)), dma((X - 1, geo.dp)), dma((X, geo.dp)), dma((X, geo.dp)),
    ]
    return pl.pallas_call(
        functools.partial(scatter_kernel, geo),
        out_shape=(
            jax.ShapeDtypeStruct((3, R, geo.F), F32),
            jax.ShapeDtypeStruct((R, geo.I4), F32),
        ),
        in_specs=[pl.BlockSpec(memory_space=pltpu.VMEM)] * 2,
        out_specs=[pl.BlockSpec(memory_space=pltpu.VMEM)] * 2,
        scratch_shapes=scratch,
        compiler_params=pltpu.CompilerParams(collective_id=1, has_side_effects=True, vmem_limit_bytes=60 << 20),
        name="scatter_grads",
    )(gf, ga)


class SeqGather:
    def __init__(self, geo, me, held, xs, xr, cs, cr):
        self.geo, self.me, self.held = geo, me, held
        self.xs, self.xr, self.cs, self.cr = xs, xr, cs, cr

    def ccopy(self, k):
        me, X = self.me, self.geo.X
        here = self.held(lax.rem(me.x - k + X, X) * 2 + me.c)
        return remote(here, here, self.cs.at[k], self.cr.at[k], me.dev(c=1 - me.c))

    def xcopy(self, k):
        me = self.me
        here = self.held(me.s)
        return remote(here, here, self.xs.at[k - 1], self.xr.at[k - 1], me.dev(x=lax.rem(me.x + k, self.geo.X)))

    def begin(self):
        for k in range(1, self.geo.X):
            self.xcopy(k).start()
        self.ccopy(0).start()

    def relay(self):
        for k in range(1, self.geo.X):
            self.xcopy(k).wait_recv()
            self.ccopy(k).start()

    def finish(self):
        for k in range(self.geo.X):
            self.ccopy(k).wait_recv()
            self.ccopy(k).wait_send()
            if k:
                self.xcopy(k).wait_send()


def dot(a, b, dims=((1,), (0,))):
    return lax.dot_general(a, b, (dims, ((), ())), preferred_element_type=F32)


NT = ((1,), (1,))
TN = ((0,), (0,))


def constants(geo):
    own, I4, S, I = geo.I4 // 4, geo.I4, geo.seq, geo.I
    perm_out = np.zeros((I, S * I4), np.float32)
    i = np.arange(own)
    for s in range(S):
        perm_out[s * own + i, s * I4 + 3 * own + i] = 1
    offset = np.arange(512) - 256
    distance = np.abs(offset)
    larger = 8 + sum((distance >= limit).astype(np.int32) for limit in LIMITS)
    bucket = np.where(offset > 0, 16, 0) + np.where(distance < 8, distance, larger)
    onehot = np.zeros((geo.dp * 16, 512), np.float32)
    for b in range(geo.dp * geo.TR):
        onehot[b // geo.TR * 16 + 16 - geo.E + 2 + b % geo.TR] = bucket == b
    return [jnp.asarray(v, BF) for v in (perm_out, onehot)]


def spread(geo, value):
    value = value.astype(F32)
    gap = jnp.zeros((geo.R - geo.W, value.shape[1]), F32)
    parts = [v for g in range(geo.dp) for v in (value[g * geo.W : (g + 1) * geo.W], gap)]
    return jnp.concatenate(parts, axis=0).T.astype(BF)


def pack(geo, value):
    value = value.T
    return jnp.concatenate([value[g * geo.R : g * geo.R + geo.W] for g in range(geo.dp)], axis=0).astype(BF)


def shear(value, sign):
    rows, lanes = value.shape
    row = lax.broadcasted_iota(jnp.int32, (rows, 1), 0)
    bit = 1
    while bit < rows:
        moved = pltpu.roll(value, bit if sign > 0 else lanes - bit, 1)
        value = jnp.where((row & bit) != 0, moved, value)
        bit *= 2
    return value


def gelu_parts(g):
    k0 = np.float32(np.sqrt(2 / np.pi))
    t = jnp.tanh(k0 * (g + np.float32(0.044715) * (g * g * g)))
    half = 0.5 * (1.0 + t)
    slope = half + 0.5 * g * (1.0 - t * t) * (k0 * (1.0 + np.float32(3 * 0.044715) * (g * g)))
    return g * half, slope


def forward_kernel(
    geo, length, x_in, c_in, wq, wkv, wo, wgu, wd, norm_gains, position_bias, cpo, conehot,
    oX, oWA, oqkv, oKV, oP, omixed, ohid, oX2, oC, oact, opart, ogain,
    WF, WA, xv, C, X2, KV, qkv, strip, mixed, hid, pst, act, part, got, gain, raw, wst, ast, gst, bst, ex, pout, onehot,
    local, outs, psem, zs, zr, ys, yr, bzs, bzr, azs, azr, ays, ayr, xs, xr, cs, cr, gxs, gxr, gcs, gcr, ps, pr,
):
    me = Place(geo)
    R, RH, NH, dp, X, T, N, I = geo.R, geo.RH, geo.NH, geo.dp, geo.X, geo.T, geo.N, geo.I
    I4, S, L = geo.I4, geo.seq, geo.L
    block = lambda i, n: pl.ds(pl.multiple_of(i * n, 16), n)
    loads = [
        (wq, ast.at[0]), (wkv.at[0], ast.at[1]), (wkv.at[1], ast.at[2]), (wo, ast.at[3]), (norm_gains, gst),
        (position_bias, bst), (wgu.at[0], wst.at[0]), (wgu.at[1], wst.at[1]), (wd, wst.at[2]), (x_in, raw.at[0]),
        (c_in, raw.at[1]), (cpo, pout), (conehot, onehot),
    ]
    loads = [pltpu.make_async_copy(src, dst, local.at[i]) for i, (src, dst) in enumerate(loads)]
    for copy in loads:
        copy.start()
    W, E = geo.W, geo.E
    ex[...] = jnp.zeros_like(ex)
    for copy in loads[:6]:
        copy.wait()
    ex[R - W - E : R - W - E + 2, :W] = gst[...]
    ex[R - W - E + 2 :, : geo.H] = bst[...]
    columns = jnp.concatenate([ast[k] for k in range(4)], axis=1)
    WA[me.s, block(me.d, R), :] = jnp.concatenate([columns, ex[...]], axis=0).astype(BF)
    enter(geo, me)

    def held_f(p, g):
        return WF.at[p // NH, pl.ds(pl.multiple_of(g * R + (p % NH) * RH, 16), RH), :]

    def held_a(s, g):
        return WA.at[s, block(g, R), :]

    last = geo.NP - 1
    ffn = LineGather(geo, me, lambda p: held_f(p, me.d), held_f, zs, zr, ys, yr, last, bzs, bzr)
    att = LineGather(geo, me, lambda p: held_a(me.s, me.d), lambda p, g: held_a(me.s, g), azs, azr, ays, ayr)

    def xcopy(k, g, src):
        to = lax.rem(me.x + k, X)
        return remote(src, held_a(me.s, g), xs.at[k - 1, g], xr.at[k - 1, g], me.dev(x=to))

    def xarrive(k, g):
        src_x = lax.rem(me.x - k + X, X)
        here = held_a(src_x * 2 + me.c, g)
        return remote(here, here, xs.at[k - 1, g], xr.at[k - 1, g], me.dev(c=1 - me.c)), here

    def ccopy(k, g, src, s):
        return remote(src, held_a(s, g), cs.at[k, g], cr.at[k, g], me.dev(c=1 - me.c))

    def share(g):
        src = held_a(me.s, g)
        for k in range(1, X):
            xcopy(k, g, src).start()
        ccopy(0, g, src, me.s).start()

    half = T // 2

    def seq_gather(i, ref, first, count):
        held = lambda s: ref.at[pl.ds(pl.multiple_of(s * T + first, 16), count), :]
        return SeqGather(geo, me, held, gxs.at[i], gxr.at[i], gcs.at[i], gcr.at[i])

    gather_c, gather_kv = seq_gather(0, C, 0, T), seq_gather(1, KV, 0, T)
    gather_x2 = [seq_gather(2, X2, 0, half), seq_gather(3, X2, half, half)]

    att.begin(0)
    share(me.d)
    for m in range(3):
        loads[6 + m].wait()
        WF[m, block(me.d, R), :] = jnp.concatenate([wst[m], jnp.zeros((R - W, geo.F), F32)], axis=0).astype(BF)
    ffn.begin_y(last)
    loop(last, ffn.begin)
    ffn.begin_z(last)
    events = [(r, p) for r in range(1, geo.A) for p in (*range(last), last)]

    def run(count):
        for _ in range(min(count, len(events))):
            r, p = events.pop(0)
            if p == last:
                ffn.step_both(r, p)
            else:
                ffn.step(r, p)

    att.ystep(0, 0, share)
    for r in range(1, geo.A):
        att.step(r, 0, share)
        att.ystep(r, 0, share)
    ffn.turn(last)
    for copy in loads[9:]:
        copy.wait()
    xv[...] = spread(geo, raw[0])
    C[block(me.s, T), :] = spread(geo, raw[1])

    def from_x(g):
        for k in range(1, X):
            copy, here = xarrive(k, g)
            copy.wait_recv()
            ccopy(k, g, here, lax.rem(me.x - k + X, X) * 2 + me.c).start()

    for g in range(dp):
        from_x(g)
        if g >= 3:
            run(1)

    def settle(g):
        for k in range(X):
            s = lax.rem(me.x - k + X, X) * 2 + 1 - me.c
            here = held_a(s, g)
            remote(here, here, cs.at[k, g], cr.at[k, g], me.dev(c=1 - me.c)).wait_recv()

    loop(dp, settle)

    extra = jnp.concatenate([WA[0, g * R + R - 16 : g * R + R, :] for g in range(dp)], axis=0)
    lines = extra.astype(F32)
    gain[...] = jnp.zeros_like(gain)
    for g in range(dp):
        for e in range(2):
            at = g * 16 + 16 - E + e
            gain[e : e + 1, g * R : (g + 1) * R] = lines[at : at + 1, :R]
    bias = dot(extra[:, :128], onehot[...], TN)

    inputs = xv[...].astype(F32)
    scale = lax.rsqrt(jnp.sum(inputs * inputs, axis=-1, keepdims=True) / np.float32(geo.D) + EPSILON)
    normed = (inputs * scale * gain[0:1, :]).astype(BF)
    columns = jnp.concatenate([dot(normed, WA[s]) for s in range(S)], axis=1)
    for kind in range(3):
        moved = pltpu.roll(columns, (3 - kind) * (I4 // 4), 1).astype(BF)
        qkv[:, kind * I : (kind + 1) * I] = dot(moved, pout[...], NT).astype(BF)
    KV[block(me.s, T), :] = qkv[:, I:]
    gather_kv.begin()
    gather_c.begin()
    run(1)
    writes = []

    def write(src, dst):
        copy = pltpu.make_async_copy(src, dst, outs.at[len(writes)])
        copy.start()
        writes.append(copy)

    write(xv, oX)
    write(WA, oWA)
    write(qkv, oqkv)
    write(gain, ogain)
    NB = L // 128
    for h in range(geo.H):
        band = shear(jnp.broadcast_to(bias[h : h + 1, :], (128, 512)), 1)[:, 128:512].astype(BF)
        strip[h, :, (NB - 2) * 128 : (NB + 1) * 128] = band
        far = (NB - 2) * 128
        strip[h, :, :far] = jnp.broadcast_to(bias[h : h + 1, 0:1], (128, far)).astype(BF)
        strip[h, :, (NB + 1) * 128 :] = jnp.broadcast_to(bias[h : h + 1, 511:512], (128, far)).astype(BF)
    run(1)
    gather_kv.relay()
    gather_kv.finish()
    run(1)
    write(KV, oKV)

    hd = I // geo.H
    per = 128 // hd
    valid = lax.broadcasted_iota(jnp.int32, (1, L), 1) < length[0]

    def pair(t, first):
        rows = slice(first, first + half)
        lanes = pl.ds(pl.multiple_of(t * 128, 128), 128)
        head = lax.broadcasted_iota(jnp.int32, (1, 128), 1) // hd
        keys = KV[:, lanes]
        values = KV[:, pl.ds(pl.multiple_of(I + t * 128, 128), 128)]
        queries = qkv[rows, lanes]
        outs_ = jnp.zeros((half, 128), F32)
        for e in range(per):
            h = t * per + e
            scores = dot(jnp.where(head == e, queries, jnp.zeros_like(queries)), keys, NT)
            shift = [
                strip[h, :, pl.ds(pl.multiple_of((NB - 1 - me.s * (T // 128) - b) * 128, 128), L)].astype(F32)
                for b in range(first // 128, (first + half) // 128)
            ]
            scores = jnp.where(valid, scores + jnp.concatenate(shift, axis=0), np.float32(NEGATIVE))
            top = jnp.max(scores, axis=-1, keepdims=True)
            probs = jnp.exp(scores - top)
            probs = probs * (1.0 / jnp.sum(probs, axis=-1, keepdims=True))
            copy = pltpu.make_async_copy(pst.at[e], oP.at[h, rows, :], psem.at[e])

            @pl.when((t > 0) | (first > 0))
            def _():
                copy.wait()

            pst[e] = probs
            copy.start()
            mine = dot(probs.astype(BF), values)
            outs_ = jnp.where(head == e, mine, outs_)
        mixed[rows, lanes] = outs_.astype(BF)

    for first in (0, half):
        rows = slice(first, first + half)
        for t in range(I // 128):
            pair(t, first)
            if t < 2:
                run(1)
        spread_mixed = dot(mixed[rows, :], pout[...]).astype(BF)
        total = xv[rows, :].astype(F32)
        for s in range(S):
            total += dot(spread_mixed[:, s * I4 : (s + 1) * I4], WA[s], NT)
        hid[rows, :] = total
        scale = lax.rsqrt(jnp.sum(total * total, axis=-1, keepdims=True) / np.float32(geo.D) + EPSILON)
        X2[pl.ds(pl.multiple_of(me.s * T + first, 16), half), :] = (total * scale * gain[1:2, :]).astype(BF)
        gather_x2[first // half].begin()
        run(1)
        if first == 0:
            gather_c.relay()
    for e in range(per):
        pltpu.make_async_copy(pst.at[e], oP.at[e, half:, :], psem.at[e]).wait()
    write(mixed, omixed)
    write(hid, ohid)
    gather_c.finish()
    write(C, oC)
    gather_x2[0].relay()
    run(len(events))
    gather_x2[1].relay()
    for r in range(geo.A):
        loop(last, lambda p: ffn.ystep(r, p))
    for part_x2 in gather_x2:
        part_x2.finish()
    write(X2, oX2)

    def pcopy(n, k):
        return remote(part.at[0, n, k], got.at[n, k], ps.at[n, k], pr.at[n, k], me.dev(c=1 - me.c))

    def tokens_block(i):
        k = X - 1 - i // 2
        e = i % 2
        s = lax.rem(me.x + k, X) * 2 + lax.rem(1 + e + me.c, 2)
        rows = block(s, T)
        xb = X2[rows, :]
        gate = dot(xb, WF[0])
        upward = dot(xb, WF[1])
        back = dot(C[rows, :], WF[2])
        value, slope = gelu_parts(gate)
        activated = (value * upward).astype(BF)
        first = (back * upward * slope).astype(BF)
        second = (back * value).astype(BF)
        act[0, rows, :] = first
        act[1, rows, :] = second
        act[2, rows, :] = activated
        part[e, 0, k] = (dot(first, WF[0], NT) + dot(second, WF[1], NT)).astype(BF)
        part[e, 1, k] = dot(activated, WF[2], NT).astype(BF)

        @pl.when(e == 0)
        def _():
            pcopy(0, k).start()
            pcopy(1, k).start()

    loop(2 * X, tokens_block)
    write(act, oact)
    for k in range(X - 1, -1, -1):
        for n in range(2):
            pcopy(n, k).wait_recv()
            part[1, n, k] = (part[1, n, k].astype(F32) + got[n, k].astype(F32)).astype(BF)
    write(part.at[1], opart)
    for k in range(X):
        for n in range(2):
            pcopy(n, k).wait_send()

    def finish(g):
        for k in range(X):
            s = lax.rem(me.x - k + X, X) * 2 + 1 - me.c
            here = held_a(s, g)
            ccopy(k, g, here, s).wait_send()
            if k:
                xcopy(k, g, here).wait_send()

    loop(dp, finish)
    att.drain(0)
    loop(last, ffn.drain)
    ffn.drain(last, (False, True), False)
    for copy in writes:
        copy.wait()


def forward(geo, *arrays):
    dma = pltpu.SemaphoreType.DMA
    S, N, F, T, L, I, H, X, I4 = geo.seq, geo.N, geo.F, geo.T, geo.L, geo.I, geo.H, geo.X, geo.I4
    per = 128 // (I // H)
    consts = constants(geo)
    out_shape = [
        ((T, N), BF), ((S, N, I4), BF), ((T, 3 * I), BF), ((L, 2 * I), BF), ((H, T, L), F32), ((T, I), BF),
        ((T, N), F32), ((L, N), BF), ((L, N), BF), ((3, L, F), BF), ((2, X, T, N), BF), ((8, N), F32),
    ]
    V = pltpu.VMEM
    scratch = [
        V((3, N, F), BF), V((S, N, I4), BF), V((T, N), BF), V((L, N), BF), V((L, N), BF), V((L, 2 * I), BF),
        V((T, 3 * I), BF), V((H, 128, 2 * L - 128), BF), V((T, I), BF), V((T, N), F32),
        V((per, T // 2, L), F32), V((3, L, F), BF), V((2, 2, X, T, N), BF), V((2, X, T, N), BF), V((8, N), F32),
        V((2, geo.D, T), BF), V((3, geo.W, F), F32), V((4, geo.W, I4 // 4), F32), V((2, geo.W), F32), V((geo.TR, H), F32),
        V((geo.R - geo.W, I4), F32),
        *[V(v.shape, v.dtype) for v in consts],
        dma((13,)), dma((12,)), dma((per,)),
        dma((geo.NZ, geo.NP)), dma((geo.NZ, geo.NP)), dma((geo.NY, geo.NP)), dma((geo.NY, geo.NP)),
        dma((geo.NZ, 1)), dma((geo.NZ, 1)),
        dma((geo.NZ, 1)), dma((geo.NZ, 1)), dma((geo.NY, 1)), dma((geo.NY, 1)),
        dma((X - 1, geo.dp)), dma((X - 1, geo.dp)), dma((X, geo.dp)), dma((X, geo.dp)),
        dma((4, X - 1)), dma((4, X - 1)), dma((4, X)), dma((4, X)),
        dma((2, X)), dma((2, X)),
    ]
    return pl.pallas_call(
        functools.partial(forward_kernel, geo),
        out_shape=[jax.ShapeDtypeStruct(*v) for v in out_shape],
        in_specs=[pl.BlockSpec(memory_space=pltpu.SMEM)] + [pl.BlockSpec(memory_space=pl.ANY)] * (len(arrays) - 1 + len(consts)),
        out_specs=[pl.BlockSpec(memory_space=pl.ANY)] * len(out_shape),
        scratch_shapes=scratch,
        compiler_params=pltpu.CompilerParams(collective_id=0, has_side_effects=True, vmem_limit_bytes=63 << 20),
        name="forward",
    )(*arrays, *consts)


class SeqScatter:
    def __init__(self, geo, me, part, cb, xb, cs, cr, xs, xr):
        self.__dict__.update(locals())

    def ccopy(self, k):
        me = self.me
        to = lax.rem(me.x + k, self.geo.X)
        return remote(self.part(to * 2 + 1 - me.c), self.cb(k), self.cs.at[k], self.cr.at[k], me.dev(c=1 - me.c))

    def xcopy(self, k):
        me = self.me
        to = lax.rem(me.x + k, self.geo.X)
        return remote(self.part(to * 2 + me.c), self.xb(k), self.xs.at[k - 1], self.xr.at[k - 1], me.dev(x=to))

    def to_core(self):
        for k in (*range(1, self.geo.X), 0):
            self.ccopy(k).start()

    def to_x(self):
        for k in range(1, self.geo.X):
            self.ccopy(k).wait_recv()
            out = self.part(lax.rem(self.me.x + k, self.geo.X) * 2 + self.me.c)
            out[...] = (out[...].astype(F32) + self.cb(k)[...].astype(F32)).astype(BF)
            self.xcopy(k).start()

    def meet(self):
        self.ccopy(0).wait_recv()
        total = self.part(self.me.s)[...].astype(F32) + self.cb(0)[...].astype(F32)
        for k in range(1, self.geo.X):
            self.xcopy(k).wait_recv()
            total += self.xb(k)[...].astype(F32)
        return total

    def drain(self):
        for k in range(self.geo.X):
            self.ccopy(k).wait_send()
            if k:
                self.xcopy(k).wait_send()


class DpScatter:
    def __init__(self, geo, me, part, ybuf, zbuf, ys, yr, zs, zr, finish, first_z=1 << 20, zbuf2=None, zs2=None, zr2=None):
        self.__dict__.update(locals())

    def owner(self, i):
        A, z = self.geo.A, self.me.z
        up, down = A - 1 - z, z
        both = jnp.minimum(up, down)
        half = i // 2
        early = jnp.where((i % 2 == 0) == (up >= down), A - 1 - half, half)
        late = jnp.where(up > down, A - 1 - (i - both), i - both)
        return jnp.where(i == A - 1, z, jnp.where(i < 2 * both, early, late))

    def ycopy(self, t, p):
        me = self.me
        return remote(
            self.part(p, t * 2 + 1 - me.y), self.ybuf(p, t), self.ys.at[t, p], self.yr.at[t, p], me.dev(y=1 - me.y)
        )

    def zparts(self, t, slot, p, other):
        if other:
            return self.zbuf2(p, slot), self.zs2.at[t, p - self.first_z], self.zr2.at[slot, p - self.first_z]
        return self.zbuf(p, slot), self.zs.at[t, p], self.zr.at[slot, p]

    def mine(self, t, p, other=False):
        return self.part(p, t * 2 + (1 - self.me.y if other else self.me.y))

    def zslot(self, up, t):
        return jnp.where(up, self.geo.A - 1 - t, self.geo.A - t)

    def zcopy(self, t, p, other=False):
        me = self.me
        up = t > me.z
        dst, ss, rs = self.zparts(t, self.zslot(up, t), p, other)
        return remote(self.mine(t, p, other), dst, ss, rs, me.dev(z=jnp.where(up, me.z + 1, me.z - 1)))

    def zarrive(self, up, t, p, other=False):
        here, ss, rs = self.zparts(t, self.zslot(up, t), p, other)
        remote(here, here, ss, rs, self.me.dev(y=1 - self.me.y)).wait_recv()
        return here[...].astype(F32)

    def ysend(self, i, p):
        self.ycopy(self.owner(i), p).start()

    def arrived(self, t, p, base, put, other=False):
        geo, me = self.geo, self.me

        @pl.when(me.z == 0)
        def _():
            put(base() + self.zarrive(False, t, p, other))

        @pl.when(me.z == geo.A - 1)
        def _():
            put(base() + self.zarrive(True, t, p, other))

        @pl.when((me.z > 0) & (me.z < geo.A - 1))
        def _():
            put(base() + self.zarrive(True, t, p, other) + self.zarrive(False, t, p, other))

    def onward(self, t, p, base, other=False, plain=False):
        geo, me = self.geo, self.me
        mine = self.mine(t, p, other)
        up = t > me.z
        comes = (up & (me.z > 0)) | (jnp.logical_not(up) & (me.z < geo.A - 1))

        @pl.when(comes)
        def _():
            mine[...] = (base() + self.zarrive(up, t, p, other)).astype(BF)

        if not plain:

            @pl.when(jnp.logical_not(comes))
            def _():
                mine[...] = base().astype(BF)

        self.zcopy(t, p, other).start()

    def event(self, i, p):
        t = self.owner(i)
        mine = self.mine(t, p)
        own = lambda: mine[...].astype(F32)
        if p >= self.first_z:
            theirs = self.mine(t, p, True)
            their = lambda: theirs[...].astype(F32)
            if i < self.geo.A - 1:
                self.onward(t, p, their, True, True)
                self.onward(t, p, own, False, True)
            else:
                self.arrived(t, p, their, lambda v: theirs.__setitem__(..., v.astype(BF)), True)
                self.ycopy(t, p).start()
            return
        self.ycopy(t, p).wait_recv()
        both = lambda: own() + self.ybuf(p, t)[...].astype(F32)
        if i == self.geo.A - 1:
            self.arrived(t, p, both, lambda v: self.finish(p, v))
        else:
            self.onward(t, p, both)

    def last(self, p):
        t = self.me.z
        mine = self.mine(t, p)
        self.ycopy(t, p).wait_recv()
        both = lambda: mine[...].astype(F32) + self.ybuf(p, t)[...].astype(F32)
        self.arrived(t, p, both, lambda v: self.finish(p, v))

    def drain(self, p, second=False):
        for i in range(self.geo.A):
            t = self.owner(i)
            if not second or i == self.geo.A - 1:
                self.ycopy(t, p).wait_send()
            if i < self.geo.A - 1:
                for other in (False, True) if second else (False,):
                    self.zcopy(t, p, other).wait_send()


def backward_kernel(
    geo, x_in, iWA, iqkv, iKV, iP, imixed, ihid, iX2, iC, iact, ipart, igain, cpo, conehot,
    of, oa, olayer, oinput,
    G, XC, act, yb, zb, WA, ayb, azb, cb, xb, xv, hid, qkv, KV, mixed, pk, px, pst, kcb, kxb, zb2,
    hgrad, gbias, extra, gain, packed, pout, onehot,
    local, psem, outs, pxs, pxr, kcs, kcr, kxs, kxr, acs, acr, axs, axr, ys, yr, zs, zr, zs2, zr2, ays, ayr, azs, azr,
):
    me = Place(geo)
    R, RH, NH, dp, X, T, N, I = geo.R, geo.RH, geo.NH, geo.dp, geo.X, geo.T, geo.N, geo.I
    I4, S, L, A, NP = geo.I4, geo.seq, geo.L, geo.A, geo.NP
    block = lambda i, n: pl.ds(pl.multiple_of(i * n, 16), n)
    dKV = act.at[0, :, : 2 * I]
    dM, dq = act.at[1, :T, :I], act.at[1, T : 2 * T, :I]
    half = S * I4 // 2
    rights = [act.at[2, : 2 * T, :half], act.at[2, 2 * T : 4 * T, :half]]
    lefts = XC.at[N : N + 2 * T, :]
    hlow = lefts.at[T:, :]
    ds = pk.at[0, :, : L + 256]
    loads = [
        (iact, act), (iX2, XC.at[:L, :]), (iC, XC.at[L:, :]), (ipart.at[:, 0], pk), (ihid, hid), (igain, gain),
        (iWA, WA), (cpo, pout), (iKV, KV), (iqkv, qkv), (imixed, mixed), (x_in, xv), (conehot, onehot),
    ]
    loads = [pltpu.make_async_copy(src, dst, local.at[i]) for i, (src, dst) in enumerate(loads)]
    for copy in loads:
        copy.start()
    hd = I // geo.H
    per = 128 // hd

    def pload(t, e):
        return pltpu.make_async_copy(iP.at[t * per + e], pst.at[e], psem.at[e])

    for e in range(per):
        pload(0, e).start()
    enter(geo, me)

    def pcopy(n, k):
        to = me.dev(x=lax.rem(me.x + k, X))
        return remote(ipart.at[n, k], px.at[n, k - 1], pxs.at[n, k - 1], pxr.at[n, k - 1], to)

    for n in range(2):
        for k in range(1, X):
            pcopy(n, k).start()

    def rows_of(g, p):
        return pl.ds(pl.multiple_of(g * R + (p % NH) * RH, 16), RH)

    def piece(buf, i, p):
        return buf.at[i, p // NH, pl.ds(pl.multiple_of((p % NH) * RH, 16), RH), :]

    def finish_f(p, value):
        of[p // NH, pl.ds(pl.multiple_of((p % NH) * RH, 16), RH), :] = value

    last = NP - 1
    ffn = DpScatter(
        geo, me, lambda p, g: G.at[p // NH, rows_of(g, p), :], lambda p, t: piece(yb, t, p),
        lambda p, i: piece(zb, i, p), ys, yr, zs, zr, finish_f,
        last, lambda p, i: zb2.at[i], zs2, zr2,
    )
    for i in range(3):
        loads[i].wait()

    def weight_rows(i):
        t = ffn.owner(i)
        lanes = pl.ds(pl.multiple_of(t * 2 * R, 128), 2 * R)
        rows = pl.ds(pl.multiple_of(t * 2 * R, 16), 2 * R)
        for m in range(3):
            left = XC[:L, lanes] if m < 2 else XC[L:, lanes]
            G[m, rows, :] = dot(left, act[m], TN).astype(BF)

            def go(h):
                p = m * NH + h

                @pl.when((p < last) & ((i < A - 1) | (p < NP // 2)))
                def _():
                    ffn.ysend(i, p)

            loop(NH, go)

    loop(A, weight_rows)

    edge = (me.z == 0) | (me.z == A - 1)
    queues = [(kind, [(i, p) for i in range(A) for p in (last, *range(last))]) for kind in (edge, jnp.logical_not(edge))]

    def run(*counts):
        for (kind, events), count in zip(queues, counts):
            now = [events.pop(0) for _ in range(min(count, len(events)))]
            if now:

                @pl.when(kind)
                def _():
                    for i, p in now:
                        ffn.event(i, p)

    run(3, 0)

    for i in range(3, len(loads)):
        loads[i].wait()
    for k in range(1, X):
        pcopy(0, k).wait_recv()
    grad = pk[0].astype(F32)
    for k in range(1, X):
        grad += px[0, k - 1].astype(F32)
    hidden = hid[...]
    scale = lax.rsqrt(jnp.sum(hidden * hidden, axis=-1, keepdims=True) / np.float32(geo.D) + EPSILON)
    unit = hidden * scale
    gain_two = jnp.sum(grad * unit, axis=0, keepdims=True)
    pull = grad * gain[1:2, :]
    inner = jnp.sum(pull * unit, axis=-1, keepdims=True) / np.float32(geo.D)
    cot = XC[pl.ds(pl.multiple_of(L + me.s * T, 16), T), :].astype(F32)
    total = cot + scale * (pull - unit * inner)
    hgrad[...] = total
    hlow[...] = total.astype(BF)
    columns = jnp.concatenate([dot(hlow[...], WA[s]) for s in range(S)], axis=1).astype(BF)
    dM[...] = dot(columns, pout[...], NT).astype(BF)
    ds[...] = jnp.zeros_like(ds)
    gbias[...] = jnp.zeros_like(gbias)
    run(3, 1)

    def pair(t):
        lanes = pl.ds(pl.multiple_of(t * 128, 128), 128)
        vlanes = pl.ds(pl.multiple_of(I + t * 128, 128), 128)
        head = lax.broadcasted_iota(jnp.int32, (1, 128), 1) // hd
        keys, values, queries, back = KV[:, lanes], KV[:, vlanes], qkv[:, lanes], dM[:, lanes]
        zero = jnp.zeros_like(queries)
        q_grad = jnp.zeros((T, 128), F32)
        k_grad = jnp.zeros((L, 128), F32)
        v_grad = jnp.zeros((L, 128), F32)
        for e in range(per):
            h = t * per + e
            own_back = jnp.where(head == e, back, zero)
            pload(t, e).wait()
            probs = pst[e]
            prob_grad = dot(own_back, values, NT)
            both = jnp.sum(probs * prob_grad, axis=-1, keepdims=True)
            score = (probs * (prob_grad - both)).astype(BF)
            v_grad += dot(probs.astype(BF), own_back, TN)

            @pl.when(t + 1 < I // 128)
            def _():
                pload(t + 1, e).start()

            q_grad = jnp.where(head == e, dot(score, keys), q_grad)
            k_grad += dot(score, jnp.where(head == e, queries, zero), TN)
            ds[:, 128 : 128 + L] = score
            near = jnp.zeros((128, 384), F32)
            place = lax.broadcasted_iota(jnp.int32, (1, L), 1)
            low = jnp.zeros((1, 1), F32)
            high = jnp.zeros((1, 1), F32)
            for b in range(T // 128):
                row_block = me.s * (T // 128) + b
                near += ds[b * 128 : (b + 1) * 128, pl.ds(pl.multiple_of(row_block * 128, 128), 384)].astype(F32)
                sums = jnp.sum(score[b * 128 : (b + 1) * 128, :].astype(F32), axis=0, keepdims=True)
                low += jnp.sum(jnp.where(place < (row_block - 1) * 128, sums, 0.0), axis=-1, keepdims=True)
                high += jnp.sum(jnp.where(place >= (row_block + 2) * 128, sums, 0.0), axis=-1, keepdims=True)
            near = jnp.concatenate([jnp.zeros((128, 128), F32), near], axis=1)
            line = jnp.sum(shear(near, -1), axis=0, keepdims=True)
            spot = lax.broadcasted_iota(jnp.int32, (1, 512), 1)
            line += jnp.where(spot == 0, low, 0.0) + jnp.where(spot == 511, high, 0.0)
            gbias[pl.ds(h, 1), :] = line
        dq[:, lanes] = q_grad.astype(BF)
        dKV[:, lanes] = k_grad.astype(BF)
        dKV[:, vlanes] = v_grad.astype(BF)

    for t in range(I // 128):
        pair(t)
        run(*((1, 1), (1, 1), (2, 1))[min(t, 2)])
    key_scatter = SeqScatter(
        geo, me, lambda s: dKV.at[block(s, T), :], lambda k: kcb.at[k], lambda k: kxb.at[k - 1], kcs, kcr, kxs, kxr
    )
    key_scatter.to_core()

    for k in range(1, X):
        pcopy(1, k).wait_recv()
    total = hid[...] + pk[1].astype(F32)
    for k in range(1, X):
        total += px[1, k - 1].astype(F32)
    packed[...] = pack(geo, total)
    layer_out = pltpu.make_async_copy(packed, olayer, outs.at[0])
    layer_out.start()
    key_scatter.to_x()
    run(1, 1)
    tokens = xv[...].astype(F32)
    scale = lax.rsqrt(jnp.sum(tokens * tokens, axis=-1, keepdims=True) / np.float32(geo.D) + EPSILON)
    lefts[:T, :] = (tokens * scale * gain[0:1, :]).astype(BF)
    columns = dot(mixed[...], pout[...]).astype(BF)
    for i, right in enumerate(rights):
        right[T:, :] = columns[:, i * half : (i + 1) * half]
    run(2, 2)
    key_value = key_scatter.meet().astype(BF)
    run(0, 3)
    columns = jnp.zeros((T, S * I4), F32)
    for kind, value in enumerate((dq[...], key_value[:, :I], key_value[:, I:])):
        columns += pltpu.roll(dot(value, pout[...]), S * I4 - (3 - kind) * (I4 // 4), 1)
    columns = columns.astype(BF)
    for i, right in enumerate(rights):
        right[:T, :] = columns[:, i * half : (i + 1) * half]
    grad = jnp.zeros((T, N), F32)
    for s in range(S):
        grad += dot(columns[:, s * I4 : (s + 1) * I4], WA[s], NT)
    unit = tokens * scale
    gain_one = jnp.sum(grad * unit, axis=0, keepdims=True)
    pull = grad * gain[0:1, :]
    inner = jnp.sum(pull * unit, axis=-1, keepdims=True) / np.float32(geo.D)
    layer_out.wait()
    packed[...] = pack(geo, hgrad[...] + scale * (pull - unit * inner))
    input_out = pltpu.make_async_copy(packed, oinput, outs.at[1])
    input_out.start()

    table = dot(onehot[...], gbias[...].astype(BF), NT)
    if I4 > 128:
        table = jnp.concatenate([table, jnp.zeros((dp * 16, I4 - 128), F32)], axis=1)
    extra[...] = table
    for g in range(dp):
        for e, line in enumerate((gain_one, gain_two)):
            at = g * 16 + 16 - geo.E + e
            extra[at : at + 1, :R] = line[:, g * R : (g + 1) * R]

    def part_g(s, g):
        return XC.at[block(g, R), pl.ds(pl.multiple_of(s * I4, 128), I4)]

    att = DpScatter(
        geo, me, lambda p, g: part_g(me.s, g), lambda p, t: ayb.at[t], lambda p, i: azb.at[i],
        ays, ayr, azs, azr, lambda p, value: oa.__setitem__(..., value),
    )
    def turn(j):
        t = att.owner(j // 2)
        return t * 2 + jnp.where(j % 2 == 0, 1 - me.y, me.y)

    def scatter(g):
        return SeqScatter(
            geo, me, lambda s: part_g(s, g), lambda k: cb.at[k, block(g, R), :], lambda k: xb.at[k - 1, block(g, R), :],
            acs.at[g], acr.at[g], axs.at[g], axr.at[g],
        )

    def attention_rows(i):
        t = att.owner(i)
        lanes = pl.ds(pl.multiple_of(t * 2 * R, 128), 2 * R)
        rows = pl.ds(pl.multiple_of(t * 2 * R, 16), 2 * R)
        for n, right in enumerate(rights):
            XC[rows, n * half : (n + 1) * half] = dot(lefts[:, lanes], right[...], TN).astype(BF)
        for y in range(2):
            g = t * 2 + y
            rows = pl.ds(pl.multiple_of(g * R + R - 16, 16), 16)
            more = extra[pl.ds(pl.multiple_of(g * 16, 16), 16), :]
            for s in range(S):
                lane = slice(s * I4, (s + 1) * I4)
                XC[rows, lane] = (XC[rows, lane].astype(F32) + more).astype(BF)
        scatter(t * 2 + 1 - me.y).to_core()
        scatter(t * 2 + me.y).to_core()

    for i in range(A):
        attention_rows(i)
        run((2, 0, 2, 1)[min(i, 3)], (3, 1, 1, 1)[min(i, 3)])
    held = [p for p in range(last) if p >= NP // 2]
    for j in range(dp):
        scatter(turn(j)).to_x()
    run(0, 1)
    for j in range(dp):
        g = turn(j)
        part_g(me.s, g)[...] = scatter(g).meet().astype(BF)
        if j % 2 == 0:
            att.ysend(j // 2, 0)
        elif held:
            ffn.ysend(A - 1, held.pop(0))
        if j >= 2:
            run(1, 1)
        if j % 2 and j >= 3:
            att.event((j - 3) // 2, 0)
    while held:
        ffn.ysend(A - 1, held.pop(0))
    att.event(A - 1, 0)
    run(*(len(events) for _, events in queues))
    ffn.last(last)

    for n in range(2):
        for k in range(1, X):
            pcopy(n, k).wait_send()
    key_scatter.drain()
    loop(dp, lambda g: scatter(g).drain())
    att.drain(0)
    loop(last, ffn.drain)
    ffn.drain(last, True)
    input_out.wait()


def backward(geo, *saved):
    dma = pltpu.SemaphoreType.DMA
    S, N, F, T, L, I, X, I4, A, R = geo.seq, geo.N, geo.F, geo.T, geo.L, geo.I, geo.X, geo.I4, geo.A, geo.R
    per = 128 // (I // geo.H)
    consts = constants(geo)
    V = pltpu.VMEM
    scratch = [
        V((3, N, F), BF), V((2 * L, N), BF), V((3, L, F), BF), V((A, 3, R, F), BF), V((A + 1, 3, R, F), BF),
        V((S, N, I4), BF), V((A, R, I4), BF), V((A + 1, R, I4), BF),
        V((X, N, I4), BF), V((X - 1, N, I4), BF),
        V((T, N), BF), V((T, N), F32), V((T, 3 * I), BF), V((L, 2 * I), BF), V((T, I), BF),
        V((2, T, N), BF), V((2, X - 1, T, N), BF), V((per, T, L), F32),
        V((X, T, 2 * I), BF), V((X - 1, T, 2 * I), BF), V((A + 1, geo.RH, F), BF),
        V((T, N), F32), V((128, 512), F32), V((geo.dp * 16, I4), F32), V((8, N), F32), V((geo.D, T), BF),
        *[V(v.shape, v.dtype) for v in consts],
        dma((13,)), dma((per,)), dma((2,)),
        dma((2, X - 1)), dma((2, X - 1)), dma((X,)), dma((X,)), dma((X - 1,)), dma((X - 1,)),
        dma((geo.dp, X)), dma((geo.dp, X)), dma((geo.dp, X - 1)), dma((geo.dp, X - 1)),
        dma((A, geo.NP)), dma((A, geo.NP)), dma((A, geo.NP)), dma((A + 1, geo.NP)),
        dma((A, 1)), dma((A + 1, 1)),
        dma((A, 1)), dma((A, 1)), dma((A, 1)), dma((A + 1, 1)),
    ]
    return pl.pallas_call(
        functools.partial(backward_kernel, geo),
        out_shape=[
            jax.ShapeDtypeStruct((3, R, F), F32), jax.ShapeDtypeStruct((R, I4), F32),
            jax.ShapeDtypeStruct((geo.D, T), BF), jax.ShapeDtypeStruct((geo.D, T), BF),
        ],
        in_specs=[pl.BlockSpec(memory_space=pl.ANY)] * (len(saved) + len(consts)),
        out_specs=[pl.BlockSpec(memory_space=pltpu.VMEM)] * 2 + [pl.BlockSpec(memory_space=pl.ANY)] * 2,
        scratch_shapes=scratch,
        compiler_params=pltpu.CompilerParams(collective_id=2, has_side_effects=True, vmem_limit_bytes=63 << 20),
        name="backward",
    )(*saved, *consts)


def finish_kernel(geo, rows, features, layer, grad, olayer, ograd, oquery, okeyval, ooutput, ogateup, odown, ogain, obias, held, blocks, sem):
    W, own = geo.W, geo.I4 // 4
    moves = [
        (layer, held.at[0], olayer), (grad, held.at[1], ograd), (features.at[0], blocks.at[0], ogateup.at[0]),
        (features.at[1], blocks.at[1], ogateup.at[1]), (features.at[2], blocks.at[2], odown),
    ]
    arrive = [pltpu.make_async_copy(src, mid, sem.at[0, i]) for i, (src, mid, _) in enumerate(moves)]
    leave = [
        pltpu.make_async_copy(mid.at[:W, :] if i > 1 else mid, dst, sem.at[1, i]) for i, (_, mid, dst) in enumerate(moves)
    ]
    for copy in arrive:
        copy.start()
    for copy, onward in zip(arrive, leave):
        copy.wait()
        onward.start()
    main = rows[...]
    oquery[...] = main[:W, :own]
    okeyval[0] = main[:W, own : 2 * own]
    okeyval[1] = main[:W, 2 * own : 3 * own]
    ooutput[...] = main[:W, 3 * own :]
    ogain[...] = main[geo.R - geo.E : geo.R - geo.TR, :W]
    obias[...] = main[geo.R - geo.TR :, : geo.H]
    for copy in leave:
        copy.wait()


def finish(geo, of, oa, layer, grad):
    W, own, F = geo.W, geo.I4 // 4, geo.F
    shapes = [
        (layer.shape, BF), (grad.shape, BF), ((W, own), F32), ((2, W, own), F32), ((W, own), F32), ((2, W, F), F32),
        ((W, F), F32), ((2, W), F32), ((geo.TR, geo.H), F32),
    ]
    whole, here = pl.BlockSpec(memory_space=pl.ANY), pl.BlockSpec(memory_space=pltpu.VMEM)
    return pl.pallas_call(
        functools.partial(finish_kernel, geo),
        out_shape=[jax.ShapeDtypeStruct(*v) for v in shapes],
        in_specs=[here, whole, whole, whole],
        out_specs=[whole, whole, here, here, here, whole, whole, here, here],
        scratch_shapes=[
            pltpu.VMEM((2, *layer.shape), BF), pltpu.VMEM((3, geo.R, F), F32), pltpu.SemaphoreType.DMA((2, 5)),
        ],
        compiler_params=pltpu.CompilerParams(vmem_limit_bytes=63 << 20),
        name="finish",
    )(oa, of, layer, grad)


def spread_features(values, geo, width):
    lead = values.shape[:-1]
    blocks = values.reshape(*lead, geo.dp, width)
    return jnp.pad(blocks, [(0, 0)] * (len(lead) + 1) + [(0, geo.R - width)]).reshape(*lead, geo.dp * geo.R)


def pack_features(values, geo, width):
    lead = values.shape[:-1]
    return values.reshape(*lead, geo.dp, geo.R)[..., :width].reshape(*lead, geo.dp * width)


def general_path(
    axes, tokens, cotangent, lengths, w_query, w_key_value, w_output, w_gate_up, w_down, norm_gains, position_bias
):
    dp, seq = axes
    width, own_inner = w_query.shape
    table_rows, head_count = position_bias.shape
    geo = Geo(dp, seq, width, w_down.shape[1], 4 * own_inner, tokens.shape[1], head_count, table_rows)
    rows = geo.R
    model_width = geo.D
    bucket_count = table_rows * dp
    inner_width = geo.I
    head_dim = inner_width // head_count

    lanes = lambda v: jnp.pad(v, ((0, 0), (0, geo.I4 - v.shape[1])))
    wa = jnp.concatenate(
        [
            jnp.concatenate([w_query, w_key_value[0], w_key_value[1], w_output], axis=1).astype(BF),
            jnp.zeros((rows - width - geo.E, geo.I4), BF),
            lanes(norm_gains.astype(BF)),
            lanes(position_bias.astype(BF)),
        ],
        axis=0,
    )
    wf = jnp.pad(jnp.concatenate([w_gate_up, w_down[None]], axis=0).astype(BF), ((0, 0), (0, rows - width), (0, 0)))
    WF, WA = gather_weights(geo, wf, wa)

    blocks = WA[0].reshape(dp, rows, geo.I4)
    first_gain = blocks[:, rows - geo.E, :width].reshape(model_width).astype(F32)
    second_gain = blocks[:, rows - geo.E + 1, :width].reshape(model_width).astype(F32)
    table_full = blocks[:, rows - table_rows :, :head_count].reshape(bucket_count, head_count)
    real = WA.reshape(seq, dp, rows, 4, own_inner)[:, :, :width]
    parts = real.transpose(3, 1, 2, 0, 4).reshape(4, model_width, inner_width)
    query_full, keyval_full, output_full = parts[0], parts[1:3], parts[3]

    inputs = tokens[0].astype(jnp.float32)
    row_count = inputs.shape[0]
    normed = norm_scale(inputs, first_gain).astype(jnp.bfloat16)
    queries = jnp.dot(normed, query_full, preferred_element_type=jnp.float32).astype(jnp.bfloat16)
    projected = jnp.einsum(
        "td,sdi->sti", normed, keyval_full, preferred_element_type=jnp.float32
    ).astype(jnp.bfloat16)
    keys_all, values_all = (
        lax.all_gather(projected[0], "seq", axis=0, tiled=True),
        lax.all_gather(projected[1], "seq", axis=0, tiled=True),
    )
    incoming_low = cotangent[0]
    incoming = incoming_low.astype(jnp.float32)
    cot_all = lax.all_gather(spread_features(incoming_low, geo, width), "seq", axis=0, tiled=True)
    length_all = keys_all.shape[0]
    block_start = lax.axis_index("seq") * row_count
    query_pos = block_start + jnp.arange(row_count, dtype=jnp.int32)
    key_pos = jnp.arange(length_all, dtype=jnp.int32)
    buckets = bucket_ids(key_pos[None, :] - query_pos[:, None])
    bucket_range = jnp.arange(bucket_count, dtype=jnp.int32)
    onehot = (buckets[:, :, None] == bucket_range).astype(jnp.bfloat16)
    score_bias = jnp.einsum("tkb,bh->htk", onehot, table_full, preferred_element_type=jnp.float32)
    key_valid = key_pos < lengths[0]
    query_heads = queries.reshape(row_count, head_count, head_dim)
    key_heads = keys_all.reshape(length_all, head_count, head_dim)
    value_heads = values_all.reshape(length_all, head_count, head_dim)
    raw_scores = (
        jnp.einsum("thc,khc->htk", query_heads, key_heads, preferred_element_type=jnp.float32) + score_bias
    )
    scores = jnp.where(key_valid[None, None, :], raw_scores, NEGATIVE)
    probs = jax.nn.softmax(scores, axis=-1)
    probs_low = probs.astype(BF)
    mixed_heads = (
        jnp.einsum("htk,khc->thc", probs_low, value_heads, preferred_element_type=jnp.float32)
        .reshape(row_count, inner_width)
        .astype(jnp.bfloat16)
    )
    attended = jnp.einsum("tc,dc->td", mixed_heads, output_full, preferred_element_type=jnp.float32)
    hidden_one = inputs + attended
    normed_two = norm_scale(hidden_one, second_gain).astype(jnp.bfloat16)
    normed_two_all = lax.all_gather(spread_features(normed_two, geo, width), "seq", axis=0, tiled=True)

    gate = jnp.dot(normed_two_all, WF[0], preferred_element_type=F32)
    upward = jnp.dot(normed_two_all, WF[1], preferred_element_type=F32)
    activated = gated(gate, upward).astype(BF)
    down_term = jnp.einsum("tf,df->td", activated, WF[2], preferred_element_type=F32)
    down_weight_grad = jnp.einsum("td,tf->df", cot_all, activated, preferred_element_type=F32)
    activated_grad = jnp.dot(cot_all, WF[2], preferred_element_type=F32)
    unused_value, gate_pull = jax.vjp(gated, gate, upward)
    gate_grad, upward_grad = gate_pull(activated_grad)
    gate_grad, upward_grad = gate_grad.astype(BF), upward_grad.astype(BF)
    gate_weight_grad = jnp.einsum("td,tf->df", normed_two_all, gate_grad, preferred_element_type=F32)
    up_weight_grad = jnp.einsum("td,tf->df", normed_two_all, upward_grad, preferred_element_type=F32)
    normed_two_term = jnp.einsum("tf,df->td", gate_grad, WF[0], preferred_element_type=F32) + jnp.einsum(
        "tf,df->td", upward_grad, WF[1], preferred_element_type=F32
    )
    down_sum = lax.psum_scatter(down_term.astype(BF), "seq", scatter_dimension=0, tiled=True)
    normed_two_sum = lax.psum_scatter(normed_two_term.astype(BF), "seq", scatter_dimension=0, tiled=True)
    outputs = (hidden_one + pack_features(down_sum, geo, width).astype(F32)).astype(BF)[None]
    normed_two_grad = pack_features(normed_two_sum, geo, width).astype(F32)
    gf = jnp.stack([gate_weight_grad.astype(BF), up_weight_grad.astype(BF), down_weight_grad.astype(BF)])

    unused_two, second_pull = jax.vjp(norm_scale, hidden_one, second_gain)
    hidden_norm_grad, second_gain_grad = second_pull(normed_two_grad)
    hidden_grad = incoming + hidden_norm_grad
    hidden_low = hidden_grad.astype(jnp.bfloat16)
    output_weight_grad = jnp.einsum("td,tc->dc", hidden_low, mixed_heads, preferred_element_type=jnp.float32)
    mixed_grad = jnp.einsum("td,dc->tc", hidden_low, output_full, preferred_element_type=jnp.float32).astype(
        jnp.bfloat16
    )
    grad_heads = mixed_grad.reshape(row_count, head_count, head_dim)
    prob_grad = jnp.einsum("thc,khc->htk", grad_heads, value_heads, preferred_element_type=jnp.float32)
    inner_sum = jnp.sum(probs * prob_grad, axis=-1, keepdims=True)
    score_grad = (probs * (prob_grad - inner_sum)).astype(jnp.bfloat16)
    query_act_grad = (
        jnp.einsum("htk,khc->thc", score_grad, key_heads, preferred_element_type=jnp.float32)
        .reshape(row_count, inner_width)
        .astype(jnp.bfloat16)
    )
    key_piece = jnp.einsum(
        "htk,thc->khc", score_grad, query_heads, preferred_element_type=jnp.float32
    ).reshape(length_all, inner_width)
    value_piece = jnp.einsum(
        "htk,thc->khc", probs_low, grad_heads, preferred_element_type=jnp.float32
    ).reshape(length_all, inner_width)
    own_terms = lax.psum_scatter(
        jnp.concatenate([key_piece, value_piece], axis=1).astype(jnp.bfloat16),
        "seq",
        scatter_dimension=0,
        tiled=True,
    )
    keyval_act_grad = jnp.stack([own_terms[:, :inner_width], own_terms[:, inner_width:]])
    query_weight_grad = jnp.einsum("td,tc->dc", normed, query_act_grad, preferred_element_type=jnp.float32)
    keyval_weight_grad = jnp.einsum("td,stc->sdc", normed, keyval_act_grad, preferred_element_type=jnp.float32)
    normed_grad = jnp.einsum(
        "tc,dc->td", query_act_grad, query_full, preferred_element_type=jnp.float32
    ) + jnp.einsum("stc,sdc->td", keyval_act_grad, keyval_full, preferred_element_type=jnp.float32)
    unused_three, first_pull = jax.vjp(norm_scale, inputs, first_gain)
    input_norm_grad, first_gain_grad = first_pull(normed_grad)
    input_grad = (hidden_grad + input_norm_grad).astype(jnp.bfloat16)[None]
    table_grad = jnp.einsum("htk,tkb->bh", score_grad, onehot, preferred_element_type=jnp.float32)

    grads = jnp.stack(
        [query_weight_grad, keyval_weight_grad[0], keyval_weight_grad[1], output_weight_grad]
    ).reshape(4, dp, width, seq, own_inner)
    grads = grads.transpose(3, 1, 2, 0, 4).reshape(seq, dp, width, geo.I4).astype(BF)
    wide = lambda v: jnp.pad(v, ((0, 0), (0, 0), (0, geo.I4 - v.shape[2])))
    more = jnp.concatenate(
        [
            jnp.zeros((dp, rows - width - geo.E, geo.I4), F32),
            wide(first_gain_grad.reshape(dp, 1, width)),
            wide(second_gain_grad.reshape(dp, 1, width)),
            wide(table_grad.reshape(dp, table_rows, head_count)),
        ],
        axis=1,
    ).astype(BF)
    ga = jnp.concatenate([grads, jnp.broadcast_to(more, (seq, *more.shape))], axis=2).reshape(seq, dp * rows, geo.I4)
    of, oa = scatter_grads(geo, gf, ga)

    main = oa[:width]
    query_part = main[:, :own_inner]
    keyval_part = jnp.stack([main[:, own_inner : 2 * own_inner], main[:, 2 * own_inner : 3 * own_inner]])
    output_part = main[:, 3 * own_inner :]
    gain_part = oa[rows - geo.E : rows - table_rows, :width]
    table_part = oa[rows - table_rows :, :head_count]
    return (
        outputs,
        input_grad,
        query_part,
        keyval_part,
        output_part,
        of[:2, :width],
        of[2, :width],
        gain_part,
        table_part,
    )

def fused_path(
    axes, tokens, cotangent, lengths, w_query, w_key_value, w_output, w_gate_up, w_down, norm_gains, position_bias
):
    geo = Geo(*axes, w_query.shape[0], w_down.shape[1], 4 * w_query.shape[1], tokens.shape[1], *position_bias.shape[::-1])
    saved = forward(
        geo, lengths, tokens[0].T, cotangent[0].T, w_query, w_key_value, w_output, w_gate_up, w_down, norm_gains, position_bias
    )
    outs = finish(geo, *backward(geo, *saved))
    return outs[0].T[None], outs[1].T[None], *outs[2:]


def per_device(axes, *arrays):
    tokens, w_query, w_down, position_bias = arrays[0], arrays[3], arrays[7], arrays[9]
    geo = Geo(*axes, w_query.shape[0], w_down.shape[1], 4 * w_query.shape[1], tokens.shape[1], position_bias.shape[1],
              position_bias.shape[0])
    aligned = geo.W % 8 == 0 and geo.F % 128 == 0 and geo.I4 % 128 == 0 and 2 * geo.R % 128 == 0 and geo.T % 128 == 0 and geo.I % 128 == 0
    aligned = aligned and max(2 * geo.I, geo.seq * geo.I4 // 2) <= geo.F and 4 * geo.T <= geo.L and geo.N + 2 * geo.T <= 2 * geo.L and geo.L + 256 <= geo.N
    small = (3 * geo.F + geo.seq * geo.I4 + 2 * geo.L) * geo.N * 2 <= 24 << 20
    return (fused_path if aligned and small else general_path)(axes, *arrays)


def solution(mesh):
    in_specs = (
        P("dp", "seq", None),
        P("dp", "seq", None),
        P("dp"),
        P("dp", "seq"),
        P(None, "dp", "seq"),
        P("dp", "seq"),
        P(None, "dp", "seq"),
        P("dp", "seq"),
        P(None, "dp"),
        P("dp", None),
    )
    out_specs = (
        P("dp", "seq", None),
        P("dp", "seq", None),
        P("dp", "seq"),
        P(None, "dp", "seq"),
        P("dp", "seq"),
        P(None, "dp", "seq"),
        P("dp", "seq"),
        P(None, "dp"),
        P("dp", None),
    )
    return jax.shard_map(
        functools.partial(per_device, (mesh.shape["dp"], mesh.shape["seq"])), mesh=mesh, in_specs=in_specs, out_specs=out_specs, check_vma=False
    )
```

```python
import functools
import jax
import jax.numpy as jnp
import numpy as np
from jax import lax
from jax.experimental import pallas as pl
from jax.experimental.pallas import tpu as pltpu

from jax.sharding import PartitionSpec as P

MESH = pl.DeviceIdType.MESH
BF = jnp.bfloat16
F32 = jnp.float32


class Geo:
    def __init__(self, dp, seq, width, ff, inner4, tokens, heads, table_rows):
        self.dp, self.seq = dp, seq
        self.W, self.TR, self.E = width, table_rows, 2 + table_rows
        rows = -(-(width + self.E) // 16) * 16
        self.D, self.N, self.T, self.L = dp * width, dp * rows, tokens, seq * tokens
        self.I, self.H = inner4 // 4 * seq, heads
        self.B, self.A, self.X = 2, dp // 2, seq // 2
        self.R, self.F, self.I4 = rows, ff, inner4
        self.NH = 2 if rows % 32 == 0 else 1
        self.RH = rows // self.NH
        self.NP = 3 * self.NH
        self.NZ = 2 * (self.A - 1)
        self.NY = 2 * self.A - 1


class Place:
    def __init__(self, geo):
        d, s = lax.axis_index("dp"), lax.axis_index("seq")
        self.d, self.s = d, s
        self.z, self.y = d // 2, d % 2
        self.x, self.c = s // 2, s % 2

    def dev(self, z=None, y=None, x=None, c=None):
        z = self.z if z is None else z
        y = self.y if y is None else y
        x = self.x if x is None else x
        c = self.c if c is None else c
        return (z * 2 + y, x * 2 + c)


def remote(src, dst, ss, rs, dev):
    return pltpu.make_async_remote_copy(
        src_ref=src, dst_ref=dst, send_sem=ss, recv_sem=rs, device_id=dev, device_id_type=MESH
    )


def loop(n, body):
    def step(i, carry):
        body(i)
        return carry

    lax.fori_loop(0, n, step, 0)


def enter(geo, me):
    bar = pltpu.get_barrier_semaphore()

    def greet(dev):
        pl.semaphore_signal(bar, 1, device_id=dev, device_id_type=MESH)

    greet(me.dev(y=1 - me.y))
    greet(me.dev(c=1 - me.c))
    for k in range(1, geo.X):
        greet(me.dev(x=lax.rem(me.x + k, geo.X)))

    @pl.when(me.z > 0)
    def _():
        greet(me.dev(z=me.z - 1))

    @pl.when(me.z < geo.A - 1)
    def _():
        greet(me.dev(z=me.z + 1))

    count = 2 + (geo.X - 1) + (me.z > 0).astype(jnp.int32) + (me.z < geo.A - 1).astype(jnp.int32)
    pl.semaphore_wait(bar, count)


class LineGather:
    def __init__(self, geo, me, own, held, zs, zr, ys, yr, first_y=1 << 20, bzs=None, bzr=None):
        self.geo, self.me, self.own, self.held = geo, me, own, held
        self.zs, self.zr, self.ys, self.yr = zs, zr, ys, yr
        self.first_y, self.bzs, self.bzr = first_y, bzs, bzr

    def from_z(self, way, r):
        q = self.me.z - r if way == 0 else self.me.z + r
        return q, (q >= 0) if way == 0 else (q <= self.geo.A - 1)

    def sems(self, way, r, p, other):
        slot = way * (self.geo.A - 1) + r - 1
        if other:
            return self.bzs.at[slot, p - self.first_y], self.bzr.at[slot, p - self.first_y]
        return self.zs.at[slot, p], self.zr.at[slot, p]

    def zcopy(self, way, r, p, other=False):
        me, geo = self.me, self.geo
        q, there = self.from_z(way, r - 1)
        to = me.z + 1 if way == 0 else me.z - 1
        valid = ((me.z < geo.A - 1) if way == 0 else (me.z > 0)) & there
        here = self.held(p, q * 2 + (1 - me.y if other else me.y))
        src = self.own(p) if r == 1 and not other else here
        return remote(src, here, *self.sems(way, r, p, other), me.dev(z=to)), valid

    def zarrive(self, way, r, p, other=False):
        q, valid = self.from_z(way, r)
        here = self.held(p, q * 2 + (1 - self.me.y if other else self.me.y))
        return remote(here, here, *self.sems(way, r, p, other), self.me.dev(y=1 - self.me.y)), valid, q

    def yslot(self, way, r):
        return 1 + way * (self.geo.A - 1) + r - 1 if r else 0

    def ycopy(self, way, r, p):
        me, slot = self.me, self.yslot(way, r)
        q, _ = self.from_z(way, r)
        src = self.held(p, q * 2 + me.y) if r else self.own(p)
        return remote(src, self.held(p, q * 2 + me.y), self.ys.at[slot, p], self.yr.at[slot, p], me.dev(y=1 - me.y))

    def yarrive(self, way, r, p):
        me, slot = self.me, self.yslot(way, r)
        q, _ = self.from_z(way, r)
        here = self.held(p, q * 2 + 1 - me.y)
        return remote(here, here, self.ys.at[slot, p], self.yr.at[slot, p], me.dev(y=1 - me.y)), q

    def begin_y(self, p):
        self.ycopy(0, 0, p).start()

    def begin_z(self, p, other=False):
        for way in (0, 1):
            copy, valid = self.zcopy(way, 1, p, other)

            @pl.when(valid)
            def _():
                copy.start()

    def begin(self, p):
        self.begin_y(p)
        self.begin_z(p)

    def turn(self, p):
        self.yarrive(0, 0, p)[0].wait_recv()
        self.begin_z(p, True)

    def step(self, r, p, on_held=None, kinds=(False,), pass_y=True):
        for other in kinds:
            for way in (0, 1):
                copy, valid, q = self.zarrive(way, r, p, other)

                @pl.when(valid)
                def _():
                    copy.wait_recv()
                    if r < self.geo.A - 1:
                        onward, may = self.zcopy(way, r + 1, p, other)

                        @pl.when(may)
                        def _():
                            onward.start()

                    if pass_y:
                        self.ycopy(way, r, p).start()
                    if on_held is not None:
                        on_held(q * 2 + self.me.y)

    def step_both(self, r, p):
        self.step(r, p, None, (False, True), False)

    def ystep(self, r, p, on_held=None):
        for way in (0, 1) if r else (0,):
            copy, q = self.yarrive(way, r, p)

            def go():
                copy.wait_recv()
                if on_held is not None:
                    on_held(q * 2 + 1 - self.me.y)

            if r:
                pl.when(self.from_z(way, r)[1])(go)
            else:
                go()

    def drain(self, p, kinds=(False,), pass_y=True):
        self.ycopy(0, 0, p).wait_send()
        for r in range(1, self.geo.A):
            for way in (0, 1):
                for other in kinds:
                    copy, valid = self.zcopy(way, r, p, other)

                    @pl.when(valid)
                    def _():
                        copy.wait_send()

                if pass_y:

                    @pl.when(self.from_z(way, r)[1])
                    def _():
                        self.ycopy(way, r, p).wait_send()


class LineScatter:
    def __init__(self, geo, me, part, ybuf, zbuf, stage, zs, zr, ys, yr, finish):
        self.__dict__.update(locals())

    def turns(self):
        geo, me = self.geo, self.me
        for k in range(geo.A - 1):
            yield 0, k, geo.A - 1 - k, k < geo.A - 1 - me.z
            yield 1, k, k, k < me.z

    def slot(self, way, k):
        return way * (self.geo.A - 1) + k

    def ycopy(self, slot, t, p):
        me = self.me
        return remote(
            self.part(p, t * 2 + 1 - me.y),
            self.ybuf(p, t),
            self.ys.at[slot, p],
            self.yr.at[slot, p],
            me.dev(y=1 - me.y),
        )

    def zcopy(self, way, k, p):
        me = self.me
        to = me.z + 1 if way == 0 else me.z - 1
        slot = self.slot(way, k)
        return remote(
            self.stage(way, p, k), self.zbuf(way, p, k), self.zs.at[slot, p], self.zr.at[slot, p], me.dev(z=to)
        )

    def ysend(self, p, k):
        for way, kk, t, valid in self.turns():
            if kk == k:

                @pl.when(valid)
                def _():
                    self.ycopy(self.slot(way, kk), t, p).start()

    def ysend_own(self, p):
        self.ycopy(self.geo.NZ, self.me.z, p).start()

    def step(self, k, p):
        geo, me = self.geo, self.me
        for way, kk, t, valid in self.turns():
            if kk == k:

                @pl.when(valid)
                def _():
                    self.ycopy(self.slot(way, k), t, p).wait_recv()
                    total = self.part(p, t * 2 + me.y)[...].astype(F32) + self.ybuf(p, t)[...].astype(F32)
                    out = self.stage(way, p, k)
                    comes = me.z > 0 if way == 0 else me.z < geo.A - 1

                    @pl.when(comes)
                    def _():
                        self.zcopy(way, k, p).wait_recv()
                        out[...] = (total + self.zbuf(way, p, k)[...].astype(F32)).astype(BF)

                    @pl.when(jnp.logical_not(comes))
                    def _():
                        out[...] = total.astype(BF)

                    self.zcopy(way, k, p).start()

    def own(self, p):
        geo, me = self.geo, self.me
        self.ycopy(geo.NZ, me.z, p).wait_recv()
        total = self.part(p, me.z * 2 + me.y)[...].astype(F32) + self.ybuf(p, me.z)[...].astype(F32)
        kup = jnp.minimum(geo.A - 1 - me.z, geo.A - 2)
        kdown = jnp.minimum(me.z, geo.A - 2)

        def arrive(way, k):
            slot = way * (geo.A - 1) + k
            here = self.zbuf(way, p, k)
            remote(here, here, self.zs.at[slot, p], self.zr.at[slot, p], me.dev(y=1 - me.y)).wait_recv()
            return here[...].astype(F32)

        @pl.when(me.z == 0)
        def _():
            self.finish(p, total + arrive(1, kdown))

        @pl.when(me.z == geo.A - 1)
        def _():
            self.finish(p, total + arrive(0, kup))

        @pl.when((me.z > 0) & (me.z < geo.A - 1))
        def _():
            self.finish(p, total + arrive(0, kup) + arrive(1, kdown))

    def drain(self, p):
        for way, k, t, valid in self.turns():

            @pl.when(valid)
            def _():
                self.ycopy(self.slot(way, k), t, p).wait_send()
                self.zcopy(way, k, p).wait_send()

        self.ycopy(self.geo.NZ, self.me.z, p).wait_send()


NEGATIVE = -1e30
EPSILON = 1e-06
LIMITS = (12, 16, 23, 32, 46, 64, 91)


def bucket_ids(offsets):
    distance = jnp.abs(offsets)
    larger = 8 + sum(((distance >= threshold).astype(jnp.int32) for threshold in LIMITS))
    nearby = jnp.where(distance < 8, distance, larger)
    return jnp.where(offsets > 0, 16, 0) + nearby


def norm_scale(values, gain_vector):
    return (
        values
        * lax.rsqrt(jnp.mean(values * values, axis=-1, keepdims=True) + EPSILON)
        * gain_vector
    )


def gated(gate_value, upward):
    return jax.nn.gelu(gate_value, approximate=True) * upward


def gather_kernel(geo, wf, wa, WF, WA, local, zs, zr, ys, yr, azs, azr, ays, ayr, xs, xr, cs, cr):
    me = Place(geo)
    R, RH, NH, dp, X = geo.R, geo.RH, geo.NH, geo.dp, geo.X
    mine = [
        pltpu.make_async_copy(wf, WF.at[:, pl.ds(pl.multiple_of(me.d * R, 16), R), :], local.at[0]),
        pltpu.make_async_copy(wa, WA.at[me.s, pl.ds(pl.multiple_of(me.d * R, 16), R), :], local.at[1]),
    ]
    for copy in mine:
        copy.start()
    enter(geo, me)

    def own_f(p):
        return wf.at[p // NH, pl.ds(pl.multiple_of((p % NH) * RH, 16), RH), :]

    def held_f(p, g):
        return WF.at[p // NH, pl.ds(pl.multiple_of(g * R + (p % NH) * RH, 16), RH), :]

    def held_a(s, g):
        return WA.at[s, pl.ds(pl.multiple_of(g * R, 16), R), :]

    ffn = LineGather(geo, me, own_f, held_f, zs, zr, ys, yr)
    att = LineGather(geo, me, lambda p: wa, lambda p, g: held_a(me.s, g), azs, azr, ays, ayr)

    def xcopy(k, g, src):
        to = lax.rem(me.x + k, X)
        return remote(src, held_a(me.s, g), xs.at[k - 1, g], xr.at[k - 1, g], me.dev(x=to))

    def xarrive(k, g):
        src_x = lax.rem(me.x - k + X, X)
        here = held_a(src_x * 2 + me.c, g)
        return remote(here, here, xs.at[k - 1, g], xr.at[k - 1, g], me.dev(c=1 - me.c)), here

    def ccopy(k, g, src, s):
        return remote(src, held_a(s, g), cs.at[k, g], cr.at[k, g], me.dev(c=1 - me.c))

    def spread(g, src=None):
        src = held_a(me.s, g) if src is None else src
        for k in range(1, X):
            xcopy(k, g, src).start()
        ccopy(0, g, src, me.s).start()

    att.begin(0)
    spread(me.d, wa)
    loop(geo.NP, ffn.begin)
    att.ystep(0, 0, spread)
    for r in range(1, geo.A):
        att.step(r, 0, spread)
        att.ystep(r, 0, spread)

    def from_x(g):
        for k in range(1, X):
            copy, here = xarrive(k, g)
            copy.wait_recv()
            ccopy(k, g, here, lax.rem(me.x - k + X, X) * 2 + me.c).start()

    loop(dp, from_x)
    for r in range(1, geo.A):
        loop(geo.NP, lambda p: ffn.step(r, p))
    for r in range(geo.A):
        loop(geo.NP, lambda p: ffn.ystep(r, p))

    def finish(g):
        for k in range(X):
            s = lax.rem(me.x - k + X, X) * 2 + 1 - me.c
            here = held_a(s, g)
            remote(here, here, cs.at[k, g], cr.at[k, g], me.dev(c=1 - me.c)).wait_recv()
            ccopy(k, g, here, s).wait_send()
            if k:
                xcopy(k, g, here).wait_send()

    loop(dp, finish)
    att.drain(0)
    loop(geo.NP, ffn.drain)
    for copy in mine:
        copy.wait()


def scatter_kernel(
    geo, gf, ga, of, oa, yb, zb, st, cb, xb, xst, pa, ayb, azb, ast,
    zs, zr, ys, yr, azs, azr, ays, ayr, xs, xr, cs, cr,
):
    me = Place(geo)
    R, RH, NH, dp, X, A = geo.R, geo.RH, geo.NH, geo.dp, geo.X, geo.A
    enter(geo, me)

    def rows(g, p):
        return pl.ds(pl.multiple_of(g * R + (p % NH) * RH, 16), RH)

    def piece(buf, i, p):
        return buf.at[i, p // NH, pl.ds(pl.multiple_of((p % NH) * RH, 16), RH), :]

    def finish_f(p, value):
        of[p // NH, pl.ds(pl.multiple_of((p % NH) * RH, 16), RH), :] = value

    ffn = LineScatter(
        geo, me,
        lambda p, g: gf.at[p // NH, rows(g, p), :],
        lambda p, t: piece(yb, t, p),
        lambda way, p, k: piece(zb, way * (A - 1) + k, p),
        lambda way, p, k: piece(st, way * (A - 1) + k, p),
        zs, zr, ys, yr, finish_f,
    )

    def block(g):
        return pl.ds(pl.multiple_of(g * R, 16), R)

    def finish_a(p, value):
        oa[...] = value

    att = LineScatter(
        geo, me,
        lambda p, g: pa.at[block(g), :],
        lambda p, t: ayb.at[t],
        lambda way, p, k: azb.at[way * (A - 1) + k],
        lambda way, p, k: ast.at[way * (A - 1) + k],
        azs, azr, ays, ayr, finish_a,
    )

    def ccopy(k, g):
        to_x = lax.rem(me.x + k, X)
        return remote(
            ga.at[to_x * 2 + 1 - me.c, block(g), :], cb.at[k, block(g), :], cs.at[k, g], cr.at[k, g], me.dev(c=1 - me.c)
        )

    def xcopy(k, g):
        return remote(
            xst.at[k - 1, block(g), :], xb.at[k - 1, block(g), :], xs.at[k - 1, g], xr.at[k - 1, g],
            me.dev(x=lax.rem(me.x + k, X)),
        )

    def to_core(g):
        for k in (*range(1, X), 0):
            ccopy(k, g).start()

    def to_x(g):
        for k in range(1, X):
            ccopy(k, g).wait_recv()
            s = lax.rem(me.x + k, X) * 2 + me.c
            xst[k - 1, block(g), :] = (
                ga[s, block(g), :].astype(F32) + cb[k, block(g), :].astype(F32)
            ).astype(BF)
            xcopy(k, g).start()

    def meet(g):
        ccopy(0, g).wait_recv()
        total = ga[me.s, block(g), :].astype(F32) + cb[0, block(g), :].astype(F32)
        for k in range(1, X):
            xcopy(k, g).wait_recv()
            total += xb[k - 1, block(g), :].astype(F32)
        pa[block(g), :] = total.astype(BF)

    def free(g):
        for k in range(X):
            ccopy(k, g).wait_send()
            if k:
                xcopy(k, g).wait_send()

    for k in range(A - 1):
        loop(geo.NP, lambda p: ffn.ysend(p, k))
    loop(geo.NP, ffn.ysend_own)
    loop(dp, to_core)
    loop(dp, to_x)
    for k in range(A - 1):
        loop(geo.NP, lambda p: ffn.step(k, p))
    loop(geo.NP, ffn.own)
    loop(dp, meet)
    for k in range(A - 1):
        att.ysend(0, k)
    att.ysend_own(0)
    for k in range(A - 1):
        att.step(k, 0)
    att.own(0)
    loop(dp, free)
    att.drain(0)
    loop(geo.NP, ffn.drain)


def gather_weights(geo, wf, wa):
    dma = pltpu.SemaphoreType.DMA
    sems = [
        dma((2,)),
        dma((geo.NZ, geo.NP)), dma((geo.NZ, geo.NP)), dma((geo.NY, geo.NP)), dma((geo.NY, geo.NP)),
        dma((geo.NZ, 1)), dma((geo.NZ, 1)), dma((geo.NY, 1)), dma((geo.NY, 1)),
        dma((geo.X - 1, geo.dp)), dma((geo.X - 1, geo.dp)), dma((geo.X, geo.dp)), dma((geo.X, geo.dp)),
    ]
    return pl.pallas_call(
        functools.partial(gather_kernel, geo),
        out_shape=(
            jax.ShapeDtypeStruct((3, geo.dp * geo.R, geo.F), BF),
            jax.ShapeDtypeStruct((geo.seq, geo.dp * geo.R, geo.I4), BF),
        ),
        in_specs=[pl.BlockSpec(memory_space=pl.ANY)] * 2,
        out_specs=[pl.BlockSpec(memory_space=pl.ANY)] * 2,
        scratch_shapes=sems,
        compiler_params=pltpu.CompilerParams(collective_id=0, has_side_effects=True, vmem_limit_bytes=48 << 20),
        name="gather_weights",
    )(wf, wa)


def scatter_grads(geo, gf, ga):
    dma = pltpu.SemaphoreType.DMA
    n, X, A, R = geo.dp * geo.R, geo.X, geo.A, geo.R
    scratch = [
        pltpu.VMEM((A, 3, R, geo.F), BF), pltpu.VMEM((geo.NZ, 3, R, geo.F), BF), pltpu.VMEM((geo.NZ, 3, R, geo.F), BF),
        pltpu.VMEM((X, n, geo.I4), BF), pltpu.VMEM((X - 1, n, geo.I4), BF), pltpu.VMEM((X - 1, n, geo.I4), BF),
        pltpu.VMEM((n, geo.I4), BF),
        pltpu.VMEM((A, R, geo.I4), BF), pltpu.VMEM((geo.NZ, R, geo.I4), BF), pltpu.VMEM((geo.NZ, R, geo.I4), BF),
        dma((geo.NZ, geo.NP)), dma((geo.NZ, geo.NP)), dma((geo.NZ + 1, geo.NP)), dma((geo.NZ + 1, geo.NP)),
        dma((geo.NZ, 1)), dma((geo.NZ, 1)), dma((geo.NZ + 1, 1)), dma((geo.NZ + 1, 1)),
        dma((X - 1, geo.dp)), dma((X - 1, geo.dp)), dma((X, geo.dp)), dma((X, geo.dp)),
    ]
    return pl.pallas_call(
        functools.partial(scatter_kernel, geo),
        out_shape=(
            jax.ShapeDtypeStruct((3, R, geo.F), F32),
            jax.ShapeDtypeStruct((R, geo.I4), F32),
        ),
        in_specs=[pl.BlockSpec(memory_space=pltpu.VMEM)] * 2,
        out_specs=[pl.BlockSpec(memory_space=pltpu.VMEM)] * 2,
        scratch_shapes=scratch,
        compiler_params=pltpu.CompilerParams(collective_id=1, has_side_effects=True, vmem_limit_bytes=60 << 20),
        name="scatter_grads",
    )(gf, ga)


class SeqGather:
    def __init__(self, geo, me, held, xs, xr, cs, cr):
        self.geo, self.me, self.held = geo, me, held
        self.xs, self.xr, self.cs, self.cr = xs, xr, cs, cr

    def ccopy(self, k):
        me, X = self.me, self.geo.X
        here = self.held(lax.rem(me.x - k + X, X) * 2 + me.c)
        return remote(here, here, self.cs.at[k], self.cr.at[k], me.dev(c=1 - me.c))

    def xcopy(self, k):
        me = self.me
        here = self.held(me.s)
        return remote(here, here, self.xs.at[k - 1], self.xr.at[k - 1], me.dev(x=lax.rem(me.x + k, self.geo.X)))

    def begin(self):
        for k in range(1, self.geo.X):
            self.xcopy(k).start()
        self.ccopy(0).start()

    def relay(self):
        for k in range(1, self.geo.X):
            self.xcopy(k).wait_recv()
            self.ccopy(k).start()

    def finish(self):
        for k in range(self.geo.X):
            self.ccopy(k).wait_recv()
            self.ccopy(k).wait_send()
            if k:
                self.xcopy(k).wait_send()


def dot(a, b, dims=((1,), (0,))):
    return lax.dot_general(a, b, (dims, ((), ())), preferred_element_type=F32)


NT = ((1,), (1,))
TN = ((0,), (0,))


def constants(geo):
    own, I4, S, I = geo.I4 // 4, geo.I4, geo.seq, geo.I
    perm_out = np.zeros((I, S * I4), np.float32)
    i = np.arange(own)
    for s in range(S):
        perm_out[s * own + i, s * I4 + 3 * own + i] = 1
    offset = np.arange(512) - 256
    distance = np.abs(offset)
    larger = 8 + sum((distance >= limit).astype(np.int32) for limit in LIMITS)
    bucket = np.where(offset > 0, 16, 0) + np.where(distance < 8, distance, larger)
    onehot = np.zeros((geo.dp * 16, 512), np.float32)
    for b in range(geo.dp * geo.TR):
        onehot[b // geo.TR * 16 + 16 - geo.E + 2 + b % geo.TR] = bucket == b
    return [jnp.asarray(v, BF) for v in (perm_out, onehot)]


def spread(geo, value):
    value = value.astype(F32)
    gap = jnp.zeros((geo.R - geo.W, value.shape[1]), F32)
    parts = [v for g in range(geo.dp) for v in (value[g * geo.W : (g + 1) * geo.W], gap)]
    return jnp.concatenate(parts, axis=0).T.astype(BF)


def pack(geo, value):
    value = value.T
    return jnp.concatenate([value[g * geo.R : g * geo.R + geo.W] for g in range(geo.dp)], axis=0).astype(BF)


def shear(value, sign):
    rows, lanes = value.shape
    row = lax.broadcasted_iota(jnp.int32, (rows, 1), 0)
    bit = 1
    while bit < rows:
        moved = pltpu.roll(value, bit if sign > 0 else lanes - bit, 1)
        value = jnp.where((row & bit) != 0, moved, value)
        bit *= 2
    return value


def gelu_parts(g):
    k0 = np.float32(np.sqrt(2 / np.pi))
    t = jnp.tanh(k0 * (g + np.float32(0.044715) * (g * g * g)))
    half = 0.5 * (1.0 + t)
    slope = half + 0.5 * g * (1.0 - t * t) * (k0 * (1.0 + np.float32(3 * 0.044715) * (g * g)))
    return g * half, slope


def forward_kernel(
    geo, length, x_in, c_in, wq, wkv, wo, wgu, wd, norm_gains, position_bias, cpo, conehot,
    oX, oWA, oqkv, oKV, oP, omixed, ohid, oX2, oC, oact, opart, ogain,
    WF0, WF1, WA, xv, C, X2, KV, qkv, strip, mixed, hid, pst, act, part, got, gain, raw, wst, ast, gst, bst, ex, pout, onehot,
    local, outs, psem, zs, zr, ys, yr, bzs, bzr, azs, azr, ays, ayr, xs, xr, cs, cr, gxs, gxr, gcs, gcr, ps, pr,
):
    me = Place(geo)
    R, RH, NH, dp, X, T, N, I = geo.R, geo.RH, geo.NH, geo.dp, geo.X, geo.T, geo.N, geo.I
    I4, S, L = geo.I4, geo.seq, geo.L
    block = lambda i, n: pl.ds(pl.multiple_of(i * n, 16), n)
    loads = [
        (wq, ast.at[0]), (wkv.at[0], ast.at[1]), (wkv.at[1], ast.at[2]), (wo, ast.at[3]), (norm_gains, gst),
        (position_bias, bst), (wgu.at[0], wst.at[0]), (wgu.at[1], wst.at[1]), (wd, wst.at[2]), (x_in, raw.at[0]),
        (c_in, raw.at[1]), (cpo, pout), (conehot, onehot),
    ]
    loads = [pltpu.make_async_copy(src, dst, local.at[i]) for i, (src, dst) in enumerate(loads)]
    for copy in loads:
        copy.start()
    W, E = geo.W, geo.E
    ex[...] = jnp.zeros_like(ex)
    for copy in loads[:6]:
        copy.wait()
    ex[R - W - E : R - W - E + 2, :W] = gst[...]
    ex[R - W - E + 2 :, : geo.H] = bst[...]
    columns = jnp.concatenate([ast[k] for k in range(4)], axis=1)
    WA[me.s, block(me.d, R), :] = jnp.concatenate([columns, ex[...]], axis=0).astype(BF)
    enter(geo, me)

    WFs = (WF0, WF1)
    cuts = ((0, WF0.shape[2]), (WF0.shape[2], geo.F))

    def held_f(p, g):
        return WFs[p // 3].at[p % 3, block(g, R), :]

    def held_a(s, g):
        return WA.at[s, block(g, R), :]

    special = 2
    others = [p for p in range(6) if p != special]
    ffn = LineGather(geo, me, lambda p: held_f(p, me.d), held_f, zs, zr, ys, yr, special, bzs, bzr)
    att = LineGather(geo, me, lambda p: held_a(me.s, me.d), lambda p, g: held_a(me.s, g), azs, azr, ays, ayr)

    def xcopy(k, g, src):
        to = lax.rem(me.x + k, X)
        return remote(src, held_a(me.s, g), xs.at[k - 1, g], xr.at[k - 1, g], me.dev(x=to))

    def xarrive(k, g):
        src_x = lax.rem(me.x - k + X, X)
        here = held_a(src_x * 2 + me.c, g)
        return remote(here, here, xs.at[k - 1, g], xr.at[k - 1, g], me.dev(c=1 - me.c)), here

    def ccopy(k, g, src, s):
        return remote(src, held_a(s, g), cs.at[k, g], cr.at[k, g], me.dev(c=1 - me.c))

    def share(g):
        src = held_a(me.s, g)
        for k in range(1, X):
            xcopy(k, g, src).start()
        ccopy(0, g, src, me.s).start()

    half = T // 2

    def seq_gather(i, ref, first, count):
        held = lambda s: ref.at[pl.ds(pl.multiple_of(s * T + first, 16), count), :]
        return SeqGather(geo, me, held, gxs.at[i], gxr.at[i], gcs.at[i], gcr.at[i])

    gather_kv = seq_gather(0, KV, 0, T)
    gather_x2 = [seq_gather(1, X2, 0, half), seq_gather(2, X2, half, half)]
    gather_c = [seq_gather(3, C, 0, half), seq_gather(4, C, half, half)]

    att.begin(0)
    share(me.d)
    for m in range(3):
        loads[6 + m].wait()
        for ref, cut in zip(WFs, cuts):
            lanes = slice(*cut)
            own = jnp.concatenate([wst[m, :, lanes], jnp.zeros((R - W, cut[1] - cut[0]), F32)], axis=0)
            ref[m, block(me.d, R), :] = own.astype(BF)
    ffn.begin_y(special)
    for p in range(6):
        if p == special:
            ffn.begin_z(p)
        else:
            ffn.begin(p)
    events = [(r, p) for r in range(1, geo.A) for p in range(6)]

    def forward_on(r, p):
        if p == special:
            ffn.step_both(r, p)
        else:
            ffn.step(r, p)

    def run(count):
        for _ in range(min(count, len(events))):
            forward_on(*events.pop(0))

    att.ystep(0, 0, share)
    for r in range(1, geo.A):
        att.step(r, 0, share)
        att.ystep(r, 0, share)
    ffn.turn(special)
    for copy in loads[9:]:
        copy.wait()
    xv[...] = spread(geo, raw[0])
    C[block(me.s, T), :] = spread(geo, raw[1])
    gather_c[0].begin()

    def from_x(g):
        for k in range(1, X):
            copy, here = xarrive(k, g)
            copy.wait_recv()
            ccopy(k, g, here, lax.rem(me.x - k + X, X) * 2 + me.c).start()

    for g in range(dp):
        from_x(g)
        if g >= 3:
            run(1)

    def settle(g):
        for k in range(X):
            s = lax.rem(me.x - k + X, X) * 2 + 1 - me.c
            here = held_a(s, g)
            remote(here, here, cs.at[k, g], cr.at[k, g], me.dev(c=1 - me.c)).wait_recv()

    loop(dp, settle)

    extra = jnp.concatenate([WA[0, g * R + R - 16 : g * R + R, :] for g in range(dp)], axis=0)
    lines = extra.astype(F32)
    gain[...] = jnp.zeros_like(gain)
    for g in range(dp):
        for e in range(2):
            at = g * 16 + 16 - E + e
            gain[e : e + 1, g * R : (g + 1) * R] = lines[at : at + 1, :R]
    bias = dot(extra[:, :128], onehot[...], TN)

    inputs = xv[...].astype(F32)
    scale = lax.rsqrt(jnp.sum(inputs * inputs, axis=-1, keepdims=True) / np.float32(geo.D) + EPSILON)
    normed = (inputs * scale * gain[0:1, :]).astype(BF)
    columns = jnp.concatenate([dot(normed, WA[s]) for s in range(S)], axis=1)
    for kind in (1, 2, 0):
        moved = pltpu.roll(columns, (3 - kind) * (I4 // 4), 1).astype(BF)
        qkv[:, kind * I : (kind + 1) * I] = dot(moved, pout[...], NT).astype(BF)
        if kind == 2:
            KV[block(me.s, T), :] = qkv[:, I:]
            gather_kv.begin()
            gather_c[1].begin()
    gather_c[0].relay()
    run(1)
    writes = []

    def write(src, dst):
        copy = pltpu.make_async_copy(src, dst, outs.at[len(writes)])
        copy.start()
        writes.append(copy)

    write(xv, oX)
    write(WA, oWA)
    write(qkv, oqkv)
    write(gain, ogain)
    NB = L // 128
    for h in range(geo.H):
        band = shear(jnp.broadcast_to(bias[h : h + 1, :], (128, 512)), 1)[:, 128:512].astype(BF)
        strip[h, :, (NB - 2) * 128 : (NB + 1) * 128] = band
        far = (NB - 2) * 128
        strip[h, :, :far] = jnp.broadcast_to(bias[h : h + 1, 0:1], (128, far)).astype(BF)
        strip[h, :, (NB + 1) * 128 :] = jnp.broadcast_to(bias[h : h + 1, 511:512], (128, far)).astype(BF)
    run(1)
    gather_kv.relay()
    gather_kv.finish()
    run(1)
    write(KV, oKV)

    hd = I // geo.H
    per = 128 // hd
    valid = lax.broadcasted_iota(jnp.int32, (1, L), 1) < length[0]

    def pair(t, first):
        rows = slice(first, first + half)
        lanes = pl.ds(pl.multiple_of(t * 128, 128), 128)
        head = lax.broadcasted_iota(jnp.int32, (1, 128), 1) // hd
        keys = KV[:, lanes]
        values = KV[:, pl.ds(pl.multiple_of(I + t * 128, 128), 128)]
        queries = qkv[rows, lanes]
        outs_ = jnp.zeros((half, 128), F32)
        for e in range(per):
            h = t * per + e
            scores = dot(jnp.where(head == e, queries, jnp.zeros_like(queries)), keys, NT)
            shift = [
                strip[h, :, pl.ds(pl.multiple_of((NB - 1 - me.s * (T // 128) - b) * 128, 128), L)].astype(F32)
                for b in range(first // 128, (first + half) // 128)
            ]
            scores = jnp.where(valid, scores + jnp.concatenate(shift, axis=0), np.float32(NEGATIVE))
            top = jnp.max(scores, axis=-1, keepdims=True)
            probs = jnp.exp(scores - top)
            probs = probs * (1.0 / jnp.sum(probs, axis=-1, keepdims=True))
            copy = pltpu.make_async_copy(pst.at[e], oP.at[h, rows, :], psem.at[e])

            @pl.when((t > 0) | (first > 0))
            def _():
                copy.wait()

            pst[e] = probs
            copy.start()
            mine = dot(probs.astype(BF), values)
            outs_ = jnp.where(head == e, mine, outs_)
        mixed[rows, lanes] = outs_.astype(BF)

    for first in (0, half):
        rows = slice(first, first + half)
        for t in range(I // 128):
            pair(t, first)
            if t < 2:
                run(1)
        spread_mixed = dot(mixed[rows, :], pout[...]).astype(BF)
        total = xv[rows, :].astype(F32)
        for s in range(S):
            total += dot(spread_mixed[:, s * I4 : (s + 1) * I4], WA[s], NT)
        hid[rows, :] = total
        scale = lax.rsqrt(jnp.sum(total * total, axis=-1, keepdims=True) / np.float32(geo.D) + EPSILON)
        X2[pl.ds(pl.multiple_of(me.s * T + first, 16), half), :] = (total * scale * gain[1:2, :]).astype(BF)
        gather_x2[first // half].begin()
        run(1)
        if first == 0:
            gather_c[1].relay()
    for e in range(per):
        pltpu.make_async_copy(pst.at[e], oP.at[e, half:, :], psem.at[e]).wait()
    write(mixed, omixed)
    write(hid, ohid)
    for part_c in gather_c:
        part_c.finish()
    write(C, oC)
    gather_x2[0].relay()
    run(len(events) - 3)
    gather_x2[1].relay()
    for part_x2 in gather_x2:
        part_x2.finish()
    write(X2, oX2)

    def pcopy(n, k):
        return remote(part.at[0, n, k], got.at[n, k], ps.at[n, k], pr.at[n, k], me.dev(c=1 - me.c))

    def tokens_block(i, group):
        k = X - 1 - i // 2
        e = i % 2
        s = lax.rem(me.x + k, X) * 2 + lax.rem(1 + e + me.c, 2)
        rows = block(s, T)
        lanes = slice(*cuts[group])
        gate_w, up_w, down_w = (WFs[group].at[m] for m in range(3))
        xb = X2[rows, :]
        gate = dot(xb, gate_w[...])
        upward = dot(xb, up_w[...])
        back = dot(C[rows, :], down_w[...])
        value, slope = gelu_parts(gate)
        activated = (value * upward).astype(BF)
        first = (back * upward * slope).astype(BF)
        second = (back * value).astype(BF)
        act[0, rows, lanes] = first
        act[1, rows, lanes] = second
        act[2, rows, lanes] = activated
        terms = dot(first, gate_w[...], NT) + dot(second, up_w[...], NT), dot(activated, down_w[...], NT)
        for n, term in enumerate(terms):
            if group:
                term += part[e, n, k].astype(F32)
            part[e, n, k] = term.astype(BF)
        if group:

            @pl.when(e == 0)
            def _():
                pcopy(0, k).start()
                pcopy(1, k).start()

    for group in range(2):
        for r in range(geo.A):
            for p in others:
                if p // 3 == group:
                    ffn.ystep(r, p)

        def with_events(i):
            tokens_block(i, group)
            for n, event in enumerate(() if group else [events.pop(0) for _ in range(len(events))]):

                @pl.when(i == n)
                def _():
                    forward_on(*event)

        loop(2 * X, with_events)
        write(act.at[:, :, slice(*cuts[group])], oact.at[:, :, slice(*cuts[group])])
    for k in range(X - 1, -1, -1):
        for n in range(2):
            pcopy(n, k).wait_recv()
            part[1, n, k] = (part[1, n, k].astype(F32) + got[n, k].astype(F32)).astype(BF)
    write(part.at[1], opart)
    for k in range(X):
        for n in range(2):
            pcopy(n, k).wait_send()

    def finish(g):
        for k in range(X):
            s = lax.rem(me.x - k + X, X) * 2 + 1 - me.c
            here = held_a(s, g)
            ccopy(k, g, here, s).wait_send()
            if k:
                xcopy(k, g, here).wait_send()

    loop(dp, finish)
    att.drain(0)
    for p in others:
        ffn.drain(p)
    ffn.drain(special, (False, True), False)
    for copy in writes:
        copy.wait()


def forward(geo, *arrays):
    dma = pltpu.SemaphoreType.DMA
    S, N, F, T, L, I, H, X, I4 = geo.seq, geo.N, geo.F, geo.T, geo.L, geo.I, geo.H, geo.X, geo.I4
    per = 128 // (I // H)
    first = (F // 128 + 1) // 2 * 128
    consts = constants(geo)
    out_shape = [
        ((T, N), BF), ((S, N, I4), BF), ((T, 3 * I), BF), ((L, 2 * I), BF), ((H, T, L), F32), ((T, I), BF),
        ((T, N), F32), ((L, N), BF), ((L, N), BF), ((3, L, F), BF), ((2, X, T, N), BF), ((8, N), F32),
    ]
    V = pltpu.VMEM
    scratch = [
        V((3, N, first), BF), V((3, N, F - first), BF), V((S, N, I4), BF), V((T, N), BF), V((L, N), BF), V((L, N), BF), V((L, 2 * I), BF),
        V((T, 3 * I), BF), V((H, 128, 2 * L - 128), BF), V((T, I), BF), V((T, N), F32),
        V((per, T // 2, L), F32), V((3, L, F), BF), V((2, 2, X, T, N), BF), V((2, X, T, N), BF), V((8, N), F32),
        V((2, geo.D, T), BF), V((3, geo.W, F), F32), V((4, geo.W, I4 // 4), F32), V((2, geo.W), F32), V((geo.TR, H), F32),
        V((geo.R - geo.W, I4), F32),
        *[V(v.shape, v.dtype) for v in consts],
        dma((13,)), dma((13,)), dma((per,)),
        dma((geo.NZ, 6)), dma((geo.NZ, 6)), dma((geo.NY, 6)), dma((geo.NY, 6)),
        dma((geo.NZ, 1)), dma((geo.NZ, 1)),
        dma((geo.NZ, 1)), dma((geo.NZ, 1)), dma((geo.NY, 1)), dma((geo.NY, 1)),
        dma((X - 1, geo.dp)), dma((X - 1, geo.dp)), dma((X, geo.dp)), dma((X, geo.dp)),
        dma((5, X - 1)), dma((5, X - 1)), dma((5, X)), dma((5, X)),
        dma((2, X)), dma((2, X)),
    ]
    return pl.pallas_call(
        functools.partial(forward_kernel, geo),
        out_shape=[jax.ShapeDtypeStruct(*v) for v in out_shape],
        in_specs=[pl.BlockSpec(memory_space=pltpu.SMEM)] + [pl.BlockSpec(memory_space=pl.ANY)] * (len(arrays) - 1 + len(consts)),
        out_specs=[pl.BlockSpec(memory_space=pl.ANY)] * len(out_shape),
        scratch_shapes=scratch,
        compiler_params=pltpu.CompilerParams(collective_id=0, has_side_effects=True, vmem_limit_bytes=63 << 20),
        name="forward",
    )(*arrays, *consts)


class SeqScatter:
    def __init__(self, geo, me, part, cb, xb, cs, cr, xs, xr):
        self.__dict__.update(locals())

    def ccopy(self, k):
        me = self.me
        to = lax.rem(me.x + k, self.geo.X)
        return remote(self.part(to * 2 + 1 - me.c), self.cb(k), self.cs.at[k], self.cr.at[k], me.dev(c=1 - me.c))

    def xcopy(self, k):
        me = self.me
        to = lax.rem(me.x + k, self.geo.X)
        return remote(self.part(to * 2 + me.c), self.xb(k), self.xs.at[k - 1], self.xr.at[k - 1], me.dev(x=to))

    def to_core(self):
        for k in (*range(1, self.geo.X), 0):
            self.ccopy(k).start()

    def to_x(self):
        for k in range(1, self.geo.X):
            self.ccopy(k).wait_recv()
            out = self.part(lax.rem(self.me.x + k, self.geo.X) * 2 + self.me.c)
            out[...] = (out[...].astype(F32) + self.cb(k)[...].astype(F32)).astype(BF)
            self.xcopy(k).start()

    def meet(self):
        self.ccopy(0).wait_recv()
        total = self.part(self.me.s)[...].astype(F32) + self.cb(0)[...].astype(F32)
        for k in range(1, self.geo.X):
            self.xcopy(k).wait_recv()
            total += self.xb(k)[...].astype(F32)
        return total

    def drain(self):
        for k in range(self.geo.X):
            self.ccopy(k).wait_send()
            if k:
                self.xcopy(k).wait_send()


class DpScatter:
    def __init__(self, geo, me, part, ybuf, zbuf, ys, yr, zs, zr, finish, first_z=1 << 20, zbuf2=None, zs2=None, zr2=None):
        self.__dict__.update(locals())

    def owner(self, i):
        A, z = self.geo.A, self.me.z
        up, down = A - 1 - z, z
        both = jnp.minimum(up, down)
        half = i // 2
        early = jnp.where((i % 2 == 0) == (up >= down), A - 1 - half, half)
        late = jnp.where(up > down, A - 1 - (i - both), i - both)
        return jnp.where(i == A - 1, z, jnp.where(i < 2 * both, early, late))

    def ycopy(self, t, p):
        me = self.me
        return remote(
            self.part(p, t * 2 + 1 - me.y), self.ybuf(p, t), self.ys.at[t, p], self.yr.at[t, p], me.dev(y=1 - me.y)
        )

    def zparts(self, t, slot, p, other):
        if other:
            return self.zbuf2(p, slot), self.zs2.at[t, p - self.first_z], self.zr2.at[slot, p - self.first_z]
        return self.zbuf(p, slot), self.zs.at[t, p], self.zr.at[slot, p]

    def mine(self, t, p, other=False):
        return self.part(p, t * 2 + (1 - self.me.y if other else self.me.y))

    def zslot(self, up, t):
        return jnp.where(up, self.geo.A - 1 - t, self.geo.A - t)

    def zcopy(self, t, p, other=False):
        me = self.me
        up = t > me.z
        dst, ss, rs = self.zparts(t, self.zslot(up, t), p, other)
        return remote(self.mine(t, p, other), dst, ss, rs, me.dev(z=jnp.where(up, me.z + 1, me.z - 1)))

    def zarrive(self, up, t, p, other=False):
        here, ss, rs = self.zparts(t, self.zslot(up, t), p, other)
        remote(here, here, ss, rs, self.me.dev(y=1 - self.me.y)).wait_recv()
        return here[...].astype(F32)

    def ysend(self, i, p):
        self.ycopy(self.owner(i), p).start()

    def arrived(self, t, p, base, put, other=False):
        geo, me = self.geo, self.me

        @pl.when(me.z == 0)
        def _():
            put(base() + self.zarrive(False, t, p, other))

        @pl.when(me.z == geo.A - 1)
        def _():
            put(base() + self.zarrive(True, t, p, other))

        @pl.when((me.z > 0) & (me.z < geo.A - 1))
        def _():
            put(base() + self.zarrive(True, t, p, other) + self.zarrive(False, t, p, other))

    def onward(self, t, p, base, other=False, plain=False):
        geo, me = self.geo, self.me
        mine = self.mine(t, p, other)
        up = t > me.z
        comes = (up & (me.z > 0)) | (jnp.logical_not(up) & (me.z < geo.A - 1))

        @pl.when(comes)
        def _():
            mine[...] = (base() + self.zarrive(up, t, p, other)).astype(BF)

        if not plain:

            @pl.when(jnp.logical_not(comes))
            def _():
                mine[...] = base().astype(BF)

        self.zcopy(t, p, other).start()

    def event(self, i, p):
        t = self.owner(i)
        mine = self.mine(t, p)
        own = lambda: mine[...].astype(F32)
        if p >= self.first_z:
            theirs = self.mine(t, p, True)
            their = lambda: theirs[...].astype(F32)
            if i < self.geo.A - 1:
                self.onward(t, p, their, True, True)
                self.onward(t, p, own, False, True)
            else:
                self.arrived(t, p, their, lambda v: theirs.__setitem__(..., v.astype(BF)), True)
                self.ycopy(t, p).start()
            return
        self.ycopy(t, p).wait_recv()
        both = lambda: own() + self.ybuf(p, t)[...].astype(F32)
        if i == self.geo.A - 1:
            self.arrived(t, p, both, lambda v: self.finish(p, v))
        else:
            self.onward(t, p, both)

    def last(self, p):
        t = self.me.z
        mine = self.mine(t, p)
        self.ycopy(t, p).wait_recv()
        both = lambda: mine[...].astype(F32) + self.ybuf(p, t)[...].astype(F32)
        self.arrived(t, p, both, lambda v: self.finish(p, v))

    def drain(self, p, second=False):
        for i in range(self.geo.A):
            t = self.owner(i)
            if not second or i == self.geo.A - 1:
                self.ycopy(t, p).wait_send()
            if i < self.geo.A - 1:
                for other in (False, True) if second else (False,):
                    self.zcopy(t, p, other).wait_send()


def backward_kernel(
    geo, x_in, iWA, iqkv, iKV, iP, imixed, ihid, iX2, iC, iact, ipart, igain, cpo, conehot,
    of, oa, olayer, oinput,
    G, XC, act, yb, zb, WA, ayb, azb, cb, xb, xv, hid, qkv, KV, mixed, pk, px, pst, kcb, kxb, zb2,
    hgrad, gbias, extra, gain, packed, pout, onehot,
    local, psem, outs, pxs, pxr, kcs, kcr, kxs, kxr, acs, acr, axs, axr, ys, yr, zs, zr, zs2, zr2, ays, ayr, azs, azr,
):
    me = Place(geo)
    R, RH, NH, dp, X, T, N, I = geo.R, geo.RH, geo.NH, geo.dp, geo.X, geo.T, geo.N, geo.I
    I4, S, L, A, NP = geo.I4, geo.seq, geo.L, geo.A, geo.NP
    block = lambda i, n: pl.ds(pl.multiple_of(i * n, 16), n)
    dKV = act.at[0, :, : 2 * I]
    dM, dq = act.at[1, :T, :I], act.at[1, T : 2 * T, :I]
    half = S * I4 // 2
    rights = [act.at[2, : 2 * T, :half], act.at[2, 2 * T : 4 * T, :half]]
    lefts = XC.at[N : N + 2 * T, :]
    hlow = lefts.at[T:, :]
    ds = pk.at[0, :, : L + 256]
    loads = [
        (iact.at[2], act.at[2]), (iC, XC.at[L:, :]), (iact.at[0], act.at[0]), (iX2, XC.at[:L, :]), (iact.at[1], act.at[1]), (ipart.at[:, 0], pk), (ihid, hid), (igain, gain),
        (iWA, WA), (cpo, pout), (iKV, KV), (iqkv, qkv), (imixed, mixed), (x_in, xv), (conehot, onehot),
    ]
    loads = [pltpu.make_async_copy(src, dst, local.at[i]) for i, (src, dst) in enumerate(loads)]
    for copy in loads:
        copy.start()
    hd = I // geo.H
    per = 128 // hd

    def pload(t, e):
        return pltpu.make_async_copy(iP.at[t * per + e], pst.at[e], psem.at[e])

    for e in range(per):
        pload(0, e).start()
    enter(geo, me)

    def pcopy(n, k):
        to = me.dev(x=lax.rem(me.x + k, X))
        return remote(ipart.at[n, k], px.at[n, k - 1], pxs.at[n, k - 1], pxr.at[n, k - 1], to)

    for n in range(2):
        for k in range(1, X):
            pcopy(n, k).start()

    def rows_of(g, p):
        return pl.ds(pl.multiple_of(g * R + (p % NH) * RH, 16), RH)

    def piece(buf, i, p):
        return buf.at[i, p // NH, pl.ds(pl.multiple_of((p % NH) * RH, 16), RH), :]

    def finish_f(p, value):
        of[p // NH, pl.ds(pl.multiple_of((p % NH) * RH, 16), RH), :] = value

    last = NP - 1
    ffn = DpScatter(
        geo, me, lambda p, g: G.at[p // NH, rows_of(g, p), :], lambda p, t: piece(yb, t, p),
        lambda p, i: piece(zb, i, p), ys, yr, zs, zr, finish_f,
        last, lambda p, i: zb2.at[i], zs2, zr2,
    )
    def weight_rows(i):
        t = ffn.owner(i)
        lanes = pl.ds(pl.multiple_of(t * 2 * R, 128), 2 * R)
        rows = pl.ds(pl.multiple_of(t * 2 * R, 16), 2 * R)
        for m in (2, 0, 1):
            if isinstance(i, int):
                for copy in loads[slice(*{2: (0, 2), 0: (2, 4), 1: (4, 5)}[m])]:
                    copy.wait()
            left = XC[:L, lanes] if m < 2 else XC[L:, lanes]
            G[m, rows, :] = dot(left, act[m], TN).astype(BF)

            def go(h):
                p = m * NH + h

                @pl.when((p < last) & ((i < A - 1) | (p < NP // 2)))
                def _():
                    ffn.ysend(i, p)

            loop(NH, go)


    edge = (me.z == 0) | (me.z == A - 1)
    queues = [(kind, [(i, p) for i in range(A) for p in (last, *range(last))]) for kind in (edge, jnp.logical_not(edge))]

    def run(*counts):
        for (kind, events), count in zip(queues, counts):
            now = [events.pop(0) for _ in range(min(count, len(events)))]
            if now:

                @pl.when(kind)
                def _():
                    for i, p in now:
                        ffn.event(i, p)

    weight_rows(0)
    run(1, 0)
    loop(A - 1, lambda i: weight_rows(i + 1))
    run(2, 0)

    for i in range(5, len(loads)):
        loads[i].wait()
    for k in range(1, X):
        pcopy(0, k).wait_recv()
    grad = pk[0].astype(F32)
    for k in range(1, X):
        grad += px[0, k - 1].astype(F32)
    hidden = hid[...]
    scale = lax.rsqrt(jnp.sum(hidden * hidden, axis=-1, keepdims=True) / np.float32(geo.D) + EPSILON)
    unit = hidden * scale
    gain_two = jnp.sum(grad * unit, axis=0, keepdims=True)
    pull = grad * gain[1:2, :]
    inner = jnp.sum(pull * unit, axis=-1, keepdims=True) / np.float32(geo.D)
    cot = XC[pl.ds(pl.multiple_of(L + me.s * T, 16), T), :].astype(F32)
    total = cot + scale * (pull - unit * inner)
    hgrad[...] = total
    hlow[...] = total.astype(BF)
    columns = jnp.concatenate([dot(hlow[...], WA[s]) for s in range(S)], axis=1).astype(BF)
    dM[...] = dot(columns, pout[...], NT).astype(BF)
    ds[...] = jnp.zeros_like(ds)
    gbias[...] = jnp.zeros_like(gbias)
    run(3, 1)

    def pair(t):
        lanes = pl.ds(pl.multiple_of(t * 128, 128), 128)
        vlanes = pl.ds(pl.multiple_of(I + t * 128, 128), 128)
        head = lax.broadcasted_iota(jnp.int32, (1, 128), 1) // hd
        keys, values, queries, back = KV[:, lanes], KV[:, vlanes], qkv[:, lanes], dM[:, lanes]
        zero = jnp.zeros_like(queries)
        q_grad = jnp.zeros((T, 128), F32)
        k_grad = jnp.zeros((L, 128), F32)
        v_grad = jnp.zeros((L, 128), F32)
        for e in range(per):
            h = t * per + e
            own_back = jnp.where(head == e, back, zero)
            pload(t, e).wait()
            probs = pst[e]
            prob_grad = dot(own_back, values, NT)
            both = jnp.sum(probs * prob_grad, axis=-1, keepdims=True)
            score = (probs * (prob_grad - both)).astype(BF)
            v_grad += dot(probs.astype(BF), own_back, TN)

            @pl.when(t + 1 < I // 128)
            def _():
                pload(t + 1, e).start()

            q_grad = jnp.where(head == e, dot(score, keys), q_grad)
            k_grad += dot(score, jnp.where(head == e, queries, zero), TN)
            ds[:, 128 : 128 + L] = score
            near = jnp.zeros((128, 384), F32)
            place = lax.broadcasted_iota(jnp.int32, (1, L), 1)
            low = jnp.zeros((1, 1), F32)
            high = jnp.zeros((1, 1), F32)
            for b in range(T // 128):
                row_block = me.s * (T // 128) + b
                near += ds[b * 128 : (b + 1) * 128, pl.ds(pl.multiple_of(row_block * 128, 128), 384)].astype(F32)
                sums = jnp.sum(score[b * 128 : (b + 1) * 128, :].astype(F32), axis=0, keepdims=True)
                low += jnp.sum(jnp.where(place < (row_block - 1) * 128, sums, 0.0), axis=-1, keepdims=True)
                high += jnp.sum(jnp.where(place >= (row_block + 2) * 128, sums, 0.0), axis=-1, keepdims=True)
            near = jnp.concatenate([jnp.zeros((128, 128), F32), near], axis=1)
            line = jnp.sum(shear(near, -1), axis=0, keepdims=True)
            spot = lax.broadcasted_iota(jnp.int32, (1, 512), 1)
            line += jnp.where(spot == 0, low, 0.0) + jnp.where(spot == 511, high, 0.0)
            gbias[pl.ds(h, 1), :] = line
        dq[:, lanes] = q_grad.astype(BF)
        dKV[:, lanes] = k_grad.astype(BF)
        dKV[:, vlanes] = v_grad.astype(BF)

    def key_scatter(i):
        lanes = slice(i * 128, (i + 1) * 128)
        return SeqScatter(
            geo, me, lambda s: dKV.at[block(s, T), lanes], lambda k: kcb.at[k, :, lanes], lambda k: kxb.at[k - 1, :, lanes],
            kcs.at[i], kcr.at[i], kxs.at[i], kxr.at[i],
        )

    pairs = I // 128
    scatters = [(key_scatter(t), key_scatter(pairs + t)) for t in range(pairs)]
    for t in range(pairs):
        pair(t)
        for one in scatters[t]:
            one.to_core()
        if t:
            for one in scatters[t - 1]:
                one.to_x()
        run(*((1, 1), (1, 1), (2, 1))[min(t, 2)])

    for k in range(1, X):
        pcopy(1, k).wait_recv()
    total = hid[...] + pk[1].astype(F32)
    for k in range(1, X):
        total += px[1, k - 1].astype(F32)
    packed[...] = pack(geo, total)
    layer_out = pltpu.make_async_copy(packed, olayer, outs.at[0])
    layer_out.start()
    for one in scatters[-1]:
        one.to_x()
    run(1, 1)
    tokens = xv[...].astype(F32)
    scale = lax.rsqrt(jnp.sum(tokens * tokens, axis=-1, keepdims=True) / np.float32(geo.D) + EPSILON)
    lefts[:T, :] = (tokens * scale * gain[0:1, :]).astype(BF)
    columns = dot(mixed[...], pout[...]).astype(BF)
    for i, right in enumerate(rights):
        right[T:, :] = columns[:, i * half : (i + 1) * half]
    run(2, 2)
    key_value = [jnp.concatenate([one[n].meet() for one in scatters], axis=1).astype(BF) for n in range(2)]
    run(0, 3)
    columns = jnp.zeros((T, S * I4), F32)
    for kind, value in enumerate((dq[...], *key_value)):
        columns += pltpu.roll(dot(value, pout[...]), S * I4 - (3 - kind) * (I4 // 4), 1)
    columns = columns.astype(BF)
    for i, right in enumerate(rights):
        right[:T, :] = columns[:, i * half : (i + 1) * half]
    grad = jnp.zeros((T, N), F32)
    for s in range(S):
        grad += dot(columns[:, s * I4 : (s + 1) * I4], WA[s], NT)
    unit = tokens * scale
    gain_one = jnp.sum(grad * unit, axis=0, keepdims=True)
    pull = grad * gain[0:1, :]
    inner = jnp.sum(pull * unit, axis=-1, keepdims=True) / np.float32(geo.D)
    layer_out.wait()
    packed[...] = pack(geo, hgrad[...] + scale * (pull - unit * inner))
    input_out = pltpu.make_async_copy(packed, oinput, outs.at[1])
    input_out.start()

    table = dot(onehot[...], gbias[...].astype(BF), NT)
    if I4 > 128:
        table = jnp.concatenate([table, jnp.zeros((dp * 16, I4 - 128), F32)], axis=1)
    extra[...] = table
    for g in range(dp):
        for e, line in enumerate((gain_one, gain_two)):
            at = g * 16 + 16 - geo.E + e
            extra[at : at + 1, :R] = line[:, g * R : (g + 1) * R]

    def part_g(s, g):
        return XC.at[block(g, R), pl.ds(pl.multiple_of(s * I4, 128), I4)]

    att = DpScatter(
        geo, me, lambda p, g: part_g(me.s, g), lambda p, t: ayb.at[t], lambda p, i: azb.at[i],
        ays, ayr, azs, azr, lambda p, value: oa.__setitem__(..., value),
    )
    def turn(j):
        t = att.owner(j // 2)
        return t * 2 + jnp.where(j % 2 == 0, 1 - me.y, me.y)

    def scatter(g):
        return SeqScatter(
            geo, me, lambda s: part_g(s, g), lambda k: cb.at[k, block(g, R), :], lambda k: xb.at[k - 1, block(g, R), :],
            acs.at[g], acr.at[g], axs.at[g], axr.at[g],
        )

    def attention_rows(i):
        t = att.owner(i)
        lanes = pl.ds(pl.multiple_of(t * 2 * R, 128), 2 * R)
        rows = pl.ds(pl.multiple_of(t * 2 * R, 16), 2 * R)
        for n, right in enumerate(rights):
            XC[rows, n * half : (n + 1) * half] = dot(lefts[:, lanes], right[...], TN).astype(BF)
        for y in range(2):
            g = t * 2 + y
            rows = pl.ds(pl.multiple_of(g * R + R - 16, 16), 16)
            more = extra[pl.ds(pl.multiple_of(g * 16, 16), 16), :]
            for s in range(S):
                lane = slice(s * I4, (s + 1) * I4)
                XC[rows, lane] = (XC[rows, lane].astype(F32) + more).astype(BF)
        scatter(t * 2 + 1 - me.y).to_core()
        scatter(t * 2 + me.y).to_core()

    for i in range(A):
        attention_rows(i)
        run((2, 0, 2, 1)[min(i, 3)], (3, 1, 1, 1)[min(i, 3)])
    held = [p for p in range(last) if p >= NP // 2]
    for j in range(dp):
        scatter(turn(j)).to_x()
    run(0, 1)
    for j in range(dp):
        g = turn(j)
        part_g(me.s, g)[...] = scatter(g).meet().astype(BF)
        if j % 2 == 0:
            att.ysend(j // 2, 0)
        elif held:
            ffn.ysend(A - 1, held.pop(0))
        if j >= 2:
            run(1, 1)
        if j % 2 and j >= 3:
            att.event((j - 3) // 2, 0)
    while held:
        ffn.ysend(A - 1, held.pop(0))
    att.event(A - 1, 0)
    run(*(len(events) for _, events in queues))
    ffn.last(last)

    for n in range(2):
        for k in range(1, X):
            pcopy(n, k).wait_send()
    for both in scatters:
        for one in both:
            one.drain()
    loop(dp, lambda g: scatter(g).drain())
    att.drain(0)
    loop(last, ffn.drain)
    ffn.drain(last, True)
    input_out.wait()


def backward(geo, *saved):
    dma = pltpu.SemaphoreType.DMA
    S, N, F, T, L, I, X, I4, A, R = geo.seq, geo.N, geo.F, geo.T, geo.L, geo.I, geo.X, geo.I4, geo.A, geo.R
    per = 128 // (I // geo.H)
    consts = constants(geo)
    V = pltpu.VMEM
    scratch = [
        V((3, N, F), BF), V((2 * L, N), BF), V((3, L, F), BF), V((A, 3, R, F), BF), V((A + 1, 3, R, F), BF),
        V((S, N, I4), BF), V((A, R, I4), BF), V((A + 1, R, I4), BF),
        V((X, N, I4), BF), V((X - 1, N, I4), BF),
        V((T, N), BF), V((T, N), F32), V((T, 3 * I), BF), V((L, 2 * I), BF), V((T, I), BF),
        V((2, T, N), BF), V((2, X - 1, T, N), BF), V((per, T, L), F32),
        V((X, T, 2 * I), BF), V((X - 1, T, 2 * I), BF), V((A + 1, geo.RH, F), BF),
        V((T, N), F32), V((128, 512), F32), V((geo.dp * 16, I4), F32), V((8, N), F32), V((geo.D, T), BF),
        *[V(v.shape, v.dtype) for v in consts],
        dma((15,)), dma((per,)), dma((2,)),
        dma((2, X - 1)), dma((2, X - 1)), dma((2 * I // 128, X)), dma((2 * I // 128, X)), dma((2 * I // 128, X - 1)), dma((2 * I // 128, X - 1)),
        dma((geo.dp, X)), dma((geo.dp, X)), dma((geo.dp, X - 1)), dma((geo.dp, X - 1)),
        dma((A, geo.NP)), dma((A, geo.NP)), dma((A, geo.NP)), dma((A + 1, geo.NP)),
        dma((A, 1)), dma((A + 1, 1)),
        dma((A, 1)), dma((A, 1)), dma((A, 1)), dma((A + 1, 1)),
    ]
    return pl.pallas_call(
        functools.partial(backward_kernel, geo),
        out_shape=[
            jax.ShapeDtypeStruct((3, R, F), F32), jax.ShapeDtypeStruct((R, I4), F32),
            jax.ShapeDtypeStruct((geo.D, T), BF), jax.ShapeDtypeStruct((geo.D, T), BF),
        ],
        in_specs=[pl.BlockSpec(memory_space=pl.ANY)] * (len(saved) + len(consts)),
        out_specs=[pl.BlockSpec(memory_space=pltpu.VMEM)] * 2 + [pl.BlockSpec(memory_space=pl.ANY)] * 2,
        scratch_shapes=scratch,
        compiler_params=pltpu.CompilerParams(collective_id=2, has_side_effects=True, vmem_limit_bytes=63 << 20),
        name="backward",
    )(*saved, *consts)


def finish_kernel(geo, rows, features, layer, grad, olayer, ograd, oquery, okeyval, ooutput, ogateup, odown, ogain, obias, held, blocks, sem):
    W, own = geo.W, geo.I4 // 4
    moves = [
        (layer, held.at[0], olayer), (grad, held.at[1], ograd), (features.at[0], blocks.at[0], ogateup.at[0]),
        (features.at[1], blocks.at[1], ogateup.at[1]), (features.at[2], blocks.at[2], odown),
    ]
    arrive = [pltpu.make_async_copy(src, mid, sem.at[0, i]) for i, (src, mid, _) in enumerate(moves)]
    leave = [
        pltpu.make_async_copy(mid.at[:W, :] if i > 1 else mid, dst, sem.at[1, i]) for i, (_, mid, dst) in enumerate(moves)
    ]
    for copy in arrive:
        copy.start()
    for copy, onward in zip(arrive, leave):
        copy.wait()
        onward.start()
    main = rows[...]
    oquery[...] = main[:W, :own]
    okeyval[0] = main[:W, own : 2 * own]
    okeyval[1] = main[:W, 2 * own : 3 * own]
    ooutput[...] = main[:W, 3 * own :]
    ogain[...] = main[geo.R - geo.E : geo.R - geo.TR, :W]
    obias[...] = main[geo.R - geo.TR :, : geo.H]
    for copy in leave:
        copy.wait()


def finish(geo, of, oa, layer, grad):
    W, own, F = geo.W, geo.I4 // 4, geo.F
    shapes = [
        (layer.shape, BF), (grad.shape, BF), ((W, own), F32), ((2, W, own), F32), ((W, own), F32), ((2, W, F), F32),
        ((W, F), F32), ((2, W), F32), ((geo.TR, geo.H), F32),
    ]
    whole, here = pl.BlockSpec(memory_space=pl.ANY), pl.BlockSpec(memory_space=pltpu.VMEM)
    return pl.pallas_call(
        functools.partial(finish_kernel, geo),
        out_shape=[jax.ShapeDtypeStruct(*v) for v in shapes],
        in_specs=[here, whole, whole, whole],
        out_specs=[whole, whole, here, here, here, whole, whole, here, here],
        scratch_shapes=[
            pltpu.VMEM((2, *layer.shape), BF), pltpu.VMEM((3, geo.R, F), F32), pltpu.SemaphoreType.DMA((2, 5)),
        ],
        compiler_params=pltpu.CompilerParams(vmem_limit_bytes=63 << 20),
        name="finish",
    )(oa, of, layer, grad)


def spread_features(values, geo, width):
    lead = values.shape[:-1]
    blocks = values.reshape(*lead, geo.dp, width)
    return jnp.pad(blocks, [(0, 0)] * (len(lead) + 1) + [(0, geo.R - width)]).reshape(*lead, geo.dp * geo.R)


def pack_features(values, geo, width):
    lead = values.shape[:-1]
    return values.reshape(*lead, geo.dp, geo.R)[..., :width].reshape(*lead, geo.dp * width)


def general_path(
    axes, tokens, cotangent, lengths, w_query, w_key_value, w_output, w_gate_up, w_down, norm_gains, position_bias
):
    dp, seq = axes
    width, own_inner = w_query.shape
    table_rows, head_count = position_bias.shape
    geo = Geo(dp, seq, width, w_down.shape[1], 4 * own_inner, tokens.shape[1], head_count, table_rows)
    rows = geo.R
    model_width = geo.D
    bucket_count = table_rows * dp
    inner_width = geo.I
    head_dim = inner_width // head_count

    lanes = lambda v: jnp.pad(v, ((0, 0), (0, geo.I4 - v.shape[1])))
    wa = jnp.concatenate(
        [
            jnp.concatenate([w_query, w_key_value[0], w_key_value[1], w_output], axis=1).astype(BF),
            jnp.zeros((rows - width - geo.E, geo.I4), BF),
            lanes(norm_gains.astype(BF)),
            lanes(position_bias.astype(BF)),
        ],
        axis=0,
    )
    wf = jnp.pad(jnp.concatenate([w_gate_up, w_down[None]], axis=0).astype(BF), ((0, 0), (0, rows - width), (0, 0)))
    WF, WA = gather_weights(geo, wf, wa)

    blocks = WA[0].reshape(dp, rows, geo.I4)
    first_gain = blocks[:, rows - geo.E, :width].reshape(model_width).astype(F32)
    second_gain = blocks[:, rows - geo.E + 1, :width].reshape(model_width).astype(F32)
    table_full = blocks[:, rows - table_rows :, :head_count].reshape(bucket_count, head_count)
    real = WA.reshape(seq, dp, rows, 4, own_inner)[:, :, :width]
    parts = real.transpose(3, 1, 2, 0, 4).reshape(4, model_width, inner_width)
    query_full, keyval_full, output_full = parts[0], parts[1:3], parts[3]

    inputs = tokens[0].astype(jnp.float32)
    row_count = inputs.shape[0]
    normed = norm_scale(inputs, first_gain).astype(jnp.bfloat16)
    queries = jnp.dot(normed, query_full, preferred_element_type=jnp.float32).astype(jnp.bfloat16)
    projected = jnp.einsum(
        "td,sdi->sti", normed, keyval_full, preferred_element_type=jnp.float32
    ).astype(jnp.bfloat16)
    keys_all, values_all = (
        lax.all_gather(projected[0], "seq", axis=0, tiled=True),
        lax.all_gather(projected[1], "seq", axis=0, tiled=True),
    )
    incoming_low = cotangent[0]
    incoming = incoming_low.astype(jnp.float32)
    cot_all = lax.all_gather(spread_features(incoming_low, geo, width), "seq", axis=0, tiled=True)
    length_all = keys_all.shape[0]
    block_start = lax.axis_index("seq") * row_count
    query_pos = block_start + jnp.arange(row_count, dtype=jnp.int32)
    key_pos = jnp.arange(length_all, dtype=jnp.int32)
    buckets = bucket_ids(key_pos[None, :] - query_pos[:, None])
    bucket_range = jnp.arange(bucket_count, dtype=jnp.int32)
    onehot = (buckets[:, :, None] == bucket_range).astype(jnp.bfloat16)
    score_bias = jnp.einsum("tkb,bh->htk", onehot, table_full, preferred_element_type=jnp.float32)
    key_valid = key_pos < lengths[0]
    query_heads = queries.reshape(row_count, head_count, head_dim)
    key_heads = keys_all.reshape(length_all, head_count, head_dim)
    value_heads = values_all.reshape(length_all, head_count, head_dim)
    raw_scores = (
        jnp.einsum("thc,khc->htk", query_heads, key_heads, preferred_element_type=jnp.float32) + score_bias
    )
    scores = jnp.where(key_valid[None, None, :], raw_scores, NEGATIVE)
    probs = jax.nn.softmax(scores, axis=-1)
    probs_low = probs.astype(BF)
    mixed_heads = (
        jnp.einsum("htk,khc->thc", probs_low, value_heads, preferred_element_type=jnp.float32)
        .reshape(row_count, inner_width)
        .astype(jnp.bfloat16)
    )
    attended = jnp.einsum("tc,dc->td", mixed_heads, output_full, preferred_element_type=jnp.float32)
    hidden_one = inputs + attended
    normed_two = norm_scale(hidden_one, second_gain).astype(jnp.bfloat16)
    normed_two_all = lax.all_gather(spread_features(normed_two, geo, width), "seq", axis=0, tiled=True)

    gate = jnp.dot(normed_two_all, WF[0], preferred_element_type=F32)
    upward = jnp.dot(normed_two_all, WF[1], preferred_element_type=F32)
    activated = gated(gate, upward).astype(BF)
    down_term = jnp.einsum("tf,df->td", activated, WF[2], preferred_element_type=F32)
    down_weight_grad = jnp.einsum("td,tf->df", cot_all, activated, preferred_element_type=F32)
    activated_grad = jnp.dot(cot_all, WF[2], preferred_element_type=F32)
    unused_value, gate_pull = jax.vjp(gated, gate, upward)
    gate_grad, upward_grad = gate_pull(activated_grad)
    gate_grad, upward_grad = gate_grad.astype(BF), upward_grad.astype(BF)
    gate_weight_grad = jnp.einsum("td,tf->df", normed_two_all, gate_grad, preferred_element_type=F32)
    up_weight_grad = jnp.einsum("td,tf->df", normed_two_all, upward_grad, preferred_element_type=F32)
    normed_two_term = jnp.einsum("tf,df->td", gate_grad, WF[0], preferred_element_type=F32) + jnp.einsum(
        "tf,df->td", upward_grad, WF[1], preferred_element_type=F32
    )
    down_sum = lax.psum_scatter(down_term.astype(BF), "seq", scatter_dimension=0, tiled=True)
    normed_two_sum = lax.psum_scatter(normed_two_term.astype(BF), "seq", scatter_dimension=0, tiled=True)
    outputs = (hidden_one + pack_features(down_sum, geo, width).astype(F32)).astype(BF)[None]
    normed_two_grad = pack_features(normed_two_sum, geo, width).astype(F32)
    gf = jnp.stack([gate_weight_grad.astype(BF), up_weight_grad.astype(BF), down_weight_grad.astype(BF)])

    unused_two, second_pull = jax.vjp(norm_scale, hidden_one, second_gain)
    hidden_norm_grad, second_gain_grad = second_pull(normed_two_grad)
    hidden_grad = incoming + hidden_norm_grad
    hidden_low = hidden_grad.astype(jnp.bfloat16)
    output_weight_grad = jnp.einsum("td,tc->dc", hidden_low, mixed_heads, preferred_element_type=jnp.float32)
    mixed_grad = jnp.einsum("td,dc->tc", hidden_low, output_full, preferred_element_type=jnp.float32).astype(
        jnp.bfloat16
    )
    grad_heads = mixed_grad.reshape(row_count, head_count, head_dim)
    prob_grad = jnp.einsum("thc,khc->htk", grad_heads, value_heads, preferred_element_type=jnp.float32)
    inner_sum = jnp.sum(probs * prob_grad, axis=-1, keepdims=True)
    score_grad = (probs * (prob_grad - inner_sum)).astype(jnp.bfloat16)
    query_act_grad = (
        jnp.einsum("htk,khc->thc", score_grad, key_heads, preferred_element_type=jnp.float32)
        .reshape(row_count, inner_width)
        .astype(jnp.bfloat16)
    )
    key_piece = jnp.einsum(
        "htk,thc->khc", score_grad, query_heads, preferred_element_type=jnp.float32
    ).reshape(length_all, inner_width)
    value_piece = jnp.einsum(
        "htk,thc->khc", probs_low, grad_heads, preferred_element_type=jnp.float32
    ).reshape(length_all, inner_width)
    own_terms = lax.psum_scatter(
        jnp.concatenate([key_piece, value_piece], axis=1).astype(jnp.bfloat16),
        "seq",
        scatter_dimension=0,
        tiled=True,
    )
    keyval_act_grad = jnp.stack([own_terms[:, :inner_width], own_terms[:, inner_width:]])
    query_weight_grad = jnp.einsum("td,tc->dc", normed, query_act_grad, preferred_element_type=jnp.float32)
    keyval_weight_grad = jnp.einsum("td,stc->sdc", normed, keyval_act_grad, preferred_element_type=jnp.float32)
    normed_grad = jnp.einsum(
        "tc,dc->td", query_act_grad, query_full, preferred_element_type=jnp.float32
    ) + jnp.einsum("stc,sdc->td", keyval_act_grad, keyval_full, preferred_element_type=jnp.float32)
    unused_three, first_pull = jax.vjp(norm_scale, inputs, first_gain)
    input_norm_grad, first_gain_grad = first_pull(normed_grad)
    input_grad = (hidden_grad + input_norm_grad).astype(jnp.bfloat16)[None]
    table_grad = jnp.einsum("htk,tkb->bh", score_grad, onehot, preferred_element_type=jnp.float32)

    grads = jnp.stack(
        [query_weight_grad, keyval_weight_grad[0], keyval_weight_grad[1], output_weight_grad]
    ).reshape(4, dp, width, seq, own_inner)
    grads = grads.transpose(3, 1, 2, 0, 4).reshape(seq, dp, width, geo.I4).astype(BF)
    wide = lambda v: jnp.pad(v, ((0, 0), (0, 0), (0, geo.I4 - v.shape[2])))
    more = jnp.concatenate(
        [
            jnp.zeros((dp, rows - width - geo.E, geo.I4), F32),
            wide(first_gain_grad.reshape(dp, 1, width)),
            wide(second_gain_grad.reshape(dp, 1, width)),
            wide(table_grad.reshape(dp, table_rows, head_count)),
        ],
        axis=1,
    ).astype(BF)
    ga = jnp.concatenate([grads, jnp.broadcast_to(more, (seq, *more.shape))], axis=2).reshape(seq, dp * rows, geo.I4)
    of, oa = scatter_grads(geo, gf, ga)

    main = oa[:width]
    query_part = main[:, :own_inner]
    keyval_part = jnp.stack([main[:, own_inner : 2 * own_inner], main[:, 2 * own_inner : 3 * own_inner]])
    output_part = main[:, 3 * own_inner :]
    gain_part = oa[rows - geo.E : rows - table_rows, :width]
    table_part = oa[rows - table_rows :, :head_count]
    return (
        outputs,
        input_grad,
        query_part,
        keyval_part,
        output_part,
        of[:2, :width],
        of[2, :width],
        gain_part,
        table_part,
    )

def fused_path(
    axes, tokens, cotangent, lengths, w_query, w_key_value, w_output, w_gate_up, w_down, norm_gains, position_bias
):
    geo = Geo(*axes, w_query.shape[0], w_down.shape[1], 4 * w_query.shape[1], tokens.shape[1], *position_bias.shape[::-1])
    saved = forward(
        geo, lengths, tokens[0].T, cotangent[0].T, w_query, w_key_value, w_output, w_gate_up, w_down, norm_gains, position_bias
    )
    outs = finish(geo, *backward(geo, *saved))
    return outs[0].T[None], outs[1].T[None], *outs[2:]


def per_device(axes, *arrays):
    tokens, w_query, w_down, position_bias = arrays[0], arrays[3], arrays[7], arrays[9]
    geo = Geo(*axes, w_query.shape[0], w_down.shape[1], 4 * w_query.shape[1], tokens.shape[1], position_bias.shape[1],
              position_bias.shape[0])
    aligned = geo.W % 8 == 0 and geo.F % 128 == 0 and geo.I4 % 128 == 0 and 2 * geo.R % 128 == 0 and geo.T % 128 == 0 and geo.I % 128 == 0
    aligned = aligned and max(2 * geo.I, geo.seq * geo.I4 // 2) <= geo.F and 4 * geo.T <= geo.L and geo.N + 2 * geo.T <= 2 * geo.L and geo.L + 256 <= geo.N
    small = (3 * geo.F + geo.seq * geo.I4 + 2 * geo.L) * geo.N * 2 <= 24 << 20
    return (fused_path if aligned and small else general_path)(axes, *arrays)


def solution(mesh):
    in_specs = (
        P("dp", "seq", None),
        P("dp", "seq", None),
        P("dp"),
        P("dp", "seq"),
        P(None, "dp", "seq"),
        P("dp", "seq"),
        P(None, "dp", "seq"),
        P("dp", "seq"),
        P(None, "dp"),
        P("dp", None),
    )
    out_specs = (
        P("dp", "seq", None),
        P("dp", "seq", None),
        P("dp", "seq"),
        P(None, "dp", "seq"),
        P("dp", "seq"),
        P(None, "dp", "seq"),
        P("dp", "seq"),
        P(None, "dp"),
        P("dp", None),
    )
    return jax.shard_map(
        functools.partial(per_device, (mesh.shape["dp"], mesh.shape["seq"])), mesh=mesh, in_specs=in_specs, out_specs=out_specs, check_vma=False
    )
```

```python
import functools
import jax
import jax.numpy as jnp
import numpy as np
from jax import lax
from jax.experimental import pallas as pl
from jax.experimental.pallas import tpu as pltpu

from jax.sharding import PartitionSpec as P

MESH = pl.DeviceIdType.MESH
BF = jnp.bfloat16
F32 = jnp.float32


class Geo:
    def __init__(self, dp, seq, width, ff, inner4, tokens, heads, table_rows):
        self.dp, self.seq = dp, seq
        self.W, self.TR, self.E = width, table_rows, 2 + table_rows
        rows = -(-(width + self.E) // 16) * 16
        self.D, self.N, self.T, self.L = dp * width, dp * rows, tokens, seq * tokens
        self.I, self.H = inner4 // 4 * seq, heads
        self.B, self.A, self.X = 2, dp // 2, seq // 2
        self.R, self.F, self.I4 = rows, ff, inner4
        self.NH = 2 if rows % 32 == 0 else 1
        self.RH = rows // self.NH
        self.NP = 3 * self.NH
        self.NZ = 2 * (self.A - 1)
        self.NY = 2 * self.A - 1


class Place:
    def __init__(self, geo):
        d, s = lax.axis_index("dp"), lax.axis_index("seq")
        self.d, self.s = d, s
        self.z, self.y = d // 2, d % 2
        self.x, self.c = s // 2, s % 2

    def dev(self, z=None, y=None, x=None, c=None):
        z = self.z if z is None else z
        y = self.y if y is None else y
        x = self.x if x is None else x
        c = self.c if c is None else c
        return (z * 2 + y, x * 2 + c)


def remote(src, dst, ss, rs, dev):
    return pltpu.make_async_remote_copy(
        src_ref=src, dst_ref=dst, send_sem=ss, recv_sem=rs, device_id=dev, device_id_type=MESH
    )


def loop(n, body):
    def step(i, carry):
        body(i)
        return carry

    lax.fori_loop(0, n, step, 0)


def enter(geo, me, work=None):
    bar = pltpu.get_barrier_semaphore()

    def greet(dev):
        pl.semaphore_signal(bar, 1, device_id=dev, device_id_type=MESH)

    greet(me.dev(y=1 - me.y))
    greet(me.dev(c=1 - me.c))
    for k in range(1, geo.X):
        greet(me.dev(x=lax.rem(me.x + k, geo.X)))

    @pl.when(me.z > 0)
    def _():
        greet(me.dev(z=me.z - 1))

    @pl.when(me.z < geo.A - 1)
    def _():
        greet(me.dev(z=me.z + 1))

    count = 2 + (geo.X - 1) + (me.z > 0).astype(jnp.int32) + (me.z < geo.A - 1).astype(jnp.int32)
    if work is not None:
        work()
    pl.semaphore_wait(bar, count)


class LineGather:
    def __init__(self, geo, me, own, held, zs, zr, ys, yr, first_y=1 << 20, bzs=None, bzr=None):
        self.geo, self.me, self.own, self.held = geo, me, own, held
        self.zs, self.zr, self.ys, self.yr = zs, zr, ys, yr
        self.first_y, self.bzs, self.bzr = first_y, bzs, bzr

    def from_z(self, way, r):
        q = self.me.z - r if way == 0 else self.me.z + r
        return q, (q >= 0) if way == 0 else (q <= self.geo.A - 1)

    def sems(self, way, r, p, other):
        slot = way * (self.geo.A - 1) + r - 1
        if other:
            return self.bzs.at[slot, p - self.first_y], self.bzr.at[slot, p - self.first_y]
        return self.zs.at[slot, p], self.zr.at[slot, p]

    def zcopy(self, way, r, p, other=False):
        me, geo = self.me, self.geo
        q, there = self.from_z(way, r - 1)
        to = me.z + 1 if way == 0 else me.z - 1
        valid = ((me.z < geo.A - 1) if way == 0 else (me.z > 0)) & there
        here = self.held(p, q * 2 + (1 - me.y if other else me.y))
        src = self.own(p) if r == 1 and not other else here
        return remote(src, here, *self.sems(way, r, p, other), me.dev(z=to)), valid

    def zarrive(self, way, r, p, other=False):
        q, valid = self.from_z(way, r)
        here = self.held(p, q * 2 + (1 - self.me.y if other else self.me.y))
        return remote(here, here, *self.sems(way, r, p, other), self.me.dev(y=1 - self.me.y)), valid, q

    def yslot(self, way, r):
        return 1 + way * (self.geo.A - 1) + r - 1 if r else 0

    def ycopy(self, way, r, p):
        me, slot = self.me, self.yslot(way, r)
        q, _ = self.from_z(way, r)
        src = self.held(p, q * 2 + me.y) if r else self.own(p)
        return remote(src, self.held(p, q * 2 + me.y), self.ys.at[slot, p], self.yr.at[slot, p], me.dev(y=1 - me.y))

    def yarrive(self, way, r, p):
        me, slot = self.me, self.yslot(way, r)
        q, _ = self.from_z(way, r)
        here = self.held(p, q * 2 + 1 - me.y)
        return remote(here, here, self.ys.at[slot, p], self.yr.at[slot, p], me.dev(y=1 - me.y)), q

    def begin_y(self, p):
        self.ycopy(0, 0, p).start()

    def begin_z(self, p, other=False):
        for way in (0, 1):
            copy, valid = self.zcopy(way, 1, p, other)

            @pl.when(valid)
            def _():
                copy.start()

    def begin(self, p):
        self.begin_y(p)
        self.begin_z(p)

    def turn(self, p):
        self.yarrive(0, 0, p)[0].wait_recv()
        self.begin_z(p, True)

    def step(self, r, p, on_held=None, kinds=(False,), pass_y=True):
        for other in kinds:
            for way in (0, 1):
                copy, valid, q = self.zarrive(way, r, p, other)

                @pl.when(valid)
                def _():
                    copy.wait_recv()
                    if r < self.geo.A - 1:
                        onward, may = self.zcopy(way, r + 1, p, other)

                        @pl.when(may)
                        def _():
                            onward.start()

                    if pass_y:
                        self.ycopy(way, r, p).start()
                    if on_held is not None:
                        on_held(q * 2 + self.me.y)

    def step_both(self, r, p):
        self.step(r, p, None, (False, True), False)

    def ystep(self, r, p, on_held=None):
        for way in (0, 1) if r else (0,):
            copy, q = self.yarrive(way, r, p)

            def go():
                copy.wait_recv()
                if on_held is not None:
                    on_held(q * 2 + 1 - self.me.y)

            if r:
                pl.when(self.from_z(way, r)[1])(go)
            else:
                go()

    def drain(self, p, kinds=(False,), pass_y=True):
        self.ycopy(0, 0, p).wait_send()
        for r in range(1, self.geo.A):
            for way in (0, 1):
                for other in kinds:
                    copy, valid = self.zcopy(way, r, p, other)

                    @pl.when(valid)
                    def _():
                        copy.wait_send()

                if pass_y:

                    @pl.when(self.from_z(way, r)[1])
                    def _():
                        self.ycopy(way, r, p).wait_send()


class LineScatter:
    def __init__(self, geo, me, part, ybuf, zbuf, stage, zs, zr, ys, yr, finish):
        self.__dict__.update(locals())

    def turns(self):
        geo, me = self.geo, self.me
        for k in range(geo.A - 1):
            yield 0, k, geo.A - 1 - k, k < geo.A - 1 - me.z
            yield 1, k, k, k < me.z

    def slot(self, way, k):
        return way * (self.geo.A - 1) + k

    def ycopy(self, slot, t, p):
        me = self.me
        return remote(
            self.part(p, t * 2 + 1 - me.y),
            self.ybuf(p, t),
            self.ys.at[slot, p],
            self.yr.at[slot, p],
            me.dev(y=1 - me.y),
        )

    def zcopy(self, way, k, p):
        me = self.me
        to = me.z + 1 if way == 0 else me.z - 1
        slot = self.slot(way, k)
        return remote(
            self.stage(way, p, k), self.zbuf(way, p, k), self.zs.at[slot, p], self.zr.at[slot, p], me.dev(z=to)
        )

    def ysend(self, p, k):
        for way, kk, t, valid in self.turns():
            if kk == k:

                @pl.when(valid)
                def _():
                    self.ycopy(self.slot(way, kk), t, p).start()

    def ysend_own(self, p):
        self.ycopy(self.geo.NZ, self.me.z, p).start()

    def step(self, k, p):
        geo, me = self.geo, self.me
        for way, kk, t, valid in self.turns():
            if kk == k:

                @pl.when(valid)
                def _():
                    self.ycopy(self.slot(way, k), t, p).wait_recv()
                    total = self.part(p, t * 2 + me.y)[...].astype(F32) + self.ybuf(p, t)[...].astype(F32)
                    out = self.stage(way, p, k)
                    comes = me.z > 0 if way == 0 else me.z < geo.A - 1

                    @pl.when(comes)
                    def _():
                        self.zcopy(way, k, p).wait_recv()
                        out[...] = (total + self.zbuf(way, p, k)[...].astype(F32)).astype(BF)

                    @pl.when(jnp.logical_not(comes))
                    def _():
                        out[...] = total.astype(BF)

                    self.zcopy(way, k, p).start()

    def own(self, p):
        geo, me = self.geo, self.me
        self.ycopy(geo.NZ, me.z, p).wait_recv()
        total = self.part(p, me.z * 2 + me.y)[...].astype(F32) + self.ybuf(p, me.z)[...].astype(F32)
        kup = jnp.minimum(geo.A - 1 - me.z, geo.A - 2)
        kdown = jnp.minimum(me.z, geo.A - 2)

        def arrive(way, k):
            slot = way * (geo.A - 1) + k
            here = self.zbuf(way, p, k)
            remote(here, here, self.zs.at[slot, p], self.zr.at[slot, p], me.dev(y=1 - me.y)).wait_recv()
            return here[...].astype(F32)

        @pl.when(me.z == 0)
        def _():
            self.finish(p, total + arrive(1, kdown))

        @pl.when(me.z == geo.A - 1)
        def _():
            self.finish(p, total + arrive(0, kup))

        @pl.when((me.z > 0) & (me.z < geo.A - 1))
        def _():
            self.finish(p, total + arrive(0, kup) + arrive(1, kdown))

    def drain(self, p):
        for way, k, t, valid in self.turns():

            @pl.when(valid)
            def _():
                self.ycopy(self.slot(way, k), t, p).wait_send()
                self.zcopy(way, k, p).wait_send()

        self.ycopy(self.geo.NZ, self.me.z, p).wait_send()


NEGATIVE = -1e30
EPSILON = 1e-06
LIMITS = (12, 16, 23, 32, 46, 64, 91)


def bucket_ids(offsets):
    distance = jnp.abs(offsets)
    larger = 8 + sum(((distance >= threshold).astype(jnp.int32) for threshold in LIMITS))
    nearby = jnp.where(distance < 8, distance, larger)
    return jnp.where(offsets > 0, 16, 0) + nearby


def norm_scale(values, gain_vector):
    return (
        values
        * lax.rsqrt(jnp.mean(values * values, axis=-1, keepdims=True) + EPSILON)
        * gain_vector
    )


def gated(gate_value, upward):
    return jax.nn.gelu(gate_value, approximate=True) * upward


def gather_kernel(geo, wf, wa, WF, WA, local, zs, zr, ys, yr, azs, azr, ays, ayr, xs, xr, cs, cr):
    me = Place(geo)
    R, RH, NH, dp, X = geo.R, geo.RH, geo.NH, geo.dp, geo.X
    mine = [
        pltpu.make_async_copy(wf, WF.at[:, pl.ds(pl.multiple_of(me.d * R, 16), R), :], local.at[0]),
        pltpu.make_async_copy(wa, WA.at[me.s, pl.ds(pl.multiple_of(me.d * R, 16), R), :], local.at[1]),
    ]
    for copy in mine:
        copy.start()
    enter(geo, me)

    def own_f(p):
        return wf.at[p // NH, pl.ds(pl.multiple_of((p % NH) * RH, 16), RH), :]

    def held_f(p, g):
        return WF.at[p // NH, pl.ds(pl.multiple_of(g * R + (p % NH) * RH, 16), RH), :]

    def held_a(s, g):
        return WA.at[s, pl.ds(pl.multiple_of(g * R, 16), R), :]

    ffn = LineGather(geo, me, own_f, held_f, zs, zr, ys, yr)
    att = LineGather(geo, me, lambda p: wa, lambda p, g: held_a(me.s, g), azs, azr, ays, ayr)

    def xcopy(k, g, src):
        to = lax.rem(me.x + k, X)
        return remote(src, held_a(me.s, g), xs.at[k - 1, g], xr.at[k - 1, g], me.dev(x=to))

    def xarrive(k, g):
        src_x = lax.rem(me.x - k + X, X)
        here = held_a(src_x * 2 + me.c, g)
        return remote(here, here, xs.at[k - 1, g], xr.at[k - 1, g], me.dev(c=1 - me.c)), here

    def ccopy(k, g, src, s):
        return remote(src, held_a(s, g), cs.at[k, g], cr.at[k, g], me.dev(c=1 - me.c))

    def spread(g, src=None):
        src = held_a(me.s, g) if src is None else src
        for k in range(1, X):
            xcopy(k, g, src).start()
        ccopy(0, g, src, me.s).start()

    att.begin(0)
    spread(me.d, wa)
    loop(geo.NP, ffn.begin)
    att.ystep(0, 0, spread)
    for r in range(1, geo.A):
        att.step(r, 0, spread)
        att.ystep(r, 0, spread)

    def from_x(g):
        for k in range(1, X):
            copy, here = xarrive(k, g)
            copy.wait_recv()
            ccopy(k, g, here, lax.rem(me.x - k + X, X) * 2 + me.c).start()

    loop(dp, from_x)
    for r in range(1, geo.A):
        loop(geo.NP, lambda p: ffn.step(r, p))
    for r in range(geo.A):
        loop(geo.NP, lambda p: ffn.ystep(r, p))

    def finish(g):
        for k in range(X):
            s = lax.rem(me.x - k + X, X) * 2 + 1 - me.c
            here = held_a(s, g)
            remote(here, here, cs.at[k, g], cr.at[k, g], me.dev(c=1 - me.c)).wait_recv()
            ccopy(k, g, here, s).wait_send()
            if k:
                xcopy(k, g, here).wait_send()

    loop(dp, finish)
    att.drain(0)
    loop(geo.NP, ffn.drain)
    for copy in mine:
        copy.wait()


def scatter_kernel(
    geo, gf, ga, of, oa, yb, zb, st, cb, xb, xst, pa, ayb, azb, ast,
    zs, zr, ys, yr, azs, azr, ays, ayr, xs, xr, cs, cr,
):
    me = Place(geo)
    R, RH, NH, dp, X, A = geo.R, geo.RH, geo.NH, geo.dp, geo.X, geo.A
    enter(geo, me)

    def rows(g, p):
        return pl.ds(pl.multiple_of(g * R + (p % NH) * RH, 16), RH)

    def piece(buf, i, p):
        return buf.at[i, p // NH, pl.ds(pl.multiple_of((p % NH) * RH, 16), RH), :]

    def finish_f(p, value):
        of[p // NH, pl.ds(pl.multiple_of((p % NH) * RH, 16), RH), :] = value

    ffn = LineScatter(
        geo, me,
        lambda p, g: gf.at[p // NH, rows(g, p), :],
        lambda p, t: piece(yb, t, p),
        lambda way, p, k: piece(zb, way * (A - 1) + k, p),
        lambda way, p, k: piece(st, way * (A - 1) + k, p),
        zs, zr, ys, yr, finish_f,
    )

    def block(g):
        return pl.ds(pl.multiple_of(g * R, 16), R)

    def finish_a(p, value):
        oa[...] = value

    att = LineScatter(
        geo, me,
        lambda p, g: pa.at[block(g), :],
        lambda p, t: ayb.at[t],
        lambda way, p, k: azb.at[way * (A - 1) + k],
        lambda way, p, k: ast.at[way * (A - 1) + k],
        azs, azr, ays, ayr, finish_a,
    )

    def ccopy(k, g):
        to_x = lax.rem(me.x + k, X)
        return remote(
            ga.at[to_x * 2 + 1 - me.c, block(g), :], cb.at[k, block(g), :], cs.at[k, g], cr.at[k, g], me.dev(c=1 - me.c)
        )

    def xcopy(k, g):
        return remote(
            xst.at[k - 1, block(g), :], xb.at[k - 1, block(g), :], xs.at[k - 1, g], xr.at[k - 1, g],
            me.dev(x=lax.rem(me.x + k, X)),
        )

    def to_core(g):
        for k in (*range(1, X), 0):
            ccopy(k, g).start()

    def to_x(g):
        for k in range(1, X):
            ccopy(k, g).wait_recv()
            s = lax.rem(me.x + k, X) * 2 + me.c
            xst[k - 1, block(g), :] = (
                ga[s, block(g), :].astype(F32) + cb[k, block(g), :].astype(F32)
            ).astype(BF)
            xcopy(k, g).start()

    def meet(g):
        ccopy(0, g).wait_recv()
        total = ga[me.s, block(g), :].astype(F32) + cb[0, block(g), :].astype(F32)
        for k in range(1, X):
            xcopy(k, g).wait_recv()
            total += xb[k - 1, block(g), :].astype(F32)
        pa[block(g), :] = total.astype(BF)

    def free(g):
        for k in range(X):
            ccopy(k, g).wait_send()
            if k:
                xcopy(k, g).wait_send()

    for k in range(A - 1):
        loop(geo.NP, lambda p: ffn.ysend(p, k))
    loop(geo.NP, ffn.ysend_own)
    loop(dp, to_core)
    loop(dp, to_x)
    for k in range(A - 1):
        loop(geo.NP, lambda p: ffn.step(k, p))
    loop(geo.NP, ffn.own)
    loop(dp, meet)
    for k in range(A - 1):
        att.ysend(0, k)
    att.ysend_own(0)
    for k in range(A - 1):
        att.step(k, 0)
    att.own(0)
    loop(dp, free)
    att.drain(0)
    loop(geo.NP, ffn.drain)


def gather_weights(geo, wf, wa):
    dma = pltpu.SemaphoreType.DMA
    sems = [
        dma((2,)),
        dma((geo.NZ, geo.NP)), dma((geo.NZ, geo.NP)), dma((geo.NY, geo.NP)), dma((geo.NY, geo.NP)),
        dma((geo.NZ, 1)), dma((geo.NZ, 1)), dma((geo.NY, 1)), dma((geo.NY, 1)),
        dma((geo.X - 1, geo.dp)), dma((geo.X - 1, geo.dp)), dma((geo.X, geo.dp)), dma((geo.X, geo.dp)),
    ]
    return pl.pallas_call(
        functools.partial(gather_kernel, geo),
        out_shape=(
            jax.ShapeDtypeStruct((3, geo.dp * geo.R, geo.F), BF),
            jax.ShapeDtypeStruct((geo.seq, geo.dp * geo.R, geo.I4), BF),
        ),
        in_specs=[pl.BlockSpec(memory_space=pl.ANY)] * 2,
        out_specs=[pl.BlockSpec(memory_space=pl.ANY)] * 2,
        scratch_shapes=sems,
        compiler_params=pltpu.CompilerParams(collective_id=0, has_side_effects=True, vmem_limit_bytes=48 << 20),
        name="gather_weights",
    )(wf, wa)


def scatter_grads(geo, gf, ga):
    dma = pltpu.SemaphoreType.DMA
    n, X, A, R = geo.dp * geo.R, geo.X, geo.A, geo.R
    scratch = [
        pltpu.VMEM((A, 3, R, geo.F), BF), pltpu.VMEM((geo.NZ, 3, R, geo.F), BF), pltpu.VMEM((geo.NZ, 3, R, geo.F), BF),
        pltpu.VMEM((X, n, geo.I4), BF), pltpu.VMEM((X - 1, n, geo.I4), BF), pltpu.VMEM((X - 1, n, geo.I4), BF),
        pltpu.VMEM((n, geo.I4), BF),
        pltpu.VMEM((A, R, geo.I4), BF), pltpu.VMEM((geo.NZ, R, geo.I4), BF), pltpu.VMEM((geo.NZ, R, geo.I4), BF),
        dma((geo.NZ, geo.NP)), dma((geo.NZ, geo.NP)), dma((geo.NZ + 1, geo.NP)), dma((geo.NZ + 1, geo.NP)),
        dma((geo.NZ, 1)), dma((geo.NZ, 1)), dma((geo.NZ + 1, 1)), dma((geo.NZ + 1, 1)),
        dma((X - 1, geo.dp)), dma((X - 1, geo.dp)), dma((X, geo.dp)), dma((X, geo.dp)),
    ]
    return pl.pallas_call(
        functools.partial(scatter_kernel, geo),
        out_shape=(
            jax.ShapeDtypeStruct((3, R, geo.F), F32),
            jax.ShapeDtypeStruct((R, geo.I4), F32),
        ),
        in_specs=[pl.BlockSpec(memory_space=pltpu.VMEM)] * 2,
        out_specs=[pl.BlockSpec(memory_space=pltpu.VMEM)] * 2,
        scratch_shapes=scratch,
        compiler_params=pltpu.CompilerParams(collective_id=1, has_side_effects=True, vmem_limit_bytes=60 << 20),
        name="scatter_grads",
    )(gf, ga)


class SeqGather:
    def __init__(self, geo, me, held, xs, xr, cs, cr):
        self.geo, self.me, self.held = geo, me, held
        self.xs, self.xr, self.cs, self.cr = xs, xr, cs, cr

    def ccopy(self, k):
        me, X = self.me, self.geo.X
        here = self.held(lax.rem(me.x - k + X, X) * 2 + me.c)
        return remote(here, here, self.cs.at[k], self.cr.at[k], me.dev(c=1 - me.c))

    def xcopy(self, k):
        me = self.me
        here = self.held(me.s)
        return remote(here, here, self.xs.at[k - 1], self.xr.at[k - 1], me.dev(x=lax.rem(me.x + k, self.geo.X)))

    def begin(self):
        for k in range(1, self.geo.X):
            self.xcopy(k).start()
        self.ccopy(0).start()

    def relay(self):
        for k in range(1, self.geo.X):
            self.xcopy(k).wait_recv()
            self.ccopy(k).start()

    def finish(self):
        for k in range(self.geo.X):
            self.ccopy(k).wait_recv()
            self.ccopy(k).wait_send()
            if k:
                self.xcopy(k).wait_send()


def dot(a, b, dims=((1,), (0,))):
    return lax.dot_general(a, b, (dims, ((), ())), preferred_element_type=F32)


NT = ((1,), (1,))
TN = ((0,), (0,))


def place_columns(geo, out):
    own = geo.I4 // 4
    c = lax.broadcasted_iota(jnp.int32, out.shape, 0)
    j = lax.broadcasted_iota(jnp.int32, out.shape, 1)
    to = c + 3 * own
    for s in range(1, geo.seq):
        to += jnp.where(c >= s * own, 3 * own, 0)
    out[...] = jnp.where(j == to, 1.0, 0.0).astype(BF)


def place_buckets(geo, out):
    row = lax.broadcasted_iota(jnp.int32, out.shape, 0)
    at = row % 16 - (16 - geo.TR)
    bucket = bucket_ids(lax.broadcasted_iota(jnp.int32, out.shape, 1) - 256)
    out[...] = jnp.where((at >= 0) & (bucket == row // 16 * geo.TR + at), 1.0, 0.0).astype(BF)


def spread(geo, value):
    value = value.astype(F32)
    gap = jnp.zeros((geo.R - geo.W, value.shape[1]), F32)
    parts = [v for g in range(geo.dp) for v in (value[g * geo.W : (g + 1) * geo.W], gap)]
    return jnp.concatenate(parts, axis=0).T.astype(BF)


def pack(geo, value):
    value = value.T
    return jnp.concatenate([value[g * geo.R : g * geo.R + geo.W] for g in range(geo.dp)], axis=0).astype(BF)


def shear(value, sign):
    rows, lanes = value.shape
    row = lax.broadcasted_iota(jnp.int32, (rows, 1), 0)
    bit = 1
    while bit < rows:
        moved = pltpu.roll(value, bit if sign > 0 else lanes - bit, 1)
        value = jnp.where((row & bit) != 0, moved, value)
        bit *= 2
    return value


def gelu_parts(g):
    k0 = np.float32(np.sqrt(2 / np.pi))
    t = jnp.tanh(k0 * (g + np.float32(0.044715) * (g * g * g)))
    half = 0.5 * (1.0 + t)
    slope = half + 0.5 * g * (1.0 - t * t) * (k0 * (1.0 + np.float32(3 * 0.044715) * (g * g)))
    return g * half, slope


def forward_kernel(
    geo, length, x_in, c_in, wq, wkv, wo, wgu, wd, norm_gains, position_bias,
    oX, oWA, oqkv, oKV, oP, omixed, ohid, oX2, oC, oact, opart, ogain,
    WF0, WF1, WA, xv, C, X2, KV, qkv, strip, mixed, hid, pst, act, part, got, gain, raw, wst, ast, gst, bst, ex, pout, onehot,
    local, outs, psem, zs, zr, ys, yr, bzs, bzr, azs, azr, ays, ayr, xs, xr, cs, cr, gxs, gxr, gcs, gcr, ps, pr, wsem,
):
    me = Place(geo)
    R, RH, NH, dp, X, T, N, I = geo.R, geo.RH, geo.NH, geo.dp, geo.X, geo.T, geo.N, geo.I
    I4, S, L = geo.I4, geo.seq, geo.L
    block = lambda i, n: pl.ds(pl.multiple_of(i * n, 16), n)
    loads = [
        (wq, ast.at[0]), (wkv.at[0], ast.at[1]), (wkv.at[1], ast.at[2]), (wo, ast.at[3]), (norm_gains, gst),
        (position_bias, bst), (wgu.at[0], wst.at[0]), (wgu.at[1], wst.at[1]), (wd, wst.at[2]), (x_in, raw.at[0]),
        (c_in, raw.at[1]),
    ]
    loads = [pltpu.make_async_copy(src, dst, local.at[i]) for i, (src, dst) in enumerate(loads)]
    for copy in loads:
        copy.start()
    W, E = geo.W, geo.E

    def own_attention():
        ex[...] = jnp.zeros_like(ex)
        for copy in loads[:6]:
            copy.wait()
        ex[R - W - E : R - W - E + 2, :W] = gst[...]
        ex[R - W - E + 2 :, : geo.H] = bst[...]
        columns = jnp.concatenate([ast[k] for k in range(4)], axis=1)
        WA[me.s, block(me.d, R), :] = jnp.concatenate([columns, ex[...]], axis=0).astype(BF)

    enter(geo, me, own_attention)

    WFs = (WF0, WF1)
    cuts = ((0, WF0.shape[2]), (WF0.shape[2], geo.F))

    def held_f(p, g):
        return WFs[p // 3].at[p % 3, block(g, R), :]

    def held_a(s, g):
        return WA.at[s, block(g, R), :]

    special = 2
    others = [p for p in range(6) if p != special]
    ffn = LineGather(geo, me, lambda p: held_f(p, me.d), held_f, zs, zr, ys, yr, special, bzs, bzr)
    att = LineGather(geo, me, lambda p: held_a(me.s, me.d), lambda p, g: held_a(me.s, g), azs, azr, ays, ayr)

    def xcopy(k, g, src):
        to = lax.rem(me.x + k, X)
        return remote(src, held_a(me.s, g), xs.at[k - 1, g], xr.at[k - 1, g], me.dev(x=to))

    def xarrive(k, g):
        src_x = lax.rem(me.x - k + X, X)
        here = held_a(src_x * 2 + me.c, g)
        return remote(here, here, xs.at[k - 1, g], xr.at[k - 1, g], me.dev(c=1 - me.c)), here

    def ccopy(k, g, src, s):
        return remote(src, held_a(s, g), cs.at[k, g], cr.at[k, g], me.dev(c=1 - me.c))

    def share(g):
        src = held_a(me.s, g)
        for k in range(1, X):
            xcopy(k, g, src).start()
        ccopy(0, g, src, me.s).start()

    half = T // 2

    def seq_gather(i, ref, first, count):
        held = lambda s: ref.at[pl.ds(pl.multiple_of(s * T + first, 16), count), :]
        return SeqGather(geo, me, held, gxs.at[i], gxr.at[i], gcs.at[i], gcr.at[i])

    gather_kv = seq_gather(0, KV, 0, T)
    gather_x2 = [seq_gather(1, X2, 0, half), seq_gather(2, X2, half, half)]
    gather_c = [seq_gather(3, C, 0, half), seq_gather(4, C, half, half)]

    att.begin(0)
    share(me.d)
    for m in range(3):
        loads[6 + m].wait()
        for ref, cut in zip(WFs, cuts):
            lanes = slice(*cut)
            own = jnp.concatenate([wst[m, :, lanes], jnp.zeros((R - W, cut[1] - cut[0]), F32)], axis=0)
            ref[m, block(me.d, R), :] = own.astype(BF)
    ffn.begin_y(special)
    for p in range(6):
        if p == special:
            ffn.begin_z(p)
        else:
            ffn.begin(p)
    events = [(r, p) for r in range(1, geo.A) for p in range(6)]

    def forward_on(r, p):
        if p == special:
            ffn.step_both(r, p)
        else:
            ffn.step(r, p)

    def run(count):
        for _ in range(min(count, len(events))):
            forward_on(*events.pop(0))

    att.ystep(0, 0, share)
    for r in range(1, geo.A):
        att.step(r, 0, share)
        att.ystep(r, 0, share)
    ffn.turn(special)
    place_columns(geo, pout)
    place_buckets(geo, onehot)
    for copy in loads[9:]:
        copy.wait()
    xv[...] = spread(geo, raw[0])
    C[block(me.s, T), :] = spread(geo, raw[1])
    gather_c[0].begin()

    def from_x(g):
        for k in range(1, X):
            copy, here = xarrive(k, g)
            copy.wait_recv()
            ccopy(k, g, here, lax.rem(me.x - k + X, X) * 2 + me.c).start()

    for g in range(dp):
        from_x(g)
        if g >= 3:
            run(1)

    def settle(g):
        for k in range(X):
            s = lax.rem(me.x - k + X, X) * 2 + 1 - me.c
            here = held_a(s, g)
            remote(here, here, cs.at[k, g], cr.at[k, g], me.dev(c=1 - me.c)).wait_recv()

    loop(dp, settle)

    extra = jnp.concatenate([WA[0, g * R + R - 16 : g * R + R, :] for g in range(dp)], axis=0)
    lines = extra.astype(F32)
    gain[...] = jnp.zeros_like(gain)
    for g in range(dp):
        for e in range(2):
            at = g * 16 + 16 - E + e
            gain[e : e + 1, g * R : (g + 1) * R] = lines[at : at + 1, :R]
    bias = dot(extra[:, :128], onehot[...], TN)

    inputs = xv[...].astype(F32)
    scale = lax.rsqrt(jnp.sum(inputs * inputs, axis=-1, keepdims=True) / np.float32(geo.D) + EPSILON)
    normed = (inputs * scale * gain[0:1, :]).astype(BF)
    columns = jnp.concatenate([dot(normed, WA[s]) for s in range(S)], axis=1)
    for kind in (1, 2, 0):
        moved = pltpu.roll(columns, (3 - kind) * (I4 // 4), 1).astype(BF)
        qkv[:, kind * I : (kind + 1) * I] = dot(moved, pout[...], NT).astype(BF)
        if kind == 2:
            KV[block(me.s, T), :] = qkv[:, I:]
            gather_kv.begin()
            gather_c[1].begin()
    gather_c[0].relay()
    run(1)
    writes = []

    def write(src, dst):
        copy = pltpu.make_async_copy(src, dst, outs.at[len(writes)])
        copy.start()
        writes.append(copy)

    write(xv, oX)
    write(WA, oWA)
    write(qkv, oqkv)
    write(gain, ogain)
    NB = L // 128
    for h in range(geo.H):
        band = shear(jnp.broadcast_to(bias[h : h + 1, :], (128, 512)), 1)[:, 128:512].astype(BF)
        strip[h, :, (NB - 2) * 128 : (NB + 1) * 128] = band
        far = (NB - 2) * 128
        strip[h, :, :far] = jnp.broadcast_to(bias[h : h + 1, 0:1], (128, far)).astype(BF)
        strip[h, :, (NB + 1) * 128 :] = jnp.broadcast_to(bias[h : h + 1, 511:512], (128, far)).astype(BF)
    run(1)
    gather_kv.relay()
    gather_kv.finish()
    run(1)
    write(KV, oKV)

    hd = I // geo.H
    per = 128 // hd
    valid = lax.broadcasted_iota(jnp.int32, (1, L), 1) < length[0]

    def pair(t, first):
        rows = slice(first, first + half)
        lanes = pl.ds(pl.multiple_of(t * 128, 128), 128)
        head = lax.broadcasted_iota(jnp.int32, (1, 128), 1) // hd
        keys = KV[:, lanes]
        values = KV[:, pl.ds(pl.multiple_of(I + t * 128, 128), 128)]
        queries = qkv[rows, lanes]
        outs_ = jnp.zeros((half, 128), F32)
        for e in range(per):
            h = t * per + e
            scores = dot(jnp.where(head == e, queries, jnp.zeros_like(queries)), keys, NT)
            shift = [
                strip[h, :, pl.ds(pl.multiple_of((NB - 1 - me.s * (T // 128) - b) * 128, 128), L)].astype(F32)
                for b in range(first // 128, (first + half) // 128)
            ]
            scores = jnp.where(valid, scores + jnp.concatenate(shift, axis=0), np.float32(NEGATIVE))
            top = jnp.max(scores, axis=-1, keepdims=True)
            probs = jnp.exp(scores - top)
            probs = probs * (1.0 / jnp.sum(probs, axis=-1, keepdims=True))
            copy = pltpu.make_async_copy(pst.at[e], oP.at[h, rows, :], psem.at[e])

            @pl.when((t > 0) | (first > 0))
            def _():
                copy.wait()

            pst[e] = probs
            copy.start()
            mine = dot(probs.astype(BF), values)
            outs_ = jnp.where(head == e, mine, outs_)
        mixed[rows, lanes] = outs_.astype(BF)

    for first in (0, half):
        rows = slice(first, first + half)
        for t in range(I // 128):
            pair(t, first)
            if t < (1 if first else 2):
                run(1)
        spread_mixed = dot(mixed[rows, :], pout[...]).astype(BF)
        total = xv[rows, :].astype(F32)
        for s in range(S):
            total += dot(spread_mixed[:, s * I4 : (s + 1) * I4], WA[s], NT)
        hid[rows, :] = total
        scale = lax.rsqrt(jnp.sum(total * total, axis=-1, keepdims=True) / np.float32(geo.D) + EPSILON)
        X2[pl.ds(pl.multiple_of(me.s * T + first, 16), half), :] = (total * scale * gain[1:2, :]).astype(BF)
        gather_x2[first // half].begin()
        run(0 if first else 1)
        if first == 0:
            gather_c[1].relay()
    for e in range(per):
        pltpu.make_async_copy(pst.at[e], oP.at[e, half:, :], psem.at[e]).wait()
    write(mixed, omixed)
    write(hid, ohid)
    for part_c in gather_c:
        part_c.finish()
    write(C, oC)
    gather_x2[0].relay()
    run(len(events) - 4)
    gather_x2[1].relay()
    run(len(events) - 3)
    for part_x2 in gather_x2:
        part_x2.finish()
    write(X2, oX2)

    def pcopy(n, k):
        return remote(part.at[0, n, k], got.at[n, k], ps.at[n, k], pr.at[n, k], me.dev(c=1 - me.c))

    def tokens_block(i, group):
        k = X - 1 - i % X
        e = i // X
        s = lax.rem(me.x + k, X) * 2 + lax.rem(1 + e + me.c, 2)
        rows = block(s, T)
        lanes = slice(*cuts[group])
        gate_w, up_w, down_w = (WFs[group].at[m] for m in range(3))
        xb = X2[rows, :]
        gate = dot(xb, gate_w[...])
        upward = dot(xb, up_w[...])
        back = dot(C[rows, :], down_w[...])
        value, slope = gelu_parts(gate)
        activated = (value * upward).astype(BF)
        first = (back * upward * slope).astype(BF)
        second = (back * value).astype(BF)
        act[0, rows, lanes] = first
        act[1, rows, lanes] = second
        act[2, rows, lanes] = activated
        terms = dot(first, gate_w[...], NT) + dot(second, up_w[...], NT), dot(activated, down_w[...], NT)
        for n, term in enumerate(terms):
            if group:
                term += part[e, n, k].astype(F32)
            part[e, n, k] = term.astype(BF)
        if group:

            @pl.when(e == 0)
            def _():
                for n in range(2):
                    pcopy(n, k).start()

            @pl.when(e == 1)
            def _():
                for n in range(2):
                    pcopy(n, k).wait_recv()
                    part[1, n, k] = (part[1, n, k].astype(F32) + got[n, k].astype(F32)).astype(BF)
                    pltpu.make_async_copy(part.at[1, n, k], opart.at[n, k], wsem.at[n, k]).start()

    for group in range(2):
        for r in range(geo.A):
            for p in others:
                if p // 3 == group:
                    ffn.ystep(r, p)

        def with_events(i):
            tokens_block(i, group)
            for n, event in enumerate(() if group else [events.pop(0) for _ in range(len(events))]):

                @pl.when(i == n)
                def _():
                    forward_on(*event)

        loop(2 * X, with_events)
        write(act.at[:, :, slice(*cuts[group])], oact.at[:, :, slice(*cuts[group])])
    for k in range(X):
        for n in range(2):
            pcopy(n, k).wait_send()
            pltpu.make_async_copy(part.at[1, n, k], opart.at[n, k], wsem.at[n, k]).wait()

    def finish(g):
        for k in range(X):
            s = lax.rem(me.x - k + X, X) * 2 + 1 - me.c
            here = held_a(s, g)
            ccopy(k, g, here, s).wait_send()
            if k:
                xcopy(k, g, here).wait_send()

    loop(dp, finish)
    att.drain(0)
    for p in others:
        ffn.drain(p)
    ffn.drain(special, (False, True), False)
    for copy in writes:
        copy.wait()


def forward(geo, *arrays):
    dma = pltpu.SemaphoreType.DMA
    S, N, F, T, L, I, H, X, I4 = geo.seq, geo.N, geo.F, geo.T, geo.L, geo.I, geo.H, geo.X, geo.I4
    per = 128 // (I // H)
    first = (F // 128 + 1) // 2 * 128
    out_shape = [
        ((T, N), BF), ((S, N, I4), BF), ((T, 3 * I), BF), ((L, 2 * I), BF), ((H, T, L), F32), ((T, I), BF),
        ((T, N), F32), ((L, N), BF), ((L, N), BF), ((3, L, F), BF), ((2, X, T, N), BF), ((8, N), F32),
    ]
    V = pltpu.VMEM
    scratch = [
        V((3, N, first), BF), V((3, N, F - first), BF), V((S, N, I4), BF), V((T, N), BF), V((L, N), BF), V((L, N), BF), V((L, 2 * I), BF),
        V((T, 3 * I), BF), V((H, 128, 2 * L - 128), BF), V((T, I), BF), V((T, N), F32),
        V((per, T // 2, L), F32), V((3, L, F), BF), V((2, 2, X, T, N), BF), V((2, X, T, N), BF), V((8, N), F32),
        V((2, geo.D, T), BF), V((3, geo.W, F), F32), V((4, geo.W, I4 // 4), F32), V((2, geo.W), F32), V((geo.TR, H), F32),
        V((geo.R - geo.W, I4), F32),
        V((I, S * I4), BF), V((geo.dp * 16, 512), BF),
        dma((11,)), dma((13,)), dma((per,)),
        dma((geo.NZ, 6)), dma((geo.NZ, 6)), dma((geo.NY, 6)), dma((geo.NY, 6)),
        dma((geo.NZ, 1)), dma((geo.NZ, 1)),
        dma((geo.NZ, 1)), dma((geo.NZ, 1)), dma((geo.NY, 1)), dma((geo.NY, 1)),
        dma((X - 1, geo.dp)), dma((X - 1, geo.dp)), dma((X, geo.dp)), dma((X, geo.dp)),
        dma((5, X - 1)), dma((5, X - 1)), dma((5, X)), dma((5, X)),
        dma((2, X)), dma((2, X)), dma((2, X)),
    ]
    return pl.pallas_call(
        functools.partial(forward_kernel, geo),
        out_shape=[jax.ShapeDtypeStruct(*v) for v in out_shape],
        in_specs=[pl.BlockSpec(memory_space=pltpu.SMEM)] + [pl.BlockSpec(memory_space=pl.ANY)] * (len(arrays) - 1),
        out_specs=[pl.BlockSpec(memory_space=pl.ANY)] * len(out_shape),
        scratch_shapes=scratch,
        compiler_params=pltpu.CompilerParams(collective_id=0, has_side_effects=True, vmem_limit_bytes=63 << 20),
        name="forward",
    )(*arrays)


class SeqScatter:
    def __init__(self, geo, me, part, cb, xb, cs, cr, xs, xr):
        self.__dict__.update(locals())

    def ccopy(self, k):
        me = self.me
        to = lax.rem(me.x + k, self.geo.X)
        return remote(self.part(to * 2 + 1 - me.c), self.cb(k), self.cs.at[k], self.cr.at[k], me.dev(c=1 - me.c))

    def xcopy(self, k):
        me = self.me
        to = lax.rem(me.x + k, self.geo.X)
        return remote(self.part(to * 2 + me.c), self.xb(k), self.xs.at[k - 1], self.xr.at[k - 1], me.dev(x=to))

    def to_core(self):
        for k in (*range(1, self.geo.X), 0):
            self.ccopy(k).start()

    def to_x(self):
        for k in range(1, self.geo.X):
            self.ccopy(k).wait_recv()
            out = self.part(lax.rem(self.me.x + k, self.geo.X) * 2 + self.me.c)
            out[...] = (out[...].astype(F32) + self.cb(k)[...].astype(F32)).astype(BF)
            self.xcopy(k).start()

    def meet(self):
        self.ccopy(0).wait_recv()
        total = self.part(self.me.s)[...].astype(F32) + self.cb(0)[...].astype(F32)
        for k in range(1, self.geo.X):
            self.xcopy(k).wait_recv()
            total += self.xb(k)[...].astype(F32)
        return total

    def drain(self):
        for k in range(self.geo.X):
            self.ccopy(k).wait_send()
            if k:
                self.xcopy(k).wait_send()


class DpScatter:
    def __init__(self, geo, me, part, ybuf, zbuf, ys, yr, zs, zr, finish, first_z=1 << 20, zbuf2=None, zs2=None, zr2=None):
        self.__dict__.update(locals())

    def owner(self, i):
        A, z = self.geo.A, self.me.z
        up, down = A - 1 - z, z
        both = jnp.minimum(up, down)
        half = i // 2
        early = jnp.where((i % 2 == 0) == (up >= down), A - 1 - half, half)
        late = jnp.where(up > down, A - 1 - (i - both), i - both)
        return jnp.where(i == A - 1, z, jnp.where(i < 2 * both, early, late))

    def ycopy(self, t, p):
        me = self.me
        return remote(
            self.part(p, t * 2 + 1 - me.y), self.ybuf(p, t), self.ys.at[t, p], self.yr.at[t, p], me.dev(y=1 - me.y)
        )

    def zparts(self, t, slot, p, other):
        if other:
            return self.zbuf2(p, slot), self.zs2.at[t, p - self.first_z], self.zr2.at[slot, p - self.first_z]
        return self.zbuf(p, slot), self.zs.at[t, p], self.zr.at[slot, p]

    def mine(self, t, p, other=False):
        return self.part(p, t * 2 + (1 - self.me.y if other else self.me.y))

    def zslot(self, up, t):
        return jnp.where(up, self.geo.A - 1 - t, self.geo.A - t)

    def zcopy(self, t, p, other=False):
        me = self.me
        up = t > me.z
        dst, ss, rs = self.zparts(t, self.zslot(up, t), p, other)
        return remote(self.mine(t, p, other), dst, ss, rs, me.dev(z=jnp.where(up, me.z + 1, me.z - 1)))

    def zarrive(self, up, t, p, other=False):
        here, ss, rs = self.zparts(t, self.zslot(up, t), p, other)
        remote(here, here, ss, rs, self.me.dev(y=1 - self.me.y)).wait_recv()
        return here[...].astype(F32)

    def ysend(self, i, p):
        self.ycopy(self.owner(i), p).start()

    def arrived(self, t, p, base, put, other=False):
        geo, me = self.geo, self.me

        @pl.when(me.z == 0)
        def _():
            put(base() + self.zarrive(False, t, p, other))

        @pl.when(me.z == geo.A - 1)
        def _():
            put(base() + self.zarrive(True, t, p, other))

        @pl.when((me.z > 0) & (me.z < geo.A - 1))
        def _():
            put(base() + self.zarrive(True, t, p, other) + self.zarrive(False, t, p, other))

    def onward(self, t, p, base, other=False, plain=False):
        geo, me = self.geo, self.me
        mine = self.mine(t, p, other)
        up = t > me.z
        comes = (up & (me.z > 0)) | (jnp.logical_not(up) & (me.z < geo.A - 1))

        @pl.when(comes)
        def _():
            mine[...] = (base() + self.zarrive(up, t, p, other)).astype(BF)

        if not plain:

            @pl.when(jnp.logical_not(comes))
            def _():
                mine[...] = base().astype(BF)

        self.zcopy(t, p, other).start()

    def event(self, i, p):
        t = self.owner(i)
        mine = self.mine(t, p)
        own = lambda: mine[...].astype(F32)
        if p >= self.first_z:
            theirs = self.mine(t, p, True)
            their = lambda: theirs[...].astype(F32)
            if i < self.geo.A - 1:
                self.onward(t, p, their, True, True)
                self.onward(t, p, own, False, True)
            else:
                self.arrived(t, p, their, lambda v: theirs.__setitem__(..., v.astype(BF)), True)
                self.ycopy(t, p).start()
            return
        self.ycopy(t, p).wait_recv()
        both = lambda: own() + self.ybuf(p, t)[...].astype(F32)
        if i == self.geo.A - 1:
            self.arrived(t, p, both, lambda v: self.finish(p, v))
        else:
            self.onward(t, p, both)

    def last(self, p):
        t = self.me.z
        mine = self.mine(t, p)
        self.ycopy(t, p).wait_recv()
        both = lambda: mine[...].astype(F32) + self.ybuf(p, t)[...].astype(F32)
        self.arrived(t, p, both, lambda v: self.finish(p, v))

    def drain(self, p, second=False):
        for i in range(self.geo.A):
            t = self.owner(i)
            if not second or i == self.geo.A - 1:
                self.ycopy(t, p).wait_send()
            if i < self.geo.A - 1:
                for other in (False, True) if second else (False,):
                    self.zcopy(t, p, other).wait_send()


def backward_kernel(
    geo, x_in, iWA, iqkv, iKV, iP, imixed, ihid, iX2, iC, iact, ipart, igain,
    of, oa, olayer, oinput,
    G, XC, act, yb, zb, WA, ayb, azb, cb, xb, xv, hid, qkv, KV, mixed, pk, px, pst, kcb, kxb, zb2,
    hgrad, gbias, extra, gain, packed, pout, onehot,
    local, psem, outs, pxs, pxr, kcs, kcr, kxs, kxr, acs, acr, axs, axr, ys, yr, zs, zr, zs2, zr2, ays, ayr, azs, azr,
):
    me = Place(geo)
    R, RH, NH, dp, X, T, N, I = geo.R, geo.RH, geo.NH, geo.dp, geo.X, geo.T, geo.N, geo.I
    I4, S, L, A, NP = geo.I4, geo.seq, geo.L, geo.A, geo.NP
    block = lambda i, n: pl.ds(pl.multiple_of(i * n, 16), n)
    dKV = act.at[0, :, : 2 * I]
    dM, dq = act.at[1, :T, :I], act.at[1, T : 2 * T, :I]
    half = S * I4 // 2
    rights = [act.at[2, : 2 * T, :half], act.at[2, 2 * T : 4 * T, :half]]
    lefts = XC.at[N : N + 2 * T, :]
    hlow = lefts.at[T:, :]
    ds = pk.at[0, :, : L + 256]
    loads = [
        (iact.at[2], act.at[2]), (iC, XC.at[L:, :]), (iact.at[0], act.at[0]), (iX2, XC.at[:L, :]), (iact.at[1], act.at[1]), (ipart.at[:, 0], pk), (ihid, hid), (igain, gain),
        (iWA, WA), (iKV, KV), (iqkv, qkv), (imixed, mixed), (x_in, xv),
    ]
    loads = [pltpu.make_async_copy(src, dst, local.at[i]) for i, (src, dst) in enumerate(loads)]
    for copy in loads:
        copy.start()
    hd = I // geo.H
    per = 128 // hd

    def pload(t, e):
        return pltpu.make_async_copy(iP.at[t * per + e], pst.at[e], psem.at[e])

    for e in range(per):
        pload(0, e).start()
    enter(geo, me)

    def pcopy(n, k):
        to = me.dev(x=lax.rem(me.x + k, X))
        return remote(ipart.at[n, k], px.at[n, k - 1], pxs.at[n, k - 1], pxr.at[n, k - 1], to)

    for n in range(2):
        for k in range(1, X):
            pcopy(n, k).start()

    def rows_of(g, p):
        return pl.ds(pl.multiple_of(g * R + (p % NH) * RH, 16), RH)

    def piece(buf, i, p):
        return buf.at[i, p // NH, pl.ds(pl.multiple_of((p % NH) * RH, 16), RH), :]

    def finish_f(p, value):
        of[p // NH, pl.ds(pl.multiple_of((p % NH) * RH, 16), RH), :] = value

    last = NP - 1
    ffn = DpScatter(
        geo, me, lambda p, g: G.at[p // NH, rows_of(g, p), :], lambda p, t: piece(yb, t, p),
        lambda p, i: piece(zb, i, p), ys, yr, zs, zr, finish_f,
        last, lambda p, i: zb2.at[i], zs2, zr2,
    )
    def weight_rows(i):
        t = ffn.owner(i)
        lanes = pl.ds(pl.multiple_of(t * 2 * R, 128), 2 * R)
        rows = pl.ds(pl.multiple_of(t * 2 * R, 16), 2 * R)
        for m in (2, 0, 1):
            if isinstance(i, int):
                for copy in loads[slice(*{2: (0, 2), 0: (2, 4), 1: (4, 5)}[m])]:
                    copy.wait()
            left = XC[:L, lanes] if m < 2 else XC[L:, lanes]
            G[m, rows, :] = dot(left, act[m], TN).astype(BF)

            def go(h):
                p = m * NH + h

                @pl.when((p < last) & ((i < A - 1) | (p < NP // 2)))
                def _():
                    ffn.ysend(i, p)

            loop(NH, go)


    edge = (me.z == 0) | (me.z == A - 1)
    queues = [(kind, [(i, p) for i in range(A) for p in (last, *range(last))]) for kind in (edge, jnp.logical_not(edge))]

    def run(*counts):
        for (kind, events), count in zip(queues, counts):
            now = [events.pop(0) for _ in range(min(count, len(events)))]
            if now:

                @pl.when(kind)
                def _():
                    for i, p in now:
                        ffn.event(i, p)

    weight_rows(0)
    run(1, 0)
    loop(A - 1, lambda i: weight_rows(i + 1))
    place_columns(geo, pout)
    place_buckets(geo, onehot)
    run(2, 0)

    for i in range(5, len(loads)):
        loads[i].wait()
    for k in range(1, X):
        pcopy(0, k).wait_recv()
    grad = pk[0].astype(F32)
    for k in range(1, X):
        grad += px[0, k - 1].astype(F32)
    hidden = hid[...]
    scale = lax.rsqrt(jnp.sum(hidden * hidden, axis=-1, keepdims=True) / np.float32(geo.D) + EPSILON)
    unit = hidden * scale
    gain_two = jnp.sum(grad * unit, axis=0, keepdims=True)
    pull = grad * gain[1:2, :]
    inner = jnp.sum(pull * unit, axis=-1, keepdims=True) / np.float32(geo.D)
    cot = XC[pl.ds(pl.multiple_of(L + me.s * T, 16), T), :].astype(F32)
    total = cot + scale * (pull - unit * inner)
    hgrad[...] = total
    hlow[...] = total.astype(BF)
    columns = jnp.concatenate([dot(hlow[...], WA[s]) for s in range(S)], axis=1).astype(BF)
    dM[...] = dot(columns, pout[...], NT).astype(BF)
    ds[...] = jnp.zeros_like(ds)
    gbias[...] = jnp.zeros_like(gbias)
    run(3, 1)

    def pair(t):
        lanes = pl.ds(pl.multiple_of(t * 128, 128), 128)
        vlanes = pl.ds(pl.multiple_of(I + t * 128, 128), 128)
        head = lax.broadcasted_iota(jnp.int32, (1, 128), 1) // hd
        keys, values, queries, back = KV[:, lanes], KV[:, vlanes], qkv[:, lanes], dM[:, lanes]
        zero = jnp.zeros_like(queries)
        q_grad = jnp.zeros((T, 128), F32)
        k_grad = jnp.zeros((L, 128), F32)
        v_grad = jnp.zeros((L, 128), F32)
        for e in range(per):
            h = t * per + e
            own_back = jnp.where(head == e, back, zero)
            pload(t, e).wait()
            probs = pst[e]
            prob_grad = dot(own_back, values, NT)
            both = jnp.sum(probs * prob_grad, axis=-1, keepdims=True)
            score = (probs * (prob_grad - both)).astype(BF)
            v_grad += dot(probs.astype(BF), own_back, TN)

            @pl.when(t + 1 < I // 128)
            def _():
                pload(t + 1, e).start()

            q_grad = jnp.where(head == e, dot(score, keys), q_grad)
            k_grad += dot(score, jnp.where(head == e, queries, zero), TN)
            ds[:, 128 : 128 + L] = score
            near = jnp.zeros((128, 384), F32)
            place = lax.broadcasted_iota(jnp.int32, (1, L), 1)
            low = jnp.zeros((1, 1), F32)
            high = jnp.zeros((1, 1), F32)
            for b in range(T // 128):
                row_block = me.s * (T // 128) + b
                near += ds[b * 128 : (b + 1) * 128, pl.ds(pl.multiple_of(row_block * 128, 128), 384)].astype(F32)
                sums = jnp.sum(score[b * 128 : (b + 1) * 128, :].astype(F32), axis=0, keepdims=True)
                low += jnp.sum(jnp.where(place < (row_block - 1) * 128, sums, 0.0), axis=-1, keepdims=True)
                high += jnp.sum(jnp.where(place >= (row_block + 2) * 128, sums, 0.0), axis=-1, keepdims=True)
            near = jnp.concatenate([jnp.zeros((128, 128), F32), near], axis=1)
            line = jnp.sum(shear(near, -1), axis=0, keepdims=True)
            spot = lax.broadcasted_iota(jnp.int32, (1, 512), 1)
            line += jnp.where(spot == 0, low, 0.0) + jnp.where(spot == 511, high, 0.0)
            gbias[pl.ds(h, 1), :] = line
        dq[:, lanes] = q_grad.astype(BF)
        dKV[:, lanes] = k_grad.astype(BF)
        dKV[:, vlanes] = v_grad.astype(BF)

    def key_scatter(i):
        lanes = slice(i * 128, (i + 1) * 128)
        return SeqScatter(
            geo, me, lambda s: dKV.at[block(s, T), lanes], lambda k: kcb.at[k, :, lanes], lambda k: kxb.at[k - 1, :, lanes],
            kcs.at[i], kcr.at[i], kxs.at[i], kxr.at[i],
        )

    pairs = I // 128
    scatters = [(key_scatter(t), key_scatter(pairs + t)) for t in range(pairs)]
    for t in range(pairs):
        pair(t)
        for one in scatters[t]:
            one.to_core()
        if t:
            for one in scatters[t - 1]:
                one.to_x()
        run(*((1, 1), (1, 1), (2, 1))[min(t, 2)])

    for k in range(1, X):
        pcopy(1, k).wait_recv()
    total = hid[...] + pk[1].astype(F32)
    for k in range(1, X):
        total += px[1, k - 1].astype(F32)
    packed[...] = pack(geo, total)
    layer_out = pltpu.make_async_copy(packed, olayer, outs.at[0])
    layer_out.start()
    for one in scatters[-1]:
        one.to_x()
    run(1, 1)
    tokens = xv[...].astype(F32)
    scale = lax.rsqrt(jnp.sum(tokens * tokens, axis=-1, keepdims=True) / np.float32(geo.D) + EPSILON)
    lefts[:T, :] = (tokens * scale * gain[0:1, :]).astype(BF)
    columns = dot(mixed[...], pout[...]).astype(BF)
    for i, right in enumerate(rights):
        right[T:, :] = columns[:, i * half : (i + 1) * half]
    run(2, 2)
    key_value = [jnp.concatenate([one[n].meet() for one in scatters], axis=1).astype(BF) for n in range(2)]
    run(0, 3)
    columns = jnp.zeros((T, S * I4), F32)
    for kind, value in enumerate((dq[...], *key_value)):
        columns += pltpu.roll(dot(value, pout[...]), S * I4 - (3 - kind) * (I4 // 4), 1)
    columns = columns.astype(BF)
    for i, right in enumerate(rights):
        right[:T, :] = columns[:, i * half : (i + 1) * half]
    grad = jnp.zeros((T, N), F32)
    for s in range(S):
        grad += dot(columns[:, s * I4 : (s + 1) * I4], WA[s], NT)
    unit = tokens * scale
    gain_one = jnp.sum(grad * unit, axis=0, keepdims=True)
    pull = grad * gain[0:1, :]
    inner = jnp.sum(pull * unit, axis=-1, keepdims=True) / np.float32(geo.D)
    layer_out.wait()
    packed[...] = pack(geo, hgrad[...] + scale * (pull - unit * inner))
    input_out = pltpu.make_async_copy(packed, oinput, outs.at[1])
    input_out.start()

    table = dot(onehot[...], gbias[...].astype(BF), NT)
    if I4 > 128:
        table = jnp.concatenate([table, jnp.zeros((dp * 16, I4 - 128), F32)], axis=1)
    extra[...] = table
    for g in range(dp):
        for e, line in enumerate((gain_one, gain_two)):
            at = g * 16 + 16 - geo.E + e
            extra[at : at + 1, :R] = line[:, g * R : (g + 1) * R]

    def part_g(s, g):
        return XC.at[block(g, R), pl.ds(pl.multiple_of(s * I4, 128), I4)]

    att = DpScatter(
        geo, me, lambda p, g: part_g(me.s, g), lambda p, t: ayb.at[t], lambda p, i: azb.at[i],
        ays, ayr, azs, azr, lambda p, value: oa.__setitem__(..., value),
    )
    def turn(j):
        t = att.owner(j // 2)
        return t * 2 + jnp.where(j % 2 == 0, 1 - me.y, me.y)

    def scatter(g):
        return SeqScatter(
            geo, me, lambda s: part_g(s, g), lambda k: cb.at[k, block(g, R), :], lambda k: xb.at[k - 1, block(g, R), :],
            acs.at[g], acr.at[g], axs.at[g], axr.at[g],
        )

    def attention_rows(i):
        t = att.owner(i)
        lanes = pl.ds(pl.multiple_of(t * 2 * R, 128), 2 * R)
        rows = pl.ds(pl.multiple_of(t * 2 * R, 16), 2 * R)
        for n, right in enumerate(rights):
            XC[rows, n * half : (n + 1) * half] = dot(lefts[:, lanes], right[...], TN).astype(BF)
        for y in range(2):
            g = t * 2 + y
            rows = pl.ds(pl.multiple_of(g * R + R - 16, 16), 16)
            more = extra[pl.ds(pl.multiple_of(g * 16, 16), 16), :]
            for s in range(S):
                lane = slice(s * I4, (s + 1) * I4)
                XC[rows, lane] = (XC[rows, lane].astype(F32) + more).astype(BF)
        scatter(t * 2 + 1 - me.y).to_core()
        scatter(t * 2 + me.y).to_core()

    for i in range(A):
        attention_rows(i)
        run((2, 0, 2, 1)[min(i, 3)], (3, 1, 1, 1)[min(i, 3)])
    held = [p for p in range(last) if p >= NP // 2]
    for j in range(dp):
        scatter(turn(j)).to_x()
    run(0, 1)
    for j in range(dp):
        g = turn(j)
        part_g(me.s, g)[...] = scatter(g).meet().astype(BF)
        if j % 2 == 0:
            att.ysend(j // 2, 0)
        elif held:
            ffn.ysend(A - 1, held.pop(0))
        if j >= 2:
            run(1, 1)
        if j % 2 and j >= 3:
            att.event((j - 3) // 2, 0)
    while held:
        ffn.ysend(A - 1, held.pop(0))
    att.event(A - 1, 0)
    run(*(len(events) for _, events in queues))
    ffn.last(last)

    for n in range(2):
        for k in range(1, X):
            pcopy(n, k).wait_send()
    for both in scatters:
        for one in both:
            one.drain()
    loop(dp, lambda g: scatter(g).drain())
    att.drain(0)
    loop(last, ffn.drain)
    ffn.drain(last, True)
    input_out.wait()


def backward(geo, *saved):
    dma = pltpu.SemaphoreType.DMA
    S, N, F, T, L, I, X, I4, A, R = geo.seq, geo.N, geo.F, geo.T, geo.L, geo.I, geo.X, geo.I4, geo.A, geo.R
    per = 128 // (I // geo.H)
    V = pltpu.VMEM
    scratch = [
        V((3, N, F), BF), V((2 * L, N), BF), V((3, L, F), BF), V((A, 3, R, F), BF), V((A + 1, 3, R, F), BF),
        V((S, N, I4), BF), V((A, R, I4), BF), V((A + 1, R, I4), BF),
        V((X, N, I4), BF), V((X - 1, N, I4), BF),
        V((T, N), BF), V((T, N), F32), V((T, 3 * I), BF), V((L, 2 * I), BF), V((T, I), BF),
        V((2, T, N), BF), V((2, X - 1, T, N), BF), V((per, T, L), F32),
        V((X, T, 2 * I), BF), V((X - 1, T, 2 * I), BF), V((A + 1, geo.RH, F), BF),
        V((T, N), F32), V((128, 512), F32), V((geo.dp * 16, I4), F32), V((8, N), F32), V((geo.D, T), BF),
        V((I, S * I4), BF), V((geo.dp * 16, 512), BF),
        dma((13,)), dma((per,)), dma((2,)),
        dma((2, X - 1)), dma((2, X - 1)), dma((2 * I // 128, X)), dma((2 * I // 128, X)), dma((2 * I // 128, X - 1)), dma((2 * I // 128, X - 1)),
        dma((geo.dp, X)), dma((geo.dp, X)), dma((geo.dp, X - 1)), dma((geo.dp, X - 1)),
        dma((A, geo.NP)), dma((A, geo.NP)), dma((A, geo.NP)), dma((A + 1, geo.NP)),
        dma((A, 1)), dma((A + 1, 1)),
        dma((A, 1)), dma((A, 1)), dma((A, 1)), dma((A + 1, 1)),
    ]
    return pl.pallas_call(
        functools.partial(backward_kernel, geo),
        out_shape=[
            jax.ShapeDtypeStruct((3, R, F), F32), jax.ShapeDtypeStruct((R, I4), F32),
            jax.ShapeDtypeStruct((geo.D, T), BF), jax.ShapeDtypeStruct((geo.D, T), BF),
        ],
        in_specs=[pl.BlockSpec(memory_space=pl.ANY)] * len(saved),
        out_specs=[pl.BlockSpec(memory_space=pltpu.VMEM)] * 2 + [pl.BlockSpec(memory_space=pl.ANY)] * 2,
        scratch_shapes=scratch,
        compiler_params=pltpu.CompilerParams(collective_id=2, has_side_effects=True, vmem_limit_bytes=63 << 20),
        name="backward",
    )(*saved)


def finish_kernel(geo, rows, features, layer, grad, *rest):
    outs, (held, blocks, main, query, keyval, output, gains, table, sem) = rest[:9], rest[9:]
    W, own = geo.W, geo.I4 // 4
    moves = [
        (rows, main, None), (layer, held.at[0], outs[0]), (grad, held.at[1], outs[1]),
        (features.at[0], blocks.at[0], outs[5].at[0]), (features.at[1], blocks.at[1], outs[5].at[1]),
        (features.at[2], blocks.at[2], outs[6]),
    ]
    arrive = [pltpu.make_async_copy(src, mid, sem.at[0, i]) for i, (src, mid, _) in enumerate(moves)]
    leave = [
        pltpu.make_async_copy(mid.at[:W, :] if i > 2 else mid, dst, sem.at[1, i])
        for i, (_, mid, dst) in enumerate(moves)
        if dst is not None
    ]
    for copy in arrive:
        copy.start()
    arrive[0].wait()
    query[...] = main[:W, :own]
    keyval[0] = main[:W, own : 2 * own]
    keyval[1] = main[:W, 2 * own : 3 * own]
    output[...] = main[:W, 3 * own :]
    gains[...] = main[geo.R - geo.E : geo.R - geo.TR, :W]
    table[...] = main[geo.R - geo.TR :, : geo.H]
    small = [(query, outs[2]), (keyval, outs[3]), (output, outs[4]), (gains, outs[7]), (table, outs[8])]
    small = [pltpu.make_async_copy(src, dst, sem.at[1, 6 + i]) for i, (src, dst) in enumerate(small)]
    for copy in small:
        copy.start()
    for copy, onward in zip(arrive[1:], leave):
        copy.wait()
        onward.start()
    for copy in small + leave:
        copy.wait()


def finish(geo, of, oa, layer, grad):
    W, own, F = geo.W, geo.I4 // 4, geo.F
    shapes = [
        (layer.shape, BF), (grad.shape, BF), ((W, own), F32), ((2, W, own), F32), ((W, own), F32), ((2, W, F), F32),
        ((W, F), F32), ((2, W), F32), ((geo.TR, geo.H), F32),
    ]
    V = pltpu.VMEM
    return pl.pallas_call(
        functools.partial(finish_kernel, geo),
        out_shape=[jax.ShapeDtypeStruct(*v) for v in shapes],
        in_specs=[pl.BlockSpec(memory_space=pl.ANY)] * 4,
        out_specs=[pl.BlockSpec(memory_space=pl.ANY)] * 9,
        scratch_shapes=[
            V((2, *layer.shape), BF), V((3, geo.R, F), F32), V((geo.R, geo.I4), F32),
            *[V(*shapes[i]) for i in (2, 3, 4, 7, 8)], pltpu.SemaphoreType.DMA((2, 11)),
        ],
        compiler_params=pltpu.CompilerParams(vmem_limit_bytes=63 << 20),
        name="finish",
    )(oa, of, layer, grad)


def spread_features(values, geo, width):
    lead = values.shape[:-1]
    blocks = values.reshape(*lead, geo.dp, width)
    return jnp.pad(blocks, [(0, 0)] * (len(lead) + 1) + [(0, geo.R - width)]).reshape(*lead, geo.dp * geo.R)


def pack_features(values, geo, width):
    lead = values.shape[:-1]
    return values.reshape(*lead, geo.dp, geo.R)[..., :width].reshape(*lead, geo.dp * width)


def general_path(
    axes, tokens, cotangent, lengths, w_query, w_key_value, w_output, w_gate_up, w_down, norm_gains, position_bias
):
    dp, seq = axes
    width, own_inner = w_query.shape
    table_rows, head_count = position_bias.shape
    geo = Geo(dp, seq, width, w_down.shape[1], 4 * own_inner, tokens.shape[1], head_count, table_rows)
    rows = geo.R
    model_width = geo.D
    bucket_count = table_rows * dp
    inner_width = geo.I
    head_dim = inner_width // head_count

    lanes = lambda v: jnp.pad(v, ((0, 0), (0, geo.I4 - v.shape[1])))
    wa = jnp.concatenate(
        [
            jnp.concatenate([w_query, w_key_value[0], w_key_value[1], w_output], axis=1).astype(BF),
            jnp.zeros((rows - width - geo.E, geo.I4), BF),
            lanes(norm_gains.astype(BF)),
            lanes(position_bias.astype(BF)),
        ],
        axis=0,
    )
    wf = jnp.pad(jnp.concatenate([w_gate_up, w_down[None]], axis=0).astype(BF), ((0, 0), (0, rows - width), (0, 0)))
    WF, WA = gather_weights(geo, wf, wa)

    blocks = WA[0].reshape(dp, rows, geo.I4)
    first_gain = blocks[:, rows - geo.E, :width].reshape(model_width).astype(F32)
    second_gain = blocks[:, rows - geo.E + 1, :width].reshape(model_width).astype(F32)
    table_full = blocks[:, rows - table_rows :, :head_count].reshape(bucket_count, head_count)
    real = WA.reshape(seq, dp, rows, 4, own_inner)[:, :, :width]
    parts = real.transpose(3, 1, 2, 0, 4).reshape(4, model_width, inner_width)
    query_full, keyval_full, output_full = parts[0], parts[1:3], parts[3]

    inputs = tokens[0].astype(jnp.float32)
    row_count = inputs.shape[0]
    normed = norm_scale(inputs, first_gain).astype(jnp.bfloat16)
    queries = jnp.dot(normed, query_full, preferred_element_type=jnp.float32).astype(jnp.bfloat16)
    projected = jnp.einsum(
        "td,sdi->sti", normed, keyval_full, preferred_element_type=jnp.float32
    ).astype(jnp.bfloat16)
    keys_all, values_all = (
        lax.all_gather(projected[0], "seq", axis=0, tiled=True),
        lax.all_gather(projected[1], "seq", axis=0, tiled=True),
    )
    incoming_low = cotangent[0]
    incoming = incoming_low.astype(jnp.float32)
    cot_all = lax.all_gather(spread_features(incoming_low, geo, width), "seq", axis=0, tiled=True)
    length_all = keys_all.shape[0]
    block_start = lax.axis_index("seq") * row_count
    query_pos = block_start + jnp.arange(row_count, dtype=jnp.int32)
    key_pos = jnp.arange(length_all, dtype=jnp.int32)
    buckets = bucket_ids(key_pos[None, :] - query_pos[:, None])
    bucket_range = jnp.arange(bucket_count, dtype=jnp.int32)
    onehot = (buckets[:, :, None] == bucket_range).astype(jnp.bfloat16)
    score_bias = jnp.einsum("tkb,bh->htk", onehot, table_full, preferred_element_type=jnp.float32)
    key_valid = key_pos < lengths[0]
    query_heads = queries.reshape(row_count, head_count, head_dim)
    key_heads = keys_all.reshape(length_all, head_count, head_dim)
    value_heads = values_all.reshape(length_all, head_count, head_dim)
    raw_scores = (
        jnp.einsum("thc,khc->htk", query_heads, key_heads, preferred_element_type=jnp.float32) + score_bias
    )
    scores = jnp.where(key_valid[None, None, :], raw_scores, NEGATIVE)
    probs = jax.nn.softmax(scores, axis=-1)
    probs_low = probs.astype(BF)
    mixed_heads = (
        jnp.einsum("htk,khc->thc", probs_low, value_heads, preferred_element_type=jnp.float32)
        .reshape(row_count, inner_width)
        .astype(jnp.bfloat16)
    )
    attended = jnp.einsum("tc,dc->td", mixed_heads, output_full, preferred_element_type=jnp.float32)
    hidden_one = inputs + attended
    normed_two = norm_scale(hidden_one, second_gain).astype(jnp.bfloat16)
    normed_two_all = lax.all_gather(spread_features(normed_two, geo, width), "seq", axis=0, tiled=True)

    gate = jnp.dot(normed_two_all, WF[0], preferred_element_type=F32)
    upward = jnp.dot(normed_two_all, WF[1], preferred_element_type=F32)
    activated = gated(gate, upward).astype(BF)
    down_term = jnp.einsum("tf,df->td", activated, WF[2], preferred_element_type=F32)
    down_weight_grad = jnp.einsum("td,tf->df", cot_all, activated, preferred_element_type=F32)
    activated_grad = jnp.dot(cot_all, WF[2], preferred_element_type=F32)
    unused_value, gate_pull = jax.vjp(gated, gate, upward)
    gate_grad, upward_grad = gate_pull(activated_grad)
    gate_grad, upward_grad = gate_grad.astype(BF), upward_grad.astype(BF)
    gate_weight_grad = jnp.einsum("td,tf->df", normed_two_all, gate_grad, preferred_element_type=F32)
    up_weight_grad = jnp.einsum("td,tf->df", normed_two_all, upward_grad, preferred_element_type=F32)
    normed_two_term = jnp.einsum("tf,df->td", gate_grad, WF[0], preferred_element_type=F32) + jnp.einsum(
        "tf,df->td", upward_grad, WF[1], preferred_element_type=F32
    )
    down_sum = lax.psum_scatter(down_term.astype(BF), "seq", scatter_dimension=0, tiled=True)
    normed_two_sum = lax.psum_scatter(normed_two_term.astype(BF), "seq", scatter_dimension=0, tiled=True)
    outputs = (hidden_one + pack_features(down_sum, geo, width).astype(F32)).astype(BF)[None]
    normed_two_grad = pack_features(normed_two_sum, geo, width).astype(F32)
    gf = jnp.stack([gate_weight_grad.astype(BF), up_weight_grad.astype(BF), down_weight_grad.astype(BF)])

    unused_two, second_pull = jax.vjp(norm_scale, hidden_one, second_gain)
    hidden_norm_grad, second_gain_grad = second_pull(normed_two_grad)
    hidden_grad = incoming + hidden_norm_grad
    hidden_low = hidden_grad.astype(jnp.bfloat16)
    output_weight_grad = jnp.einsum("td,tc->dc", hidden_low, mixed_heads, preferred_element_type=jnp.float32)
    mixed_grad = jnp.einsum("td,dc->tc", hidden_low, output_full, preferred_element_type=jnp.float32).astype(
        jnp.bfloat16
    )
    grad_heads = mixed_grad.reshape(row_count, head_count, head_dim)
    prob_grad = jnp.einsum("thc,khc->htk", grad_heads, value_heads, preferred_element_type=jnp.float32)
    inner_sum = jnp.sum(probs * prob_grad, axis=-1, keepdims=True)
    score_grad = (probs * (prob_grad - inner_sum)).astype(jnp.bfloat16)
    query_act_grad = (
        jnp.einsum("htk,khc->thc", score_grad, key_heads, preferred_element_type=jnp.float32)
        .reshape(row_count, inner_width)
        .astype(jnp.bfloat16)
    )
    key_piece = jnp.einsum(
        "htk,thc->khc", score_grad, query_heads, preferred_element_type=jnp.float32
    ).reshape(length_all, inner_width)
    value_piece = jnp.einsum(
        "htk,thc->khc", probs_low, grad_heads, preferred_element_type=jnp.float32
    ).reshape(length_all, inner_width)
    own_terms = lax.psum_scatter(
        jnp.concatenate([key_piece, value_piece], axis=1).astype(jnp.bfloat16),
        "seq",
        scatter_dimension=0,
        tiled=True,
    )
    keyval_act_grad = jnp.stack([own_terms[:, :inner_width], own_terms[:, inner_width:]])
    query_weight_grad = jnp.einsum("td,tc->dc", normed, query_act_grad, preferred_element_type=jnp.float32)
    keyval_weight_grad = jnp.einsum("td,stc->sdc", normed, keyval_act_grad, preferred_element_type=jnp.float32)
    normed_grad = jnp.einsum(
        "tc,dc->td", query_act_grad, query_full, preferred_element_type=jnp.float32
    ) + jnp.einsum("stc,sdc->td", keyval_act_grad, keyval_full, preferred_element_type=jnp.float32)
    unused_three, first_pull = jax.vjp(norm_scale, inputs, first_gain)
    input_norm_grad, first_gain_grad = first_pull(normed_grad)
    input_grad = (hidden_grad + input_norm_grad).astype(jnp.bfloat16)[None]
    table_grad = jnp.einsum("htk,tkb->bh", score_grad, onehot, preferred_element_type=jnp.float32)

    grads = jnp.stack(
        [query_weight_grad, keyval_weight_grad[0], keyval_weight_grad[1], output_weight_grad]
    ).reshape(4, dp, width, seq, own_inner)
    grads = grads.transpose(3, 1, 2, 0, 4).reshape(seq, dp, width, geo.I4).astype(BF)
    wide = lambda v: jnp.pad(v, ((0, 0), (0, 0), (0, geo.I4 - v.shape[2])))
    more = jnp.concatenate(
        [
            jnp.zeros((dp, rows - width - geo.E, geo.I4), F32),
            wide(first_gain_grad.reshape(dp, 1, width)),
            wide(second_gain_grad.reshape(dp, 1, width)),
            wide(table_grad.reshape(dp, table_rows, head_count)),
        ],
        axis=1,
    ).astype(BF)
    ga = jnp.concatenate([grads, jnp.broadcast_to(more, (seq, *more.shape))], axis=2).reshape(seq, dp * rows, geo.I4)
    of, oa = scatter_grads(geo, gf, ga)

    main = oa[:width]
    query_part = main[:, :own_inner]
    keyval_part = jnp.stack([main[:, own_inner : 2 * own_inner], main[:, 2 * own_inner : 3 * own_inner]])
    output_part = main[:, 3 * own_inner :]
    gain_part = oa[rows - geo.E : rows - table_rows, :width]
    table_part = oa[rows - table_rows :, :head_count]
    return (
        outputs,
        input_grad,
        query_part,
        keyval_part,
        output_part,
        of[:2, :width],
        of[2, :width],
        gain_part,
        table_part,
    )

def fused_path(
    axes, tokens, cotangent, lengths, w_query, w_key_value, w_output, w_gate_up, w_down, norm_gains, position_bias
):
    geo = Geo(*axes, w_query.shape[0], w_down.shape[1], 4 * w_query.shape[1], tokens.shape[1], *position_bias.shape[::-1])
    saved = forward(
        geo, lengths, tokens[0].T, cotangent[0].T, w_query, w_key_value, w_output, w_gate_up, w_down, norm_gains, position_bias
    )
    outs = finish(geo, *backward(geo, *saved))
    return outs[0].T[None], outs[1].T[None], *outs[2:]


def per_device(axes, *arrays):
    tokens, w_query, w_down, position_bias = arrays[0], arrays[3], arrays[7], arrays[9]
    geo = Geo(*axes, w_query.shape[0], w_down.shape[1], 4 * w_query.shape[1], tokens.shape[1], position_bias.shape[1],
              position_bias.shape[0])
    aligned = geo.W % 8 == 0 and geo.F % 128 == 0 and geo.I4 % 128 == 0 and 2 * geo.R % 128 == 0 and geo.T % 128 == 0 and geo.I % 128 == 0
    aligned = aligned and max(2 * geo.I, geo.seq * geo.I4 // 2) <= geo.F and 4 * geo.T <= geo.L and geo.N + 2 * geo.T <= 2 * geo.L and geo.L + 256 <= geo.N
    small = (3 * geo.F + geo.seq * geo.I4 + 2 * geo.L) * geo.N * 2 <= 24 << 20
    return (fused_path if aligned and small else general_path)(axes, *arrays)


def solution(mesh):
    in_specs = (
        P("dp", "seq", None),
        P("dp", "seq", None),
        P("dp"),
        P("dp", "seq"),
        P(None, "dp", "seq"),
        P("dp", "seq"),
        P(None, "dp", "seq"),
        P("dp", "seq"),
        P(None, "dp"),
        P("dp", None),
    )
    out_specs = (
        P("dp", "seq", None),
        P("dp", "seq", None),
        P("dp", "seq"),
        P(None, "dp", "seq"),
        P("dp", "seq"),
        P(None, "dp", "seq"),
        P("dp", "seq"),
        P(None, "dp"),
        P("dp", None),
    )
    return jax.shard_map(
        functools.partial(per_device, (mesh.shape["dp"], mesh.shape["seq"])), mesh=mesh, in_specs=in_specs, out_specs=out_specs, check_vma=False
    )
```

```python
import functools
import jax
import jax.numpy as jnp
import numpy as np
from jax import lax
from jax.experimental import pallas as pl
from jax.experimental.pallas import tpu as pltpu

from jax.sharding import PartitionSpec as P

MESH = pl.DeviceIdType.MESH
BF = jnp.bfloat16
F32 = jnp.float32


class Geo:
    def __init__(self, dp, seq, width, ff, inner4, tokens, heads, table_rows):
        self.dp, self.seq = dp, seq
        self.W, self.TR, self.E = width, table_rows, 2 + table_rows
        rows = -(-(width + self.E) // 16) * 16
        self.D, self.N, self.T, self.L = dp * width, dp * rows, tokens, seq * tokens
        self.I, self.H = inner4 // 4 * seq, heads
        self.B, self.A, self.X = 2, dp // 2, seq // 2
        self.R, self.F, self.I4 = rows, ff, inner4
        self.NH = 2 if rows % 32 == 0 else 1
        self.RH = rows // self.NH
        self.NP = 3 * self.NH
        self.NZ = 2 * (self.A - 1)
        self.NY = 2 * self.A - 1


class Place:
    def __init__(self, geo):
        d, s = lax.axis_index("dp"), lax.axis_index("seq")
        self.d, self.s = d, s
        self.z, self.y = d // 2, d % 2
        self.x, self.c = s // 2, s % 2

    def dev(self, z=None, y=None, x=None, c=None):
        z = self.z if z is None else z
        y = self.y if y is None else y
        x = self.x if x is None else x
        c = self.c if c is None else c
        return (z * 2 + y, x * 2 + c)


def remote(src, dst, ss, rs, dev):
    return pltpu.make_async_remote_copy(
        src_ref=src, dst_ref=dst, send_sem=ss, recv_sem=rs, device_id=dev, device_id_type=MESH
    )


def loop(n, body):
    def step(i, carry):
        body(i)
        return carry

    lax.fori_loop(0, n, step, 0)


def enter(geo, me, work=None):
    bar = pltpu.get_barrier_semaphore()

    def greet(dev):
        pl.semaphore_signal(bar, 1, device_id=dev, device_id_type=MESH)

    greet(me.dev(y=1 - me.y))
    greet(me.dev(c=1 - me.c))
    for k in range(1, geo.X):
        greet(me.dev(x=lax.rem(me.x + k, geo.X)))

    @pl.when(me.z > 0)
    def _():
        greet(me.dev(z=me.z - 1))

    @pl.when(me.z < geo.A - 1)
    def _():
        greet(me.dev(z=me.z + 1))

    count = 2 + (geo.X - 1) + (me.z > 0).astype(jnp.int32) + (me.z < geo.A - 1).astype(jnp.int32)
    if work is not None:
        work()
    pl.semaphore_wait(bar, count)


class LineGather:
    def __init__(self, geo, me, own, held, zs, zr, ys, yr, first_y=1 << 20, bzs=None, bzr=None):
        self.geo, self.me, self.own, self.held = geo, me, own, held
        self.zs, self.zr, self.ys, self.yr = zs, zr, ys, yr
        self.first_y, self.bzs, self.bzr = first_y, bzs, bzr

    def from_z(self, way, r):
        q = self.me.z - r if way == 0 else self.me.z + r
        return q, (q >= 0) if way == 0 else (q <= self.geo.A - 1)

    def sems(self, way, r, p, other):
        slot = way * (self.geo.A - 1) + r - 1
        if other:
            return self.bzs.at[slot, p - self.first_y], self.bzr.at[slot, p - self.first_y]
        return self.zs.at[slot, p], self.zr.at[slot, p]

    def zcopy(self, way, r, p, other=False):
        me, geo = self.me, self.geo
        q, there = self.from_z(way, r - 1)
        to = me.z + 1 if way == 0 else me.z - 1
        valid = ((me.z < geo.A - 1) if way == 0 else (me.z > 0)) & there
        here = self.held(p, q * 2 + (1 - me.y if other else me.y))
        src = self.own(p) if r == 1 and not other else here
        return remote(src, here, *self.sems(way, r, p, other), me.dev(z=to)), valid

    def zarrive(self, way, r, p, other=False):
        q, valid = self.from_z(way, r)
        here = self.held(p, q * 2 + (1 - self.me.y if other else self.me.y))
        return remote(here, here, *self.sems(way, r, p, other), self.me.dev(y=1 - self.me.y)), valid, q

    def yslot(self, way, r):
        return 1 + way * (self.geo.A - 1) + r - 1 if r else 0

    def ycopy(self, way, r, p):
        me, slot = self.me, self.yslot(way, r)
        q, _ = self.from_z(way, r)
        src = self.held(p, q * 2 + me.y) if r else self.own(p)
        return remote(src, self.held(p, q * 2 + me.y), self.ys.at[slot, p], self.yr.at[slot, p], me.dev(y=1 - me.y))

    def yarrive(self, way, r, p):
        me, slot = self.me, self.yslot(way, r)
        q, _ = self.from_z(way, r)
        here = self.held(p, q * 2 + 1 - me.y)
        return remote(here, here, self.ys.at[slot, p], self.yr.at[slot, p], me.dev(y=1 - me.y)), q

    def begin_y(self, p):
        self.ycopy(0, 0, p).start()

    def begin_z(self, p, other=False):
        for way in (0, 1):
            copy, valid = self.zcopy(way, 1, p, other)

            @pl.when(valid)
            def _():
                copy.start()

    def begin(self, p):
        self.begin_y(p)
        self.begin_z(p)

    def turn(self, p):
        self.yarrive(0, 0, p)[0].wait_recv()
        self.begin_z(p, True)

    def step(self, r, p, on_held=None, kinds=(False,), pass_y=True):
        for other in kinds:
            for way in (0, 1):
                copy, valid, q = self.zarrive(way, r, p, other)

                @pl.when(valid)
                def _():
                    copy.wait_recv()
                    if r < self.geo.A - 1:
                        onward, may = self.zcopy(way, r + 1, p, other)

                        @pl.when(may)
                        def _():
                            onward.start()

                    if pass_y:
                        self.ycopy(way, r, p).start()
                    if on_held is not None:
                        on_held(q * 2 + self.me.y)

    def step_both(self, r, p):
        self.step(r, p, None, (False, True), False)

    def ystep(self, r, p, on_held=None):
        for way in (0, 1) if r else (0,):
            copy, q = self.yarrive(way, r, p)

            def go():
                copy.wait_recv()
                if on_held is not None:
                    on_held(q * 2 + 1 - self.me.y)

            if r:
                pl.when(self.from_z(way, r)[1])(go)
            else:
                go()

    def drain(self, p, kinds=(False,), pass_y=True):
        self.ycopy(0, 0, p).wait_send()
        for r in range(1, self.geo.A):
            for way in (0, 1):
                for other in kinds:
                    copy, valid = self.zcopy(way, r, p, other)

                    @pl.when(valid)
                    def _():
                        copy.wait_send()

                if pass_y:

                    @pl.when(self.from_z(way, r)[1])
                    def _():
                        self.ycopy(way, r, p).wait_send()


class LineScatter:
    def __init__(self, geo, me, part, ybuf, zbuf, stage, zs, zr, ys, yr, finish):
        self.__dict__.update(locals())

    def turns(self):
        geo, me = self.geo, self.me
        for k in range(geo.A - 1):
            yield 0, k, geo.A - 1 - k, k < geo.A - 1 - me.z
            yield 1, k, k, k < me.z

    def slot(self, way, k):
        return way * (self.geo.A - 1) + k

    def ycopy(self, slot, t, p):
        me = self.me
        return remote(
            self.part(p, t * 2 + 1 - me.y),
            self.ybuf(p, t),
            self.ys.at[slot, p],
            self.yr.at[slot, p],
            me.dev(y=1 - me.y),
        )

    def zcopy(self, way, k, p):
        me = self.me
        to = me.z + 1 if way == 0 else me.z - 1
        slot = self.slot(way, k)
        return remote(
            self.stage(way, p, k), self.zbuf(way, p, k), self.zs.at[slot, p], self.zr.at[slot, p], me.dev(z=to)
        )

    def ysend(self, p, k):
        for way, kk, t, valid in self.turns():
            if kk == k:

                @pl.when(valid)
                def _():
                    self.ycopy(self.slot(way, kk), t, p).start()

    def ysend_own(self, p):
        self.ycopy(self.geo.NZ, self.me.z, p).start()

    def step(self, k, p):
        geo, me = self.geo, self.me
        for way, kk, t, valid in self.turns():
            if kk == k:

                @pl.when(valid)
                def _():
                    self.ycopy(self.slot(way, k), t, p).wait_recv()
                    total = self.part(p, t * 2 + me.y)[...].astype(F32) + self.ybuf(p, t)[...].astype(F32)
                    out = self.stage(way, p, k)
                    comes = me.z > 0 if way == 0 else me.z < geo.A - 1

                    @pl.when(comes)
                    def _():
                        self.zcopy(way, k, p).wait_recv()
                        out[...] = (total + self.zbuf(way, p, k)[...].astype(F32)).astype(BF)

                    @pl.when(jnp.logical_not(comes))
                    def _():
                        out[...] = total.astype(BF)

                    self.zcopy(way, k, p).start()

    def own(self, p):
        geo, me = self.geo, self.me
        self.ycopy(geo.NZ, me.z, p).wait_recv()
        total = self.part(p, me.z * 2 + me.y)[...].astype(F32) + self.ybuf(p, me.z)[...].astype(F32)
        kup = jnp.minimum(geo.A - 1 - me.z, geo.A - 2)
        kdown = jnp.minimum(me.z, geo.A - 2)

        def arrive(way, k):
            slot = way * (geo.A - 1) + k
            here = self.zbuf(way, p, k)
            remote(here, here, self.zs.at[slot, p], self.zr.at[slot, p], me.dev(y=1 - me.y)).wait_recv()
            return here[...].astype(F32)

        @pl.when(me.z == 0)
        def _():
            self.finish(p, total + arrive(1, kdown))

        @pl.when(me.z == geo.A - 1)
        def _():
            self.finish(p, total + arrive(0, kup))

        @pl.when((me.z > 0) & (me.z < geo.A - 1))
        def _():
            self.finish(p, total + arrive(0, kup) + arrive(1, kdown))

    def drain(self, p):
        for way, k, t, valid in self.turns():

            @pl.when(valid)
            def _():
                self.ycopy(self.slot(way, k), t, p).wait_send()
                self.zcopy(way, k, p).wait_send()

        self.ycopy(self.geo.NZ, self.me.z, p).wait_send()


NEGATIVE = -1e30
EPSILON = 1e-06
LIMITS = (12, 16, 23, 32, 46, 64, 91)


def bucket_ids(offsets):
    distance = jnp.abs(offsets)
    larger = 8 + sum(((distance >= threshold).astype(jnp.int32) for threshold in LIMITS))
    nearby = jnp.where(distance < 8, distance, larger)
    return jnp.where(offsets > 0, 16, 0) + nearby


def norm_scale(values, gain_vector):
    return (
        values
        * lax.rsqrt(jnp.mean(values * values, axis=-1, keepdims=True) + EPSILON)
        * gain_vector
    )


def gated(gate_value, upward):
    return jax.nn.gelu(gate_value, approximate=True) * upward


def gather_kernel(geo, wf, wa, WF, WA, local, zs, zr, ys, yr, azs, azr, ays, ayr, xs, xr, cs, cr):
    me = Place(geo)
    R, RH, NH, dp, X = geo.R, geo.RH, geo.NH, geo.dp, geo.X
    mine = [
        pltpu.make_async_copy(wf, WF.at[:, pl.ds(pl.multiple_of(me.d * R, 16), R), :], local.at[0]),
        pltpu.make_async_copy(wa, WA.at[me.s, pl.ds(pl.multiple_of(me.d * R, 16), R), :], local.at[1]),
    ]
    for copy in mine:
        copy.start()
    enter(geo, me)

    def own_f(p):
        return wf.at[p // NH, pl.ds(pl.multiple_of((p % NH) * RH, 16), RH), :]

    def held_f(p, g):
        return WF.at[p // NH, pl.ds(pl.multiple_of(g * R + (p % NH) * RH, 16), RH), :]

    def held_a(s, g):
        return WA.at[s, pl.ds(pl.multiple_of(g * R, 16), R), :]

    ffn = LineGather(geo, me, own_f, held_f, zs, zr, ys, yr)
    att = LineGather(geo, me, lambda p: wa, lambda p, g: held_a(me.s, g), azs, azr, ays, ayr)

    def xcopy(k, g, src):
        to = lax.rem(me.x + k, X)
        return remote(src, held_a(me.s, g), xs.at[k - 1, g], xr.at[k - 1, g], me.dev(x=to))

    def xarrive(k, g):
        src_x = lax.rem(me.x - k + X, X)
        here = held_a(src_x * 2 + me.c, g)
        return remote(here, here, xs.at[k - 1, g], xr.at[k - 1, g], me.dev(c=1 - me.c)), here

    def ccopy(k, g, src, s):
        return remote(src, held_a(s, g), cs.at[k, g], cr.at[k, g], me.dev(c=1 - me.c))

    def spread(g, src=None):
        src = held_a(me.s, g) if src is None else src
        for k in range(1, X):
            xcopy(k, g, src).start()
        ccopy(0, g, src, me.s).start()

    att.begin(0)
    spread(me.d, wa)
    loop(geo.NP, ffn.begin)
    att.ystep(0, 0, spread)
    for r in range(1, geo.A):
        att.step(r, 0, spread)
        att.ystep(r, 0, spread)

    def from_x(g):
        for k in range(1, X):
            copy, here = xarrive(k, g)
            copy.wait_recv()
            ccopy(k, g, here, lax.rem(me.x - k + X, X) * 2 + me.c).start()

    loop(dp, from_x)
    for r in range(1, geo.A):
        loop(geo.NP, lambda p: ffn.step(r, p))
    for r in range(geo.A):
        loop(geo.NP, lambda p: ffn.ystep(r, p))

    def finish(g):
        for k in range(X):
            s = lax.rem(me.x - k + X, X) * 2 + 1 - me.c
            here = held_a(s, g)
            remote(here, here, cs.at[k, g], cr.at[k, g], me.dev(c=1 - me.c)).wait_recv()
            ccopy(k, g, here, s).wait_send()
            if k:
                xcopy(k, g, here).wait_send()

    loop(dp, finish)
    att.drain(0)
    loop(geo.NP, ffn.drain)
    for copy in mine:
        copy.wait()


def scatter_kernel(
    geo, gf, ga, of, oa, yb, zb, st, cb, xb, xst, pa, ayb, azb, ast,
    zs, zr, ys, yr, azs, azr, ays, ayr, xs, xr, cs, cr,
):
    me = Place(geo)
    R, RH, NH, dp, X, A = geo.R, geo.RH, geo.NH, geo.dp, geo.X, geo.A
    enter(geo, me)

    def rows(g, p):
        return pl.ds(pl.multiple_of(g * R + (p % NH) * RH, 16), RH)

    def piece(buf, i, p):
        return buf.at[i, p // NH, pl.ds(pl.multiple_of((p % NH) * RH, 16), RH), :]

    def finish_f(p, value):
        of[p // NH, pl.ds(pl.multiple_of((p % NH) * RH, 16), RH), :] = value

    ffn = LineScatter(
        geo, me,
        lambda p, g: gf.at[p // NH, rows(g, p), :],
        lambda p, t: piece(yb, t, p),
        lambda way, p, k: piece(zb, way * (A - 1) + k, p),
        lambda way, p, k: piece(st, way * (A - 1) + k, p),
        zs, zr, ys, yr, finish_f,
    )

    def block(g):
        return pl.ds(pl.multiple_of(g * R, 16), R)

    def finish_a(p, value):
        oa[...] = value

    att = LineScatter(
        geo, me,
        lambda p, g: pa.at[block(g), :],
        lambda p, t: ayb.at[t],
        lambda way, p, k: azb.at[way * (A - 1) + k],
        lambda way, p, k: ast.at[way * (A - 1) + k],
        azs, azr, ays, ayr, finish_a,
    )

    def ccopy(k, g):
        to_x = lax.rem(me.x + k, X)
        return remote(
            ga.at[to_x * 2 + 1 - me.c, block(g), :], cb.at[k, block(g), :], cs.at[k, g], cr.at[k, g], me.dev(c=1 - me.c)
        )

    def xcopy(k, g):
        return remote(
            xst.at[k - 1, block(g), :], xb.at[k - 1, block(g), :], xs.at[k - 1, g], xr.at[k - 1, g],
            me.dev(x=lax.rem(me.x + k, X)),
        )

    def to_core(g):
        for k in (*range(1, X), 0):
            ccopy(k, g).start()

    def to_x(g):
        for k in range(1, X):
            ccopy(k, g).wait_recv()
            s = lax.rem(me.x + k, X) * 2 + me.c
            xst[k - 1, block(g), :] = (
                ga[s, block(g), :].astype(F32) + cb[k, block(g), :].astype(F32)
            ).astype(BF)
            xcopy(k, g).start()

    def meet(g):
        ccopy(0, g).wait_recv()
        total = ga[me.s, block(g), :].astype(F32) + cb[0, block(g), :].astype(F32)
        for k in range(1, X):
            xcopy(k, g).wait_recv()
            total += xb[k - 1, block(g), :].astype(F32)
        pa[block(g), :] = total.astype(BF)

    def free(g):
        for k in range(X):
            ccopy(k, g).wait_send()
            if k:
                xcopy(k, g).wait_send()

    for k in range(A - 1):
        loop(geo.NP, lambda p: ffn.ysend(p, k))
    loop(geo.NP, ffn.ysend_own)
    loop(dp, to_core)
    loop(dp, to_x)
    for k in range(A - 1):
        loop(geo.NP, lambda p: ffn.step(k, p))
    loop(geo.NP, ffn.own)
    loop(dp, meet)
    for k in range(A - 1):
        att.ysend(0, k)
    att.ysend_own(0)
    for k in range(A - 1):
        att.step(k, 0)
    att.own(0)
    loop(dp, free)
    att.drain(0)
    loop(geo.NP, ffn.drain)


def gather_weights(geo, wf, wa):
    dma = pltpu.SemaphoreType.DMA
    sems = [
        dma((2,)),
        dma((geo.NZ, geo.NP)), dma((geo.NZ, geo.NP)), dma((geo.NY, geo.NP)), dma((geo.NY, geo.NP)),
        dma((geo.NZ, 1)), dma((geo.NZ, 1)), dma((geo.NY, 1)), dma((geo.NY, 1)),
        dma((geo.X - 1, geo.dp)), dma((geo.X - 1, geo.dp)), dma((geo.X, geo.dp)), dma((geo.X, geo.dp)),
    ]
    return pl.pallas_call(
        functools.partial(gather_kernel, geo),
        out_shape=(
            jax.ShapeDtypeStruct((3, geo.dp * geo.R, geo.F), BF),
            jax.ShapeDtypeStruct((geo.seq, geo.dp * geo.R, geo.I4), BF),
        ),
        in_specs=[pl.BlockSpec(memory_space=pl.ANY)] * 2,
        out_specs=[pl.BlockSpec(memory_space=pl.ANY)] * 2,
        scratch_shapes=sems,
        compiler_params=pltpu.CompilerParams(collective_id=0, has_side_effects=True, vmem_limit_bytes=48 << 20),
        name="gather_weights",
    )(wf, wa)


def scatter_grads(geo, gf, ga):
    dma = pltpu.SemaphoreType.DMA
    n, X, A, R = geo.dp * geo.R, geo.X, geo.A, geo.R
    scratch = [
        pltpu.VMEM((A, 3, R, geo.F), BF), pltpu.VMEM((geo.NZ, 3, R, geo.F), BF), pltpu.VMEM((geo.NZ, 3, R, geo.F), BF),
        pltpu.VMEM((X, n, geo.I4), BF), pltpu.VMEM((X - 1, n, geo.I4), BF), pltpu.VMEM((X - 1, n, geo.I4), BF),
        pltpu.VMEM((n, geo.I4), BF),
        pltpu.VMEM((A, R, geo.I4), BF), pltpu.VMEM((geo.NZ, R, geo.I4), BF), pltpu.VMEM((geo.NZ, R, geo.I4), BF),
        dma((geo.NZ, geo.NP)), dma((geo.NZ, geo.NP)), dma((geo.NZ + 1, geo.NP)), dma((geo.NZ + 1, geo.NP)),
        dma((geo.NZ, 1)), dma((geo.NZ, 1)), dma((geo.NZ + 1, 1)), dma((geo.NZ + 1, 1)),
        dma((X - 1, geo.dp)), dma((X - 1, geo.dp)), dma((X, geo.dp)), dma((X, geo.dp)),
    ]
    return pl.pallas_call(
        functools.partial(scatter_kernel, geo),
        out_shape=(
            jax.ShapeDtypeStruct((3, R, geo.F), F32),
            jax.ShapeDtypeStruct((R, geo.I4), F32),
        ),
        in_specs=[pl.BlockSpec(memory_space=pltpu.VMEM)] * 2,
        out_specs=[pl.BlockSpec(memory_space=pltpu.VMEM)] * 2,
        scratch_shapes=scratch,
        compiler_params=pltpu.CompilerParams(collective_id=1, has_side_effects=True, vmem_limit_bytes=60 << 20),
        name="scatter_grads",
    )(gf, ga)


class SeqGather:
    def __init__(self, geo, me, held, xs, xr, cs, cr):
        self.geo, self.me, self.held = geo, me, held
        self.xs, self.xr, self.cs, self.cr = xs, xr, cs, cr

    def ccopy(self, k):
        me, X = self.me, self.geo.X
        here = self.held(lax.rem(me.x - k + X, X) * 2 + me.c)
        return remote(here, here, self.cs.at[k], self.cr.at[k], me.dev(c=1 - me.c))

    def xcopy(self, k):
        me = self.me
        here = self.held(me.s)
        return remote(here, here, self.xs.at[k - 1], self.xr.at[k - 1], me.dev(x=lax.rem(me.x + k, self.geo.X)))

    def begin(self):
        for k in range(1, self.geo.X):
            self.xcopy(k).start()
        self.ccopy(0).start()

    def relay(self):
        for k in range(1, self.geo.X):
            self.xcopy(k).wait_recv()
            self.ccopy(k).start()

    def finish(self):
        for k in range(self.geo.X):
            self.ccopy(k).wait_recv()
            self.ccopy(k).wait_send()
            if k:
                self.xcopy(k).wait_send()


def dot(a, b, dims=((1,), (0,))):
    return lax.dot_general(a, b, (dims, ((), ())), preferred_element_type=F32)


NT = ((1,), (1,))
TN = ((0,), (0,))


def place_columns(geo, out):
    own = geo.I4 // 4
    c = lax.broadcasted_iota(jnp.int32, out.shape, 0)
    j = lax.broadcasted_iota(jnp.int32, out.shape, 1)
    to = c + 3 * own
    for s in range(1, geo.seq):
        to += jnp.where(c >= s * own, 3 * own, 0)
    out[...] = jnp.where(j == to, 1.0, 0.0).astype(BF)


def place_buckets(geo, out):
    row = lax.broadcasted_iota(jnp.int32, out.shape, 0)
    at = row % 16 - (16 - geo.TR)
    bucket = bucket_ids(lax.broadcasted_iota(jnp.int32, out.shape, 1) - 256)
    out[...] = jnp.where((at >= 0) & (bucket == row // 16 * geo.TR + at), 1.0, 0.0).astype(BF)


def spread(geo, value):
    value = value.astype(F32)
    gap = jnp.zeros((geo.R - geo.W, value.shape[1]), F32)
    parts = [v for g in range(geo.dp) for v in (value[g * geo.W : (g + 1) * geo.W], gap)]
    return jnp.concatenate(parts, axis=0).T.astype(BF)


def pack(geo, value):
    value = value.T
    return jnp.concatenate([value[g * geo.R : g * geo.R + geo.W] for g in range(geo.dp)], axis=0).astype(BF)


def shear(value, sign):
    rows, lanes = value.shape
    row = lax.broadcasted_iota(jnp.int32, (rows, 1), 0)
    bit = 1
    while bit < rows:
        moved = pltpu.roll(value, bit if sign > 0 else lanes - bit, 1)
        value = jnp.where((row & bit) != 0, moved, value)
        bit *= 2
    return value


def gelu_parts(g):
    k0 = np.float32(np.sqrt(2 / np.pi))
    t = jnp.tanh(k0 * (g + np.float32(0.044715) * (g * g * g)))
    half = 0.5 * (1.0 + t)
    slope = half + 0.5 * g * (1.0 - t * t) * (k0 * (1.0 + np.float32(3 * 0.044715) * (g * g)))
    return g * half, slope


def forward_kernel(
    geo, length_in, x_in, c_in, wq, wkv, wo, wgu, wd, norm_gains, position_bias,
    oX, oWA, oqkv, oKV, oP, omixed, ohid, oX2, oC, oact, opart, ogain,
    WF0, WF1, WA, xv, C, X2, KV, qkv, strip, mixed, hid, pst, act, part, got, gain, raw, wst, ast, gst, bst, ex, pout, onehot, length,
    local, outs, psem, zs, zr, ys, yr, bzs, bzr, azs, azr, ays, ayr, xs, xr, cs, cr, gxs, gxr, gcs, gcr, ps, pr, wsem, asem,
):
    me = Place(geo)
    R, RH, NH, dp, X, T, N, I = geo.R, geo.RH, geo.NH, geo.dp, geo.X, geo.T, geo.N, geo.I
    I4, S, L = geo.I4, geo.seq, geo.L
    block = lambda i, n: pl.ds(pl.multiple_of(i * n, 16), n)
    loads = [
        (wq, ast.at[0]), (wkv.at[0], ast.at[1]), (wkv.at[1], ast.at[2]), (wo, ast.at[3]), (norm_gains, gst),
        (position_bias, bst), (wgu.at[0], wst.at[0]), (wgu.at[1], wst.at[1]), (wd, wst.at[2]), (x_in, raw.at[0]),
        (c_in, raw.at[1]), (length_in, length),
    ]
    loads = [pltpu.make_async_copy(src, dst, local.at[i]) for i, (src, dst) in enumerate(loads)]
    for copy in loads:
        copy.start()
    W, E = geo.W, geo.E

    def own_attention():
        ex[...] = jnp.zeros_like(ex)
        for copy in loads[:6]:
            copy.wait()
        ex[R - W - E : R - W - E + 2, :W] = gst[...]
        ex[R - W - E + 2 :, : geo.H] = bst[...]
        columns = jnp.concatenate([ast[k] for k in range(4)], axis=1)
        WA[me.s, block(me.d, R), :] = jnp.concatenate([columns, ex[...]], axis=0).astype(BF)

    enter(geo, me, own_attention)

    WFs = (WF0, WF1)
    cuts = ((0, WF0.shape[2]), (WF0.shape[2], geo.F))

    def held_f(p, g):
        return WFs[p // 3].at[p % 3, block(g, R), :]

    def held_a(s, g):
        return WA.at[s, block(g, R), :]

    special = 2
    others = [p for p in range(6) if p != special]
    ffn = LineGather(geo, me, lambda p: held_f(p, me.d), held_f, zs, zr, ys, yr, special, bzs, bzr)
    att = LineGather(geo, me, lambda p: held_a(me.s, me.d), lambda p, g: held_a(me.s, g), azs, azr, ays, ayr)

    def xcopy(k, g, src):
        to = lax.rem(me.x + k, X)
        return remote(src, held_a(me.s, g), xs.at[k - 1, g], xr.at[k - 1, g], me.dev(x=to))

    def xarrive(k, g):
        src_x = lax.rem(me.x - k + X, X)
        here = held_a(src_x * 2 + me.c, g)
        return remote(here, here, xs.at[k - 1, g], xr.at[k - 1, g], me.dev(c=1 - me.c)), here

    def ccopy(k, g, src, s):
        return remote(src, held_a(s, g), cs.at[k, g], cr.at[k, g], me.dev(c=1 - me.c))

    def share(g):
        src = held_a(me.s, g)
        for k in range(1, X):
            xcopy(k, g, src).start()
        ccopy(0, g, src, me.s).start()

    half = T // 2

    def seq_gather(i, ref, first, count):
        held = lambda s: ref.at[pl.ds(pl.multiple_of(s * T + first, 16), count), :]
        return SeqGather(geo, me, held, gxs.at[i], gxr.at[i], gcs.at[i], gcr.at[i])

    gather_kv = seq_gather(0, KV, 0, T)
    gather_x2 = [seq_gather(1, X2, 0, half), seq_gather(2, X2, half, half)]
    gather_c = [seq_gather(3, C, 0, half), seq_gather(4, C, half, half)]

    att.begin(0)
    share(me.d)
    for m in range(3):
        loads[6 + m].wait()
        for ref, cut in zip(WFs, cuts):
            lanes = slice(*cut)
            own = jnp.concatenate([wst[m, :, lanes], jnp.zeros((R - W, cut[1] - cut[0]), F32)], axis=0)
            ref[m, block(me.d, R), :] = own.astype(BF)
    ffn.begin_y(special)
    for p in range(6):
        if p == special:
            ffn.begin_z(p)
        else:
            ffn.begin(p)
    events = [(r, p) for r in range(1, geo.A) for p in range(6)]

    def forward_on(r, p):
        if p == special:
            ffn.step_both(r, p)
        else:
            ffn.step(r, p)

    def run(count):
        for _ in range(min(count, len(events))):
            forward_on(*events.pop(0))

    att.ystep(0, 0, share)
    for r in range(1, geo.A):
        att.step(r, 0, share)
        att.ystep(r, 0, share)
    ffn.turn(special)
    place_columns(geo, pout)
    place_buckets(geo, onehot)
    for copy in loads[9:]:
        copy.wait()
    xv[...] = spread(geo, raw[0])
    C[block(me.s, T), :] = spread(geo, raw[1])
    gather_c[0].begin()

    def from_x(g):
        for k in range(1, X):
            copy, here = xarrive(k, g)
            copy.wait_recv()
            ccopy(k, g, here, lax.rem(me.x - k + X, X) * 2 + me.c).start()

    for g in range(dp):
        from_x(g)
        if g >= 3:
            run(1)

    def settle(g):
        for k in range(X):
            s = lax.rem(me.x - k + X, X) * 2 + 1 - me.c
            here = held_a(s, g)
            remote(here, here, cs.at[k, g], cr.at[k, g], me.dev(c=1 - me.c)).wait_recv()

    loop(dp, settle)

    extra = jnp.concatenate([WA[0, g * R + R - 16 : g * R + R, :] for g in range(dp)], axis=0)
    lines = extra.astype(F32)
    gain[...] = jnp.zeros_like(gain)
    for g in range(dp):
        for e in range(2):
            at = g * 16 + 16 - E + e
            gain[e : e + 1, g * R : (g + 1) * R] = lines[at : at + 1, :R]
    bias = dot(extra[:, :128], onehot[...], TN)

    inputs = xv[...].astype(F32)
    scale = lax.rsqrt(jnp.sum(inputs * inputs, axis=-1, keepdims=True) / np.float32(geo.D) + EPSILON)
    normed = (inputs * scale * gain[0:1, :]).astype(BF)
    columns = jnp.concatenate([dot(normed, WA[s]) for s in range(S)], axis=1)
    for kind in (1, 2, 0):
        moved = pltpu.roll(columns, (3 - kind) * (I4 // 4), 1).astype(BF)
        qkv[:, kind * I : (kind + 1) * I] = dot(moved, pout[...], NT).astype(BF)
        if kind == 2:
            KV[block(me.s, T), :] = qkv[:, I:]
            gather_kv.begin()
            gather_c[1].begin()
    gather_c[0].relay()
    run(1)
    writes = []

    def write(src, dst):
        copy = pltpu.make_async_copy(src, dst, outs.at[len(writes)])
        copy.start()
        writes.append(copy)

    write(xv, oX)
    write(WA, oWA)
    write(qkv, oqkv)
    write(gain, ogain)
    NB = L // 128
    for h in range(geo.H):
        band = shear(jnp.broadcast_to(bias[h : h + 1, :], (128, 512)), 1)[:, 128:512].astype(BF)
        strip[h, :, (NB - 2) * 128 : (NB + 1) * 128] = band
        far = (NB - 2) * 128
        strip[h, :, :far] = jnp.broadcast_to(bias[h : h + 1, 0:1], (128, far)).astype(BF)
        strip[h, :, (NB + 1) * 128 :] = jnp.broadcast_to(bias[h : h + 1, 511:512], (128, far)).astype(BF)
    run(1)
    gather_kv.relay()
    gather_kv.finish()
    run(1)
    write(KV, oKV)

    hd = I // geo.H
    per = 128 // hd
    valid = lax.broadcasted_iota(jnp.int32, (1, L), 1) < length[0]

    def pair(t, first):
        rows = slice(first, first + half)
        lanes = pl.ds(pl.multiple_of(t * 128, 128), 128)
        head = lax.broadcasted_iota(jnp.int32, (1, 128), 1) // hd
        keys = KV[:, lanes]
        values = KV[:, pl.ds(pl.multiple_of(I + t * 128, 128), 128)]
        queries = qkv[rows, lanes]
        outs_ = jnp.zeros((half, 128), F32)
        for e in range(per):
            h = t * per + e
            scores = dot(jnp.where(head == e, queries, jnp.zeros_like(queries)), keys, NT)
            shift = [
                strip[h, :, pl.ds(pl.multiple_of((NB - 1 - me.s * (T // 128) - b) * 128, 128), L)].astype(F32)
                for b in range(first // 128, (first + half) // 128)
            ]
            scores = jnp.where(valid, scores + jnp.concatenate(shift, axis=0), np.float32(NEGATIVE))
            top = jnp.max(scores, axis=-1, keepdims=True)
            probs = jnp.exp(scores - top)
            probs = probs * (1.0 / jnp.sum(probs, axis=-1, keepdims=True))
            copy = pltpu.make_async_copy(pst.at[e], oP.at[h, rows, :], psem.at[e])

            @pl.when((t > 0) | (first > 0))
            def _():
                copy.wait()

            pst[e] = probs
            copy.start()
            mine = dot(probs.astype(BF), values)
            outs_ = jnp.where(head == e, mine, outs_)
        mixed[rows, lanes] = outs_.astype(BF)

    for first in (0, half):
        rows = slice(first, first + half)
        for t in range(I // 128):
            pair(t, first)
            if t < (1 if first else 2):
                run(1)
        spread_mixed = dot(mixed[rows, :], pout[...]).astype(BF)
        total = xv[rows, :].astype(F32)
        for s in range(S):
            total += dot(spread_mixed[:, s * I4 : (s + 1) * I4], WA[s], NT)
        hid[rows, :] = total
        scale = lax.rsqrt(jnp.sum(total * total, axis=-1, keepdims=True) / np.float32(geo.D) + EPSILON)
        X2[pl.ds(pl.multiple_of(me.s * T + first, 16), half), :] = (total * scale * gain[1:2, :]).astype(BF)
        gather_x2[first // half].begin()
        run(0 if first else 1)
        if first == 0:
            gather_c[1].relay()
    for e in range(per):
        pltpu.make_async_copy(pst.at[e], oP.at[e, half:, :], psem.at[e]).wait()
    write(mixed, omixed)
    write(hid, ohid)
    for part_c in gather_c:
        part_c.finish()
    write(C, oC)
    run(1)
    gather_x2[0].relay()
    run(len(events) - 3)
    gather_x2[1].relay()
    run(len(events) - 2)
    for part_x2 in gather_x2:
        part_x2.finish()
    write(X2, oX2)

    def pcopy(n, k):
        return remote(part.at[0, n, k], got.at[n, k], ps.at[n, k], pr.at[n, k], me.dev(c=1 - me.c))

    def act_out(i):
        k = X - 1 - i % X
        s = lax.rem(me.x + k, X) * 2 + lax.rem(1 + i // X + me.c, 2)
        rows, lanes = block(s, T), slice(*cuts[1])
        return pltpu.make_async_copy(act.at[:, rows, lanes], oact.at[:, rows, lanes], asem.at[i])

    def tokens_block(i, group):
        k = X - 1 - i % X
        e = i // X
        s = lax.rem(me.x + k, X) * 2 + lax.rem(1 + e + me.c, 2)
        rows = block(s, T)
        lanes = slice(*cuts[group])
        gate_w, up_w, down_w = (WFs[group].at[m] for m in range(3))
        xb = X2[rows, :]
        gate = dot(xb, gate_w[...])
        upward = dot(xb, up_w[...])
        back = dot(C[rows, :], down_w[...])
        value, slope = gelu_parts(gate)
        activated = (value * upward).astype(BF)
        first = (back * upward * slope).astype(BF)
        second = (back * value).astype(BF)
        act[0, rows, lanes] = first
        act[1, rows, lanes] = second
        act[2, rows, lanes] = activated
        if group:
            act_out(i).start()
        terms = dot(first, gate_w[...], NT) + dot(second, up_w[...], NT), dot(activated, down_w[...], NT)
        for n, term in enumerate(terms):
            if group:
                term += part[e, n, k].astype(F32)
            part[e, n, k] = term.astype(BF)
        if group:

            @pl.when(e == 0)
            def _():
                for n in range(2):
                    pcopy(n, k).start()

            @pl.when(e == 1)
            def _():
                for n in range(2):
                    pcopy(n, k).wait_recv()
                    part[1, n, k] = (part[1, n, k].astype(F32) + got[n, k].astype(F32)).astype(BF)
                    pltpu.make_async_copy(part.at[1, n, k], opart.at[n, k], wsem.at[n, k]).start()

    for group in range(2):
        for r in range(geo.A):
            for p in others:
                if p // 3 == group:
                    ffn.ystep(r, p)

        def with_events(i):
            tokens_block(i, group)
            for n, event in enumerate(() if group else [events.pop(0) for _ in range(len(events))]):

                @pl.when(i == n)
                def _():
                    forward_on(*event)

        loop(2 * X, with_events)
        if not group:
            write(act.at[:, :, slice(*cuts[0])], oact.at[:, :, slice(*cuts[0])])
    for k in range(X):
        for n in range(2):
            pcopy(n, k).wait_send()
            pltpu.make_async_copy(part.at[1, n, k], opart.at[n, k], wsem.at[n, k]).wait()

    def finish(g):
        for k in range(X):
            s = lax.rem(me.x - k + X, X) * 2 + 1 - me.c
            here = held_a(s, g)
            ccopy(k, g, here, s).wait_send()
            if k:
                xcopy(k, g, here).wait_send()

    loop(dp, finish)
    att.drain(0)
    for p in others:
        ffn.drain(p)
    ffn.drain(special, (False, True), False)
    for copy in writes:
        copy.wait()
    loop(2 * X, lambda i: act_out(i).wait())


def forward(geo, *arrays):
    dma = pltpu.SemaphoreType.DMA
    S, N, F, T, L, I, H, X, I4 = geo.seq, geo.N, geo.F, geo.T, geo.L, geo.I, geo.H, geo.X, geo.I4
    per = 128 // (I // H)
    first = (F // 128 + 1) // 2 * 128
    out_shape = [
        ((T, N), BF), ((S, N, I4), BF), ((T, 3 * I), BF), ((L, 2 * I), BF), ((H, T, L), F32), ((T, I), BF),
        ((T, N), F32), ((L, N), BF), ((L, N), BF), ((3, L, F), BF), ((2, X, T, N), BF), ((8, N), F32),
    ]
    V = pltpu.VMEM
    scratch = [
        V((3, N, first), BF), V((3, N, F - first), BF), V((S, N, I4), BF), V((T, N), BF), V((L, N), BF), V((L, N), BF), V((L, 2 * I), BF),
        V((T, 3 * I), BF), V((H, 128, 2 * L - 128), BF), V((T, I), BF), V((T, N), F32),
        V((per, T // 2, L), F32), V((3, L, F), BF), V((2, 2, X, T, N), BF), V((2, X, T, N), BF), V((8, N), F32),
        V((2, geo.D, T), BF), V((3, geo.W, F), F32), V((4, geo.W, I4 // 4), F32), V((2, geo.W), F32), V((geo.TR, H), F32),
        V((geo.R - geo.W, I4), F32),
        V((I, S * I4), BF), V((geo.dp * 16, 512), BF), pltpu.SMEM((1,), jnp.int32),
        dma((12,)), dma((13,)), dma((per,)),
        dma((geo.NZ, 6)), dma((geo.NZ, 6)), dma((geo.NY, 6)), dma((geo.NY, 6)),
        dma((geo.NZ, 1)), dma((geo.NZ, 1)),
        dma((geo.NZ, 1)), dma((geo.NZ, 1)), dma((geo.NY, 1)), dma((geo.NY, 1)),
        dma((X - 1, geo.dp)), dma((X - 1, geo.dp)), dma((X, geo.dp)), dma((X, geo.dp)),
        dma((5, X - 1)), dma((5, X - 1)), dma((5, X)), dma((5, X)),
        dma((2, X)), dma((2, X)), dma((2, X)), dma((2 * X,)),
    ]
    return pl.pallas_call(
        functools.partial(forward_kernel, geo),
        out_shape=[jax.ShapeDtypeStruct(*v) for v in out_shape],
        in_specs=[pl.BlockSpec(memory_space=pl.ANY)] * len(arrays),
        out_specs=[pl.BlockSpec(memory_space=pl.ANY)] * len(out_shape),
        scratch_shapes=scratch,
        compiler_params=pltpu.CompilerParams(collective_id=0, has_side_effects=True, vmem_limit_bytes=63 << 20),
        name="forward",
    )(*arrays)


class SeqScatter:
    def __init__(self, geo, me, part, cb, xb, cs, cr, xs, xr):
        self.__dict__.update(locals())

    def ccopy(self, k):
        me = self.me
        to = lax.rem(me.x + k, self.geo.X)
        return remote(self.part(to * 2 + 1 - me.c), self.cb(k), self.cs.at[k], self.cr.at[k], me.dev(c=1 - me.c))

    def xcopy(self, k):
        me = self.me
        to = lax.rem(me.x + k, self.geo.X)
        return remote(self.part(to * 2 + me.c), self.xb(k), self.xs.at[k - 1], self.xr.at[k - 1], me.dev(x=to))

    def to_core(self):
        for k in (*range(1, self.geo.X), 0):
            self.ccopy(k).start()

    def to_x(self):
        for k in range(1, self.geo.X):
            self.ccopy(k).wait_recv()
            out = self.part(lax.rem(self.me.x + k, self.geo.X) * 2 + self.me.c)
            out[...] = (out[...].astype(F32) + self.cb(k)[...].astype(F32)).astype(BF)
            self.xcopy(k).start()

    def meet(self):
        self.ccopy(0).wait_recv()
        total = self.part(self.me.s)[...].astype(F32) + self.cb(0)[...].astype(F32)
        for k in range(1, self.geo.X):
            self.xcopy(k).wait_recv()
            total += self.xb(k)[...].astype(F32)
        return total

    def drain(self):
        for k in range(self.geo.X):
            self.ccopy(k).wait_send()
            if k:
                self.xcopy(k).wait_send()


class DpScatter:
    def __init__(self, geo, me, part, ybuf, zbuf, ys, yr, zs, zr, finish, first_z=1 << 20, zbuf2=None, zs2=None, zr2=None):
        self.__dict__.update(locals())

    def owner(self, i):
        A, z = self.geo.A, self.me.z
        up, down = A - 1 - z, z
        both = jnp.minimum(up, down)
        half = i // 2
        early = jnp.where((i % 2 == 0) == (up >= down), A - 1 - half, half)
        late = jnp.where(up > down, A - 1 - (i - both), i - both)
        return jnp.where(i == A - 1, z, jnp.where(i < 2 * both, early, late))

    def ycopy(self, t, p):
        me = self.me
        return remote(
            self.part(p, t * 2 + 1 - me.y), self.ybuf(p, t), self.ys.at[t, p], self.yr.at[t, p], me.dev(y=1 - me.y)
        )

    def zparts(self, t, slot, p, other):
        if other:
            return self.zbuf2(p, slot), self.zs2.at[t, p - self.first_z], self.zr2.at[slot, p - self.first_z]
        return self.zbuf(p, slot), self.zs.at[t, p], self.zr.at[slot, p]

    def mine(self, t, p, other=False):
        return self.part(p, t * 2 + (1 - self.me.y if other else self.me.y))

    def zslot(self, up, t):
        return jnp.where(up, self.geo.A - 1 - t, self.geo.A - t)

    def zcopy(self, t, p, other=False):
        me = self.me
        up = t > me.z
        dst, ss, rs = self.zparts(t, self.zslot(up, t), p, other)
        return remote(self.mine(t, p, other), dst, ss, rs, me.dev(z=jnp.where(up, me.z + 1, me.z - 1)))

    def zarrive(self, up, t, p, other=False):
        here, ss, rs = self.zparts(t, self.zslot(up, t), p, other)
        remote(here, here, ss, rs, self.me.dev(y=1 - self.me.y)).wait_recv()
        return here[...].astype(F32)

    def ysend(self, i, p):
        self.ycopy(self.owner(i), p).start()

    def arrived(self, t, p, base, put, other=False):
        geo, me = self.geo, self.me

        @pl.when(me.z == 0)
        def _():
            put(base() + self.zarrive(False, t, p, other))

        @pl.when(me.z == geo.A - 1)
        def _():
            put(base() + self.zarrive(True, t, p, other))

        @pl.when((me.z > 0) & (me.z < geo.A - 1))
        def _():
            put(base() + self.zarrive(True, t, p, other) + self.zarrive(False, t, p, other))

    def onward(self, t, p, base, other=False, plain=False):
        geo, me = self.geo, self.me
        mine = self.mine(t, p, other)
        up = t > me.z
        comes = (up & (me.z > 0)) | (jnp.logical_not(up) & (me.z < geo.A - 1))

        @pl.when(comes)
        def _():
            mine[...] = (base() + self.zarrive(up, t, p, other)).astype(BF)

        if not plain:

            @pl.when(jnp.logical_not(comes))
            def _():
                mine[...] = base().astype(BF)

        self.zcopy(t, p, other).start()

    def event(self, i, p):
        t = self.owner(i)
        mine = self.mine(t, p)
        own = lambda: mine[...].astype(F32)
        if p >= self.first_z:
            theirs = self.mine(t, p, True)
            their = lambda: theirs[...].astype(F32)
            if i < self.geo.A - 1:
                self.onward(t, p, their, True, True)
                self.onward(t, p, own, False, True)
            else:
                self.arrived(t, p, their, lambda v: theirs.__setitem__(..., v.astype(BF)), True)
                self.ycopy(t, p).start()
            return
        self.ycopy(t, p).wait_recv()
        both = lambda: own() + self.ybuf(p, t)[...].astype(F32)
        if i == self.geo.A - 1:
            self.arrived(t, p, both, lambda v: self.finish(p, v))
        else:
            self.onward(t, p, both)

    def last(self, p):
        t = self.me.z
        mine = self.mine(t, p)
        self.ycopy(t, p).wait_recv()
        both = lambda: mine[...].astype(F32) + self.ybuf(p, t)[...].astype(F32)
        self.arrived(t, p, both, lambda v: self.finish(p, v))

    def drain(self, p, second=False):
        for i in range(self.geo.A):
            t = self.owner(i)
            if not second or i == self.geo.A - 1:
                self.ycopy(t, p).wait_send()
            if i < self.geo.A - 1:
                for other in (False, True) if second else (False,):
                    self.zcopy(t, p, other).wait_send()


def backward_kernel(
    geo, x_in, iWA, iqkv, iKV, iP, imixed, ihid, iX2, iC, iact, ipart, igain,
    of, oa, olayer, oinput,
    G, XC, act, yb, zb, WA, ayb, azb, cb, xb, xv, hid, qkv, KV, mixed, pk, px, pst, kcb, kxb, zb2,
    hgrad, gbias, extra, gain, packed, sums, pout, onehot,
    local, psem, outs, csem, osem, pxs, pxr, kcs, kcr, kxs, kxr, acs, acr, axs, axr, ys, yr, zs, zr, zs2, zr2, ays, ayr, azs, azr,
):
    me = Place(geo)
    R, RH, NH, dp, X, T, N, I = geo.R, geo.RH, geo.NH, geo.dp, geo.X, geo.T, geo.N, geo.I
    I4, S, L, A, NP = geo.I4, geo.seq, geo.L, geo.A, geo.NP
    block = lambda i, n: pl.ds(pl.multiple_of(i * n, 16), n)
    dKV = act.at[0, :, : 2 * I]
    dM, dq = act.at[1, :T, :I], act.at[1, T : 2 * T, :I]
    half = S * I4 // 2
    rights = [act.at[2, : 2 * T, :half], act.at[2, 2 * T : 4 * T, :half]]
    lefts = XC.at[N : N + 2 * T, :]
    hlow = lefts.at[T:, :]
    ds = pk.at[0, :, : L + 256]
    loads = [
        (iact.at[2], act.at[2]), (iact.at[0], act.at[0]), (iact.at[1], act.at[1]), (ipart.at[:, 0], pk), (ihid, hid), (igain, gain),
        (iWA, WA), (iKV, KV), (iqkv, qkv), (imixed, mixed), (x_in, xv),
    ]
    loads = [pltpu.make_async_copy(src, dst, local.at[i]) for i, (src, dst) in enumerate(loads)]
    turns = DpScatter(geo, me, *[None] * 8)

    def columns_in(i, n):
        t = turns.owner(i)
        lanes = pl.ds(pl.multiple_of(t * 2 * R, 128), 2 * R)
        src, dst = ((iX2, XC.at[:L, lanes]), (iC, XC.at[L:, lanes]))[n]
        return pltpu.make_async_copy(src.at[:, lanes], dst, csem.at[n, i])

    loads[0].start()
    columns_in(0, 1).start()
    loads[1].start()
    columns_in(0, 0).start()
    loads[2].start()
    for i in range(1, A):
        for n in (1, 0):
            columns_in(i, n).start()
    for copy in loads[3:]:
        copy.start()
    hd = I // geo.H
    per = 128 // hd

    def pload(t, e):
        return pltpu.make_async_copy(iP.at[t * per + e], pst.at[e], psem.at[e])

    for e in range(per):
        pload(0, e).start()
    enter(geo, me)

    def pcopy(n, k):
        to = me.dev(x=lax.rem(me.x + k, X))
        return remote(ipart.at[n, k], px.at[n, k - 1], pxs.at[n, k - 1], pxr.at[n, k - 1], to)

    for n in range(2):
        for k in range(1, X):
            pcopy(n, k).start()

    def rows_of(g, p):
        return pl.ds(pl.multiple_of(g * R + (p % NH) * RH, 16), RH)

    def piece(buf, i, p):
        return buf.at[i, p // NH, pl.ds(pl.multiple_of((p % NH) * RH, 16), RH), :]

    def out_f(p):
        rows = pl.ds(pl.multiple_of((p % NH) * RH, 16), RH)
        return pltpu.make_async_copy(sums.at[p // NH, rows, :], of.at[p // NH, rows, :], osem.at[p])

    def finish_f(p, value):
        sums[p // NH, pl.ds(pl.multiple_of((p % NH) * RH, 16), RH), :] = value
        out_f(p).start()

    last = NP - 1
    ffn = DpScatter(
        geo, me, lambda p, g: G.at[p // NH, rows_of(g, p), :], lambda p, t: piece(yb, t, p),
        lambda p, i: piece(zb, i, p), ys, yr, zs, zr, finish_f,
        last, lambda p, i: zb2.at[i], zs2, zr2,
    )
    def weight_rows(i):
        t = ffn.owner(i)
        lanes = pl.ds(pl.multiple_of(t * 2 * R, 128), 2 * R)
        rows = pl.ds(pl.multiple_of(t * 2 * R, 16), 2 * R)
        for m in (2, 0, 1):
            if isinstance(i, int):
                loads[{2: 0, 0: 1, 1: 2}[m]].wait()
            if m != 1:
                columns_in(i, m // 2).wait()
            left = XC[:L, lanes] if m < 2 else XC[L:, lanes]
            G[m, rows, :] = dot(left, act[m], TN).astype(BF)

            def go(h):
                p = m * NH + h

                @pl.when((p < last) & ((i < A - 1) | (p < NP // 2)))
                def _():
                    ffn.ysend(i, p)

            loop(NH, go)


    edge = (me.z == 0) | (me.z == A - 1)
    queues = [(kind, [(i, p) for i in range(A) for p in (last, *range(last))]) for kind in (edge, jnp.logical_not(edge))]

    def run(*counts):
        for (kind, events), count in zip(queues, counts):
            now = [events.pop(0) for _ in range(min(count, len(events)))]
            if now:

                @pl.when(kind)
                def _():
                    for i, p in now:
                        ffn.event(i, p)

    weight_rows(0)
    run(1, 0)
    loop(A - 1, lambda i: weight_rows(i + 1))
    place_columns(geo, pout)
    place_buckets(geo, onehot)
    run(2, 0)

    for i in range(3, len(loads)):
        loads[i].wait()
    for k in range(1, X):
        pcopy(0, k).wait_recv()
    grad = pk[0].astype(F32)
    for k in range(1, X):
        grad += px[0, k - 1].astype(F32)
    hidden = hid[...]
    scale = lax.rsqrt(jnp.sum(hidden * hidden, axis=-1, keepdims=True) / np.float32(geo.D) + EPSILON)
    unit = hidden * scale
    gain_two = jnp.sum(grad * unit, axis=0, keepdims=True)
    pull = grad * gain[1:2, :]
    inner = jnp.sum(pull * unit, axis=-1, keepdims=True) / np.float32(geo.D)
    cot = XC[pl.ds(pl.multiple_of(L + me.s * T, 16), T), :].astype(F32)
    total = cot + scale * (pull - unit * inner)
    hgrad[...] = total
    hlow[...] = total.astype(BF)
    columns = jnp.concatenate([dot(hlow[...], WA[s]) for s in range(S)], axis=1).astype(BF)
    dM[...] = dot(columns, pout[...], NT).astype(BF)
    ds[...] = jnp.zeros_like(ds)
    gbias[...] = jnp.zeros_like(gbias)
    run(3, 1)

    def pair(t):
        lanes = pl.ds(pl.multiple_of(t * 128, 128), 128)
        vlanes = pl.ds(pl.multiple_of(I + t * 128, 128), 128)
        head = lax.broadcasted_iota(jnp.int32, (1, 128), 1) // hd
        keys, values, queries, back = KV[:, lanes], KV[:, vlanes], qkv[:, lanes], dM[:, lanes]
        zero = jnp.zeros_like(queries)
        q_grad = jnp.zeros((T, 128), F32)
        k_grad = jnp.zeros((L, 128), F32)
        v_grad = jnp.zeros((L, 128), F32)
        for e in range(per):
            h = t * per + e
            own_back = jnp.where(head == e, back, zero)
            pload(t, e).wait()
            probs = pst[e]
            prob_grad = dot(own_back, values, NT)
            both = jnp.sum(probs * prob_grad, axis=-1, keepdims=True)
            score = (probs * (prob_grad - both)).astype(BF)
            v_grad += dot(probs.astype(BF), own_back, TN)

            @pl.when(t + 1 < I // 128)
            def _():
                pload(t + 1, e).start()

            q_grad = jnp.where(head == e, dot(score, keys), q_grad)
            k_grad += dot(score, jnp.where(head == e, queries, zero), TN)
            ds[:, 128 : 128 + L] = score
            near = jnp.zeros((128, 384), F32)
            place = lax.broadcasted_iota(jnp.int32, (1, L), 1)
            low = jnp.zeros((1, 1), F32)
            high = jnp.zeros((1, 1), F32)
            for b in range(T // 128):
                row_block = me.s * (T // 128) + b
                near += ds[b * 128 : (b + 1) * 128, pl.ds(pl.multiple_of(row_block * 128, 128), 384)].astype(F32)
                sums = jnp.sum(score[b * 128 : (b + 1) * 128, :].astype(F32), axis=0, keepdims=True)
                low += jnp.sum(jnp.where(place < (row_block - 1) * 128, sums, 0.0), axis=-1, keepdims=True)
                high += jnp.sum(jnp.where(place >= (row_block + 2) * 128, sums, 0.0), axis=-1, keepdims=True)
            near = jnp.concatenate([jnp.zeros((128, 128), F32), near], axis=1)
            line = jnp.sum(shear(near, -1), axis=0, keepdims=True)
            spot = lax.broadcasted_iota(jnp.int32, (1, 512), 1)
            line += jnp.where(spot == 0, low, 0.0) + jnp.where(spot == 511, high, 0.0)
            gbias[pl.ds(h, 1), :] = line
        dq[:, lanes] = q_grad.astype(BF)
        dKV[:, lanes] = k_grad.astype(BF)
        dKV[:, vlanes] = v_grad.astype(BF)

    def key_scatter(i):
        lanes = slice(i * 128, (i + 1) * 128)
        return SeqScatter(
            geo, me, lambda s: dKV.at[block(s, T), lanes], lambda k: kcb.at[k, :, lanes], lambda k: kxb.at[k - 1, :, lanes],
            kcs.at[i], kcr.at[i], kxs.at[i], kxr.at[i],
        )

    pairs = I // 128
    scatters = [(key_scatter(t), key_scatter(pairs + t)) for t in range(pairs)]
    for t in range(pairs):
        pair(t)
        for one in scatters[t]:
            one.to_core()
        if t:
            for one in scatters[t - 1]:
                one.to_x()
        run(*((1, 1), (1, 1), (2, 1))[min(t, 2)])

    for k in range(1, X):
        pcopy(1, k).wait_recv()
    total = hid[...] + pk[1].astype(F32)
    for k in range(1, X):
        total += px[1, k - 1].astype(F32)
    packed[...] = pack(geo, total)
    layer_out = pltpu.make_async_copy(packed, olayer, outs.at[0])
    layer_out.start()
    for one in scatters[-1]:
        one.to_x()
    run(1, 1)
    tokens = xv[...].astype(F32)
    scale = lax.rsqrt(jnp.sum(tokens * tokens, axis=-1, keepdims=True) / np.float32(geo.D) + EPSILON)
    lefts[:T, :] = (tokens * scale * gain[0:1, :]).astype(BF)
    columns = dot(mixed[...], pout[...]).astype(BF)
    for i, right in enumerate(rights):
        right[T:, :] = columns[:, i * half : (i + 1) * half]
    run(2, 2)
    key_value = [jnp.concatenate([one[n].meet() for one in scatters], axis=1).astype(BF) for n in range(2)]
    run(0, 3)
    columns = jnp.zeros((T, S * I4), F32)
    for kind, value in enumerate((dq[...], *key_value)):
        columns += pltpu.roll(dot(value, pout[...]), S * I4 - (3 - kind) * (I4 // 4), 1)
    columns = columns.astype(BF)
    for i, right in enumerate(rights):
        right[:T, :] = columns[:, i * half : (i + 1) * half]
    grad = jnp.zeros((T, N), F32)
    for s in range(S):
        grad += dot(columns[:, s * I4 : (s + 1) * I4], WA[s], NT)
    unit = tokens * scale
    gain_one = jnp.sum(grad * unit, axis=0, keepdims=True)
    pull = grad * gain[0:1, :]
    inner = jnp.sum(pull * unit, axis=-1, keepdims=True) / np.float32(geo.D)
    layer_out.wait()
    packed[...] = pack(geo, hgrad[...] + scale * (pull - unit * inner))
    input_out = pltpu.make_async_copy(packed, oinput, outs.at[1])
    input_out.start()

    table = dot(onehot[...], gbias[...].astype(BF), NT)
    if I4 > 128:
        table = jnp.concatenate([table, jnp.zeros((dp * 16, I4 - 128), F32)], axis=1)
    extra[...] = table
    for g in range(dp):
        for e, line in enumerate((gain_one, gain_two)):
            at = g * 16 + 16 - geo.E + e
            extra[at : at + 1, :R] = line[:, g * R : (g + 1) * R]

    def part_g(s, g):
        return XC.at[block(g, R), pl.ds(pl.multiple_of(s * I4, 128), I4)]

    att = DpScatter(
        geo, me, lambda p, g: part_g(me.s, g), lambda p, t: ayb.at[t], lambda p, i: azb.at[i],
        ays, ayr, azs, azr, lambda p, value: oa.__setitem__(..., value),
    )
    def turn(j):
        t = att.owner(j // 2)
        return t * 2 + jnp.where(j % 2 == 0, 1 - me.y, me.y)

    def scatter(g):
        return SeqScatter(
            geo, me, lambda s: part_g(s, g), lambda k: cb.at[k, block(g, R), :], lambda k: xb.at[k - 1, block(g, R), :],
            acs.at[g], acr.at[g], axs.at[g], axr.at[g],
        )

    def attention_rows(i):
        t = att.owner(i)
        lanes = pl.ds(pl.multiple_of(t * 2 * R, 128), 2 * R)
        rows = pl.ds(pl.multiple_of(t * 2 * R, 16), 2 * R)
        for n, right in enumerate(rights):
            XC[rows, n * half : (n + 1) * half] = dot(lefts[:, lanes], right[...], TN).astype(BF)
        for y in range(2):
            g = t * 2 + y
            rows = pl.ds(pl.multiple_of(g * R + R - 16, 16), 16)
            more = extra[pl.ds(pl.multiple_of(g * 16, 16), 16), :]
            for s in range(S):
                lane = slice(s * I4, (s + 1) * I4)
                XC[rows, lane] = (XC[rows, lane].astype(F32) + more).astype(BF)
        scatter(t * 2 + 1 - me.y).to_core()
        scatter(t * 2 + me.y).to_core()

    for i in range(A):
        attention_rows(i)
        run((2, 0, 2, 1)[min(i, 3)], (3, 1, 1, 1)[min(i, 3)])
    held = [p for p in range(last) if p >= NP // 2]
    for j in range(dp):
        scatter(turn(j)).to_x()
    run(0, 1)
    for j in range(dp):
        g = turn(j)
        part_g(me.s, g)[...] = scatter(g).meet().astype(BF)
        if j % 2 == 0:
            att.ysend(j // 2, 0)
        elif held:
            ffn.ysend(A - 1, held.pop(0))
        if j >= 2:
            run(1, 1)
        if j % 2 and j >= 3:
            att.event((j - 3) // 2, 0)
    while held:
        ffn.ysend(A - 1, held.pop(0))
    att.event(A - 1, 0)
    run(*(len(events) for _, events in queues))
    ffn.last(last)

    for n in range(2):
        for k in range(1, X):
            pcopy(n, k).wait_send()
    for both in scatters:
        for one in both:
            one.drain()
    loop(dp, lambda g: scatter(g).drain())
    att.drain(0)
    loop(last, ffn.drain)
    ffn.drain(last, True)
    input_out.wait()
    loop(NP, lambda p: out_f(p).wait())


def backward(geo, *saved):
    dma = pltpu.SemaphoreType.DMA
    S, N, F, T, L, I, X, I4, A, R = geo.seq, geo.N, geo.F, geo.T, geo.L, geo.I, geo.X, geo.I4, geo.A, geo.R
    per = 128 // (I // geo.H)
    V = pltpu.VMEM
    scratch = [
        V((3, N, F), BF), V((2 * L, N), BF), V((3, L, F), BF), V((A, 3, R, F), BF), V((A + 1, 3, R, F), BF),
        V((S, N, I4), BF), V((A, R, I4), BF), V((A + 1, R, I4), BF),
        V((X, N, I4), BF), V((X - 1, N, I4), BF),
        V((T, N), BF), V((T, N), F32), V((T, 3 * I), BF), V((L, 2 * I), BF), V((T, I), BF),
        V((2, T, N), BF), V((2, X - 1, T, N), BF), V((per, T, L), F32),
        V((X, T, 2 * I), BF), V((X - 1, T, 2 * I), BF), V((A + 1, geo.RH, F), BF),
        V((T, N), F32), V((128, 512), F32), V((geo.dp * 16, I4), F32), V((8, N), F32), V((geo.D, T), BF), V((3, R, F), F32),
        V((I, S * I4), BF), V((geo.dp * 16, 512), BF),
        dma((11,)), dma((per,)), dma((2,)), dma((2, A)), dma((geo.NP,)),
        dma((2, X - 1)), dma((2, X - 1)), dma((2 * I // 128, X)), dma((2 * I // 128, X)), dma((2 * I // 128, X - 1)), dma((2 * I // 128, X - 1)),
        dma((geo.dp, X)), dma((geo.dp, X)), dma((geo.dp, X - 1)), dma((geo.dp, X - 1)),
        dma((A, geo.NP)), dma((A, geo.NP)), dma((A, geo.NP)), dma((A + 1, geo.NP)),
        dma((A, 1)), dma((A + 1, 1)),
        dma((A, 1)), dma((A, 1)), dma((A, 1)), dma((A + 1, 1)),
    ]
    return pl.pallas_call(
        functools.partial(backward_kernel, geo),
        out_shape=[
            jax.ShapeDtypeStruct((3, R, F), F32), jax.ShapeDtypeStruct((R, I4), F32),
            jax.ShapeDtypeStruct((geo.D, T), BF), jax.ShapeDtypeStruct((geo.D, T), BF),
        ],
        in_specs=[pl.BlockSpec(memory_space=pl.ANY)] * len(saved),
        out_specs=[pl.BlockSpec(memory_space=v) for v in (pl.ANY, pltpu.VMEM, pl.ANY, pl.ANY)],
        scratch_shapes=scratch,
        compiler_params=pltpu.CompilerParams(collective_id=2, has_side_effects=True, vmem_limit_bytes=63 << 20),
        name="backward",
    )(*saved)


def finish_kernel(geo, rows, features, layer, grad, *rest):
    outs, (held, blocks, main, query, keyval, output, gains, table, sem) = rest[:9], rest[9:]
    W, own = geo.W, geo.I4 // 4
    moves = [
        (rows, main, None), (layer, held.at[0], outs[0]), (grad, held.at[1], outs[1]),
        (features.at[0], blocks.at[0], outs[5].at[0]), (features.at[1], blocks.at[1], outs[5].at[1]),
        (features.at[2], blocks.at[2], outs[6]),
    ]
    arrive = [pltpu.make_async_copy(src, mid, sem.at[0, i]) for i, (src, mid, _) in enumerate(moves)]
    leave = [
        pltpu.make_async_copy(mid.at[:W, :] if i > 2 else mid, dst, sem.at[1, i])
        for i, (_, mid, dst) in enumerate(moves)
        if dst is not None
    ]
    for copy in arrive:
        copy.start()
    arrive[0].wait()
    query[...] = main[:W, :own]
    keyval[0] = main[:W, own : 2 * own]
    keyval[1] = main[:W, 2 * own : 3 * own]
    output[...] = main[:W, 3 * own :]
    gains[...] = main[geo.R - geo.E : geo.R - geo.TR, :W]
    table[...] = main[geo.R - geo.TR :, : geo.H]
    small = [(query, outs[2]), (keyval, outs[3]), (output, outs[4]), (gains, outs[7]), (table, outs[8])]
    small = [pltpu.make_async_copy(src, dst, sem.at[1, 6 + i]) for i, (src, dst) in enumerate(small)]
    for copy in small:
        copy.start()
    for copy, onward in zip(arrive[1:], leave):
        copy.wait()
        onward.start()
    for copy in small + leave:
        copy.wait()


def finish(geo, of, oa, layer, grad):
    W, own, F = geo.W, geo.I4 // 4, geo.F
    shapes = [
        (layer.shape, BF), (grad.shape, BF), ((W, own), F32), ((2, W, own), F32), ((W, own), F32), ((2, W, F), F32),
        ((W, F), F32), ((2, W), F32), ((geo.TR, geo.H), F32),
    ]
    V = pltpu.VMEM
    return pl.pallas_call(
        functools.partial(finish_kernel, geo),
        out_shape=[jax.ShapeDtypeStruct(*v) for v in shapes],
        in_specs=[pl.BlockSpec(memory_space=pl.ANY)] * 4,
        out_specs=[pl.BlockSpec(memory_space=pl.ANY)] * 9,
        scratch_shapes=[
            V((2, *layer.shape), BF), V((3, geo.R, F), F32), V((geo.R, geo.I4), F32),
            *[V(*shapes[i]) for i in (2, 3, 4, 7, 8)], pltpu.SemaphoreType.DMA((2, 11)),
        ],
        compiler_params=pltpu.CompilerParams(vmem_limit_bytes=63 << 20),
        name="finish",
    )(oa, of, layer, grad)


def spread_features(values, geo, width):
    lead = values.shape[:-1]
    blocks = values.reshape(*lead, geo.dp, width)
    return jnp.pad(blocks, [(0, 0)] * (len(lead) + 1) + [(0, geo.R - width)]).reshape(*lead, geo.dp * geo.R)


def pack_features(values, geo, width):
    lead = values.shape[:-1]
    return values.reshape(*lead, geo.dp, geo.R)[..., :width].reshape(*lead, geo.dp * width)


def general_path(
    axes, tokens, cotangent, lengths, w_query, w_key_value, w_output, w_gate_up, w_down, norm_gains, position_bias
):
    dp, seq = axes
    width, own_inner = w_query.shape
    table_rows, head_count = position_bias.shape
    geo = Geo(dp, seq, width, w_down.shape[1], 4 * own_inner, tokens.shape[1], head_count, table_rows)
    rows = geo.R
    model_width = geo.D
    bucket_count = table_rows * dp
    inner_width = geo.I
    head_dim = inner_width // head_count

    lanes = lambda v: jnp.pad(v, ((0, 0), (0, geo.I4 - v.shape[1])))
    wa = jnp.concatenate(
        [
            jnp.concatenate([w_query, w_key_value[0], w_key_value[1], w_output], axis=1).astype(BF),
            jnp.zeros((rows - width - geo.E, geo.I4), BF),
            lanes(norm_gains.astype(BF)),
            lanes(position_bias.astype(BF)),
        ],
        axis=0,
    )
    wf = jnp.pad(jnp.concatenate([w_gate_up, w_down[None]], axis=0).astype(BF), ((0, 0), (0, rows - width), (0, 0)))
    WF, WA = gather_weights(geo, wf, wa)

    blocks = WA[0].reshape(dp, rows, geo.I4)
    first_gain = blocks[:, rows - geo.E, :width].reshape(model_width).astype(F32)
    second_gain = blocks[:, rows - geo.E + 1, :width].reshape(model_width).astype(F32)
    table_full = blocks[:, rows - table_rows :, :head_count].reshape(bucket_count, head_count)
    real = WA.reshape(seq, dp, rows, 4, own_inner)[:, :, :width]
    parts = real.transpose(3, 1, 2, 0, 4).reshape(4, model_width, inner_width)
    query_full, keyval_full, output_full = parts[0], parts[1:3], parts[3]

    inputs = tokens[0].astype(jnp.float32)
    row_count = inputs.shape[0]
    normed = norm_scale(inputs, first_gain).astype(jnp.bfloat16)
    queries = jnp.dot(normed, query_full, preferred_element_type=jnp.float32).astype(jnp.bfloat16)
    projected = jnp.einsum(
        "td,sdi->sti", normed, keyval_full, preferred_element_type=jnp.float32
    ).astype(jnp.bfloat16)
    keys_all, values_all = (
        lax.all_gather(projected[0], "seq", axis=0, tiled=True),
        lax.all_gather(projected[1], "seq", axis=0, tiled=True),
    )
    incoming_low = cotangent[0]
    incoming = incoming_low.astype(jnp.float32)
    cot_all = lax.all_gather(spread_features(incoming_low, geo, width), "seq", axis=0, tiled=True)
    length_all = keys_all.shape[0]
    block_start = lax.axis_index("seq") * row_count
    query_pos = block_start + jnp.arange(row_count, dtype=jnp.int32)
    key_pos = jnp.arange(length_all, dtype=jnp.int32)
    buckets = bucket_ids(key_pos[None, :] - query_pos[:, None])
    bucket_range = jnp.arange(bucket_count, dtype=jnp.int32)
    onehot = (buckets[:, :, None] == bucket_range).astype(jnp.bfloat16)
    score_bias = jnp.einsum("tkb,bh->htk", onehot, table_full, preferred_element_type=jnp.float32)
    key_valid = key_pos < lengths[0]
    query_heads = queries.reshape(row_count, head_count, head_dim)
    key_heads = keys_all.reshape(length_all, head_count, head_dim)
    value_heads = values_all.reshape(length_all, head_count, head_dim)
    raw_scores = (
        jnp.einsum("thc,khc->htk", query_heads, key_heads, preferred_element_type=jnp.float32) + score_bias
    )
    scores = jnp.where(key_valid[None, None, :], raw_scores, NEGATIVE)
    probs = jax.nn.softmax(scores, axis=-1)
    probs_low = probs.astype(BF)
    mixed_heads = (
        jnp.einsum("htk,khc->thc", probs_low, value_heads, preferred_element_type=jnp.float32)
        .reshape(row_count, inner_width)
        .astype(jnp.bfloat16)
    )
    attended = jnp.einsum("tc,dc->td", mixed_heads, output_full, preferred_element_type=jnp.float32)
    hidden_one = inputs + attended
    normed_two = norm_scale(hidden_one, second_gain).astype(jnp.bfloat16)
    normed_two_all = lax.all_gather(spread_features(normed_two, geo, width), "seq", axis=0, tiled=True)

    gate = jnp.dot(normed_two_all, WF[0], preferred_element_type=F32)
    upward = jnp.dot(normed_two_all, WF[1], preferred_element_type=F32)
    activated = gated(gate, upward).astype(BF)
    down_term = jnp.einsum("tf,df->td", activated, WF[2], preferred_element_type=F32)
    down_weight_grad = jnp.einsum("td,tf->df", cot_all, activated, preferred_element_type=F32)
    activated_grad = jnp.dot(cot_all, WF[2], preferred_element_type=F32)
    unused_value, gate_pull = jax.vjp(gated, gate, upward)
    gate_grad, upward_grad = gate_pull(activated_grad)
    gate_grad, upward_grad = gate_grad.astype(BF), upward_grad.astype(BF)
    gate_weight_grad = jnp.einsum("td,tf->df", normed_two_all, gate_grad, preferred_element_type=F32)
    up_weight_grad = jnp.einsum("td,tf->df", normed_two_all, upward_grad, preferred_element_type=F32)
    normed_two_term = jnp.einsum("tf,df->td", gate_grad, WF[0], preferred_element_type=F32) + jnp.einsum(
        "tf,df->td", upward_grad, WF[1], preferred_element_type=F32
    )
    down_sum = lax.psum_scatter(down_term.astype(BF), "seq", scatter_dimension=0, tiled=True)
    normed_two_sum = lax.psum_scatter(normed_two_term.astype(BF), "seq", scatter_dimension=0, tiled=True)
    outputs = (hidden_one + pack_features(down_sum, geo, width).astype(F32)).astype(BF)[None]
    normed_two_grad = pack_features(normed_two_sum, geo, width).astype(F32)
    gf = jnp.stack([gate_weight_grad.astype(BF), up_weight_grad.astype(BF), down_weight_grad.astype(BF)])

    unused_two, second_pull = jax.vjp(norm_scale, hidden_one, second_gain)
    hidden_norm_grad, second_gain_grad = second_pull(normed_two_grad)
    hidden_grad = incoming + hidden_norm_grad
    hidden_low = hidden_grad.astype(jnp.bfloat16)
    output_weight_grad = jnp.einsum("td,tc->dc", hidden_low, mixed_heads, preferred_element_type=jnp.float32)
    mixed_grad = jnp.einsum("td,dc->tc", hidden_low, output_full, preferred_element_type=jnp.float32).astype(
        jnp.bfloat16
    )
    grad_heads = mixed_grad.reshape(row_count, head_count, head_dim)
    prob_grad = jnp.einsum("thc,khc->htk", grad_heads, value_heads, preferred_element_type=jnp.float32)
    inner_sum = jnp.sum(probs * prob_grad, axis=-1, keepdims=True)
    score_grad = (probs * (prob_grad - inner_sum)).astype(jnp.bfloat16)
    query_act_grad = (
        jnp.einsum("htk,khc->thc", score_grad, key_heads, preferred_element_type=jnp.float32)
        .reshape(row_count, inner_width)
        .astype(jnp.bfloat16)
    )
    key_piece = jnp.einsum(
        "htk,thc->khc", score_grad, query_heads, preferred_element_type=jnp.float32
    ).reshape(length_all, inner_width)
    value_piece = jnp.einsum(
        "htk,thc->khc", probs_low, grad_heads, preferred_element_type=jnp.float32
    ).reshape(length_all, inner_width)
    own_terms = lax.psum_scatter(
        jnp.concatenate([key_piece, value_piece], axis=1).astype(jnp.bfloat16),
        "seq",
        scatter_dimension=0,
        tiled=True,
    )
    keyval_act_grad = jnp.stack([own_terms[:, :inner_width], own_terms[:, inner_width:]])
    query_weight_grad = jnp.einsum("td,tc->dc", normed, query_act_grad, preferred_element_type=jnp.float32)
    keyval_weight_grad = jnp.einsum("td,stc->sdc", normed, keyval_act_grad, preferred_element_type=jnp.float32)
    normed_grad = jnp.einsum(
        "tc,dc->td", query_act_grad, query_full, preferred_element_type=jnp.float32
    ) + jnp.einsum("stc,sdc->td", keyval_act_grad, keyval_full, preferred_element_type=jnp.float32)
    unused_three, first_pull = jax.vjp(norm_scale, inputs, first_gain)
    input_norm_grad, first_gain_grad = first_pull(normed_grad)
    input_grad = (hidden_grad + input_norm_grad).astype(jnp.bfloat16)[None]
    table_grad = jnp.einsum("htk,tkb->bh", score_grad, onehot, preferred_element_type=jnp.float32)

    grads = jnp.stack(
        [query_weight_grad, keyval_weight_grad[0], keyval_weight_grad[1], output_weight_grad]
    ).reshape(4, dp, width, seq, own_inner)
    grads = grads.transpose(3, 1, 2, 0, 4).reshape(seq, dp, width, geo.I4).astype(BF)
    wide = lambda v: jnp.pad(v, ((0, 0), (0, 0), (0, geo.I4 - v.shape[2])))
    more = jnp.concatenate(
        [
            jnp.zeros((dp, rows - width - geo.E, geo.I4), F32),
            wide(first_gain_grad.reshape(dp, 1, width)),
            wide(second_gain_grad.reshape(dp, 1, width)),
            wide(table_grad.reshape(dp, table_rows, head_count)),
        ],
        axis=1,
    ).astype(BF)
    ga = jnp.concatenate([grads, jnp.broadcast_to(more, (seq, *more.shape))], axis=2).reshape(seq, dp * rows, geo.I4)
    of, oa = scatter_grads(geo, gf, ga)

    main = oa[:width]
    query_part = main[:, :own_inner]
    keyval_part = jnp.stack([main[:, own_inner : 2 * own_inner], main[:, 2 * own_inner : 3 * own_inner]])
    output_part = main[:, 3 * own_inner :]
    gain_part = oa[rows - geo.E : rows - table_rows, :width]
    table_part = oa[rows - table_rows :, :head_count]
    return (
        outputs,
        input_grad,
        query_part,
        keyval_part,
        output_part,
        of[:2, :width],
        of[2, :width],
        gain_part,
        table_part,
    )

def fused_path(
    axes, tokens, cotangent, lengths, w_query, w_key_value, w_output, w_gate_up, w_down, norm_gains, position_bias
):
    geo = Geo(*axes, w_query.shape[0], w_down.shape[1], 4 * w_query.shape[1], tokens.shape[1], *position_bias.shape[::-1])
    saved = forward(
        geo, lengths, tokens[0].T, cotangent[0].T, w_query, w_key_value, w_output, w_gate_up, w_down, norm_gains, position_bias
    )
    outs = finish(geo, *backward(geo, *saved))
    return outs[0].T[None], outs[1].T[None], *outs[2:]


def per_device(axes, *arrays):
    tokens, w_query, w_down, position_bias = arrays[0], arrays[3], arrays[7], arrays[9]
    geo = Geo(*axes, w_query.shape[0], w_down.shape[1], 4 * w_query.shape[1], tokens.shape[1], position_bias.shape[1],
              position_bias.shape[0])
    aligned = geo.W % 8 == 0 and geo.F % 128 == 0 and geo.I4 % 128 == 0 and 2 * geo.R % 128 == 0 and geo.T % 128 == 0 and geo.I % 128 == 0
    aligned = aligned and max(2 * geo.I, geo.seq * geo.I4 // 2) <= geo.F and 4 * geo.T <= geo.L and geo.N + 2 * geo.T <= 2 * geo.L and geo.L + 256 <= geo.N
    small = (3 * geo.F + geo.seq * geo.I4 + 2 * geo.L) * geo.N * 2 <= 24 << 20
    return (fused_path if aligned and small else general_path)(axes, *arrays)


def solution(mesh):
    in_specs = (
        P("dp", "seq", None),
        P("dp", "seq", None),
        P("dp"),
        P("dp", "seq"),
        P(None, "dp", "seq"),
        P("dp", "seq"),
        P(None, "dp", "seq"),
        P("dp", "seq"),
        P(None, "dp"),
        P("dp", None),
    )
    out_specs = (
        P("dp", "seq", None),
        P("dp", "seq", None),
        P("dp", "seq"),
        P(None, "dp", "seq"),
        P("dp", "seq"),
        P(None, "dp", "seq"),
        P("dp", "seq"),
        P(None, "dp"),
        P("dp", None),
    )
    return jax.shard_map(
        functools.partial(per_device, (mesh.shape["dp"], mesh.shape["seq"])), mesh=mesh, in_specs=in_specs, out_specs=out_specs, check_vma=False
    )
```

```python
import functools
import jax
import jax.numpy as jnp
import numpy as np
from jax import lax
from jax.experimental import pallas as pl
from jax.experimental.pallas import tpu as pltpu

from jax.sharding import PartitionSpec as P

MESH = pl.DeviceIdType.MESH
BF = jnp.bfloat16
F32 = jnp.float32


class Geo:
    def __init__(self, dp, seq, width, ff, inner4, tokens, heads, table_rows):
        self.dp, self.seq = dp, seq
        self.W, self.TR, self.E = width, table_rows, 2 + table_rows
        rows = -(-(width + self.E) // 16) * 16
        self.D, self.N, self.T, self.L = dp * width, dp * rows, tokens, seq * tokens
        self.I, self.H = inner4 // 4 * seq, heads
        self.B, self.A, self.X = 2, dp // 2, seq // 2
        self.R, self.F, self.I4 = rows, ff, inner4
        self.NH = 2 if rows % 32 == 0 else 1
        self.RH = rows // self.NH
        self.NP = 3 * self.NH
        self.NZ = 2 * (self.A - 1)
        self.NY = 2 * self.A - 1


class Place:
    def __init__(self, geo):
        d, s = lax.axis_index("dp"), lax.axis_index("seq")
        self.d, self.s = d, s
        self.z, self.y = d // 2, d % 2
        self.x, self.c = s // 2, s % 2

    def dev(self, z=None, y=None, x=None, c=None):
        z = self.z if z is None else z
        y = self.y if y is None else y
        x = self.x if x is None else x
        c = self.c if c is None else c
        return (z * 2 + y, x * 2 + c)


def remote(src, dst, ss, rs, dev):
    return pltpu.make_async_remote_copy(
        src_ref=src, dst_ref=dst, send_sem=ss, recv_sem=rs, device_id=dev, device_id_type=MESH
    )


def loop(n, body):
    def step(i, carry):
        body(i)
        return carry

    lax.fori_loop(0, n, step, 0)


def enter(geo, me, work=None):
    bar = pltpu.get_barrier_semaphore()

    def greet(dev):
        pl.semaphore_signal(bar, 1, device_id=dev, device_id_type=MESH)

    greet(me.dev(y=1 - me.y))
    greet(me.dev(c=1 - me.c))
    for k in range(1, geo.X):
        greet(me.dev(x=lax.rem(me.x + k, geo.X)))

    @pl.when(me.z > 0)
    def _():
        greet(me.dev(z=me.z - 1))

    @pl.when(me.z < geo.A - 1)
    def _():
        greet(me.dev(z=me.z + 1))

    count = 2 + (geo.X - 1) + (me.z > 0).astype(jnp.int32) + (me.z < geo.A - 1).astype(jnp.int32)
    if work is not None:
        work()
    pl.semaphore_wait(bar, count)


class LineGather:
    def __init__(self, geo, me, own, held, zs, zr, ys, yr, first_y=1 << 20, bzs=None, bzr=None):
        self.geo, self.me, self.own, self.held = geo, me, own, held
        self.zs, self.zr, self.ys, self.yr = zs, zr, ys, yr
        self.first_y, self.bzs, self.bzr = first_y, bzs, bzr

    def from_z(self, way, r):
        q = self.me.z - r if way == 0 else self.me.z + r
        return q, (q >= 0) if way == 0 else (q <= self.geo.A - 1)

    def sems(self, way, r, p, other):
        slot = way * (self.geo.A - 1) + r - 1
        if other:
            return self.bzs.at[slot, p - self.first_y], self.bzr.at[slot, p - self.first_y]
        return self.zs.at[slot, p], self.zr.at[slot, p]

    def zcopy(self, way, r, p, other=False):
        me, geo = self.me, self.geo
        q, there = self.from_z(way, r - 1)
        to = me.z + 1 if way == 0 else me.z - 1
        valid = ((me.z < geo.A - 1) if way == 0 else (me.z > 0)) & there
        here = self.held(p, q * 2 + (1 - me.y if other else me.y))
        src = self.own(p) if r == 1 and not other else here
        return remote(src, here, *self.sems(way, r, p, other), me.dev(z=to)), valid

    def zarrive(self, way, r, p, other=False):
        q, valid = self.from_z(way, r)
        here = self.held(p, q * 2 + (1 - self.me.y if other else self.me.y))
        return remote(here, here, *self.sems(way, r, p, other), self.me.dev(y=1 - self.me.y)), valid, q

    def yslot(self, way, r):
        return 1 + way * (self.geo.A - 1) + r - 1 if r else 0

    def ycopy(self, way, r, p):
        me, slot = self.me, self.yslot(way, r)
        q, _ = self.from_z(way, r)
        src = self.held(p, q * 2 + me.y) if r else self.own(p)
        return remote(src, self.held(p, q * 2 + me.y), self.ys.at[slot, p], self.yr.at[slot, p], me.dev(y=1 - me.y))

    def yarrive(self, way, r, p):
        me, slot = self.me, self.yslot(way, r)
        q, _ = self.from_z(way, r)
        here = self.held(p, q * 2 + 1 - me.y)
        return remote(here, here, self.ys.at[slot, p], self.yr.at[slot, p], me.dev(y=1 - me.y)), q

    def begin_y(self, p):
        self.ycopy(0, 0, p).start()

    def begin_z(self, p, other=False):
        for way in (0, 1):
            copy, valid = self.zcopy(way, 1, p, other)

            @pl.when(valid)
            def _():
                copy.start()

    def begin(self, p):
        self.begin_y(p)
        self.begin_z(p)

    def turn(self, p):
        self.yarrive(0, 0, p)[0].wait_recv()
        self.begin_z(p, True)

    def step(self, r, p, on_held=None, kinds=(False,), pass_y=True):
        for other in kinds:
            for way in (0, 1):
                copy, valid, q = self.zarrive(way, r, p, other)

                @pl.when(valid)
                def _():
                    copy.wait_recv()
                    if r < self.geo.A - 1:
                        onward, may = self.zcopy(way, r + 1, p, other)

                        @pl.when(may)
                        def _():
                            onward.start()

                    if pass_y:
                        self.ycopy(way, r, p).start()
                    if on_held is not None:
                        on_held(q * 2 + self.me.y)

    def step_both(self, r, p):
        self.step(r, p, None, (False, True), False)

    def ystep(self, r, p, on_held=None):
        for way in (0, 1) if r else (0,):
            copy, q = self.yarrive(way, r, p)

            def go():
                copy.wait_recv()
                if on_held is not None:
                    on_held(q * 2 + 1 - self.me.y)

            if r:
                pl.when(self.from_z(way, r)[1])(go)
            else:
                go()

    def drain(self, p, kinds=(False,), pass_y=True):
        self.ycopy(0, 0, p).wait_send()
        for r in range(1, self.geo.A):
            for way in (0, 1):
                for other in kinds:
                    copy, valid = self.zcopy(way, r, p, other)

                    @pl.when(valid)
                    def _():
                        copy.wait_send()

                if pass_y:

                    @pl.when(self.from_z(way, r)[1])
                    def _():
                        self.ycopy(way, r, p).wait_send()


class LineScatter:
    def __init__(self, geo, me, part, ybuf, zbuf, stage, zs, zr, ys, yr, finish):
        self.__dict__.update(locals())

    def turns(self):
        geo, me = self.geo, self.me
        for k in range(geo.A - 1):
            yield 0, k, geo.A - 1 - k, k < geo.A - 1 - me.z
            yield 1, k, k, k < me.z

    def slot(self, way, k):
        return way * (self.geo.A - 1) + k

    def ycopy(self, slot, t, p):
        me = self.me
        return remote(
            self.part(p, t * 2 + 1 - me.y),
            self.ybuf(p, t),
            self.ys.at[slot, p],
            self.yr.at[slot, p],
            me.dev(y=1 - me.y),
        )

    def zcopy(self, way, k, p):
        me = self.me
        to = me.z + 1 if way == 0 else me.z - 1
        slot = self.slot(way, k)
        return remote(
            self.stage(way, p, k), self.zbuf(way, p, k), self.zs.at[slot, p], self.zr.at[slot, p], me.dev(z=to)
        )

    def ysend(self, p, k):
        for way, kk, t, valid in self.turns():
            if kk == k:

                @pl.when(valid)
                def _():
                    self.ycopy(self.slot(way, kk), t, p).start()

    def ysend_own(self, p):
        self.ycopy(self.geo.NZ, self.me.z, p).start()

    def step(self, k, p):
        geo, me = self.geo, self.me
        for way, kk, t, valid in self.turns():
            if kk == k:

                @pl.when(valid)
                def _():
                    self.ycopy(self.slot(way, k), t, p).wait_recv()
                    total = self.part(p, t * 2 + me.y)[...].astype(F32) + self.ybuf(p, t)[...].astype(F32)
                    out = self.stage(way, p, k)
                    comes = me.z > 0 if way == 0 else me.z < geo.A - 1

                    @pl.when(comes)
                    def _():
                        self.zcopy(way, k, p).wait_recv()
                        out[...] = (total + self.zbuf(way, p, k)[...].astype(F32)).astype(BF)

                    @pl.when(jnp.logical_not(comes))
                    def _():
                        out[...] = total.astype(BF)

                    self.zcopy(way, k, p).start()

    def own(self, p):
        geo, me = self.geo, self.me
        self.ycopy(geo.NZ, me.z, p).wait_recv()
        total = self.part(p, me.z * 2 + me.y)[...].astype(F32) + self.ybuf(p, me.z)[...].astype(F32)
        kup = jnp.minimum(geo.A - 1 - me.z, geo.A - 2)
        kdown = jnp.minimum(me.z, geo.A - 2)

        def arrive(way, k):
            slot = way * (geo.A - 1) + k
            here = self.zbuf(way, p, k)
            remote(here, here, self.zs.at[slot, p], self.zr.at[slot, p], me.dev(y=1 - me.y)).wait_recv()
            return here[...].astype(F32)

        @pl.when(me.z == 0)
        def _():
            self.finish(p, total + arrive(1, kdown))

        @pl.when(me.z == geo.A - 1)
        def _():
            self.finish(p, total + arrive(0, kup))

        @pl.when((me.z > 0) & (me.z < geo.A - 1))
        def _():
            self.finish(p, total + arrive(0, kup) + arrive(1, kdown))

    def drain(self, p):
        for way, k, t, valid in self.turns():

            @pl.when(valid)
            def _():
                self.ycopy(self.slot(way, k), t, p).wait_send()
                self.zcopy(way, k, p).wait_send()

        self.ycopy(self.geo.NZ, self.me.z, p).wait_send()


NEGATIVE = -1e30
EPSILON = 1e-06
LIMITS = (12, 16, 23, 32, 46, 64, 91)


def bucket_ids(offsets):
    distance = jnp.abs(offsets)
    larger = 8 + sum(((distance >= threshold).astype(jnp.int32) for threshold in LIMITS))
    nearby = jnp.where(distance < 8, distance, larger)
    return jnp.where(offsets > 0, 16, 0) + nearby


def norm_scale(values, gain_vector):
    return (
        values
        * lax.rsqrt(jnp.mean(values * values, axis=-1, keepdims=True) + EPSILON)
        * gain_vector
    )


def gated(gate_value, upward):
    return jax.nn.gelu(gate_value, approximate=True) * upward


def gather_kernel(geo, wf, wa, WF, WA, local, zs, zr, ys, yr, azs, azr, ays, ayr, xs, xr, cs, cr):
    me = Place(geo)
    R, RH, NH, dp, X = geo.R, geo.RH, geo.NH, geo.dp, geo.X
    mine = [
        pltpu.make_async_copy(wf, WF.at[:, pl.ds(pl.multiple_of(me.d * R, 16), R), :], local.at[0]),
        pltpu.make_async_copy(wa, WA.at[me.s, pl.ds(pl.multiple_of(me.d * R, 16), R), :], local.at[1]),
    ]
    for copy in mine:
        copy.start()
    enter(geo, me)

    def own_f(p):
        return wf.at[p // NH, pl.ds(pl.multiple_of((p % NH) * RH, 16), RH), :]

    def held_f(p, g):
        return WF.at[p // NH, pl.ds(pl.multiple_of(g * R + (p % NH) * RH, 16), RH), :]

    def held_a(s, g):
        return WA.at[s, pl.ds(pl.multiple_of(g * R, 16), R), :]

    ffn = LineGather(geo, me, own_f, held_f, zs, zr, ys, yr)
    att = LineGather(geo, me, lambda p: wa, lambda p, g: held_a(me.s, g), azs, azr, ays, ayr)

    def xcopy(k, g, src):
        to = lax.rem(me.x + k, X)
        return remote(src, held_a(me.s, g), xs.at[k - 1, g], xr.at[k - 1, g], me.dev(x=to))

    def xarrive(k, g):
        src_x = lax.rem(me.x - k + X, X)
        here = held_a(src_x * 2 + me.c, g)
        return remote(here, here, xs.at[k - 1, g], xr.at[k - 1, g], me.dev(c=1 - me.c)), here

    def ccopy(k, g, src, s):
        return remote(src, held_a(s, g), cs.at[k, g], cr.at[k, g], me.dev(c=1 - me.c))

    def spread(g, src=None):
        src = held_a(me.s, g) if src is None else src
        for k in range(1, X):
            xcopy(k, g, src).start()
        ccopy(0, g, src, me.s).start()

    att.begin(0)
    spread(me.d, wa)
    loop(geo.NP, ffn.begin)
    att.ystep(0, 0, spread)
    for r in range(1, geo.A):
        att.step(r, 0, spread)
        att.ystep(r, 0, spread)

    def from_x(g):
        for k in range(1, X):
            copy, here = xarrive(k, g)
            copy.wait_recv()
            ccopy(k, g, here, lax.rem(me.x - k + X, X) * 2 + me.c).start()

    loop(dp, from_x)
    for r in range(1, geo.A):
        loop(geo.NP, lambda p: ffn.step(r, p))
    for r in range(geo.A):
        loop(geo.NP, lambda p: ffn.ystep(r, p))

    def finish(g):
        for k in range(X):
            s = lax.rem(me.x - k + X, X) * 2 + 1 - me.c
            here = held_a(s, g)
            remote(here, here, cs.at[k, g], cr.at[k, g], me.dev(c=1 - me.c)).wait_recv()
            ccopy(k, g, here, s).wait_send()
            if k:
                xcopy(k, g, here).wait_send()

    loop(dp, finish)
    att.drain(0)
    loop(geo.NP, ffn.drain)
    for copy in mine:
        copy.wait()


def scatter_kernel(
    geo, gf, ga, of, oa, yb, zb, st, cb, xb, xst, pa, ayb, azb, ast,
    zs, zr, ys, yr, azs, azr, ays, ayr, xs, xr, cs, cr,
):
    me = Place(geo)
    R, RH, NH, dp, X, A = geo.R, geo.RH, geo.NH, geo.dp, geo.X, geo.A
    enter(geo, me)

    def rows(g, p):
        return pl.ds(pl.multiple_of(g * R + (p % NH) * RH, 16), RH)

    def piece(buf, i, p):
        return buf.at[i, p // NH, pl.ds(pl.multiple_of((p % NH) * RH, 16), RH), :]

    def finish_f(p, value):
        of[p // NH, pl.ds(pl.multiple_of((p % NH) * RH, 16), RH), :] = value

    ffn = LineScatter(
        geo, me,
        lambda p, g: gf.at[p // NH, rows(g, p), :],
        lambda p, t: piece(yb, t, p),
        lambda way, p, k: piece(zb, way * (A - 1) + k, p),
        lambda way, p, k: piece(st, way * (A - 1) + k, p),
        zs, zr, ys, yr, finish_f,
    )

    def block(g):
        return pl.ds(pl.multiple_of(g * R, 16), R)

    def finish_a(p, value):
        oa[...] = value

    att = LineScatter(
        geo, me,
        lambda p, g: pa.at[block(g), :],
        lambda p, t: ayb.at[t],
        lambda way, p, k: azb.at[way * (A - 1) + k],
        lambda way, p, k: ast.at[way * (A - 1) + k],
        azs, azr, ays, ayr, finish_a,
    )

    def ccopy(k, g):
        to_x = lax.rem(me.x + k, X)
        return remote(
            ga.at[to_x * 2 + 1 - me.c, block(g), :], cb.at[k, block(g), :], cs.at[k, g], cr.at[k, g], me.dev(c=1 - me.c)
        )

    def xcopy(k, g):
        return remote(
            xst.at[k - 1, block(g), :], xb.at[k - 1, block(g), :], xs.at[k - 1, g], xr.at[k - 1, g],
            me.dev(x=lax.rem(me.x + k, X)),
        )

    def to_core(g):
        for k in (*range(1, X), 0):
            ccopy(k, g).start()

    def to_x(g):
        for k in range(1, X):
            ccopy(k, g).wait_recv()
            s = lax.rem(me.x + k, X) * 2 + me.c
            xst[k - 1, block(g), :] = (
                ga[s, block(g), :].astype(F32) + cb[k, block(g), :].astype(F32)
            ).astype(BF)
            xcopy(k, g).start()

    def meet(g):
        ccopy(0, g).wait_recv()
        total = ga[me.s, block(g), :].astype(F32) + cb[0, block(g), :].astype(F32)
        for k in range(1, X):
            xcopy(k, g).wait_recv()
            total += xb[k - 1, block(g), :].astype(F32)
        pa[block(g), :] = total.astype(BF)

    def free(g):
        for k in range(X):
            ccopy(k, g).wait_send()
            if k:
                xcopy(k, g).wait_send()

    for k in range(A - 1):
        loop(geo.NP, lambda p: ffn.ysend(p, k))
    loop(geo.NP, ffn.ysend_own)
    loop(dp, to_core)
    loop(dp, to_x)
    for k in range(A - 1):
        loop(geo.NP, lambda p: ffn.step(k, p))
    loop(geo.NP, ffn.own)
    loop(dp, meet)
    for k in range(A - 1):
        att.ysend(0, k)
    att.ysend_own(0)
    for k in range(A - 1):
        att.step(k, 0)
    att.own(0)
    loop(dp, free)
    att.drain(0)
    loop(geo.NP, ffn.drain)


def gather_weights(geo, wf, wa):
    dma = pltpu.SemaphoreType.DMA
    sems = [
        dma((2,)),
        dma((geo.NZ, geo.NP)), dma((geo.NZ, geo.NP)), dma((geo.NY, geo.NP)), dma((geo.NY, geo.NP)),
        dma((geo.NZ, 1)), dma((geo.NZ, 1)), dma((geo.NY, 1)), dma((geo.NY, 1)),
        dma((geo.X - 1, geo.dp)), dma((geo.X - 1, geo.dp)), dma((geo.X, geo.dp)), dma((geo.X, geo.dp)),
    ]
    return pl.pallas_call(
        functools.partial(gather_kernel, geo),
        out_shape=(
            jax.ShapeDtypeStruct((3, geo.dp * geo.R, geo.F), BF),
            jax.ShapeDtypeStruct((geo.seq, geo.dp * geo.R, geo.I4), BF),
        ),
        in_specs=[pl.BlockSpec(memory_space=pl.ANY)] * 2,
        out_specs=[pl.BlockSpec(memory_space=pl.ANY)] * 2,
        scratch_shapes=sems,
        compiler_params=pltpu.CompilerParams(collective_id=0, has_side_effects=True, vmem_limit_bytes=48 << 20),
        name="gather_weights",
    )(wf, wa)


def scatter_grads(geo, gf, ga):
    dma = pltpu.SemaphoreType.DMA
    n, X, A, R = geo.dp * geo.R, geo.X, geo.A, geo.R
    scratch = [
        pltpu.VMEM((A, 3, R, geo.F), BF), pltpu.VMEM((geo.NZ, 3, R, geo.F), BF), pltpu.VMEM((geo.NZ, 3, R, geo.F), BF),
        pltpu.VMEM((X, n, geo.I4), BF), pltpu.VMEM((X - 1, n, geo.I4), BF), pltpu.VMEM((X - 1, n, geo.I4), BF),
        pltpu.VMEM((n, geo.I4), BF),
        pltpu.VMEM((A, R, geo.I4), BF), pltpu.VMEM((geo.NZ, R, geo.I4), BF), pltpu.VMEM((geo.NZ, R, geo.I4), BF),
        dma((geo.NZ, geo.NP)), dma((geo.NZ, geo.NP)), dma((geo.NZ + 1, geo.NP)), dma((geo.NZ + 1, geo.NP)),
        dma((geo.NZ, 1)), dma((geo.NZ, 1)), dma((geo.NZ + 1, 1)), dma((geo.NZ + 1, 1)),
        dma((X - 1, geo.dp)), dma((X - 1, geo.dp)), dma((X, geo.dp)), dma((X, geo.dp)),
    ]
    return pl.pallas_call(
        functools.partial(scatter_kernel, geo),
        out_shape=(
            jax.ShapeDtypeStruct((3, R, geo.F), F32),
            jax.ShapeDtypeStruct((R, geo.I4), F32),
        ),
        in_specs=[pl.BlockSpec(memory_space=pltpu.VMEM)] * 2,
        out_specs=[pl.BlockSpec(memory_space=pltpu.VMEM)] * 2,
        scratch_shapes=scratch,
        compiler_params=pltpu.CompilerParams(collective_id=1, has_side_effects=True, vmem_limit_bytes=60 << 20),
        name="scatter_grads",
    )(gf, ga)


class SeqGather:
    def __init__(self, geo, me, held, xs, xr, cs, cr):
        self.geo, self.me, self.held = geo, me, held
        self.xs, self.xr, self.cs, self.cr = xs, xr, cs, cr

    def ccopy(self, k):
        me, X = self.me, self.geo.X
        here = self.held(lax.rem(me.x - k + X, X) * 2 + me.c)
        return remote(here, here, self.cs.at[k], self.cr.at[k], me.dev(c=1 - me.c))

    def xcopy(self, k):
        me = self.me
        here = self.held(me.s)
        return remote(here, here, self.xs.at[k - 1], self.xr.at[k - 1], me.dev(x=lax.rem(me.x + k, self.geo.X)))

    def begin(self):
        for k in range(1, self.geo.X):
            self.xcopy(k).start()
        self.ccopy(0).start()

    def relay(self):
        for k in range(1, self.geo.X):
            self.xcopy(k).wait_recv()
            self.ccopy(k).start()

    def finish(self):
        for k in range(self.geo.X):
            self.ccopy(k).wait_recv()
            self.ccopy(k).wait_send()
            if k:
                self.xcopy(k).wait_send()


def dot(a, b, dims=((1,), (0,))):
    return lax.dot_general(a, b, (dims, ((), ())), preferred_element_type=F32)


NT = ((1,), (1,))
TN = ((0,), (0,))


def place_columns(geo, out):
    own = geo.I4 // 4
    c = lax.broadcasted_iota(jnp.int32, out.shape, 0)
    j = lax.broadcasted_iota(jnp.int32, out.shape, 1)
    to = c + 3 * own
    for s in range(1, geo.seq):
        to += jnp.where(c >= s * own, 3 * own, 0)
    out[...] = jnp.where(j == to, 1.0, 0.0).astype(BF)


def place_buckets(geo, out):
    row = lax.broadcasted_iota(jnp.int32, out.shape, 0)
    at = row % 16 - (16 - geo.TR)
    bucket = bucket_ids(lax.broadcasted_iota(jnp.int32, out.shape, 1) - 256)
    out[...] = jnp.where((at >= 0) & (bucket == row // 16 * geo.TR + at), 1.0, 0.0).astype(BF)


def spread(geo, value):
    value = value.astype(F32)
    gap = jnp.zeros((geo.R - geo.W, value.shape[1]), F32)
    parts = [v for g in range(geo.dp) for v in (value[g * geo.W : (g + 1) * geo.W], gap)]
    return jnp.concatenate(parts, axis=0).T.astype(BF)


def pack(geo, value):
    value = value.T
    return jnp.concatenate([value[g * geo.R : g * geo.R + geo.W] for g in range(geo.dp)], axis=0).astype(BF)


def shear(value, sign):
    rows, lanes = value.shape
    row = lax.broadcasted_iota(jnp.int32, (rows, 1), 0)
    bit = 1
    while bit < rows:
        moved = pltpu.roll(value, bit if sign > 0 else lanes - bit, 1)
        value = jnp.where((row & bit) != 0, moved, value)
        bit *= 2
    return value


def gelu_parts(g):
    k0 = np.float32(np.sqrt(2 / np.pi))
    t = jnp.tanh(k0 * (g + np.float32(0.044715) * (g * g * g)))
    half = 0.5 * (1.0 + t)
    slope = half + 0.5 * g * (1.0 - t * t) * (k0 * (1.0 + np.float32(3 * 0.044715) * (g * g)))
    return g * half, slope


def forward_kernel(
    geo, length_in, x_in, c_in, wq, wkv, wo, wgu, wd, norm_gains, position_bias,
    oX, oWA, oqkv, oKV, oP, omixed, ohid, oX2, oC, oact, opart, ogain,
    WF0, WF1, WA, xv, C, X2, KV, qkv, strip, mixed, hid, pst, act, part, got, gain, raw, wst, ast, gst, bst, ex, pout, onehot, length,
    local, outs, psem, zs, zr, ys, yr, bzs, bzr, azs, azr, ays, ayr, xs, xr, cs, cr, gxs, gxr, gcs, gcr, ps, pr, wsem, asem,
):
    me = Place(geo)
    R, RH, NH, dp, X, T, N, I = geo.R, geo.RH, geo.NH, geo.dp, geo.X, geo.T, geo.N, geo.I
    I4, S, L = geo.I4, geo.seq, geo.L
    block = lambda i, n: pl.ds(pl.multiple_of(i * n, 16), n)
    loads = [
        (wq, ast.at[0]), (wkv.at[0], ast.at[1]), (wkv.at[1], ast.at[2]), (wo, ast.at[3]), (norm_gains, gst),
        (position_bias, bst), (wgu.at[0], wst.at[0]), (wgu.at[1], wst.at[1]), (wd, wst.at[2]), (x_in, raw.at[0]),
        (c_in, raw.at[1]), (length_in, length),
    ]
    loads = [pltpu.make_async_copy(src, dst, local.at[i]) for i, (src, dst) in enumerate(loads)]
    for copy in loads:
        copy.start()
    W, E = geo.W, geo.E

    def own_attention():
        ex[...] = jnp.zeros_like(ex)
        for copy in loads[:6]:
            copy.wait()
        ex[R - W - E : R - W - E + 2, :W] = gst[...]
        ex[R - W - E + 2 :, : geo.H] = bst[...]
        columns = jnp.concatenate([ast[k] for k in range(4)], axis=1)
        WA[me.s, block(me.d, R), :] = jnp.concatenate([columns, ex[...]], axis=0).astype(BF)

    enter(geo, me, own_attention)

    WFs = (WF0, WF1)
    cuts = ((0, WF0.shape[2]), (WF0.shape[2], geo.F))

    def held_f(p, g):
        return WFs[p // 3].at[p % 3, block(g, R), :]

    def held_a(s, g):
        return WA.at[s, block(g, R), :]

    special = 2
    others = [p for p in range(6) if p != special]
    ffn = LineGather(geo, me, lambda p: held_f(p, me.d), held_f, zs, zr, ys, yr, special, bzs, bzr)
    att = LineGather(geo, me, lambda p: held_a(me.s, me.d), lambda p, g: held_a(me.s, g), azs, azr, ays, ayr)

    def xcopy(k, g, src):
        to = lax.rem(me.x + k, X)
        return remote(src, held_a(me.s, g), xs.at[k - 1, g], xr.at[k - 1, g], me.dev(x=to))

    def xarrive(k, g):
        src_x = lax.rem(me.x - k + X, X)
        here = held_a(src_x * 2 + me.c, g)
        return remote(here, here, xs.at[k - 1, g], xr.at[k - 1, g], me.dev(c=1 - me.c)), here

    def ccopy(k, g, src, s):
        return remote(src, held_a(s, g), cs.at[k, g], cr.at[k, g], me.dev(c=1 - me.c))

    def share(g):
        src = held_a(me.s, g)
        for k in range(1, X):
            xcopy(k, g, src).start()
        ccopy(0, g, src, me.s).start()

    half = T // 2

    def seq_gather(i, ref, first, count):
        held = lambda s: ref.at[pl.ds(pl.multiple_of(s * T + first, 16), count), :]
        return SeqGather(geo, me, held, gxs.at[i], gxr.at[i], gcs.at[i], gcr.at[i])

    gather_kv = seq_gather(0, KV, 0, T)
    gather_x2 = [seq_gather(1, X2, 0, half), seq_gather(2, X2, half, half)]
    gather_c = [seq_gather(3, C, 0, half), seq_gather(4, C, half, half)]

    att.begin(0)
    share(me.d)
    for m in range(3):
        loads[6 + m].wait()
        for ref, cut in zip(WFs, cuts):
            lanes = slice(*cut)
            own = jnp.concatenate([wst[m, :, lanes], jnp.zeros((R - W, cut[1] - cut[0]), F32)], axis=0)
            ref[m, block(me.d, R), :] = own.astype(BF)
    ffn.begin_y(special)
    for p in range(6):
        if p == special:
            ffn.begin_z(p)
        else:
            ffn.begin(p)
    events = [(r, p) for r in range(1, geo.A) for p in range(6)]

    def forward_on(r, p):
        if p == special:
            ffn.step_both(r, p)
        else:
            ffn.step(r, p)

    def run(count):
        for _ in range(min(count, len(events))):
            forward_on(*events.pop(0))

    att.ystep(0, 0, share)
    for r in range(1, geo.A):
        att.step(r, 0, share)
        att.ystep(r, 0, share)
    ffn.turn(special)
    place_columns(geo, pout)
    place_buckets(geo, onehot)
    for copy in loads[9:]:
        copy.wait()
    xv[...] = spread(geo, raw[0])
    C[block(me.s, T), :] = spread(geo, raw[1])
    gather_c[0].begin()

    def from_x(g):
        for k in range(1, X):
            copy, here = xarrive(k, g)
            copy.wait_recv()
            ccopy(k, g, here, lax.rem(me.x - k + X, X) * 2 + me.c).start()

    for g in range(dp):
        from_x(g)
        if g >= 3:
            run(1)

    def settle(g):
        for k in range(X):
            s = lax.rem(me.x - k + X, X) * 2 + 1 - me.c
            here = held_a(s, g)
            remote(here, here, cs.at[k, g], cr.at[k, g], me.dev(c=1 - me.c)).wait_recv()

    loop(dp, settle)

    extra = jnp.concatenate([WA[0, g * R + R - 16 : g * R + R, :] for g in range(dp)], axis=0)
    lines = extra.astype(F32)
    gain[...] = jnp.zeros_like(gain)
    for g in range(dp):
        for e in range(2):
            at = g * 16 + 16 - E + e
            gain[e : e + 1, g * R : (g + 1) * R] = lines[at : at + 1, :R]
    bias = dot(extra[:, :128], onehot[...], TN)

    inputs = xv[...].astype(F32)
    scale = lax.rsqrt(jnp.sum(inputs * inputs, axis=-1, keepdims=True) / np.float32(geo.D) + EPSILON)
    normed = (inputs * scale * gain[0:1, :]).astype(BF)
    columns = jnp.concatenate([dot(normed, WA[s]) for s in range(S)], axis=1)
    for kind in (1, 2, 0):
        moved = pltpu.roll(columns, (3 - kind) * (I4 // 4), 1).astype(BF)
        qkv[:, kind * I : (kind + 1) * I] = dot(moved, pout[...], NT).astype(BF)
        if kind == 2:
            KV[block(me.s, T), :] = qkv[:, I:]
            gather_kv.begin()
            gather_c[1].begin()
    gather_c[0].relay()
    run(1)
    writes = []

    def write(src, dst):
        copy = pltpu.make_async_copy(src, dst, outs.at[len(writes)])
        copy.start()
        writes.append(copy)

    write(xv, oX)
    write(WA, oWA)
    write(qkv, oqkv)
    write(gain, ogain)
    NB = L // 128
    for h in range(geo.H):
        band = shear(jnp.broadcast_to(bias[h : h + 1, :], (128, 512)), 1)[:, 128:512].astype(BF)
        strip[h, :, (NB - 2) * 128 : (NB + 1) * 128] = band
        far = (NB - 2) * 128
        strip[h, :, :far] = jnp.broadcast_to(bias[h : h + 1, 0:1], (128, far)).astype(BF)
        strip[h, :, (NB + 1) * 128 :] = jnp.broadcast_to(bias[h : h + 1, 511:512], (128, far)).astype(BF)
    run(1)
    gather_kv.relay()
    gather_kv.finish()
    run(1)
    write(KV, oKV)

    hd = I // geo.H
    per = 128 // hd
    valid = lax.broadcasted_iota(jnp.int32, (1, L), 1) < length[0]

    def pair(t, first):
        rows = slice(first, first + half)
        lanes = pl.ds(pl.multiple_of(t * 128, 128), 128)
        head = lax.broadcasted_iota(jnp.int32, (1, 128), 1) // hd
        keys = KV[:, lanes]
        values = KV[:, pl.ds(pl.multiple_of(I + t * 128, 128), 128)]
        queries = qkv[rows, lanes]
        outs_ = jnp.zeros((half, 128), F32)
        for e in range(per):
            h = t * per + e
            scores = dot(jnp.where(head == e, queries, jnp.zeros_like(queries)), keys, NT)
            shift = [
                strip[h, :, pl.ds(pl.multiple_of((NB - 1 - me.s * (T // 128) - b) * 128, 128), L)].astype(F32)
                for b in range(first // 128, (first + half) // 128)
            ]
            scores = jnp.where(valid, scores + jnp.concatenate(shift, axis=0), np.float32(NEGATIVE))
            top = jnp.max(scores, axis=-1, keepdims=True)
            probs = jnp.exp(scores - top)
            probs = probs * (1.0 / jnp.sum(probs, axis=-1, keepdims=True))
            copy = pltpu.make_async_copy(pst.at[e], oP.at[h, rows, :], psem.at[e])

            @pl.when((t > 0) | (first > 0))
            def _():
                copy.wait()

            pst[e] = probs
            copy.start()
            mine = dot(probs.astype(BF), values)
            outs_ = jnp.where(head == e, mine, outs_)
        mixed[rows, lanes] = outs_.astype(BF)

    for first in (0, half):
        rows = slice(first, first + half)
        for t in range(I // 128):
            pair(t, first)
            if t < (0 if first else 2):
                run(1)
        spread_mixed = dot(mixed[rows, :], pout[...]).astype(BF)
        total = xv[rows, :].astype(F32)
        for s in range(S):
            total += dot(spread_mixed[:, s * I4 : (s + 1) * I4], WA[s], NT)
        hid[rows, :] = total
        scale = lax.rsqrt(jnp.sum(total * total, axis=-1, keepdims=True) / np.float32(geo.D) + EPSILON)
        X2[pl.ds(pl.multiple_of(me.s * T + first, 16), half), :] = (total * scale * gain[1:2, :]).astype(BF)
        gather_x2[first // half].begin()
        run(1)
        if first == 0:
            gather_c[1].relay()
    for e in range(per):
        pltpu.make_async_copy(pst.at[e], oP.at[e, half:, :], psem.at[e]).wait()
    write(mixed, omixed)
    write(hid, ohid)
    for part_c in gather_c:
        part_c.finish()
    write(C, oC)
    run(1)
    gather_x2[0].relay()
    run(len(events) - 3)
    gather_x2[1].relay()
    run(len(events) - 2)
    for part_x2 in gather_x2:
        part_x2.finish()
    write(X2, oX2)

    def pcopy(n, k):
        return remote(part.at[0, n, k], got.at[n, k], ps.at[n, k], pr.at[n, k], me.dev(c=1 - me.c))

    def act_out(i):
        k = X - 1 - i % X
        s = lax.rem(me.x + k, X) * 2 + lax.rem(1 + i // X + me.c, 2)
        rows, lanes = block(s, T), slice(*cuts[1])
        return pltpu.make_async_copy(act.at[:, rows, lanes], oact.at[:, rows, lanes], asem.at[i])

    def tokens_block(i, group):
        k = X - 1 - i % X
        e = i // X
        s = lax.rem(me.x + k, X) * 2 + lax.rem(1 + e + me.c, 2)
        rows = block(s, T)
        lanes = slice(*cuts[group])
        gate_w, up_w, down_w = (WFs[group].at[m] for m in range(3))
        xb = X2[rows, :]
        gate = dot(xb, gate_w[...])
        upward = dot(xb, up_w[...])
        back = dot(C[rows, :], down_w[...])
        value, slope = gelu_parts(gate)
        activated = (value * upward).astype(BF)
        first = (back * upward * slope).astype(BF)
        second = (back * value).astype(BF)
        act[0, rows, lanes] = first
        act[1, rows, lanes] = second
        act[2, rows, lanes] = activated
        if group:
            act_out(i).start()
        terms = dot(first, gate_w[...], NT) + dot(second, up_w[...], NT), dot(activated, down_w[...], NT)
        for n, term in enumerate(terms):
            if group:
                term += part[e, n, k].astype(F32)
            part[e, n, k] = term.astype(BF)
        if group:

            @pl.when(e == 0)
            def _():
                for n in range(2):
                    pcopy(n, k).start()

            @pl.when(e == 1)
            def _():
                for n in range(2):
                    pcopy(n, k).wait_recv()
                    part[1, n, k] = (part[1, n, k].astype(F32) + got[n, k].astype(F32)).astype(BF)
                    pltpu.make_async_copy(part.at[1, n, k], opart.at[n, k], wsem.at[n, k]).start()

    for group in range(2):
        for r in range(geo.A):
            for p in others:
                if p // 3 == group:
                    ffn.ystep(r, p)

        def with_events(i):
            tokens_block(i, group)
            for n, event in enumerate(() if group else [events.pop(0) for _ in range(len(events))]):

                @pl.when(i == n)
                def _():
                    forward_on(*event)

        loop(2 * X, with_events)
        if not group:
            write(act.at[:, :, slice(*cuts[0])], oact.at[:, :, slice(*cuts[0])])
    for k in range(X):
        for n in range(2):
            pcopy(n, k).wait_send()
            pltpu.make_async_copy(part.at[1, n, k], opart.at[n, k], wsem.at[n, k]).wait()

    def finish(g):
        for k in range(X):
            s = lax.rem(me.x - k + X, X) * 2 + 1 - me.c
            here = held_a(s, g)
            ccopy(k, g, here, s).wait_send()
            if k:
                xcopy(k, g, here).wait_send()

    loop(dp, finish)
    att.drain(0)
    for p in others:
        ffn.drain(p)
    ffn.drain(special, (False, True), False)
    for copy in writes:
        copy.wait()
    loop(2 * X, lambda i: act_out(i).wait())


def forward(geo, *arrays):
    dma = pltpu.SemaphoreType.DMA
    S, N, F, T, L, I, H, X, I4 = geo.seq, geo.N, geo.F, geo.T, geo.L, geo.I, geo.H, geo.X, geo.I4
    per = 128 // (I // H)
    first = (F // 128 + 1) // 2 * 128
    out_shape = [
        ((T, N), BF), ((S, N, I4), BF), ((T, 3 * I), BF), ((L, 2 * I), BF), ((H, T, L), F32), ((T, I), BF),
        ((T, N), F32), ((L, N), BF), ((L, N), BF), ((3, L, F), BF), ((2, X, T, N), BF), ((8, N), F32),
    ]
    V = pltpu.VMEM
    scratch = [
        V((3, N, first), BF), V((3, N, F - first), BF), V((S, N, I4), BF), V((T, N), BF), V((L, N), BF), V((L, N), BF), V((L, 2 * I), BF),
        V((T, 3 * I), BF), V((H, 128, 2 * L - 128), BF), V((T, I), BF), V((T, N), F32),
        V((per, T // 2, L), F32), V((3, L, F), BF), V((2, 2, X, T, N), BF), V((2, X, T, N), BF), V((8, N), F32),
        V((2, geo.D, T), BF), V((3, geo.W, F), F32), V((4, geo.W, I4 // 4), F32), V((2, geo.W), F32), V((geo.TR, H), F32),
        V((geo.R - geo.W, I4), F32),
        V((I, S * I4), BF), V((geo.dp * 16, 512), BF), pltpu.SMEM((1,), jnp.int32),
        dma((12,)), dma((13,)), dma((per,)),
        dma((geo.NZ, 6)), dma((geo.NZ, 6)), dma((geo.NY, 6)), dma((geo.NY, 6)),
        dma((geo.NZ, 1)), dma((geo.NZ, 1)),
        dma((geo.NZ, 1)), dma((geo.NZ, 1)), dma((geo.NY, 1)), dma((geo.NY, 1)),
        dma((X - 1, geo.dp)), dma((X - 1, geo.dp)), dma((X, geo.dp)), dma((X, geo.dp)),
        dma((5, X - 1)), dma((5, X - 1)), dma((5, X)), dma((5, X)),
        dma((2, X)), dma((2, X)), dma((2, X)), dma((2 * X,)),
    ]
    return pl.pallas_call(
        functools.partial(forward_kernel, geo),
        out_shape=[jax.ShapeDtypeStruct(*v) for v in out_shape],
        in_specs=[pl.BlockSpec(memory_space=pl.ANY)] * len(arrays),
        out_specs=[pl.BlockSpec(memory_space=pl.ANY)] * len(out_shape),
        scratch_shapes=scratch,
        compiler_params=pltpu.CompilerParams(collective_id=0, has_side_effects=True, vmem_limit_bytes=63 << 20),
        name="forward",
    )(*arrays)


class SeqScatter:
    def __init__(self, geo, me, part, cb, xb, cs, cr, xs, xr):
        self.__dict__.update(locals())

    def ccopy(self, k):
        me = self.me
        to = lax.rem(me.x + k, self.geo.X)
        return remote(self.part(to * 2 + 1 - me.c), self.cb(k), self.cs.at[k], self.cr.at[k], me.dev(c=1 - me.c))

    def xcopy(self, k):
        me = self.me
        to = lax.rem(me.x + k, self.geo.X)
        return remote(self.part(to * 2 + me.c), self.xb(k), self.xs.at[k - 1], self.xr.at[k - 1], me.dev(x=to))

    def to_core(self):
        for k in (*range(1, self.geo.X), 0):
            self.ccopy(k).start()

    def to_x(self):
        for k in range(1, self.geo.X):
            self.ccopy(k).wait_recv()
            out = self.part(lax.rem(self.me.x + k, self.geo.X) * 2 + self.me.c)
            out[...] = (out[...].astype(F32) + self.cb(k)[...].astype(F32)).astype(BF)
            self.xcopy(k).start()

    def meet(self):
        self.ccopy(0).wait_recv()
        total = self.part(self.me.s)[...].astype(F32) + self.cb(0)[...].astype(F32)
        for k in range(1, self.geo.X):
            self.xcopy(k).wait_recv()
            total += self.xb(k)[...].astype(F32)
        return total

    def drain(self):
        for k in range(self.geo.X):
            self.ccopy(k).wait_send()
            if k:
                self.xcopy(k).wait_send()


class DpScatter:
    def __init__(self, geo, me, part, ybuf, zbuf, ys, yr, zs, zr, finish, first_z=1 << 20, zbuf2=None, zs2=None, zr2=None):
        self.__dict__.update(locals())

    def owner(self, i):
        A, z = self.geo.A, self.me.z
        up, down = A - 1 - z, z
        both = jnp.minimum(up, down)
        half = i // 2
        early = jnp.where((i % 2 == 0) == (up >= down), A - 1 - half, half)
        late = jnp.where(up > down, A - 1 - (i - both), i - both)
        return jnp.where(i == A - 1, z, jnp.where(i < 2 * both, early, late))

    def ycopy(self, t, p):
        me = self.me
        return remote(
            self.part(p, t * 2 + 1 - me.y), self.ybuf(p, t), self.ys.at[t, p], self.yr.at[t, p], me.dev(y=1 - me.y)
        )

    def zparts(self, t, slot, p, other):
        if other:
            return self.zbuf2(p, slot), self.zs2.at[t, p - self.first_z], self.zr2.at[slot, p - self.first_z]
        return self.zbuf(p, slot), self.zs.at[t, p], self.zr.at[slot, p]

    def mine(self, t, p, other=False):
        return self.part(p, t * 2 + (1 - self.me.y if other else self.me.y))

    def zslot(self, up, t):
        return jnp.where(up, self.geo.A - 1 - t, self.geo.A - t)

    def zcopy(self, t, p, other=False):
        me = self.me
        up = t > me.z
        dst, ss, rs = self.zparts(t, self.zslot(up, t), p, other)
        return remote(self.mine(t, p, other), dst, ss, rs, me.dev(z=jnp.where(up, me.z + 1, me.z - 1)))

    def zarrive(self, up, t, p, other=False):
        here, ss, rs = self.zparts(t, self.zslot(up, t), p, other)
        remote(here, here, ss, rs, self.me.dev(y=1 - self.me.y)).wait_recv()
        return here[...].astype(F32)

    def ysend(self, i, p):
        self.ycopy(self.owner(i), p).start()

    def arrived(self, t, p, base, put, other=False):
        geo, me = self.geo, self.me

        @pl.when(me.z == 0)
        def _():
            put(base() + self.zarrive(False, t, p, other))

        @pl.when(me.z == geo.A - 1)
        def _():
            put(base() + self.zarrive(True, t, p, other))

        @pl.when((me.z > 0) & (me.z < geo.A - 1))
        def _():
            put(base() + self.zarrive(True, t, p, other) + self.zarrive(False, t, p, other))

    def onward(self, t, p, base, other=False, plain=False):
        geo, me = self.geo, self.me
        mine = self.mine(t, p, other)
        up = t > me.z
        comes = (up & (me.z > 0)) | (jnp.logical_not(up) & (me.z < geo.A - 1))

        @pl.when(comes)
        def _():
            mine[...] = (base() + self.zarrive(up, t, p, other)).astype(BF)

        if not plain:

            @pl.when(jnp.logical_not(comes))
            def _():
                mine[...] = base().astype(BF)

        self.zcopy(t, p, other).start()

    def event(self, i, p):
        t = self.owner(i)
        mine = self.mine(t, p)
        own = lambda: mine[...].astype(F32)
        if p >= self.first_z:
            theirs = self.mine(t, p, True)
            their = lambda: theirs[...].astype(F32)
            if i < self.geo.A - 1:
                self.onward(t, p, their, True, True)
                self.onward(t, p, own, False, True)
            else:
                self.arrived(t, p, their, lambda v: theirs.__setitem__(..., v.astype(BF)), True)
                self.ycopy(t, p).start()
            return
        self.ycopy(t, p).wait_recv()
        both = lambda: own() + self.ybuf(p, t)[...].astype(F32)
        if i == self.geo.A - 1:
            self.arrived(t, p, both, lambda v: self.finish(p, v))
        else:
            self.onward(t, p, both)

    def last(self, p):
        t = self.me.z
        mine = self.mine(t, p)
        self.ycopy(t, p).wait_recv()
        both = lambda: mine[...].astype(F32) + self.ybuf(p, t)[...].astype(F32)
        self.arrived(t, p, both, lambda v: self.finish(p, v))

    def drain(self, p, second=False):
        for i in range(self.geo.A):
            t = self.owner(i)
            if not second or i == self.geo.A - 1:
                self.ycopy(t, p).wait_send()
            if i < self.geo.A - 1:
                for other in (False, True) if second else (False,):
                    self.zcopy(t, p, other).wait_send()


def backward_kernel(
    geo, x_in, iWA, iqkv, iKV, iP, imixed, ihid, iX2, iC, iact, ipart, igain,
    of, oa, olayer, oinput,
    G, XC, act, yb, zb, WA, ayb, azb, cb, xb, xv, hid, qkv, KV, mixed, pk, px, pst, kcb, kxb, zb2,
    hgrad, gbias, extra, gain, packed, sums, pout, onehot,
    local, psem, outs, csem, osem, pxs, pxr, kcs, kcr, kxs, kxr, acs, acr, axs, axr, ys, yr, zs, zr, zs2, zr2, ays, ayr, azs, azr,
):
    me = Place(geo)
    R, RH, NH, dp, X, T, N, I = geo.R, geo.RH, geo.NH, geo.dp, geo.X, geo.T, geo.N, geo.I
    I4, S, L, A, NP = geo.I4, geo.seq, geo.L, geo.A, geo.NP
    block = lambda i, n: pl.ds(pl.multiple_of(i * n, 16), n)
    dKV = act.at[0, :, : 2 * I]
    dM, dq = act.at[1, :T, :I], act.at[1, T : 2 * T, :I]
    half = S * I4 // 2
    rights = [act.at[2, : 2 * T, :half], act.at[2, 2 * T : 4 * T, :half]]
    lefts = XC.at[N : N + 2 * T, :]
    hlow = lefts.at[T:, :]
    ds = pk.at[0, :, : L + 256]
    loads = [
        (iact.at[2], act.at[2]), (iact.at[0], act.at[0]), (iact.at[1], act.at[1]), (ipart.at[:, 0], pk), (ihid, hid), (igain, gain),
        (iWA, WA), (iKV, KV), (iqkv, qkv), (imixed, mixed), (x_in, xv),
    ]
    loads = [pltpu.make_async_copy(src, dst, local.at[i]) for i, (src, dst) in enumerate(loads)]
    turns = DpScatter(geo, me, *[None] * 8)

    def columns_in(i, n):
        t = turns.owner(i)
        lanes = pl.ds(pl.multiple_of(t * 2 * R, 128), 2 * R)
        src, dst = ((iX2, XC.at[:L, lanes]), (iC, XC.at[L:, lanes]))[n]
        return pltpu.make_async_copy(src.at[:, lanes], dst, csem.at[n, i])

    loads[0].start()
    columns_in(0, 1).start()
    loads[1].start()
    columns_in(0, 0).start()
    loads[2].start()
    for i in range(1, A):
        for n in (1, 0):
            columns_in(i, n).start()
    for copy in loads[3:]:
        copy.start()
    hd = I // geo.H
    per = 128 // hd

    def pload(t, e):
        return pltpu.make_async_copy(iP.at[t * per + e], pst.at[e], psem.at[e])

    for e in range(per):
        pload(0, e).start()
    enter(geo, me)

    def pcopy(n, k):
        to = me.dev(x=lax.rem(me.x + k, X))
        return remote(ipart.at[n, k], px.at[n, k - 1], pxs.at[n, k - 1], pxr.at[n, k - 1], to)

    for n in range(2):
        for k in range(1, X):
            pcopy(n, k).start()

    def rows_of(g, p):
        return pl.ds(pl.multiple_of(g * R + (p % NH) * RH, 16), RH)

    def piece(buf, i, p):
        return buf.at[i, p // NH, pl.ds(pl.multiple_of((p % NH) * RH, 16), RH), :]

    def out_f(p):
        rows = pl.ds(pl.multiple_of((p % NH) * RH, 16), RH)
        return pltpu.make_async_copy(sums.at[p // NH, rows, :], of.at[p // NH, rows, :], osem.at[p])

    def finish_f(p, value):
        sums[p // NH, pl.ds(pl.multiple_of((p % NH) * RH, 16), RH), :] = value
        out_f(p).start()

    last = NP - 1
    ffn = DpScatter(
        geo, me, lambda p, g: G.at[p // NH, rows_of(g, p), :], lambda p, t: piece(yb, t, p),
        lambda p, i: piece(zb, i, p), ys, yr, zs, zr, finish_f,
        last, lambda p, i: zb2.at[i], zs2, zr2,
    )
    def weight_rows(i):
        t = ffn.owner(i)
        lanes = pl.ds(pl.multiple_of(t * 2 * R, 128), 2 * R)
        rows = pl.ds(pl.multiple_of(t * 2 * R, 16), 2 * R)
        for m in (2, 0, 1):
            if isinstance(i, int):
                loads[{2: 0, 0: 1, 1: 2}[m]].wait()
            if m != 1:
                columns_in(i, m // 2).wait()
            left = XC[:L, lanes] if m < 2 else XC[L:, lanes]
            G[m, rows, :] = dot(left, act[m], TN).astype(BF)

            def go(h):
                p = m * NH + h

                @pl.when((p < last) & ((i < A - 1) | (p < NP // 2)))
                def _():
                    ffn.ysend(i, p)

            loop(NH, go)
            if isinstance(i, int) and m == 2:
                run(1, 0)


    edge = (me.z == 0) | (me.z == A - 1)
    queues = [(kind, [(i, p) for i in range(A) for p in (last, *range(last))]) for kind in (edge, jnp.logical_not(edge))]

    def run(*counts):
        for (kind, events), count in zip(queues, counts):
            now = [events.pop(0) for _ in range(min(count, len(events)))]
            if now:

                @pl.when(kind)
                def _():
                    for i, p in now:
                        ffn.event(i, p)

    weight_rows(0)
    loop(A - 1, lambda i: weight_rows(i + 1))
    place_columns(geo, pout)
    place_buckets(geo, onehot)
    run(2, 0)

    for i in range(3, len(loads)):
        loads[i].wait()
    for k in range(1, X):
        pcopy(0, k).wait_recv()
    grad = pk[0].astype(F32)
    for k in range(1, X):
        grad += px[0, k - 1].astype(F32)
    hidden = hid[...]
    scale = lax.rsqrt(jnp.sum(hidden * hidden, axis=-1, keepdims=True) / np.float32(geo.D) + EPSILON)
    unit = hidden * scale
    gain_two = jnp.sum(grad * unit, axis=0, keepdims=True)
    pull = grad * gain[1:2, :]
    inner = jnp.sum(pull * unit, axis=-1, keepdims=True) / np.float32(geo.D)
    cot = XC[pl.ds(pl.multiple_of(L + me.s * T, 16), T), :].astype(F32)
    total = cot + scale * (pull - unit * inner)
    hgrad[...] = total
    hlow[...] = total.astype(BF)
    columns = jnp.concatenate([dot(hlow[...], WA[s]) for s in range(S)], axis=1).astype(BF)
    dM[...] = dot(columns, pout[...], NT).astype(BF)
    ds[...] = jnp.zeros_like(ds)
    gbias[...] = jnp.zeros_like(gbias)
    run(3, 1)

    def pair(t):
        lanes = pl.ds(pl.multiple_of(t * 128, 128), 128)
        vlanes = pl.ds(pl.multiple_of(I + t * 128, 128), 128)
        head = lax.broadcasted_iota(jnp.int32, (1, 128), 1) // hd
        keys, values, queries, back = KV[:, lanes], KV[:, vlanes], qkv[:, lanes], dM[:, lanes]
        zero = jnp.zeros_like(queries)
        q_grad = jnp.zeros((T, 128), F32)
        k_grad = jnp.zeros((L, 128), F32)
        v_grad = jnp.zeros((L, 128), F32)
        for e in range(per):
            h = t * per + e
            own_back = jnp.where(head == e, back, zero)
            pload(t, e).wait()
            probs = pst[e]
            prob_grad = dot(own_back, values, NT)
            both = jnp.sum(probs * prob_grad, axis=-1, keepdims=True)
            score = (probs * (prob_grad - both)).astype(BF)
            v_grad += dot(probs.astype(BF), own_back, TN)

            @pl.when(t + 1 < I // 128)
            def _():
                pload(t + 1, e).start()

            q_grad = jnp.where(head == e, dot(score, keys), q_grad)
            k_grad += dot(score, jnp.where(head == e, queries, zero), TN)
            ds[:, 128 : 128 + L] = score
            near = jnp.zeros((128, 384), F32)
            place = lax.broadcasted_iota(jnp.int32, (1, L), 1)
            low = jnp.zeros((1, 1), F32)
            high = jnp.zeros((1, 1), F32)
            for b in range(T // 128):
                row_block = me.s * (T // 128) + b
                near += ds[b * 128 : (b + 1) * 128, pl.ds(pl.multiple_of(row_block * 128, 128), 384)].astype(F32)
                sums = jnp.sum(score[b * 128 : (b + 1) * 128, :].astype(F32), axis=0, keepdims=True)
                low += jnp.sum(jnp.where(place < (row_block - 1) * 128, sums, 0.0), axis=-1, keepdims=True)
                high += jnp.sum(jnp.where(place >= (row_block + 2) * 128, sums, 0.0), axis=-1, keepdims=True)
            near = jnp.concatenate([jnp.zeros((128, 128), F32), near], axis=1)
            line = jnp.sum(shear(near, -1), axis=0, keepdims=True)
            spot = lax.broadcasted_iota(jnp.int32, (1, 512), 1)
            line += jnp.where(spot == 0, low, 0.0) + jnp.where(spot == 511, high, 0.0)
            gbias[pl.ds(h, 1), :] = line
        dq[:, lanes] = q_grad.astype(BF)
        dKV[:, lanes] = k_grad.astype(BF)
        dKV[:, vlanes] = v_grad.astype(BF)

    def key_scatter(i):
        lanes = slice(i * 128, (i + 1) * 128)
        return SeqScatter(
            geo, me, lambda s: dKV.at[block(s, T), lanes], lambda k: kcb.at[k, :, lanes], lambda k: kxb.at[k - 1, :, lanes],
            kcs.at[i], kcr.at[i], kxs.at[i], kxr.at[i],
        )

    pairs = I // 128
    scatters = [(key_scatter(t), key_scatter(pairs + t)) for t in range(pairs)]
    for t in range(pairs):
        pair(t)
        for one in scatters[t]:
            one.to_core()
        if t:
            for one in scatters[t - 1]:
                one.to_x()
        run(*((1, 1), (1, 1), (2, 1))[min(t, 2)])

    for k in range(1, X):
        pcopy(1, k).wait_recv()
    total = hid[...] + pk[1].astype(F32)
    for k in range(1, X):
        total += px[1, k - 1].astype(F32)
    packed[...] = pack(geo, total)
    layer_out = pltpu.make_async_copy(packed, olayer, outs.at[0])
    layer_out.start()
    for one in scatters[-1]:
        one.to_x()
    run(1, 1)
    tokens = xv[...].astype(F32)
    scale = lax.rsqrt(jnp.sum(tokens * tokens, axis=-1, keepdims=True) / np.float32(geo.D) + EPSILON)
    lefts[:T, :] = (tokens * scale * gain[0:1, :]).astype(BF)
    columns = dot(mixed[...], pout[...]).astype(BF)
    for i, right in enumerate(rights):
        right[T:, :] = columns[:, i * half : (i + 1) * half]
    run(2, 2)
    key_value = [jnp.concatenate([one[n].meet() for one in scatters], axis=1).astype(BF) for n in range(2)]
    run(0, 3)
    columns = jnp.zeros((T, S * I4), F32)
    for kind, value in enumerate((dq[...], *key_value)):
        columns += pltpu.roll(dot(value, pout[...]), S * I4 - (3 - kind) * (I4 // 4), 1)
    columns = columns.astype(BF)
    for i, right in enumerate(rights):
        right[:T, :] = columns[:, i * half : (i + 1) * half]
    grad = jnp.zeros((T, N), F32)
    for s in range(S):
        grad += dot(columns[:, s * I4 : (s + 1) * I4], WA[s], NT)
    unit = tokens * scale
    gain_one = jnp.sum(grad * unit, axis=0, keepdims=True)
    pull = grad * gain[0:1, :]
    inner = jnp.sum(pull * unit, axis=-1, keepdims=True) / np.float32(geo.D)
    layer_out.wait()
    packed[...] = pack(geo, hgrad[...] + scale * (pull - unit * inner))
    input_out = pltpu.make_async_copy(packed, oinput, outs.at[1])
    input_out.start()

    table = dot(onehot[...], gbias[...].astype(BF), NT)
    if I4 > 128:
        table = jnp.concatenate([table, jnp.zeros((dp * 16, I4 - 128), F32)], axis=1)
    extra[...] = table
    for g in range(dp):
        for e, line in enumerate((gain_one, gain_two)):
            at = g * 16 + 16 - geo.E + e
            extra[at : at + 1, :R] = line[:, g * R : (g + 1) * R]

    def part_g(s, g):
        return XC.at[block(g, R), pl.ds(pl.multiple_of(s * I4, 128), I4)]

    att = DpScatter(
        geo, me, lambda p, g: part_g(me.s, g), lambda p, t: ayb.at[t], lambda p, i: azb.at[i],
        ays, ayr, azs, azr, lambda p, value: oa.__setitem__(..., value),
    )
    def turn(j):
        t = att.owner(j // 2)
        return t * 2 + jnp.where(j % 2 == 0, 1 - me.y, me.y)

    def scatter(g):
        return SeqScatter(
            geo, me, lambda s: part_g(s, g), lambda k: cb.at[k, block(g, R), :], lambda k: xb.at[k - 1, block(g, R), :],
            acs.at[g], acr.at[g], axs.at[g], axr.at[g],
        )

    def attention_rows(i):
        t = att.owner(i)
        lanes = pl.ds(pl.multiple_of(t * 2 * R, 128), 2 * R)
        rows = pl.ds(pl.multiple_of(t * 2 * R, 16), 2 * R)
        for n, right in enumerate(rights):
            XC[rows, n * half : (n + 1) * half] = dot(lefts[:, lanes], right[...], TN).astype(BF)
        for y in range(2):
            g = t * 2 + y
            rows = pl.ds(pl.multiple_of(g * R + R - 16, 16), 16)
            more = extra[pl.ds(pl.multiple_of(g * 16, 16), 16), :]
            for s in range(S):
                lane = slice(s * I4, (s + 1) * I4)
                XC[rows, lane] = (XC[rows, lane].astype(F32) + more).astype(BF)
        scatter(t * 2 + 1 - me.y).to_core()
        scatter(t * 2 + me.y).to_core()

    for i in range(A):
        attention_rows(i)
        run((2, 0, 2, 1)[min(i, 3)], (3, 1, 1, 1)[min(i, 3)])
    held = [p for p in range(last) if p >= NP // 2]
    for j in range(dp):
        scatter(turn(j)).to_x()
    run(0, 1)
    for j in range(dp):
        g = turn(j)
        part_g(me.s, g)[...] = scatter(g).meet().astype(BF)
        if j % 2 == 0:
            att.ysend(j // 2, 0)
        elif held:
            ffn.ysend(A - 1, held.pop(0))
        if j >= 2:
            run(1, 1)
        if j % 2 and j >= 3:
            att.event((j - 3) // 2, 0)
    while held:
        ffn.ysend(A - 1, held.pop(0))
    att.event(A - 1, 0)
    run(*(len(events) for _, events in queues))
    ffn.last(last)

    for n in range(2):
        for k in range(1, X):
            pcopy(n, k).wait_send()
    for both in scatters:
        for one in both:
            one.drain()
    loop(dp, lambda g: scatter(g).drain())
    att.drain(0)
    loop(last, ffn.drain)
    ffn.drain(last, True)
    input_out.wait()
    loop(NP, lambda p: out_f(p).wait())


def backward(geo, *saved):
    dma = pltpu.SemaphoreType.DMA
    S, N, F, T, L, I, X, I4, A, R = geo.seq, geo.N, geo.F, geo.T, geo.L, geo.I, geo.X, geo.I4, geo.A, geo.R
    per = 128 // (I // geo.H)
    V = pltpu.VMEM
    scratch = [
        V((3, N, F), BF), V((2 * L, N), BF), V((3, L, F), BF), V((A, 3, R, F), BF), V((A + 1, 3, R, F), BF),
        V((S, N, I4), BF), V((A, R, I4), BF), V((A + 1, R, I4), BF),
        V((X, N, I4), BF), V((X - 1, N, I4), BF),
        V((T, N), BF), V((T, N), F32), V((T, 3 * I), BF), V((L, 2 * I), BF), V((T, I), BF),
        V((2, T, N), BF), V((2, X - 1, T, N), BF), V((per, T, L), F32),
        V((X, T, 2 * I), BF), V((X - 1, T, 2 * I), BF), V((A + 1, geo.RH, F), BF),
        V((T, N), F32), V((128, 512), F32), V((geo.dp * 16, I4), F32), V((8, N), F32), V((geo.D, T), BF), V((3, R, F), F32),
        V((I, S * I4), BF), V((geo.dp * 16, 512), BF),
        dma((11,)), dma((per,)), dma((2,)), dma((2, A)), dma((geo.NP,)),
        dma((2, X - 1)), dma((2, X - 1)), dma((2 * I // 128, X)), dma((2 * I // 128, X)), dma((2 * I // 128, X - 1)), dma((2 * I // 128, X - 1)),
        dma((geo.dp, X)), dma((geo.dp, X)), dma((geo.dp, X - 1)), dma((geo.dp, X - 1)),
        dma((A, geo.NP)), dma((A, geo.NP)), dma((A, geo.NP)), dma((A + 1, geo.NP)),
        dma((A, 1)), dma((A + 1, 1)),
        dma((A, 1)), dma((A, 1)), dma((A, 1)), dma((A + 1, 1)),
    ]
    return pl.pallas_call(
        functools.partial(backward_kernel, geo),
        out_shape=[
            jax.ShapeDtypeStruct((3, R, F), F32), jax.ShapeDtypeStruct((R, I4), F32),
            jax.ShapeDtypeStruct((geo.D, T), BF), jax.ShapeDtypeStruct((geo.D, T), BF),
        ],
        in_specs=[pl.BlockSpec(memory_space=pl.ANY)] * len(saved),
        out_specs=[pl.BlockSpec(memory_space=v) for v in (pl.ANY, pltpu.VMEM, pl.ANY, pl.ANY)],
        scratch_shapes=scratch,
        compiler_params=pltpu.CompilerParams(collective_id=2, has_side_effects=True, vmem_limit_bytes=63 << 20),
        name="backward",
    )(*saved)


def finish_kernel(geo, rows, features, layer, grad, *rest):
    outs, (held, blocks, main, query, keyval, output, gains, table, sem) = rest[:9], rest[9:]
    W, own = geo.W, geo.I4 // 4
    moves = [
        (rows, main, None), (layer, held.at[0], outs[0]), (grad, held.at[1], outs[1]),
        (features.at[0], blocks.at[0], outs[5].at[0]), (features.at[1], blocks.at[1], outs[5].at[1]),
        (features.at[2], blocks.at[2], outs[6]),
    ]
    arrive = [pltpu.make_async_copy(src, mid, sem.at[0, i]) for i, (src, mid, _) in enumerate(moves)]
    leave = [
        pltpu.make_async_copy(mid.at[:W, :] if i > 2 else mid, dst, sem.at[1, i])
        for i, (_, mid, dst) in enumerate(moves)
        if dst is not None
    ]
    for copy in arrive:
        copy.start()
    arrive[0].wait()
    query[...] = main[:W, :own]
    keyval[0] = main[:W, own : 2 * own]
    keyval[1] = main[:W, 2 * own : 3 * own]
    output[...] = main[:W, 3 * own :]
    gains[...] = main[geo.R - geo.E : geo.R - geo.TR, :W]
    table[...] = main[geo.R - geo.TR :, : geo.H]
    small = [(query, outs[2]), (keyval, outs[3]), (output, outs[4]), (gains, outs[7]), (table, outs[8])]
    small = [pltpu.make_async_copy(src, dst, sem.at[1, 6 + i]) for i, (src, dst) in enumerate(small)]
    for copy in small:
        copy.start()
    for copy, onward in zip(arrive[1:], leave):
        copy.wait()
        onward.start()
    for copy in small + leave:
        copy.wait()


def finish(geo, of, oa, layer, grad):
    W, own, F = geo.W, geo.I4 // 4, geo.F
    shapes = [
        (layer.shape, BF), (grad.shape, BF), ((W, own), F32), ((2, W, own), F32), ((W, own), F32), ((2, W, F), F32),
        ((W, F), F32), ((2, W), F32), ((geo.TR, geo.H), F32),
    ]
    V = pltpu.VMEM
    return pl.pallas_call(
        functools.partial(finish_kernel, geo),
        out_shape=[jax.ShapeDtypeStruct(*v) for v in shapes],
        in_specs=[pl.BlockSpec(memory_space=pl.ANY)] * 4,
        out_specs=[pl.BlockSpec(memory_space=pl.ANY)] * 9,
        scratch_shapes=[
            V((2, *layer.shape), BF), V((3, geo.R, F), F32), V((geo.R, geo.I4), F32),
            *[V(*shapes[i]) for i in (2, 3, 4, 7, 8)], pltpu.SemaphoreType.DMA((2, 11)),
        ],
        compiler_params=pltpu.CompilerParams(vmem_limit_bytes=63 << 20),
        name="finish",
    )(oa, of, layer, grad)


def spread_features(values, geo, width):
    lead = values.shape[:-1]
    blocks = values.reshape(*lead, geo.dp, width)
    return jnp.pad(blocks, [(0, 0)] * (len(lead) + 1) + [(0, geo.R - width)]).reshape(*lead, geo.dp * geo.R)


def pack_features(values, geo, width):
    lead = values.shape[:-1]
    return values.reshape(*lead, geo.dp, geo.R)[..., :width].reshape(*lead, geo.dp * width)


def general_path(
    axes, tokens, cotangent, lengths, w_query, w_key_value, w_output, w_gate_up, w_down, norm_gains, position_bias
):
    dp, seq = axes
    width, own_inner = w_query.shape
    table_rows, head_count = position_bias.shape
    geo = Geo(dp, seq, width, w_down.shape[1], 4 * own_inner, tokens.shape[1], head_count, table_rows)
    rows = geo.R
    model_width = geo.D
    bucket_count = table_rows * dp
    inner_width = geo.I
    head_dim = inner_width // head_count

    lanes = lambda v: jnp.pad(v, ((0, 0), (0, geo.I4 - v.shape[1])))
    wa = jnp.concatenate(
        [
            jnp.concatenate([w_query, w_key_value[0], w_key_value[1], w_output], axis=1).astype(BF),
            jnp.zeros((rows - width - geo.E, geo.I4), BF),
            lanes(norm_gains.astype(BF)),
            lanes(position_bias.astype(BF)),
        ],
        axis=0,
    )
    wf = jnp.pad(jnp.concatenate([w_gate_up, w_down[None]], axis=0).astype(BF), ((0, 0), (0, rows - width), (0, 0)))
    WF, WA = gather_weights(geo, wf, wa)

    blocks = WA[0].reshape(dp, rows, geo.I4)
    first_gain = blocks[:, rows - geo.E, :width].reshape(model_width).astype(F32)
    second_gain = blocks[:, rows - geo.E + 1, :width].reshape(model_width).astype(F32)
    table_full = blocks[:, rows - table_rows :, :head_count].reshape(bucket_count, head_count)
    real = WA.reshape(seq, dp, rows, 4, own_inner)[:, :, :width]
    parts = real.transpose(3, 1, 2, 0, 4).reshape(4, model_width, inner_width)
    query_full, keyval_full, output_full = parts[0], parts[1:3], parts[3]

    inputs = tokens[0].astype(jnp.float32)
    row_count = inputs.shape[0]
    normed = norm_scale(inputs, first_gain).astype(jnp.bfloat16)
    queries = jnp.dot(normed, query_full, preferred_element_type=jnp.float32).astype(jnp.bfloat16)
    projected = jnp.einsum(
        "td,sdi->sti", normed, keyval_full, preferred_element_type=jnp.float32
    ).astype(jnp.bfloat16)
    keys_all, values_all = (
        lax.all_gather(projected[0], "seq", axis=0, tiled=True),
        lax.all_gather(projected[1], "seq", axis=0, tiled=True),
    )
    incoming_low = cotangent[0]
    incoming = incoming_low.astype(jnp.float32)
    cot_all = lax.all_gather(spread_features(incoming_low, geo, width), "seq", axis=0, tiled=True)
    length_all = keys_all.shape[0]
    block_start = lax.axis_index("seq") * row_count
    query_pos = block_start + jnp.arange(row_count, dtype=jnp.int32)
    key_pos = jnp.arange(length_all, dtype=jnp.int32)
    buckets = bucket_ids(key_pos[None, :] - query_pos[:, None])
    bucket_range = jnp.arange(bucket_count, dtype=jnp.int32)
    onehot = (buckets[:, :, None] == bucket_range).astype(jnp.bfloat16)
    score_bias = jnp.einsum("tkb,bh->htk", onehot, table_full, preferred_element_type=jnp.float32)
    key_valid = key_pos < lengths[0]
    query_heads = queries.reshape(row_count, head_count, head_dim)
    key_heads = keys_all.reshape(length_all, head_count, head_dim)
    value_heads = values_all.reshape(length_all, head_count, head_dim)
    raw_scores = (
        jnp.einsum("thc,khc->htk", query_heads, key_heads, preferred_element_type=jnp.float32) + score_bias
    )
    scores = jnp.where(key_valid[None, None, :], raw_scores, NEGATIVE)
    probs = jax.nn.softmax(scores, axis=-1)
    probs_low = probs.astype(BF)
    mixed_heads = (
        jnp.einsum("htk,khc->thc", probs_low, value_heads, preferred_element_type=jnp.float32)
        .reshape(row_count, inner_width)
        .astype(jnp.bfloat16)
    )
    attended = jnp.einsum("tc,dc->td", mixed_heads, output_full, preferred_element_type=jnp.float32)
    hidden_one = inputs + attended
    normed_two = norm_scale(hidden_one, second_gain).astype(jnp.bfloat16)
    normed_two_all = lax.all_gather(spread_features(normed_two, geo, width), "seq", axis=0, tiled=True)

    gate = jnp.dot(normed_two_all, WF[0], preferred_element_type=F32)
    upward = jnp.dot(normed_two_all, WF[1], preferred_element_type=F32)
    activated = gated(gate, upward).astype(BF)
    down_term = jnp.einsum("tf,df->td", activated, WF[2], preferred_element_type=F32)
    down_weight_grad = jnp.einsum("td,tf->df", cot_all, activated, preferred_element_type=F32)
    activated_grad = jnp.dot(cot_all, WF[2], preferred_element_type=F32)
    unused_value, gate_pull = jax.vjp(gated, gate, upward)
    gate_grad, upward_grad = gate_pull(activated_grad)
    gate_grad, upward_grad = gate_grad.astype(BF), upward_grad.astype(BF)
    gate_weight_grad = jnp.einsum("td,tf->df", normed_two_all, gate_grad, preferred_element_type=F32)
    up_weight_grad = jnp.einsum("td,tf->df", normed_two_all, upward_grad, preferred_element_type=F32)
    normed_two_term = jnp.einsum("tf,df->td", gate_grad, WF[0], preferred_element_type=F32) + jnp.einsum(
        "tf,df->td", upward_grad, WF[1], preferred_element_type=F32
    )
    down_sum = lax.psum_scatter(down_term.astype(BF), "seq", scatter_dimension=0, tiled=True)
    normed_two_sum = lax.psum_scatter(normed_two_term.astype(BF), "seq", scatter_dimension=0, tiled=True)
    outputs = (hidden_one + pack_features(down_sum, geo, width).astype(F32)).astype(BF)[None]
    normed_two_grad = pack_features(normed_two_sum, geo, width).astype(F32)
    gf = jnp.stack([gate_weight_grad.astype(BF), up_weight_grad.astype(BF), down_weight_grad.astype(BF)])

    unused_two, second_pull = jax.vjp(norm_scale, hidden_one, second_gain)
    hidden_norm_grad, second_gain_grad = second_pull(normed_two_grad)
    hidden_grad = incoming + hidden_norm_grad
    hidden_low = hidden_grad.astype(jnp.bfloat16)
    output_weight_grad = jnp.einsum("td,tc->dc", hidden_low, mixed_heads, preferred_element_type=jnp.float32)
    mixed_grad = jnp.einsum("td,dc->tc", hidden_low, output_full, preferred_element_type=jnp.float32).astype(
        jnp.bfloat16
    )
    grad_heads = mixed_grad.reshape(row_count, head_count, head_dim)
    prob_grad = jnp.einsum("thc,khc->htk", grad_heads, value_heads, preferred_element_type=jnp.float32)
    inner_sum = jnp.sum(probs * prob_grad, axis=-1, keepdims=True)
    score_grad = (probs * (prob_grad - inner_sum)).astype(jnp.bfloat16)
    query_act_grad = (
        jnp.einsum("htk,khc->thc", score_grad, key_heads, preferred_element_type=jnp.float32)
        .reshape(row_count, inner_width)
        .astype(jnp.bfloat16)
    )
    key_piece = jnp.einsum(
        "htk,thc->khc", score_grad, query_heads, preferred_element_type=jnp.float32
    ).reshape(length_all, inner_width)
    value_piece = jnp.einsum(
        "htk,thc->khc", probs_low, grad_heads, preferred_element_type=jnp.float32
    ).reshape(length_all, inner_width)
    own_terms = lax.psum_scatter(
        jnp.concatenate([key_piece, value_piece], axis=1).astype(jnp.bfloat16),
        "seq",
        scatter_dimension=0,
        tiled=True,
    )
    keyval_act_grad = jnp.stack([own_terms[:, :inner_width], own_terms[:, inner_width:]])
    query_weight_grad = jnp.einsum("td,tc->dc", normed, query_act_grad, preferred_element_type=jnp.float32)
    keyval_weight_grad = jnp.einsum("td,stc->sdc", normed, keyval_act_grad, preferred_element_type=jnp.float32)
    normed_grad = jnp.einsum(
        "tc,dc->td", query_act_grad, query_full, preferred_element_type=jnp.float32
    ) + jnp.einsum("stc,sdc->td", keyval_act_grad, keyval_full, preferred_element_type=jnp.float32)
    unused_three, first_pull = jax.vjp(norm_scale, inputs, first_gain)
    input_norm_grad, first_gain_grad = first_pull(normed_grad)
    input_grad = (hidden_grad + input_norm_grad).astype(jnp.bfloat16)[None]
    table_grad = jnp.einsum("htk,tkb->bh", score_grad, onehot, preferred_element_type=jnp.float32)

    grads = jnp.stack(
        [query_weight_grad, keyval_weight_grad[0], keyval_weight_grad[1], output_weight_grad]
    ).reshape(4, dp, width, seq, own_inner)
    grads = grads.transpose(3, 1, 2, 0, 4).reshape(seq, dp, width, geo.I4).astype(BF)
    wide = lambda v: jnp.pad(v, ((0, 0), (0, 0), (0, geo.I4 - v.shape[2])))
    more = jnp.concatenate(
        [
            jnp.zeros((dp, rows - width - geo.E, geo.I4), F32),
            wide(first_gain_grad.reshape(dp, 1, width)),
            wide(second_gain_grad.reshape(dp, 1, width)),
            wide(table_grad.reshape(dp, table_rows, head_count)),
        ],
        axis=1,
    ).astype(BF)
    ga = jnp.concatenate([grads, jnp.broadcast_to(more, (seq, *more.shape))], axis=2).reshape(seq, dp * rows, geo.I4)
    of, oa = scatter_grads(geo, gf, ga)

    main = oa[:width]
    query_part = main[:, :own_inner]
    keyval_part = jnp.stack([main[:, own_inner : 2 * own_inner], main[:, 2 * own_inner : 3 * own_inner]])
    output_part = main[:, 3 * own_inner :]
    gain_part = oa[rows - geo.E : rows - table_rows, :width]
    table_part = oa[rows - table_rows :, :head_count]
    return (
        outputs,
        input_grad,
        query_part,
        keyval_part,
        output_part,
        of[:2, :width],
        of[2, :width],
        gain_part,
        table_part,
    )

def fused_path(
    axes, tokens, cotangent, lengths, w_query, w_key_value, w_output, w_gate_up, w_down, norm_gains, position_bias
):
    geo = Geo(*axes, w_query.shape[0], w_down.shape[1], 4 * w_query.shape[1], tokens.shape[1], *position_bias.shape[::-1])
    saved = forward(
        geo, lengths, tokens[0].T, cotangent[0].T, w_query, w_key_value, w_output, w_gate_up, w_down, norm_gains, position_bias
    )
    outs = finish(geo, *backward(geo, *saved))
    return outs[0].T[None], outs[1].T[None], *outs[2:]


def per_device(axes, *arrays):
    tokens, w_query, w_down, position_bias = arrays[0], arrays[3], arrays[7], arrays[9]
    geo = Geo(*axes, w_query.shape[0], w_down.shape[1], 4 * w_query.shape[1], tokens.shape[1], position_bias.shape[1],
              position_bias.shape[0])
    aligned = geo.W % 8 == 0 and geo.F % 128 == 0 and geo.I4 % 128 == 0 and 2 * geo.R % 128 == 0 and geo.T % 128 == 0 and geo.I % 128 == 0
    aligned = aligned and max(2 * geo.I, geo.seq * geo.I4 // 2) <= geo.F and 4 * geo.T <= geo.L and geo.N + 2 * geo.T <= 2 * geo.L and geo.L + 256 <= geo.N
    small = (3 * geo.F + geo.seq * geo.I4 + 2 * geo.L) * geo.N * 2 <= 24 << 20
    return (fused_path if aligned and small else general_path)(axes, *arrays)


def solution(mesh):
    in_specs = (
        P("dp", "seq", None),
        P("dp", "seq", None),
        P("dp"),
        P("dp", "seq"),
        P(None, "dp", "seq"),
        P("dp", "seq"),
        P(None, "dp", "seq"),
        P("dp", "seq"),
        P(None, "dp"),
        P("dp", None),
    )
    out_specs = (
        P("dp", "seq", None),
        P("dp", "seq", None),
        P("dp", "seq"),
        P(None, "dp", "seq"),
        P("dp", "seq"),
        P(None, "dp", "seq"),
        P("dp", "seq"),
        P(None, "dp"),
        P("dp", None),
    )
    return jax.shard_map(
        functools.partial(per_device, (mesh.shape["dp"], mesh.shape["seq"])), mesh=mesh, in_specs=in_specs, out_specs=out_specs, check_vma=False
    )
```
